32 devices in a mesh: expert: 8 (over z, y), shard: 4 (over x, core).
Axes of the slice: x: 2, y: 2, z: 4, core: 2. Of those that a mesh axis runs over, the one named last changes fastest.
Arguments:
- tokens: bfloat16 [20480, 768], P(('expert', 'shard')), may hold values from -6 to 6
- gain_attn: bfloat16 [768], P('shard'), may hold values from 0.5 to 1.5
- w_query: bfloat16 [768, 768], P('shard'), may hold values from -0.21875 to 0.21875
- w_key: bfloat16 [768, 768], P('shard'), may hold values from -0.21875 to 0.21875
- w_value: bfloat16 [768, 768], P('shard'), may hold values from -0.21875 to 0.21875
- w_output: bfloat16 [768, 768], P('shard'), may hold values from -1.75 to 1.75
- rel_table: bfloat16 [12, 16], P('shard'), may hold values from -4 to 4
- gain_moe: bfloat16 [768], P('shard'), may hold values from 0.5 to 1.5
- router: bfloat16 [768, 8], P('shard'), may hold values from -0.15625 to 0.15625
- w_in: bfloat16 [8, 768, 3072], P('expert', 'shard'), may hold values from -0.21875 to 0.21875
- w_out: bfloat16 [8, 3072, 768], P('expert', 'shard'), may hold values from -0.15625 to 0.15625
- routes: int32 [20480, 2], P(('expert', 'shard')), may hold values from 0 to 7, all different within a row; in each aligned block of 640 rows (0 to 639, 640 to 1279, ...) at most 228 rows name the same one
- parents: int32 [8, 20], P('expert'), may hold values from -1 to 19, as said below
- cotangent: bfloat16 [20480, 768], P(('expert', 'shard')), may hold values from -6 to 6
Outputs:
- output: bfloat16 [20480, 768], P(('expert', 'shard'))
- grad_tokens: bfloat16 [20480, 768], P(('expert', 'shard'))
- grad_gain_attn: float32 [768], P('shard')
- grad_w_query: float32 [768, 768], P('shard')
- grad_w_key: float32 [768, 768], P('shard')
- grad_w_value: float32 [768, 768], P('shard')
- grad_w_output: float32 [768, 768], P('shard')
- grad_table: float32 [12, 16], P('shard')
- grad_gain_moe: float32 [768], P('shard')
- grad_router: float32 [768, 8], P('shard')
- grad_w_in: float32 [8, 768, 3072], P('expert', 'shard')
- grad_w_out: float32 [8, 3072, 768], P('expert', 'shard')
The draws below stay inside these ranges and needn't reach their ends.
Inputs may be any that keep to these rules, and one draw needn't show every extreme that they name: `routes`: in each aligned block of 640 rows (the tokens of one device) no expert is named by more than 228 rows; the two ids of a row differ. `parents`: segments 0 to 7 form the trunk: segment 0 is the root (parent -1) and each trunk segment is the parent of the next. 4 other segments, the last segment always among them, have segment 8 - 1 as parent; each of them is the parent of 2 of the remaining segments.
All inputs are finite; a program needn't handle non-finite values.
Results may differ from the reference program's by a relative error of at most 0.018.
Values may be sent and summed in bfloat16 or wider, within the bound.
No kernel may reach another device: no remote copies, remote signals or barrier semaphores. Data moves between devices by JAX's collectives and lax.ppermute only.
A program may use at most 192 MiB of HBM per device.

```python
import math
import jax
import jax.numpy as jnp
import numpy as np
from jax import lax

D = 768
H = 12
DH = 64
FF = 3072
NB = 16
TRUNK = 8
BRANCHES = 4
LEAVES = 2
SEG = 128
SEGS = 20
TREE = 2560
TOK_DEV = 640
TREES = 8
TOKENS = 20480
EXPERTS = 8
CAP = 228
DEVICES = 32


def draw_parents(key, part):
    key = jax.random.fold_in(key, 11)
    tree_keys = jax.random.split(key, TREES)

    def one_tree(tree_key):
        order = jax.random.permutation(tree_key, SEGS - TRUNK - 1) + TRUNK
        branch_pos = jnp.concatenate([jnp.array([SEGS - 1], jnp.int32), order[:BRANCHES - 1].astype(jnp.int32)])
        leaf_pos = order[BRANCHES - 1:].astype(jnp.int32)
        parent_row = jnp.zeros((SEGS,), jnp.int32)
        parent_row = parent_row.at[:TRUNK].set(jnp.arange(TRUNK, dtype=jnp.int32) - 1)
        parent_row = parent_row.at[branch_pos].set(TRUNK - 1)
        parent_row = parent_row.at[leaf_pos].set(jnp.repeat(branch_pos, LEAVES))
        return parent_row
    return jax.vmap(one_tree)(tree_keys)


def shard_levels(stream_key, dims, cuts, least, largest):
    loudness, own = 1.0, jax.random.fold_in(stream_key, 6)
    for axis_at, blocks in cuts:
        draws = jnp.exp(jax.random.uniform(jax.random.fold_in(own, axis_at), (blocks,), jnp.float32, least / len(cuts), largest / len(cuts)))
        loudness = loudness * jnp.repeat(draws, dims[axis_at] // blocks).reshape([-1 if axis == axis_at else 1 for axis in range(len(dims))])
    return loudness


def deal_out(own_key, own, number, rows, number_of, top, most, lean):
    ranking = jax.random.permutation(own_key, number_of)
    packed, common = portions_of(number_of, rows * top, most, lean, True), portions_of(number_of, rows * top, most, lean, False)
    places = jnp.arange(number_of)

    def named(tallies, turn):
        used = int((tallies > 0).sum())
        fixed = max(1, used // 4)
        moved = fixed + (places - fixed + turn * (used - fixed)) % max(1, number_of - fixed)
        return jnp.zeros((number_of,), jnp.int32).at[ranking[jnp.where(places < fixed, places, moved)]].set(jnp.asarray(tallies, jnp.int32))

    tallies = jnp.where(number % 4 == 0, named(packed, number // 4), named(common, number - number // 4 - 1))
    mixed = jax.random.permutation(jax.random.fold_in(own, 3), number_of)
    giver, receiver = mixed[0:number_of // 2 * 2:2], mixed[1:number_of // 2 * 2:2]
    margin = jnp.minimum(tallies[giver] - 1, most - tallies[receiver]) // 2
    margin = jnp.where((giver == ranking[0]) | (receiver == ranking[0]) | (tallies[receiver] == 0), 0, jnp.maximum(margin, 0))
    moved = jax.random.randint(jax.random.fold_in(own, 4), (number_of // 2,), 0, 1 << 20) % (margin + 1)
    tallies = tallies.at[giver].add(-moved).at[receiver].add(moved)
    members = jnp.searchsorted(jnp.cumsum(tallies), jnp.arange(rows * top), side="right").astype(jnp.int32)
    table = members.reshape(top, rows).T
    table = table[jax.random.permutation(jax.random.fold_in(own, 1), rows)]
    turn = jax.random.randint(jax.random.fold_in(own, 2), (rows, 1), 0, top)
    return jnp.take_along_axis(table, (jnp.arange(top)[None, :] + turn) % top, axis=1)


def portions_of(count, total, most, lean, full):
    portions = [(1 << 20) // math.isqrt(standing ** lean) + 1 for standing in range(1, count + 1)]
    largest = most if full else min(most, max(-(-total // count), total * portions[0] // sum(portions)))
    least = 1 if total - largest >= count - 1 else 0
    holding, surplus = [largest] + [least] * (count - 1), total - largest - least * (count - 1)
    while surplus > 0:
        free = [i for i in range(1, count) if holding[i] < largest] or [i for i in range(1, count) if holding[i] < most]
        whole, remaining = sum([portions[i] for i in free]), surplus
        for i in free:
            more = min(most - holding[i], max(1, remaining * portions[i] // whole), surplus)
            holding[i] = holding[i] + more
            surplus = surplus - more
    return np.array(holding)


def noise(key, shape, scale, limit, cuts=(), kind=jnp.bfloat16):
    drawn = scale * jax.random.normal(key, shape, jnp.float32)
    if cuts:
        drawn = drawn * shard_levels(key, shape, cuts, -0.22, 0.18)
    return jnp.clip(drawn, -limit, limit).astype(kind)


def setup_inputs(seed: int = 0) -> dict:
    streams_of = jax.random.split(jax.random.key(seed), 15)
    tokens = noise(streams_of[0], (TOKENS, D), 1.0, 6.0, ((0, 32),))
    gain_attn = jnp.clip(1.0 + 0.1 * jax.random.normal(streams_of[1], (D,), jnp.float32), 0.5, 1.5).astype(jnp.bfloat16)
    w_query = noise(streams_of[2], (D, D), D ** -0.5, 0.21875, ((0, 4),))
    w_key = noise(streams_of[3], (D, D), D ** -0.5, 0.21875, ((0, 4),))
    w_value = noise(streams_of[4], (D, D), D ** -0.5, 0.21875, ((0, 4),))
    w_output = noise(streams_of[5], (D, D), (max(D // 64, 4)) ** -0.5, 1.75, ((0, 4),))
    rel_table = noise(streams_of[6], (H, NB), 1.0, 4.0, ((0, 4),))
    gain_moe = jnp.clip(1.0 + 0.1 * jax.random.normal(streams_of[7], (D,), jnp.float32), 0.5, 1.5).astype(jnp.bfloat16)
    router = noise(streams_of[8], (D, EXPERTS), (2 * D) ** -0.5, 0.15625, ((0, 4),))
    w_in = noise(streams_of[9], (EXPERTS, D, FF), D ** -0.5, 0.21875, ((0, 8), (1, 4)))
    w_out = noise(streams_of[10], (EXPERTS, FF, D), (FF // 2) ** -0.5, 0.15625, ((0, 8), (1, 4)))
    routes_keys = jax.random.split(jax.random.fold_in(streams_of[11], 1), TOKENS // TOK_DEV)
    routes_turns = jax.random.permutation(jax.random.fold_in(streams_of[11], 3), TOKENS // TOK_DEV)
    routes = jax.vmap(lambda own, number: deal_out(jax.random.fold_in(streams_of[11], 2), own, number, TOK_DEV, EXPERTS, 2, CAP, 2))(routes_keys, routes_turns).reshape((TOKENS, 2))
    parents = draw_parents(jax.random.fold_in(streams_of[14], 71), 0)
    cotangent = noise(streams_of[13], (TOKENS, D), 1.0, 6.0, ((0, 32),))
    return {"tokens": tokens, "gain_attn": gain_attn, "w_query": w_query, "w_key": w_key, "w_value": w_value, "w_output": w_output, "rel_table": rel_table, "gain_moe": gain_moe, "router": router, "w_in": w_in, "w_out": w_out, "routes": routes, "parents": parents, "cotangent": cotangent}


THRESHOLDS = (1, 2, 3, 4, 5, 6, 7, 8, 12, 16, 24, 32, 48, 64, 96)
EPS = 1e-06
MASKED = -1e+30

@jax.custom_vjp
def low(v):
    return lax.optimization_barrier(v.astype(jnp.bfloat16)).astype(jnp.float32)

@jax.custom_vjp
def low_back(v):
    return v

def low_keep(v):
    return (low(v), None)

def low_pass(kept, grad):
    return (grad,)

def back_keep(v):
    return (v, None)

def back_low(kept, grad):
    return (low(grad),)
low.defvjp(low_keep, low_pass)
low_back.defvjp(back_keep, back_low)

def rounded(value):
    return low(low_back(value))

def matmul(left, right):
    return jnp.dot(left, right, precision=lax.Precision.HIGHEST, preferred_element_type=jnp.float32)

def tree_tables(parent_row):
    segment_ids = jnp.arange(SEGS, dtype=jnp.int32)
    parent_hot = parent_row[:, None] == segment_ids[None, :]
    identity = segment_ids[:, None] == segment_ids[None, :]
    ancestry = identity
    for hop_step in range(SEGS):
        ancestry = identity | jnp.any(parent_hot[:, :, None] & ancestry[None, :, :], axis=1)
    seg_depth = (lax.optimization_barrier(jnp.sum(ancestry.astype(jnp.int32), axis=1)) - 1) * SEG
    return (ancestry, seg_depth)

def pair_tables(ancestry, seg_depth, query_pos, key_pos):
    segment_ids = jnp.arange(SEGS, dtype=jnp.int32)
    query_seg = query_pos // SEG
    key_seg = key_pos // SEG
    query_hot = query_seg[:, None] == segment_ids[None, :]
    key_hot = key_seg[:, None] == segment_ids[None, :]
    query_depth = lax.optimization_barrier(jnp.sum(jnp.where(query_hot, seg_depth[None, :], 0), axis=1)) + query_pos % SEG
    key_depth = lax.optimization_barrier(jnp.sum(jnp.where(key_hot, seg_depth[None, :], 0), axis=1)) + key_pos % SEG
    path_keys = jnp.dot(ancestry.astype(jnp.float32), key_hot.astype(jnp.float32).T)
    linked = jnp.dot(query_hot.astype(jnp.float32), path_keys) > 0.5
    same_segment = query_seg[:, None] == key_seg[None, :]
    allowed = linked & (~same_segment | (key_pos[None, :] <= query_pos[:, None]))
    depth_gap = query_depth[:, None] - key_depth[None, :]
    bucket = jnp.zeros(depth_gap.shape, jnp.int32)
    for threshold in THRESHOLDS:
        bucket = bucket + (depth_gap >= threshold).astype(jnp.int32)
    return (allowed, bucket)

def rms_scaled(values, gain_row):
    factor = lax.rsqrt(lax.optimization_barrier(jnp.mean(values * values, axis=-1, keepdims=True)) + EPS)
    return values * factor * gain_row

def attend_tree(weights, tree_rows, parent_row):
    gain_attn, w_query, w_key, w_value, w_output, rel_table = weights
    normed = low(rms_scaled(tree_rows, gain_attn))
    queries = rounded(matmul(normed, w_query))
    keys_all = rounded(matmul(normed, w_key))
    values_all = rounded(matmul(normed, w_value))
    ancestry, seg_depth = tree_tables(parent_row)
    positions = jnp.arange(TREE, dtype=jnp.int32)
    allowed, bucket = pair_tables(ancestry, seg_depth, positions, positions)

    def split_heads(matrix):
        return matrix.reshape(TREE, H, DH).transpose(1, 0, 2)

    def one_head(head_items):
        head_query, head_key, head_value, table_row = head_items
        raw_scores = matmul(head_query, head_key.T) * DH ** (-0.5) + table_row[bucket]
        raw_scores = low_back(raw_scores)
        scores = jnp.where(allowed, raw_scores, MASKED)
        attn_prob = jax.nn.softmax(scores, axis=-1)
        return matmul(low(attn_prob), head_value)
    head_outs = lax.map(jax.checkpoint(one_head), (split_heads(queries), split_heads(keys_all), split_heads(values_all), rel_table))
    mixed_heads = rounded(head_outs.transpose(1, 0, 2).reshape(TREE, D))
    return tree_rows + low_back(matmul(mixed_heads, w_output))

def expert_slots(routes):
    flat_routes = routes.reshape(DEVICES, TOK_DEV * 2)
    expert_hot = (flat_routes[:, :, None] == jnp.arange(EXPERTS, dtype=jnp.int32)).astype(jnp.int32)
    earlier = jnp.cumsum(expert_hot, axis=1) - expert_hot
    slot_index = lax.optimization_barrier(jnp.sum(earlier * expert_hot, axis=-1))
    source = jnp.arange(DEVICES, dtype=jnp.int32)[:, None]
    return (flat_routes.reshape(-1), (source * CAP + slot_index).reshape(-1))

def moe_block(params, routes, parents):
    tokens, gain_attn, w_query, w_key, w_value, w_output, rel_table, gain_moe, router, w_in, w_out = params
    weights = (gain_attn, w_query, w_key, w_value, w_output, rel_table)
    tree_rows = tokens.reshape(TREES, TREE, D)
    after_attn = lax.map(jax.checkpoint(lambda tree_items: attend_tree(weights, tree_items[0], tree_items[1])), (tree_rows, parents))
    after_attn = after_attn.reshape(TOKENS, D)
    normed_moe = low(rms_scaled(after_attn, gain_moe))
    logits = low_back(matmul(normed_moe, router))
    routes_hot = routes[:, :, None] == jnp.arange(EXPERTS, dtype=jnp.int32)
    chosen = lax.optimization_barrier(jnp.sum(jnp.where(routes_hot, logits[:, None, :], 0.0), axis=-1))
    gate_probs = jax.nn.softmax(chosen, axis=-1)
    expert_ids, places = expert_slots(routes)
    sent = low_back(jnp.repeat(normed_moe, 2, axis=0))
    buffers = jnp.zeros((EXPERTS, DEVICES * CAP, D), jnp.float32).at[expert_ids, places].set(sent)

    def one_expert(expert_items):
        row_block, first_w, second_w = expert_items
        inner_act = low_back(matmul(row_block, first_w))
        return rounded(matmul(low(jax.nn.gelu(inner_act)), second_w))
    outputs = lax.map(jax.checkpoint(one_expert), (buffers, w_in, w_out))
    returned = outputs[expert_ids, places].reshape(TOKENS, 2, D)
    return after_attn + lax.optimization_barrier(jnp.sum(gate_probs[:, :, None] * returned, axis=1))

def reference(tokens, gain_attn, w_query, w_key, w_value, w_output, rel_table, gain_moe, router, w_in, w_out, routes, parents, cotangent):
    params = tuple((member.astype(jnp.float32) for member in (tokens, gain_attn, w_query, w_key, w_value, w_output, rel_table, gain_moe, router, w_in, w_out)))
    result, pullback = jax.vjp(lambda *values: moe_block(values, routes, parents), *params)
    gradients = pullback(cotangent.astype(jnp.float32))
    return (result.astype(jnp.bfloat16), gradients[0].astype(jnp.bfloat16), gradients[1], gradients[2], gradients[3], gradients[4], gradients[5], gradients[6], gradients[7], gradients[8], gradients[9], gradients[10])
```

```python
import functools

import jax
import jax.numpy as jnp
from jax import lax
from jax.experimental import pallas as pl
from jax.experimental.pallas import tpu as pltpu
from jax.sharding import PartitionSpec as P

DH = 64
NB = 16
SEG = 128
SEGS = 20
TRUNK = 8

THRESHOLDS = (1, 2, 3, 4, 5, 6, 7, 8, 12, 16, 24, 32, 48, 64, 96)
EPS = 1e-06
MASKED = -1e30
HW = 256

F32 = jnp.float32
BF16 = jnp.bfloat16
VMEM = pl.BlockSpec(memory_space=pltpu.VMEM)
SMEM = pl.BlockSpec(memory_space=pltpu.SMEM)


def params(mib=56, **more):
    return pltpu.CompilerParams(vmem_limit_bytes=mib << 20, **more)


def dot(left, right, contract):
    return lax.dot_general(left, right, ((contract[0], contract[1]), ((), ())), preferred_element_type=F32)


NN = ((1,), (0,))
NT = ((1,), (1,))
TN = ((0,), (0,))


def rms_parts(values):
    factor = lax.rsqrt(jnp.mean(values * values, axis=-1, keepdims=True) + EPS)
    return values * factor, factor


def rms_grad(grad_out, gain_row, unit_rows, factor):
    scaled = grad_out * gain_row
    return factor * (scaled - unit_rows * jnp.mean(scaled * unit_rows, axis=-1, keepdims=True))


def bias_tiles(table):
    key = jnp.arange(SEG, dtype=jnp.int32)[:, None]
    query = jnp.arange(SEG, dtype=jnp.int32)[None, :]
    relative = table - table[:, NB - 1:]

    def looked_up(gap):
        bucket = jnp.zeros(gap.shape, jnp.int32)
        for threshold in THRESHOLDS:
            bucket = bucket + (gap >= threshold).astype(jnp.int32)
        total = jnp.zeros((table.shape[0],) + gap.shape, F32)
        for at in range(NB):
            total = total + jnp.where((bucket == at)[None], relative[:, at][:, None, None], 0.0)
        return total, bucket

    parent, parent_bucket = looked_up(query - key + SEG)
    own, own_bucket = looked_up(query - key)
    own = jnp.where((key <= query)[None], own, MASKED)
    own_bucket = jnp.where(key <= query, own_bucket, NB)
    tiles = jnp.stack([jnp.zeros_like(own), parent, own, jnp.full_like(own, MASKED)])
    tiles = tiles.transpose(0, 2, 1, 3).reshape(4, SEG, -1)
    return tiles, parent_bucket, own_bucket


def by_head(rows, heads):
    lane = lax.broadcasted_iota(jnp.int32, rows.shape, 1)
    zero = jnp.zeros_like(rows)
    return jnp.concatenate(
        [jnp.where((lane >= h * DH) & (lane < (h + 1) * DH), rows, zero) for h in range(heads)], axis=0
    )


def seg_at(index):
    return pl.ds(pl.multiple_of(index * SEG, SEG), SEG)


def attn_forward_kernel(heads, parent_ref, q_ref, k_ref, v_ref, vt_ref, bias_ref, out_ref, raw_ref, lse_ref):
    cols = heads * SEG
    trunk_len = TRUNK * SEG

    def finish(b, parts, v_parts):
        top = functools.reduce(jnp.maximum, [jnp.max(part, axis=0, keepdims=True) for part in parts])
        total = jnp.zeros((1, cols), F32)
        acc = jnp.zeros((HW, cols), F32)
        for part, vt in zip(parts, v_parts):
            prob = jnp.exp(part - top)
            total = total + jnp.sum(prob, axis=0, keepdims=True)
            acc = acc + dot(vt, prob.astype(BF16), NN)
        lse_ref[pl.ds(pl.multiple_of(b * 8, 8), 8), :] = jnp.broadcast_to(top + jnp.log(total), (8, cols))
        acc = acc / total
        pieces = [acc[h * DH:(h + 1) * DH, h * SEG:(h + 1) * SEG] for h in range(heads)]
        pieces.append(jnp.zeros((HW - heads * DH, SEG), F32))
        rows = jnp.transpose(jnp.concatenate(pieces, axis=0))
        raw_ref[seg_at(b), :] = rows
        out_ref[seg_at(b), :] = rows[:, :heads * DH].astype(BF16)

    def trunk_step(b, carry):
        q3 = by_head(q_ref[seg_at(b), :] * jnp.asarray(DH ** -0.5, BF16), heads)
        scores = dot(k_ref[0:trunk_len, :], q3, NT)
        parts = [
            scores[i * SEG:(i + 1) * SEG] + bias_ref[jnp.clip(i - b + 2, 0, 3)] for i in range(TRUNK)
        ]
        finish(b, parts, [vt_ref[:, i * SEG:(i + 1) * SEG] for i in range(TRUNK)])
        return carry

    def other_step(b, carry):
        parent = parent_ref[b]
        leaf = (parent >= TRUNK).astype(jnp.int32)
        q3 = by_head(q_ref[seg_at(b), :] * jnp.asarray(DH ** -0.5, BF16), heads)
        scores = dot(k_ref[0:trunk_len, :], q3, NT)
        last = (TRUNK - 1) * SEG
        parts = [
            scores[:last],
            scores[last:] + bias_ref[1 - leaf],
            dot(k_ref[seg_at(parent), :], q3, NT) + bias_ref[3 - 2 * leaf],
            dot(k_ref[seg_at(b), :], q3, NT) + bias_ref[2],
        ]
        finish(b, parts, [vt_ref[:, :last], vt_ref[:, last:trunk_len], vt_ref[:, seg_at(parent)], vt_ref[:, seg_at(b)]])
        return carry

    lax.fori_loop(0, TRUNK, trunk_step, 0)
    lax.fori_loop(TRUNK, SEGS, other_step, 0)


def attn_backward_kernel(
    heads, parent_ref, q_ref, k_ref, v_ref, kt_ref, raw_ref, lse_ref, grad_ref, bias_ref,
    dq_ref, dk_ref, dv_ref, bins_ref, dk_acc, dv_acc,
):
    cols = heads * SEG
    trunk_len = TRUNK * SEG
    dk_acc[...] = jnp.zeros_like(dk_acc)
    dv_acc[...] = jnp.zeros_like(dv_acc)
    bins_ref[...] = jnp.zeros_like(bins_ref)

    def common(b):
        q3 = by_head(q_ref[seg_at(b), :] * jnp.asarray(DH ** -0.5, BF16), heads)
        grad = grad_ref[seg_at(b), :]
        g3 = by_head(grad, heads)
        raw = raw_ref[seg_at(b), :]
        product = by_head(grad.astype(F32) * raw, heads)
        high = product.astype(BF16)
        low = (product - high.astype(F32)).astype(BF16)
        ones = jnp.ones((8, HW), BF16)
        row_dot = (dot(ones, high, NT) + dot(ones, low, NT))[0:1]
        lse = lse_ref[pl.ds(pl.multiple_of(b * 8, 8), 1), :]
        return q3, g3, row_dot, lse

    def block(scores, grad_prob, row_dot, lse):
        prob = jnp.exp(scores - lse)
        grad_score = prob * (grad_prob - row_dot)
        return prob.astype(BF16), grad_score

    def write_dq(b, acc):
        pieces = [acc[h * DH:(h + 1) * DH, h * SEG:(h + 1) * SEG] for h in range(heads)]
        pieces.append(jnp.zeros((HW - heads * DH, SEG), F32))
        rows = jnp.transpose(jnp.concatenate(pieces, axis=0)) * DH ** -0.5
        dq_ref[seg_at(b), :] = rows[:, :heads * DH].astype(BF16)

    def trunk_step(b, carry):
        q3, g3, row_dot, lse = common(b)
        acc = jnp.zeros((HW, cols), F32)
        for i in range(TRUNK):
            at = slice(i * SEG, (i + 1) * SEG)
            kind = jnp.clip(i - b + 2, 0, 3)
            scores = dot(k_ref[at, :], q3, NT) + bias_ref[kind]
            prob, grad_score = block(scores, dot(v_ref[at, :], g3, NT), row_dot, lse)
            bins_ref[kind] += grad_score
            grad_score = grad_score.astype(BF16)
            dv_acc[at, :] += dot(prob, g3, NN)
            dk_acc[at, :] += dot(grad_score, q3, NN)
            acc = acc + dot(kt_ref[:, at], grad_score, NN)
        write_dq(b, acc)
        return carry

    def other_step(b, carry):
        parent = parent_ref[b]
        leaf = (parent >= TRUNK).astype(jnp.int32)
        q3, g3, row_dot, lse = common(b)
        acc = jnp.zeros((HW, cols), F32)
        far = jnp.zeros((SEG, cols), F32)
        last = (TRUNK - 1) * SEG
        for i in range(TRUNK + 2):
            if i < TRUNK:
                at = slice(i * SEG, (i + 1) * SEG)
            else:
                at = seg_at(parent if i == TRUNK else b)
            scores = dot(k_ref[at, :], q3, NT)
            kind = None
            if i >= TRUNK - 1:
                kind = (1 - leaf, 3 - 2 * leaf, 2)[i - TRUNK + 1]
                scores = scores + bias_ref[kind]
            prob, grad_score = block(scores, dot(v_ref[at, :], g3, NT), row_dot, lse)
            if kind is None:
                far = far + grad_score
            else:
                bins_ref[kind] += grad_score
            grad_score = grad_score.astype(BF16)
            dv_acc[at, :] += dot(prob, g3, NN)
            dk_acc[at, :] += dot(grad_score, q3, NN)
            acc = acc + dot(kt_ref[:, at], grad_score, NN)
        bins_ref[0] += far
        write_dq(b, acc)
        return carry

    lax.fori_loop(0, TRUNK, trunk_step, 0)
    lax.fori_loop(TRUNK, SEGS, other_step, 0)
    dk_ref[...] = dk_acc[:, :heads * DH].astype(BF16)
    dv_ref[...] = dv_acc[:, :heads * DH].astype(BF16)


def one_hot_rows(first, count, places_ref):
    tokens = places_ref.shape[1]
    slot = first + lax.broadcasted_iota(jnp.int32, (count, tokens), 0)
    hit = (slot == places_ref[0:1, :]) | (slot == places_ref[1:2, :])
    return jnp.where(hit, 1.0, 0.0).astype(BF16)


def send_rows(rows, places_ref, out_refs):
    first = 0
    for out_ref in out_refs:
        slots = out_ref.shape[0]
        step = 128
        while slots % step:
            step //= 2

        def one(i, carry, out_ref=out_ref, first=first, step=step):
            at = pl.multiple_of(i * step, step)
            hot = one_hot_rows(first + at, step, places_ref)
            out_ref[pl.ds(at, step), :] = dot(hot, rows, NN).astype(BF16)
            return carry

        lax.fori_loop(0, slots // step, one, 0, unroll=2 if (slots // step) % 2 == 0 else 1)
        first += slots


def dispatch_kernel(places_ref, rows_ref, *out_refs):
    send_rows(rows_ref[...], places_ref, out_refs)


def post_kernel(
    x_ref, mixed_ref, w_ref, gain_ref, router_ref, routes_ref, places_ref,
    after_ref, normed_ref, gates_ref, *out_refs,
):
    groups, _, width = mixed_ref.shape
    after = x_ref[...].astype(F32)
    for s in range(groups):
        after = after + dot(mixed_ref[s], w_ref[s * width:(s + 1) * width, :], NN)
    after_ref[...] = after
    unit, _ = rms_parts(after)
    normed = (unit * gain_ref[...]).astype(BF16)
    normed_ref[...] = normed
    send_rows(normed_ref[...], places_ref, out_refs)
    logits = dot(normed, router_ref[...], NN)
    expert = lax.broadcasted_iota(jnp.int32, logits.shape, 1)
    first = jnp.sum(jnp.where(expert == routes_ref[:, 0:1], logits, 0.0), axis=-1, keepdims=True)
    second = jnp.sum(jnp.where(expert == routes_ref[:, 1:2], logits, 0.0), axis=-1, keepdims=True)
    top = jnp.maximum(first, second)
    first, second = jnp.exp(first - top), jnp.exp(second - top)
    gates_ref[...] = jnp.concatenate([first / (first + second), second / (first + second)], axis=1)


def expert_kernel(
    me_ref, x_ref, g_ref, other_ref, router_ref, first_ref, second_ref,
    out_ref, dx_ref, gg_ref, grad_ref, act_ref, inner_ref, out_acc, dx_acc,
):
    step = pl.program_id(0)
    rows = x_ref.shape[0]
    part = 128
    while rows % part:
        part //= 2

    @pl.when(step == 0)
    def _():
        logits = dot(x_ref[...], router_ref[...], NN)
        expert = lax.broadcasted_iota(jnp.int32, logits.shape, 1)
        mine = jnp.sum(jnp.where(expert == me_ref[0], logits, 0.0), axis=-1, keepdims=True)
        its = jnp.sum(jnp.where(expert == other_ref[...], logits, 0.0), axis=-1, keepdims=True)
        top = jnp.maximum(mine, its)
        mine, its = jnp.exp(mine - top), jnp.exp(its - top)
        grad_ref[...] = (mine / (mine + its) * g_ref[...].astype(F32)).astype(BF16)
        out_acc[...] = jnp.zeros_like(out_acc)
        dx_acc[...] = jnp.zeros_like(dx_acc)

    def one(i, carry):
        at = pl.ds(pl.multiple_of(i * part, part), part)
        value = dot(x_ref[at, :], first_ref[...], NN)
        grad_act = dot(grad_ref[at, :], second_ref[...], NT)
        square = value * value
        half = 0.5 * value
        scale = 0.7978845608028654
        th = jnp.tanh(value * (scale + (scale * 0.044715) * square))
        act = (half + half * th).astype(BF16)
        slope = 0.5 + 0.5 * th + (half * (1.0 - th * th)) * (scale + (3 * scale * 0.044715) * square)
        inner = (grad_act * slope).astype(BF16)
        act_ref[at, :] = act
        inner_ref[at, :] = inner
        out_acc[at, :] += dot(act, second_ref[...], NN)
        dx_acc[at, :] += dot(inner, first_ref[...], NT)
        return carry

    lax.fori_loop(0, rows // part, one, 0, unroll=2 if (rows // part) % 2 == 0 else 1)

    @pl.when(step == pl.num_programs(0) - 1)
    def _():
        out = out_acc[...].astype(BF16)
        out_ref[...] = out
        dx_ref[...] = dx_acc[...].astype(BF16)
        gg_ref[...] = jnp.sum(out.astype(F32) * g_ref[...].astype(F32), axis=-1, keepdims=True)


def run_expert(me, rows, grads, other, router, first_w, second_w):
    count, width = rows.shape
    hidden = first_w.shape[1]
    block = 512
    whole = lambda shape: pl.BlockSpec(shape, lambda i: (0, 0))
    return pl.pallas_call(
        expert_kernel,
        grid=(hidden // block,),
        in_specs=[
            SMEM,
            whole((count, width)),
            whole((count, width)),
            whole((count, 1)),
            whole(router.shape),
            pl.BlockSpec((width, block), lambda i: (0, i)),
            pl.BlockSpec((block, width), lambda i: (i, 0)),
        ],
        out_specs=[
            whole((count, width)),
            whole((count, width)),
            whole((count, 1)),
            whole((count, width)),
            pl.BlockSpec((count, block), lambda i: (0, i)),
            pl.BlockSpec((count, block), lambda i: (0, i)),
        ],
        out_shape=[
            jax.ShapeDtypeStruct((count, width), BF16),
            jax.ShapeDtypeStruct((count, width), BF16),
            jax.ShapeDtypeStruct((count, 1), F32),
            jax.ShapeDtypeStruct((count, width), BF16),
            jax.ShapeDtypeStruct((count, hidden), BF16),
            jax.ShapeDtypeStruct((count, hidden), BF16),
        ],
        scratch_shapes=[pltpu.VMEM((count, width), F32), pltpu.VMEM((count, width), F32)],
        compiler_params=params(dimension_semantics=("arbitrary",)),
        cost_estimate=pl.CostEstimate(
            flops=8 * count * width * hidden, bytes_accessed=4 * width * hidden, transcendentals=count * hidden
        ),
    )(me, rows, grads, other, router, first_w, second_w)


def back_kernel(
    *refs, parts,
):
    ret_refs = refs[:parts]
    (
        gg_ref, places_ref, routes_ref, gates_ref, after_ref, gain_ref, router_ref, g_ref, w_ref,
        grad_after_ref, branch_ref, gmixed_ref, glogits_ref, ggain_ref,
    ) = refs[parts:]
    tokens = after_ref.shape[0]
    groups, _, width = gmixed_ref.shape
    part = 128
    ggain_ref[...] = jnp.zeros_like(ggain_ref)

    def one(i, carry):
        at = pl.ds(pl.multiple_of(i * part, part), part)
        place0, place1 = places_ref[at, 0:1], places_ref[at, 1:2]
        first = 0
        total = jnp.zeros((part, after_ref.shape[1]), F32)
        gg0 = jnp.zeros((part, 1), F32)
        gg1 = jnp.zeros((part, 1), F32)
        for ret_ref in ret_refs:
            slots = ret_ref.shape[0]
            slot = first + lax.broadcasted_iota(jnp.int32, (part, slots), 1)
            hit0, hit1 = slot == place0, slot == place1
            gg = gg_ref[0:1, first:first + slots]
            gg0 = gg0 + jnp.sum(jnp.where(hit0, gg, 0.0), axis=-1, keepdims=True)
            gg1 = gg1 + jnp.sum(jnp.where(hit1, gg, 0.0), axis=-1, keepdims=True)
            hot = jnp.where(hit0 | hit1, 1.0, 0.0).astype(BF16)
            total = total + dot(hot, ret_ref[...], NN)
            first += slots
        gate0, gate1 = gates_ref[at, 0:1], gates_ref[at, 1:2]
        mean = gate0 * gg0 + gate1 * gg1
        expert = lax.broadcasted_iota(jnp.int32, (part, router_ref.shape[1]), 1)
        glogits = jnp.where(expert == routes_ref[at, 0:1], gate0 * (gg0 - mean), 0.0) + jnp.where(
            expert == routes_ref[at, 1:2], gate1 * (gg1 - mean), 0.0
        )
        glogits = glogits.astype(BF16)
        glogits_ref[at, :] = glogits
        incoming = dot(glogits, router_ref[...], NT) + total
        unit, factor = rms_parts(after_ref[at, :])
        grad_after = g_ref[at, :].astype(F32) + rms_grad(incoming, gain_ref[...], unit, factor)
        ggain_ref[0:1, :] += jnp.sum(incoming * unit, axis=0, keepdims=True)
        grad_after_ref[at, :] = grad_after
        branch = grad_after.astype(BF16)
        branch_ref[at, :] = branch
        for s in range(groups):
            gmixed_ref[s, at, :] = dot(branch, w_ref[s * width:(s + 1) * width, :], NT).astype(BF16)
        return carry

    lax.fori_loop(0, tokens // part, one, 0)


def combine_kernel(*refs, parts):
    ret_refs = refs[:parts]
    places_ref, gates_ref, after_ref, out_ref = refs[parts:]
    part = 128

    def one(i, carry):
        at = pl.ds(pl.multiple_of(i * part, part), part)
        total = after_ref[at, :]
        for j in range(2):
            first = 0
            picked = jnp.zeros((part, after_ref.shape[1]), F32)
            for ret_ref in ret_refs:
                slots = ret_ref.shape[0]
                slot = first + lax.broadcasted_iota(jnp.int32, (part, slots), 1)
                hot = jnp.where(slot == places_ref[at, j:j + 1], 1.0, 0.0).astype(BF16)
                picked = picked + dot(hot, ret_ref[...], NN)
                first += slots
            total = total + gates_ref[at, j:j + 1] * picked
        out_ref[at, :] = total.astype(BF16)
        return carry

    lax.fori_loop(0, after_ref.shape[0] // part, one, 0)


def per_device(
    tokens, gain_attn, w_query, w_key, w_value, w_output, rel_table, gain_moe, router,
    w_in, w_out, routes, parents, cotangent,
):
    n_shard = lax.axis_size("shard")
    n_expert = lax.axis_size("expert")
    tok, width = tokens.shape
    tree_len = tok * n_shard
    n_experts = router.shape[1]
    heads = rel_table.shape[0]
    hw = heads * DH
    capacity = max(2, tok * 20 // (7 * n_experts))
    padded = -(-capacity // 16) * 16
    half = -(-padded // 32) * 16
    cuts = (half, padded - half)

    def over_experts(array):
        return lax.all_to_all(array, "expert", split_axis=0, concat_axis=0, tiled=True)

    def over_shards(array):
        return lax.all_to_all(array, "shard", split_axis=0, concat_axis=0, tiled=True)

    tree = lax.all_gather(tokens, "shard", axis=0, tiled=True)
    small = jnp.concatenate([gain_attn, gain_moe, router.reshape(-1)])
    small = lax.all_gather(small, "shard", axis=0)
    rows = width // n_shard
    gain_one = small[:, :rows].reshape(1, width).astype(F32)
    gain_two = small[:, rows:2 * rows].reshape(1, width).astype(F32)
    router_w = small[:, 2 * rows:].reshape(width, n_experts)
    w_qkv = jnp.stack([w_query, w_key, w_value], axis=1).reshape(rows, 3, n_shard, hw).transpose(2, 0, 1, 3)
    w_cols = over_shards(w_qkv).reshape(width, 3, hw)

    expert_range = jnp.arange(n_experts, dtype=jnp.int32)
    flat_routes = routes.reshape(-1)
    expert_hot = (flat_routes[:, None] == expert_range[None, :]).astype(jnp.int32)
    earlier = jnp.cumsum(expert_hot, axis=0) - expert_hot
    rank = jnp.sum(earlier * expert_hot, axis=-1)
    places = jnp.where(
        rank < cuts[0],
        flat_routes * cuts[0] + rank,
        n_experts * cuts[0] + flat_routes * cuts[1] + rank - cuts[0],
    ).reshape(tok, 2)
    places_row = places.T
    slots = [n_experts * cut for cut in cuts]

    def dispatch(rows_of):
        return pl.pallas_call(
            dispatch_kernel,
            in_specs=[VMEM, VMEM],
            out_specs=[VMEM] * len(slots),
            out_shape=[jax.ShapeDtypeStruct((count, width), BF16) for count in slots],
            compiler_params=params(),
        )(places_row, rows_of)

    sent_grads = dispatch(cotangent)
    others = jnp.zeros((sum(slots),), F32).at[places.reshape(-1)].set(routes[:, ::-1].reshape(-1).astype(F32))
    got_grads = [over_experts(block) for block in sent_grads]
    got_others = [
        over_experts(block.reshape(n_experts, -1)).reshape(-1, 1).astype(jnp.int32)
        for block in jnp.split(others, [slots[0]])
    ]

    unit, _ = rms_parts(tree.astype(F32))
    normed_one = (unit * gain_one).astype(BF16)
    w_pad = jnp.pad(w_cols, ((0, 0), (0, 0), (0, HW - hw)))
    qkv = jnp.dot(normed_one, w_pad.reshape(width, 3 * HW), preferred_element_type=F32).astype(BF16)
    queries, keys, values = qkv[:, :HW], qkv[:, HW:2 * HW], qkv[:, 2 * HW:]
    keys_t = lax.dot_general(w_pad[:, 1], normed_one, (((0,), (1,)), ((), ())), preferred_element_type=F32).astype(BF16)
    values_t = lax.dot_general(w_pad[:, 2], normed_one, (((0,), (1,)), ((), ())), preferred_element_type=F32).astype(BF16)
    bias, parent_bucket, own_bucket = bias_tiles(rel_table.astype(F32))
    parent_row = parents[0]
    mixed, raw, lse = pl.pallas_call(
        functools.partial(attn_forward_kernel, heads),
        in_specs=[SMEM] + [VMEM] * 5,
        out_specs=[VMEM] * 3,
        out_shape=[
            jax.ShapeDtypeStruct((tree_len, hw), BF16),
            jax.ShapeDtypeStruct((tree_len, HW), F32),
            jax.ShapeDtypeStruct((SEGS * 8, heads * SEG), F32),
        ],
        compiler_params=params(),
    )(parent_row, queries, keys, values, values_t, bias)
    mixed_own = over_shards(mixed.reshape(n_shard, tok, hw))

    w_o = lax.all_gather(w_output, "shard", axis=0, tiled=True)
    after, normed_two, gates, *sent_rows = pl.pallas_call(
        post_kernel,
        in_specs=[VMEM] * 7,
        out_specs=[VMEM] * (3 + len(slots)),
        out_shape=[
            jax.ShapeDtypeStruct((tok, width), F32),
            jax.ShapeDtypeStruct((tok, width), BF16),
            jax.ShapeDtypeStruct((tok, 2), F32),
        ] + [jax.ShapeDtypeStruct((count, width), BF16) for count in slots],
        compiler_params=params(),
    )(tokens, mixed_own, w_o, gain_two, router_w, routes, places_row)
    got_rows = [over_experts(block) for block in sent_rows]

    first_w = lax.all_gather(w_in[0], "shard", axis=0, tiled=True)
    second_w = lax.all_gather(w_out[0], "shard", axis=0, tiled=True)
    me = lax.axis_index("expert").astype(jnp.int32).reshape(1)
    done = [
        run_expert(me, got_rows[c], got_grads[c], got_others[c], router_w, first_w, second_w) for c in range(len(slots))
    ]
    back_dx = [over_experts(item[1]) for item in done]
    back_gg = [over_experts(item[2].reshape(n_experts, -1)).reshape(1, -1) for item in done]
    back_out = [over_experts(item[0]) for item in done]

    def weight_grad(left, right):
        return functools.reduce(
            jnp.add, [lax.dot_general(a, b, (((0,), (0,)), ((), ())), preferred_element_type=F32) for a, b in zip(left, right)]
        ).astype(BF16)

    grad_w_in = weight_grad(got_rows, [item[5] for item in done])
    grad_w_out = weight_grad([item[4] for item in done], [item[3] for item in done])
    grad_w_in = lax.psum_scatter(grad_w_in, "shard", scatter_dimension=0, tiled=True).astype(F32)[None]
    grad_w_out = lax.psum_scatter(grad_w_out, "shard", scatter_dimension=0, tiled=True).astype(F32)[None]

    grad_after, branch, gmixed, glogits, ggain_two = pl.pallas_call(
        functools.partial(back_kernel, parts=len(slots)),
        in_specs=[VMEM] * (len(slots) + 9),
        out_specs=[VMEM] * 5,
        out_shape=[
            jax.ShapeDtypeStruct((tok, width), F32),
            jax.ShapeDtypeStruct((tok, width), BF16),
            jax.ShapeDtypeStruct((n_shard, tok, hw), BF16),
            jax.ShapeDtypeStruct((tok, n_experts), BF16),
            jax.ShapeDtypeStruct((8, width), F32),
        ],
        compiler_params=params(),
    )(*back_dx, jnp.concatenate(back_gg, axis=1), places, routes, gates, after, gain_two, router_w, cotangent, w_o)
    gmixed_tree = over_shards(gmixed).reshape(tree_len, hw)
    gmixed_tree = jnp.pad(gmixed_tree, ((0, 0), (0, HW - hw)))
    grad_router = lax.dot_general(normed_two, glogits, (((0,), (0,)), ((), ())), preferred_element_type=F32)
    grad_w_o = lax.dot_general(
        mixed_own, branch, (((1,), (0,)), ((), ())), preferred_element_type=F32
    ).astype(BF16).reshape(width, width)
    grad_w_o = lax.psum_scatter(grad_w_o, "shard", scatter_dimension=0, tiled=True).astype(F32)
    grad_w_o = lax.psum(grad_w_o, "expert")

    dq, dk, dv, bins = pl.pallas_call(
        functools.partial(attn_backward_kernel, heads),
        in_specs=[SMEM] + [VMEM] * 8,
        out_specs=[VMEM] * 4,
        out_shape=[jax.ShapeDtypeStruct((tree_len, hw), BF16)] * 3
        + [jax.ShapeDtypeStruct((4, SEG, heads * SEG), F32)],
        scratch_shapes=[pltpu.VMEM((tree_len, HW), F32), pltpu.VMEM((tree_len, HW), F32)],
        compiler_params=params(),
    )(parent_row, queries, keys, values, keys_t, raw, lse, gmixed_tree, bias)
    dqkv = jnp.concatenate([dq, dk, dv], axis=1)
    dqkv_own = over_shards(dqkv.reshape(n_shard, tok, 3 * hw))

    w_all = lax.all_gather(w_cols.reshape(width, 3 * hw), "shard", axis=0)
    grad_normed = functools.reduce(
        jnp.add,
        [
            lax.dot_general(dqkv_own[s], w_all[s], (((1,), (1,)), ((), ())), preferred_element_type=F32)
            for s in range(n_shard)
        ],
    )
    unit_own, factor_own = rms_parts(tokens.astype(F32))
    grad_tokens = (grad_after + rms_grad(grad_normed, gain_one, unit_own, factor_own)).astype(BF16)
    ggain_one = jnp.sum(grad_normed * unit_own, axis=0)

    grad_cols = lax.dot_general(normed_one, dqkv, (((0,), (0,)), ((), ())), preferred_element_type=F32)
    grad_cols = over_experts(grad_cols.astype(BF16).reshape(n_expert, width // n_expert, 3 * hw))
    grad_cols = jnp.sum(grad_cols.astype(F32), axis=0).astype(BF16)
    grad_cols = lax.all_gather(grad_cols, "expert", axis=0, tiled=True)
    grad_cols = over_shards(grad_cols.reshape(n_shard, rows, 3 * hw))
    grad_qkv = grad_cols.reshape(n_shard, rows, 3, hw).transpose(2, 1, 0, 3).reshape(3, rows, width).astype(F32)

    parent_sums = bins[1].reshape(SEG, heads, SEG)
    own_sums = bins[2].reshape(SEG, heads, SEG)
    grad_table = jnp.stack(
        [
            jnp.sum(
                jnp.where((parent_bucket == at)[:, None, :], parent_sums, 0.0)
                + jnp.where((own_bucket == at)[:, None, :], own_sums, 0.0),
                axis=(0, 2),
            )
            for at in range(NB)
        ],
        axis=1,
    )
    far = jnp.sum(bins[0].reshape(SEG, heads, SEG), axis=(0, 2))
    grad_table = grad_table.at[:, NB - 1].add(far)
    own_shard = lax.axis_index("shard")
    sums = jnp.concatenate([ggain_one, ggain_two[0], grad_router.reshape(-1)])
    table_at = jnp.zeros((n_shard, heads * NB), F32).at[own_shard].set(grad_table.reshape(-1))
    sums = lax.psum(jnp.concatenate([sums, table_at.reshape(-1)]), ("expert", "shard"))
    own = lambda array: lax.dynamic_slice_in_dim(array, own_shard * (array.shape[0] // n_shard), array.shape[0] // n_shard, 0)
    final_g1 = own(sums[:width])
    final_g2 = own(sums[width:2 * width])
    final_r = own(sums[2 * width:2 * width + width * n_experts].reshape(width, n_experts))
    final_t = own(sums[2 * width + width * n_experts:].reshape(n_shard * heads, NB))

    output = pl.pallas_call(
        functools.partial(combine_kernel, parts=len(slots)),
        in_specs=[VMEM] * (len(slots) + 3),
        out_specs=VMEM,
        out_shape=jax.ShapeDtypeStruct((tok, width), BF16),
        compiler_params=params(),
    )(*back_out, places, gates, after)

    return (
        output, grad_tokens, final_g1, grad_qkv[0], grad_qkv[1], grad_qkv[2], grad_w_o, final_t, final_g2,
        final_r, grad_w_in, grad_w_out,
    )


def solution(mesh):
    both, shard = P(("expert", "shard"), None), P("shard", None)
    three = P("expert", "shard", None)
    return jax.shard_map(
        per_device,
        mesh=mesh,
        in_specs=(
            both, P("shard"), shard, shard, shard, shard, shard, P("shard"), shard, three, three, both,
            P("expert", None), both,
        ),
        out_specs=(both, both, P("shard"), shard, shard, shard, shard, shard, P("shard"), shard, three, three),
        check_vma=False,
    )
```

```python
import functools
import math

import jax
import jax.numpy as jnp
from jax import lax
from jax.experimental import pallas as pl
from jax.experimental.pallas import tpu as pltpu
from jax.sharding import PartitionSpec as P

DH = 64
NB = 16
SEG = 128
SEGS = 20
TRUNK = 8
SPARE = 3

THRESHOLDS = (1, 2, 3, 4, 5, 6, 7, 8, 12, 16, 24, 32, 48, 64, 96)
EPS = 1e-06
MASKED = -1e30
HW = 256

F32 = jnp.float32
BF16 = jnp.bfloat16
VMEM = pl.BlockSpec(memory_space=pltpu.VMEM)
SMEM = pl.BlockSpec(memory_space=pltpu.SMEM)
ANY = pl.BlockSpec(memory_space=pl.ANY)

NN = ((1,), (0,))
NT = ((1,), (1,))
TN = ((0,), (0,))


def params(mib=60, **more):
    return pltpu.CompilerParams(vmem_limit_bytes=mib << 20, **more)


SHORT = pl.CostEstimate(flops=0, bytes_accessed=1024, transcendentals=0)
LONG = pl.CostEstimate(flops=1 << 40, bytes_accessed=1 << 32, transcendentals=0)


def dot(left, right, contract):
    return lax.dot_general(left, right, (contract, ((), ())), preferred_element_type=F32)


def arrays(*shapes):
    return [jax.ShapeDtypeStruct(shape, dtype) for shape, dtype in shapes]


def rms_parts(values):
    factor = lax.rsqrt(jnp.mean(values * values, axis=-1, keepdims=True) + EPS)
    return values * factor, factor


def rms_grad(grad_out, gain_row, unit_rows, factor):
    scaled = grad_out * gain_row
    return factor * (scaled - unit_rows * jnp.mean(scaled * unit_rows, axis=-1, keepdims=True))


def columns_kernel(me_ref, q_ref, k_ref, v_ref, more_ref, out_ref):
    groups, depth, width = out_ref.shape
    hw = q_ref.shape[1] // groups
    blank = jnp.zeros((depth, width - 3 * hw - more_ref.shape[1]), BF16)
    for s in range(groups):
        at = slice(s * hw, (s + 1) * hw)
        out_ref[jnp.bitwise_xor(me_ref[0], s)] = jnp.concatenate(
            [q_ref[:, at], k_ref[:, at], v_ref[:, at], more_ref[...], blank], axis=1
        )


def project_kernel(
    heads, me_ref, table_ref, w0, w1, w2, w3, t0, t1, t2, t3, before_ref,
    n0, n1, n2, n3, q_ref, k_ref, v_ref, kt_ref, vt_ref, w_ref, bias_ref, gain_ref, gain_two_ref, router_ref, w_pad,
):
    hw = heads * DH
    blank = jnp.zeros((w0.shape[0], HW - hw), BF16)
    for rel, piece_ref in enumerate((w0, w1, w2, w3)):
        depth = piece_ref.shape[0]
        at = pl.ds(pl.multiple_of(jnp.bitwise_xor(me_ref[0], rel) * depth, 16), depth)
        piece = piece_ref[...]
        blank_end = jnp.zeros((depth, w_ref.shape[1] - 3 * hw), BF16)
        w_ref[at, :] = jnp.concatenate([piece[:, :3 * hw], blank_end], axis=1)
        router_ref[at, :] = piece[:, 3 * hw + 2:3 * hw + 2 + router_ref.shape[1]]
        padded = [part for c in range(3) for part in (piece[:, c * hw:(c + 1) * hw], blank)]
        padded.append(piece[:, 3 * hw:3 * hw + 2])
        padded.append(jnp.zeros((depth, w_pad.shape[1] - 3 * HW - 2), BF16))
        w_pad[at, :] = jnp.concatenate(padded, axis=1)
    gains = jnp.transpose(w_pad[:, 3 * HW:].astype(F32))
    gain_ref[...] = gains[0:1]
    gain_two_ref[...] = gains[1:2]
    for rel, (t_ref, n_ref) in enumerate(zip((t0, t1, t2, t3), (n0, n1, n2, n3))):
        count = t_ref.shape[0]
        unit, _ = rms_parts(t_ref[...].astype(F32))
        n_ref[...] = (unit * gain_ref[...]).astype(BF16)
        at = pl.ds(pl.multiple_of(jnp.bitwise_xor(me_ref[0], rel) * count, SEG), count)
        qkv = dot(n_ref[...], w_pad[:, :3 * HW], NN)
        q_ref[at, :] = qkv[:, :HW].astype(BF16) * jnp.asarray(DH ** -0.5, BF16)
        k_ref[at, :] = qkv[:, HW:2 * HW].astype(BF16)
        v_ref[at, :] = qkv[:, 2 * HW:].astype(BF16)
        kt_ref[:, at] = jnp.transpose(qkv[:, HW:2 * HW]).astype(BF16)
        vt_ref[:, at] = jnp.transpose(qkv[:, 2 * HW:]).astype(BF16)
    key = lax.broadcasted_iota(jnp.int32, (SEG, SEG), 0)
    query = lax.broadcasted_iota(jnp.int32, (SEG, SEG), 1)
    bias_ref[0] = jnp.zeros((SEG, heads * SEG), F32)
    bias_ref[3] = jnp.full((SEG, heads * SEG), MASKED, F32)
    for h in range(heads):
        last = table_ref[h, NB - 1]
        at = slice(h * SEG, (h + 1) * SEG)
        for kind, gap in ((1, query - key + SEG), (2, query - key)):
            tile = jnp.zeros((SEG, SEG), F32) + (table_ref[h, 0] - last)
            for i, threshold in enumerate(THRESHOLDS):
                tile = jnp.where(gap >= threshold, table_ref[h, i + 1] - last, tile)
            bias_ref[kind, :, at] = jnp.where(gap >= 0, tile, MASKED)


def by_head(rows, heads):
    lane = lax.broadcasted_iota(jnp.int32, rows.shape, 1)
    zero = jnp.zeros_like(rows)
    return jnp.concatenate(
        [jnp.where((lane >= h * DH) & (lane < (h + 1) * DH), rows, zero) for h in range(heads)], axis=0
    )


def seg_at(index):
    if isinstance(index, int):
        return slice(index * SEG, (index + 1) * SEG)
    return pl.ds(pl.multiple_of(index * SEG, SEG), SEG)


def head_rows(acc, heads):
    pieces = [acc[h * DH:(h + 1) * DH, h * SEG:(h + 1) * SEG] for h in range(heads)]
    pieces.append(jnp.zeros((HW - heads * DH, SEG), F32))
    return jnp.transpose(jnp.concatenate(pieces, axis=0))


def pair_bias(bias_ref, first, second):
    return jnp.concatenate([bias_ref[first], bias_ref[second]], axis=1)


def attn_forward_kernel(
    heads, me_ref, parent_ref, q_ref, k_ref, v_ref, vt_ref, bias_ref, o0, o1, o2, o3, raw_ref, lse_ref, out_all
):
    cols = heads * SEG
    trunk_len = TRUNK * SEG
    last = trunk_len - SEG

    def queries(b):
        return by_head(q_ref[seg_at(b), :], heads)

    def finish(b, acc, total, top):
        lse_ref[pl.ds(b * 8, 8), :] = jnp.broadcast_to(top + jnp.log(total), (8, cols))
        rows = head_rows(acc / total, heads)
        raw_ref[seg_at(b), :] = rows
        out_all[seg_at(b), :] = rows.astype(BF16)

    for j in range(TRUNK // 2):
        q6 = jnp.concatenate([queries(2 * j), queries(2 * j + 1)], axis=0)
        scores = dot(k_ref[0:(j + 1) * 2 * SEG, :], q6, NT)
        parts = []
        if j > 0:
            far = (2 * j - 1) * SEG
            parts = [scores[:far], scores[far:far + SEG] + pair_bias(bias_ref, 1, 0)]
        parts.append(scores[2 * j * SEG:(2 * j + 1) * SEG] + pair_bias(bias_ref, 2, 1))
        parts.append(scores[(2 * j + 1) * SEG:] + pair_bias(bias_ref, 3, 2))
        top = functools.reduce(jnp.maximum, [jnp.max(part, axis=0, keepdims=True) for part in parts])
        parts = [jnp.exp(part - top) for part in parts]
        total = functools.reduce(jnp.add, [jnp.sum(part, axis=0, keepdims=True) for part in parts])
        acc = dot(vt_ref[:, 0:(j + 1) * 2 * SEG], jnp.concatenate([p.astype(BF16) for p in parts], axis=0), NN)
        for s in range(2):
            at = slice(s * cols, (s + 1) * cols)
            finish(2 * j + s, acc[:, at], total[:, at], top[:, at])

    def other_step(i, carry):
        segs = [TRUNK + 2 * i, TRUNK + 2 * i + 1]
        parents = [parent_ref[b] for b in segs]
        leaf = [(parent >= TRUNK).astype(jnp.int32) for parent in parents]
        q3 = [queries(b) for b in segs]
        q6 = jnp.concatenate(q3, axis=0)
        scores = dot(k_ref[0:trunk_len, :], q6, NT)
        near = scores[last:] + pair_bias(bias_ref, 1 - leaf[0], 1 - leaf[1])
        far = scores[:last]
        extra = []
        for s in range(2):
            keys = jnp.concatenate([k_ref[seg_at(parents[s]), :], k_ref[seg_at(segs[s]), :]], axis=0)
            bias = jnp.concatenate([bias_ref[3 - 2 * leaf[s]], bias_ref[2]], axis=0)
            extra.append(dot(keys, q3[s], NT) + bias)
        top = jnp.maximum(jnp.max(far, axis=0, keepdims=True), jnp.max(near, axis=0, keepdims=True))
        top = jnp.maximum(top, jnp.concatenate([jnp.max(e, axis=0, keepdims=True) for e in extra], axis=1))
        far, near = jnp.exp(far - top), jnp.exp(near - top)
        extra = [jnp.exp(extra[s] - top[:, s * cols:(s + 1) * cols]) for s in range(2)]
        total = jnp.sum(far, axis=0, keepdims=True) + jnp.sum(near, axis=0, keepdims=True)
        total = total + jnp.concatenate([jnp.sum(e, axis=0, keepdims=True) for e in extra], axis=1)
        acc = dot(vt_ref[:, 0:trunk_len], jnp.concatenate([far.astype(BF16), near.astype(BF16)], axis=0), NN)
        for s in range(2):
            at = slice(s * cols, (s + 1) * cols)
            values = jnp.concatenate([vt_ref[:, seg_at(parents[s])], vt_ref[:, seg_at(segs[s])]], axis=1)
            finish(segs[s], acc[:, at] + dot(values, extra[s].astype(BF16), NN), total[:, at], top[:, at])
        return carry

    lax.fori_loop(0, (SEGS - TRUNK) // 2, other_step, 0)
    for rel, o_ref in enumerate((o0, o1, o2, o3)):
        count, width = o_ref.shape
        at = pl.ds(pl.multiple_of(jnp.bitwise_xor(me_ref[0], rel) * count, SEG), count)
        o_ref[...] = out_all[at, :][:, :width]


def attn_backward_kernel(
    heads, me_ref, parent_ref, q_ref, k_ref, v_ref, kt_ref, raw_ref, lse_ref, g0, g1, g2, g3_ref, bias_ref,
    d0, d1, d2, d3, bins_ref, grad_all, dq_all, dk_acc, dv_acc, bins_acc,
):
    cols = heads * SEG
    trunk_len = TRUNK * SEG
    dk_acc[...] = jnp.zeros_like(dk_acc)
    dv_acc[...] = jnp.zeros_like(dv_acc)
    bins_acc[...] = jnp.zeros_like(bins_acc)
    for rel, g_ref in enumerate((g0, g1, g2, g3_ref)):
        count, width = g_ref.shape
        at = pl.ds(pl.multiple_of(jnp.bitwise_xor(me_ref[0], rel) * count, SEG), count)
        grad_all[at, :] = jnp.concatenate([g_ref[...], jnp.zeros((count, HW - width), BF16)], axis=1)

    def common(b):
        q3 = by_head(q_ref[seg_at(b), :], heads)
        grad = grad_all[seg_at(b), :]
        product = by_head(grad.astype(F32) * raw_ref[seg_at(b), :], heads)
        high = product.astype(BF16)
        low = (product - high.astype(F32)).astype(BF16)
        ones = jnp.ones((8, HW), BF16)
        row_dot = (dot(ones, high, NT) + dot(ones, low, NT))[0:1]
        return q3, by_head(grad, heads), row_dot, lse_ref[pl.ds(b * 8, 8), :][0:1]

    def block(keys, values, q, g, row_dot, lse, bias):
        scores = dot(keys, q, NT)
        if bias is not None:
            scores = scores + bias
        prob = jnp.exp(scores - lse)
        grad_score = prob * (dot(values, g, NT) - row_dot)
        return prob.astype(BF16), grad_score

    def write_dq(b, acc):
        dq_all[seg_at(b), :] = (head_rows(acc, heads) * DH ** -0.5).astype(BF16)

    def both(pair):
        return [jnp.concatenate([a, b], axis=0 if a.shape[0] > 1 else 1) for a, b in zip(*pair)]

    zero = 0
    for j in range(TRUNK // 2):
        q6, g6, row_dot, lse = both([common(2 * j), common(2 * j + 1)])
        kept = []
        for i in range(j + 1):
            at = slice(2 * i * SEG, 2 * (i + 1) * SEG)
            bias = None
            if i == j:
                bias = jnp.concatenate([pair_bias(bias_ref, 2, 1), pair_bias(bias_ref, 3, 2)], axis=0)
            if i == j - 1:
                bias = jnp.concatenate([pair_bias(bias_ref, zero, zero), pair_bias(bias_ref, 1, zero)], axis=0)
            prob, score = block(k_ref[at, :], v_ref[at, :], q6, g6, row_dot, lse, bias)
            if i == j:
                bins_acc[0] += score[:SEG, cols:]
                bins_acc[1] += score[:SEG, :cols] + score[SEG:, cols:]
            if i == j - 1:
                bins_acc[0] += score[SEG:, :cols]
            score = score.astype(BF16)
            dv_acc[at, :] += dot(prob, g6, NN)
            dk_acc[at, :] += dot(score, q6, NN)
            kept.append(score)
        acc = dot(kt_ref[:, 0:(j + 1) * 2 * SEG], jnp.concatenate(kept, axis=0), NN)
        for s in range(2):
            write_dq(2 * j + s, acc[:, s * cols:(s + 1) * cols])

    def other_step(step, carry):
        segs = [TRUNK + 2 * step, TRUNK + 2 * step + 1]
        parents = [parent_ref[b] for b in segs]
        leaf = [(parent >= TRUNK).astype(jnp.int32) for parent in parents]
        each = [common(b) for b in segs]
        q6, g6, row_dot, lse = both(each)
        kept = []
        for i in range(TRUNK // 2):
            at = slice(2 * i * SEG, 2 * (i + 1) * SEG)
            bias = None
            if i == TRUNK // 2 - 1:
                near = pair_bias(bias_ref, 1 - leaf[0], 1 - leaf[1])
                bias = jnp.concatenate([jnp.zeros_like(near), near], axis=0)
            prob, score = block(k_ref[at, :], v_ref[at, :], q6, g6, row_dot, lse, bias)
            if i == TRUNK // 2 - 1:
                for s in range(2):
                    bins_acc[0] += jnp.where(leaf[s] == 0, score[SEG:, s * cols:(s + 1) * cols], 0.0)
            score = score.astype(BF16)
            dv_acc[at, :] += dot(prob, g6, NN)
            dk_acc[at, :] += dot(score, q6, NN)
            kept.append(score)
        acc = dot(kt_ref[:, 0:trunk_len], jnp.concatenate(kept, axis=0), NN)
        for s in range(2):
            q3, g3, row, own_lse = each[s]
            first, second = seg_at(parents[s]), seg_at(segs[s])
            keys = jnp.concatenate([k_ref[first, :], k_ref[second, :]], axis=0)
            values = jnp.concatenate([v_ref[first, :], v_ref[second, :]], axis=0)
            keys_t = jnp.concatenate([kt_ref[:, first], kt_ref[:, second]], axis=1)
            bias = jnp.concatenate([bias_ref[3 - 2 * leaf[s]], bias_ref[2]], axis=0)
            prob, score = block(keys, values, q3, g3, row, own_lse, bias)
            bins_acc[0] += score[:SEG]
            bins_acc[1] += score[SEG:]
            score = score.astype(BF16)
            grad_v, grad_k = dot(prob, g3, NN), dot(score, q3, NN)
            dv_acc[first, :] += grad_v[:SEG]
            dv_acc[second, :] += grad_v[SEG:]
            dk_acc[first, :] += grad_k[:SEG]
            dk_acc[second, :] += grad_k[SEG:]
            write_dq(segs[s], acc[:, s * cols:(s + 1) * cols] + dot(keys_t, score, NN))
        return carry

    lax.fori_loop(0, (SEGS - TRUNK) // 2, other_step, 0)
    for rel, d_ref in enumerate((d0, d1, d2, d3)):
        count = d_ref.shape[0]
        width = heads * DH
        at = pl.ds(pl.multiple_of(jnp.bitwise_xor(me_ref[0], rel) * count, SEG), count)
        parts = [dq_all[at, :][:, :width], dk_acc[at, :][:, :width].astype(BF16), dv_acc[at, :][:, :width].astype(BF16)]
        parts.append(jnp.zeros((count, d_ref.shape[1] - 3 * width), BF16))
        d_ref[...] = jnp.concatenate(parts, axis=1)
    key = lax.broadcasted_iota(jnp.int32, (SEG, cols), 0)
    query = lax.broadcasted_iota(jnp.int32, (SEG, cols), 1) % SEG
    gap = query - key
    parent_sum, own_sum = bins_acc[0], bins_acc[1]
    lines = [jnp.sum(parent_sum + own_sum, axis=0, keepdims=True)]
    for threshold in THRESHOLDS:
        hit = jnp.where(gap + SEG >= threshold, parent_sum, 0.0) + jnp.where(gap >= threshold, own_sum, 0.0)
        lines.append(jnp.sum(hit, axis=0, keepdims=True))
    bins_ref[...] = jnp.concatenate(lines, axis=0)


class Slots:
    def __init__(self, n_expert, capacity):
        self.n_expert = n_expert
        self.cut = n_expert == 8
        self.near = n_expert // 2 if self.cut else n_expert
        self.block = -(-(capacity + SPARE) // 16) * 16
        self.chunks = [[list(range(self.near))]]
        if self.cut:
            self.chunks += [[[4], [5]], [[6], [7]]]
        self.arrays = [array for chunk in self.chunks for array in chunk]

    def block_of(self, expert, me):
        if not self.cut:
            return expert
        inside = jnp.bitwise_xor(expert, me) & (self.near - 1)
        return jnp.where((expert & self.near) == (me & self.near), expert & (self.near - 1), self.near + inside)

    def expert_of(self, block, me):
        if not self.cut:
            return block
        if block < self.near:
            return (me & self.near) + block
        return jnp.bitwise_xor(me, block)

    def split(self, flat):
        flat = list(flat)
        return [[flat.pop(0) for _ in chunk] for chunk in self.chunks]

    def exchange(self, c, blocks):
        if c == 0:
            groups = [[g * self.near + i for i in range(self.near)] for g in range(self.n_expert // self.near)]
            return [
                lax.all_to_all(
                    blocks[0], "expert", split_axis=0, concat_axis=0, tiled=True,
                    axis_index_groups=groups if self.cut else None,
                )
            ]
        return [swap(block, "expert", array[0]) for array, block in zip(self.chunks[c], blocks)]


def over_experts(block):
    return lax.all_to_all(block, "expert", split_axis=0, concat_axis=0, tiled=True)


def swap(block, axis, rel):
    if rel == 0:
        return block
    return lax.ppermute(block, axis, [(i, i ^ rel) for i in range(lax.axis_size(axis))])


def swap_all(blocks, axis):
    return [swap(block, axis, rel) for rel, block in enumerate(blocks)]


def from_all(block):
    near, far = swap(block, "shard", 1), swap(block, "shard", 2)
    return [block, near, far, swap(far, "shard", 1)]


def reorder(parts, me):
    bit = 1
    while bit < len(parts):
        parts = [jnp.where(me & bit, parts[i ^ bit], parts[i]) for i in range(len(parts))]
        bit *= 2
    return parts


def send_rows(slots, rows, places_ref, out_refs):
    tokens = places_ref.shape[1]
    for array, out_ref in zip(slots.arrays, out_refs):
        for i, block in enumerate(array):
            slot = block * slots.block + lax.broadcasted_iota(jnp.int32, (slots.block, tokens), 0)
            hit = (slot == places_ref[0:1, :]) | (slot == places_ref[1:2, :])
            picked = dot(jnp.where(hit, 1.0, 0.0).astype(BF16), rows, NN).astype(BF16)
            out_ref[i * slots.block:(i + 1) * slots.block, :] = picked


def diagonal(count):
    return lax.broadcasted_iota(jnp.int32, (count, count), 0) == lax.broadcasted_iota(jnp.int32, (count, count), 1)


def padded_row(row, width):
    count = row.shape[1]
    return row if count == width else jnp.concatenate([row, jnp.zeros((1, width - count), row.dtype)], axis=1)


def dispatch_kernel(slots, me_ref, places_ref, others_ref, rows_ref, *refs):
    out_ref = refs[-1]
    tokens = places_ref.shape[1]
    width = rows_ref.shape[1]
    rows = rows_ref[...]
    count = slots.block

    def one(expert, carry):
        slot = slots.block_of(expert, me_ref[0]) * count + lax.broadcasted_iota(jnp.int32, (count, tokens), 0)
        hot = [jnp.where(slot == places_ref[j:j + 1, :], 1.0, 0.0).astype(BF16) for j in range(2)]
        picked = dot(hot[0] + hot[1], rows, NN)
        ids = sum(dot(others_ref[8 * j:8 * j + 8, :], hot[j], NT) for j in range(2))
        line = lax.broadcasted_iota(jnp.int32, picked.shape, 0)
        picked = jnp.where(line == count - 1, padded_row(ids[0:1], width), picked)
        out_ref[pl.ds(pl.multiple_of(expert * count, 16), count), :] = picked.astype(BF16)
        return carry

    lax.fori_loop(0, slots.n_expert, one, 0)


def post_kernel(
    slots, me_ref, x_ref, gain_ref, router_ref, routes_ref, places_ref, m0, m1, m2, m3, w_ref, before_ref,
    after_ref, normed_ref, gates_ref, *out_refs,
):
    after = x_ref[...].astype(F32)
    for rel, m_ref in enumerate((m0, m1, m2, m3)):
        after = after + dot(m_ref[...], w_ref[jnp.bitwise_xor(me_ref[0], rel)], NN)
    after_ref[...] = after
    unit, _ = rms_parts(after)
    normed = (unit * gain_ref[...]).astype(BF16)
    normed_ref[...] = normed
    send_rows(slots, normed_ref[...], places_ref, out_refs)
    logits = dot(normed, router_ref[...], NN)
    expert = lax.broadcasted_iota(jnp.int32, logits.shape, 1)
    first = jnp.sum(jnp.where(expert == routes_ref[:, 0:1], logits, 0.0), axis=-1, keepdims=True)
    second = jnp.sum(jnp.where(expert == routes_ref[:, 1:2], logits, 0.0), axis=-1, keepdims=True)
    top = jnp.maximum(first, second)
    first, second = jnp.exp(first - top), jnp.exp(second - top)
    gates_ref[...] = jnp.concatenate([first / (first + second), second / (first + second)], axis=1)


def expert_kernel(slots, chunk, fresh, me_ref, *refs):
    refs = list(refs)
    take = lambda n: [refs.pop(0) for _ in range(n)]
    x_refs = take(len(chunk))
    g_all, router_ref, first_ref, second_ref = take(4)
    if not fresh:
        take(2)
    (out_all,) = take(1)
    dx_refs = take(len(chunk))
    if not fresh:
        take(1)
    rows_ref, grad_ref, act_ref, inner_ref, g_buf, out_buf, out_acc, dx_acc, sem = refs
    step = pl.program_id(0)
    total, width = rows_ref.shape
    rows = slots.block
    pieces = []
    for x_ref, dx_ref, array in zip(x_refs, dx_refs, chunk):
        for i, block in enumerate(array):
            pieces.append((block, x_ref, dx_ref, i * rows, len(pieces) * rows))

    def home(block):
        return pl.ds(pl.multiple_of(slots.expert_of(block, me_ref[0]) * rows, 16), rows)

    @pl.when(step == 0)
    def _():
        copies = [
            pltpu.make_async_copy(g_all.at[home(block), :], g_buf.at[pl.ds(first, rows), :], sem.at[i])
            for i, (block, _, _, _, first) in enumerate(pieces)
        ]
        for copy in copies:
            copy.start()
        out_acc[...] = jnp.zeros_like(out_acc)
        dx_acc[...] = jnp.zeros_like(dx_acc)
        for _, x_ref, _, inside, first in pieces:
            rows_ref[first:first + rows, :] = x_ref[inside:inside + rows, :]
        for copy in copies:
            copy.wait()
        for *_, first in pieces:
            at = slice(first, first + rows)
            grads = g_buf[at, :].astype(F32)
            other = jnp.sum(jnp.where(diagonal(rows), grads[rows - 1:, :rows], 0.0), axis=1, keepdims=True).astype(jnp.int32)
            logits = dot(rows_ref[at, :], router_ref[...], NN)
            expert = lax.broadcasted_iota(jnp.int32, logits.shape, 1)
            mine = jnp.sum(jnp.where(expert == me_ref[0], logits, 0.0), axis=-1, keepdims=True)
            its = jnp.sum(jnp.where(expert == other, logits, 0.0), axis=-1, keepdims=True)
            top = jnp.maximum(mine, its)
            mine, its = jnp.exp(mine - top), jnp.exp(its - top)
            line = lax.broadcasted_iota(jnp.int32, grads.shape, 0)
            grad_ref[at, :] = jnp.where(line < rows - SPARE, mine / (mine + its) * grads, 0.0).astype(BF16)

    parts = 1
    while total // parts > 512 or total % parts or (total // parts) % 16:
        parts += 1
    part = total // parts
    for i in range(parts):
        at = slice(i * part, (i + 1) * part)
        first_w, second_w = first_ref[...], second_ref[...]
        value = dot(rows_ref[at, :], first_w, NN)
        grad_act = dot(grad_ref[at, :], second_w, NT)
        square = value * value
        half = 0.5 * value
        scale = 0.7978845608028654
        th = jnp.tanh(value * (scale + (scale * 0.044715) * square))
        act = (half + half * th).astype(BF16)
        slope = 0.5 + 0.5 * th + (half * (1.0 - th * th)) * (scale + (3 * scale * 0.044715) * square)
        inner = (grad_act * slope).astype(BF16)
        act_ref[at, :] = act
        inner_ref[at, :] = inner
        out_acc[at, :] += dot(act, second_w, NN)
        dx_acc[at, :] += dot(inner, first_w, NT)

    @pl.when(step == pl.num_programs(0) - 1)
    def _():
        out_buf[...] = out_acc[...].astype(BF16)
        copies = [
            pltpu.make_async_copy(out_buf.at[pl.ds(first, rows), :], out_all.at[home(block), :], sem.at[i])
            for i, (block, _, _, _, first) in enumerate(pieces)
        ]
        for copy in copies:
            copy.start()
        for _, _, dx_ref, inside, first in pieces:
            at = slice(first, first + rows)
            gates = jnp.sum(out_buf[at, :].astype(F32) * g_buf[at, :].astype(F32), axis=1, keepdims=True)
            gates = jnp.sum(jnp.where(diagonal(rows), gates, 0.0), axis=0, keepdims=True)
            dx_ref[inside:inside + rows, :] = dx_acc[at, :].astype(BF16)
            tail = dx_acc[first + rows - 16:first + rows, :]
            line = lax.broadcasted_iota(jnp.int32, tail.shape, 0)
            for place in range(SPARE):
                piece = gates.astype(BF16).astype(F32)
                gates = gates - piece
                tail = jnp.where(line == 16 - SPARE + place, padded_row(piece, width), tail)
            dx_ref[inside + rows - 16:inside + rows, :] = tail.astype(BF16)
        for copy in copies:
            copy.wait()


def run_expert(slots, chunk, me, blocks, g_all, router, first_w, second_w, out_all, near):
    width, hidden = first_w.shape
    total = sum(block.shape[0] for block in blocks)
    block = hidden // 4
    whole = lambda a: pl.BlockSpec(a.shape, lambda i: (0, 0))
    column = pl.BlockSpec((total, block), lambda i: (0, i))
    rows = pl.BlockSpec((total, width), lambda i: (0, 0))
    fresh = out_all is None
    inputs = [me, *blocks, g_all, router, first_w, second_w] + ([] if fresh else [out_all, near])
    return pl.pallas_call(
        functools.partial(expert_kernel, slots, chunk, fresh),
        grid=(4,),
        in_specs=[SMEM]
        + [whole(b) for b in blocks]
        + [ANY, whole(router), pl.BlockSpec((width, block), lambda i: (0, i)), pl.BlockSpec((block, width), lambda i: (i, 0))]
        + ([] if fresh else [ANY, ANY]),
        out_specs=[ANY] + [whole(b) for b in blocks] + ([] if fresh else [ANY]) + [rows, rows, column, column],
        out_shape=arrays(
            (g_all.shape, BF16), *[(b.shape, BF16) for b in blocks], *([] if fresh else [(near.shape, BF16)]), *[((total, width), BF16)] * 2, *[((total, hidden), BF16)] * 2
        ),
        scratch_shapes=[
            pltpu.VMEM((total, width), BF16),
            pltpu.VMEM((total, width), BF16),
            pltpu.VMEM((total, width), F32),
            pltpu.VMEM((total, width), F32),
            pltpu.SemaphoreType.DMA((sum(len(array) for array in chunk),)),
        ],
        input_output_aliases={} if fresh else {len(inputs) - 2: 0, len(inputs) - 1: 1 + len(blocks)},
        compiler_params=params(dimension_semantics=("arbitrary",)),
        cost_estimate=SHORT,
    )(*inputs)


def first_grad_kernel(parts, *refs):
    out_ref = refs[-1]
    out_ref[...] = sum(dot(x[...], inner[...], TN) for x, inner in zip(refs[:parts], refs[parts:2 * parts])).astype(BF16)


def run_first_grad(rows, inners, more):
    width, hidden = rows[0].shape[1], inners[0].shape[1]
    block = hidden // 4
    total = sum(a.shape[0] for a in rows)
    return pl.pallas_call(
        functools.partial(first_grad_kernel, len(rows)),
        grid=(4,),
        in_specs=[pl.BlockSpec(a.shape, lambda i: (0, 0)) for a in rows]
        + [pl.BlockSpec((a.shape[0], block), lambda i: (0, i)) for a in inners],
        out_specs=pl.BlockSpec((width, block), lambda i: (0, i)),
        out_shape=jax.ShapeDtypeStruct((width, hidden + more), BF16),
        compiler_params=params(dimension_semantics=("arbitrary",)),
        cost_estimate=SHORT,
    )(*rows, *inners)


def run_second_grad(acts, grads):
    width, hidden = grads[0].shape[1], acts[0].shape[1]
    block = hidden // 4
    total = sum(a.shape[0] for a in acts)
    return pl.pallas_call(
        functools.partial(first_grad_kernel, len(acts)),
        grid=(4,),
        in_specs=[pl.BlockSpec((a.shape[0], block), lambda i: (0, i)) for a in acts]
        + [pl.BlockSpec(a.shape, lambda i: (0, 0)) for a in grads],
        out_specs=pl.BlockSpec((block, width), lambda i: (i, 0)),
        out_shape=jax.ShapeDtypeStruct((hidden, width), BF16),
        compiler_params=params(dimension_semantics=("arbitrary",)),
        cost_estimate=SHORT,
    )(*acts, *grads)


def gather_blocks(slots, refs, scratch):
    for array, ref in zip(slots.arrays, refs):
        scratch[array[0] * slots.block:(array[-1] + 1) * slots.block, :] = ref[...]


def back_kernel(slots, me_ref, *refs):
    refs_left = list(refs)
    take = lambda n: [refs_left.pop(0) for _ in range(n)]
    ret_refs = take(len(slots.arrays))
    places_ref, routes_ref, gates_ref, after_ref, gain_ref, router_ref, g_ref = take(7)
    (w_ref,) = take(1)
    grad_after_ref, branch_ref = take(2)
    mixed_refs = take(4)
    glogits_ref, ggain_ref, scratch = refs_left
    tokens = after_ref.shape[0]
    part = 128
    gather_blocks(slots, ret_refs, scratch)
    pieces = []
    for end in range(slots.block, scratch.shape[0] + 1, slots.block):
        tail = scratch[end - 16:end, :].astype(F32)[16 - SPARE:, :slots.block]
        pieces.append(jnp.sum(tail, axis=0, keepdims=True))
    gg = jnp.concatenate(pieces, axis=1)
    ggain_ref[...] = jnp.zeros_like(ggain_ref)

    def one(i, carry):
        at = pl.ds(pl.multiple_of(i * part, part), part)
        slot = lax.broadcasted_iota(jnp.int32, (part, gg.shape[1]), 1)
        hit0, hit1 = slot == places_ref[at, 0:1], slot == places_ref[at, 1:2]
        gg0 = jnp.sum(jnp.where(hit0, gg, 0.0), axis=-1, keepdims=True)
        gg1 = jnp.sum(jnp.where(hit1, gg, 0.0), axis=-1, keepdims=True)
        total = dot(jnp.where(hit0 | hit1, 1.0, 0.0).astype(BF16), scratch[...], NN)
        gate0, gate1 = gates_ref[at, 0:1], gates_ref[at, 1:2]
        mean = gate0 * gg0 + gate1 * gg1
        expert = lax.broadcasted_iota(jnp.int32, (part, router_ref.shape[1]), 1)
        glogits = jnp.where(expert == routes_ref[at, 0:1], gate0 * (gg0 - mean), 0.0) + jnp.where(
            expert == routes_ref[at, 1:2], gate1 * (gg1 - mean), 0.0
        )
        glogits = glogits.astype(BF16)
        glogits_ref[at, :] = glogits
        incoming = dot(glogits, router_ref[...], NT) + total
        unit, factor = rms_parts(after_ref[at, :])
        grad_after = g_ref[at, :].astype(F32) + rms_grad(incoming, gain_ref[...], unit, factor)
        ggain_ref[0:1, :] += jnp.sum(incoming * unit, axis=0, keepdims=True)
        grad_after_ref[at, :] = grad_after
        branch = grad_after.astype(BF16)
        branch_ref[at, :] = branch
        for rel, mixed_ref in enumerate(mixed_refs):
            mixed_ref[at, :] = dot(branch, w_ref[jnp.bitwise_xor(me_ref[0], rel)], NT).astype(BF16)
        return carry

    lax.fori_loop(0, tokens // part, one, 0)


def combine_kernel(slots, me_ref, ret_ref, places_ref, gates_ref, after_ref, out_ref, scratch):
    part = 128
    for block in range(slots.n_expert):
        first = pl.multiple_of(slots.expert_of(block, me_ref[0]) * slots.block, 16)
        scratch[block * slots.block:(block + 1) * slots.block, :] = ret_ref[pl.ds(first, slots.block), :]

    def one(i, carry):
        at = pl.ds(pl.multiple_of(i * part, part), part)
        total = after_ref[at, :]
        slot = lax.broadcasted_iota(jnp.int32, (part, scratch.shape[0]), 1)
        for j in range(2):
            hot = jnp.where(slot == places_ref[at, j:j + 1], 1.0, 0.0).astype(BF16)
            total = total + gates_ref[at, j:j + 1] * dot(hot, scratch[...], NN)
        out_ref[at, :] = total.astype(BF16)
        return carry

    lax.fori_loop(0, after_ref.shape[0] // part, one, 0)


def output_grad_kernel(me_ref, branch_ref, normed_ref, glogits_ref, ggain_ref, m0, m1, m2, m3, room_ref, out_ref, buf, sem):
    width = branch_ref.shape[1]
    for rel, m_ref in enumerate((m0, m1, m2, m3)):
        count = m_ref.shape[1]
        at = pl.ds(pl.multiple_of(jnp.bitwise_xor(me_ref[0], rel) * count, 16), count)
        buf[at, 0:width] = dot(m_ref[...], branch_ref[...], TN).astype(BF16)
    grad_router = dot(normed_ref[...], glogits_ref[...], TN)
    gain = jnp.transpose(jnp.concatenate([ggain_ref[...]] * 16, axis=0))[:, 0:1]
    blank = jnp.zeros((width, buf.shape[1] - width - grad_router.shape[1] - 1), F32)
    buf[:, width:] = jnp.concatenate([grad_router, gain, blank], axis=1).astype(BF16)
    hidden = out_ref.shape[1] - buf.shape[1]
    copy = pltpu.make_async_copy(buf, out_ref.at[:, hidden:], sem)
    copy.start()
    copy.wait()


def final_kernel(me_ref, x_ref, gain_ref, after_ref, d0, d1, d2, d3, w_ref, out_ref):
    grad = sum(
        dot(d_ref[...], w_ref[jnp.bitwise_xor(me_ref[0], rel)], NT) for rel, d_ref in enumerate((d0, d1, d2, d3))
    )
    unit, factor = rms_parts(x_ref[...].astype(F32))
    out_ref[...] = (after_ref[...] + rms_grad(grad, gain_ref[...], unit, factor)).astype(BF16)


def column_grad_kernel(order, heads, me_ref, bins_ref, n0, n1, n2, n3, d0, d1, d2, d3, out_ref, acc):
    acc[...] = sum(dot(n[...], d[...], TN) for n, d in ((n0, d0), (n1, d1), (n2, d2), (n3, d3)))
    cols = 3 * heads * DH
    lane = lax.broadcasted_iota(jnp.int32, (NB, acc.shape[1]), 1)
    table = jnp.zeros((NB, acc.shape[1]), F32)
    for h in range(heads):
        above = jnp.sum(bins_ref[:, h * SEG:(h + 1) * SEG], axis=1, keepdims=True)
        column = above - jnp.concatenate([above[1:], jnp.zeros((1, 1), F32)], axis=0)
        column = jnp.concatenate([column[:-1], -jnp.sum(column[:-1], axis=0, keepdims=True)], axis=0)
        table = jnp.where(lane == cols + h, column, table)
    group = acc.shape[0] // 4
    share = group // len(order)
    for i, rel in enumerate(order):
        first = jnp.bitwise_xor(me_ref[0], rel) * share
        block = [acc[pl.ds(pl.multiple_of(p * group + first, 8), share), :] for p in range(4)]
        block[0] = jnp.concatenate([block[0][:NB] + table, block[0][NB:]], axis=0)
        out_ref[i * 4 * share:(i + 1) * 4 * share, :] = jnp.concatenate(block, axis=0).astype(BF16)


def place_kernel(me_ref, wq_ref, wk_ref, wv_ref, *refs):
    *piece_refs, q_ref, k_ref, v_ref, more_ref, gain_ref = refs
    width = q_ref.shape[1]
    for rel, piece_ref in enumerate(piece_refs):
        count = piece_ref.shape[0]
        at = pl.ds(pl.multiple_of(jnp.bitwise_xor(me_ref[0], rel) * count, 8), count)
        piece = piece_ref[...].astype(F32)
        for c, out_ref in enumerate((q_ref, k_ref, v_ref)):
            out_ref[at, :] = piece[:, c * width:(c + 1) * width]
        more_ref[at, :] = piece[:, 3 * width:]
    total = sum(
        w_ref[...].astype(F32) * out_ref[...] for w_ref, out_ref in ((wq_ref, q_ref), (wk_ref, k_ref), (wv_ref, v_ref))
    )
    gain_ref[...] = jnp.sum(total, axis=1, keepdims=True)


def per_device(
    tokens, gain_attn, w_query, w_key, w_value, w_output, rel_table, gain_moe, router,
    w_in, w_out, routes, parents, cotangent,
):
    n_shard = lax.axis_size("shard")
    n_expert = lax.axis_size("expert")
    tok, width = tokens.shape
    tree_len = tok * n_shard
    n_experts = router.shape[1]
    heads = rel_table.shape[0]
    hw = heads * DH
    wide = -(-3 * hw // 128) * 128
    rows = width // n_shard
    slots = Slots(n_expert, max(2, tok * 20 // (7 * n_experts)))
    me_s, me_e = lax.axis_index("shard").astype(jnp.int32), lax.axis_index("expert").astype(jnp.int32)
    me_shard, me_expert = me_s.reshape(1), me_e.reshape(1)

    more = jnp.concatenate([gain_attn[:, None], gain_moe[:, None], router], axis=1)
    w_rel = pl.pallas_call(
        columns_kernel,
        in_specs=[SMEM] + [VMEM] * 4,
        out_specs=VMEM,
        out_shape=jax.ShapeDtypeStruct((n_shard, rows, -(-(3 * hw + 2 + n_experts) // 128) * 128), BF16),
        compiler_params=params(),
        cost_estimate=SHORT,
    )(me_shard, w_query, w_key, w_value, more)
    near_tokens, far_tokens = swap(tokens, "shard", 1), swap(tokens, "shard", 2)
    w_pieces = swap_all([w_rel[rel] for rel in range(n_shard)], "shard")

    expert_range = jnp.arange(n_experts, dtype=jnp.int32)
    flat_routes = routes.reshape(-1)
    expert_hot = (flat_routes[:, None] == expert_range[None, :]).astype(jnp.int32)
    earlier = jnp.cumsum(expert_hot, axis=0) - expert_hot
    rank = jnp.sum(earlier * expert_hot, axis=-1)
    places = (slots.block_of(flat_routes, me_e) * slots.block + rank).reshape(tok, 2)
    places_row = places.T
    others = jnp.repeat(routes.T[::-1], 8, axis=0).astype(BF16)
    block_shapes = [((len(array) * slots.block, width), BF16) for array in slots.arrays]

    sent_grads = pl.pallas_call(
        functools.partial(dispatch_kernel, slots),
        in_specs=[SMEM] + [VMEM] * 3 + [ANY],
        out_specs=VMEM,
        out_shape=jax.ShapeDtypeStruct((n_expert * slots.block, width), BF16),
        compiler_params=params(),
        cost_estimate=SHORT,
    )(me_expert, places_row, others, cotangent, w_rel)
    got_grads = over_experts(sent_grads)
    far_tokens, _ = lax.optimization_barrier((far_tokens, sent_grads))
    tree = [tokens, near_tokens, far_tokens, swap(far_tokens, "shard", 1)]

    *normed_one, queries, keys, values, keys_t, values_t, w_cols, bias, gain_one, gain_two, router_w = pl.pallas_call(
        functools.partial(project_kernel, heads),
        in_specs=[SMEM] * 2 + [VMEM] * 8 + [ANY],
        out_specs=[VMEM] * 14,
        out_shape=arrays(
            *[((tok, width), BF16)] * 4, *[((tree_len, HW), BF16)] * 3, *[((HW, tree_len), BF16)] * 2,
            ((width, wide), BF16), ((4, SEG, heads * SEG), F32), *[((1, width), F32)] * 2, ((width, n_experts), BF16),
        ),
        scratch_shapes=[pltpu.VMEM((width, 3 * HW + 128), BF16)],
        compiler_params=params(),
        cost_estimate=LONG,
    )(me_shard, rel_table.astype(F32), *w_pieces, *tree, sent_grads)
    parent_row = parents[0]
    *mixed, raw, lse = pl.pallas_call(
        functools.partial(attn_forward_kernel, heads),
        in_specs=[SMEM] * 2 + [VMEM] * 5,
        out_specs=[VMEM] * 6,
        out_shape=arrays(*[((tok, hw), BF16)] * 4, ((tree_len, HW), F32), ((SEGS * 8, heads * SEG), F32)),
        scratch_shapes=[pltpu.VMEM((tree_len, HW), BF16)],
        compiler_params=params(),
        cost_estimate=LONG,
    )(me_shard, parent_row, queries, keys, values, values_t, bias)
    mixed = swap_all(mixed, "shard")

    w_o = lax.all_gather(w_output, "shard", axis=0)
    after, normed_two, gates, *sent_rows = pl.pallas_call(
        functools.partial(post_kernel, slots),
        in_specs=[SMEM] + [VMEM] * 10 + [ANY],
        out_specs=[VMEM] * (3 + len(block_shapes)),
        out_shape=arrays(((tok, width), F32), ((tok, width), BF16), ((tok, 2), F32), *block_shapes),
        compiler_params=params(),
        cost_estimate=LONG,
    )(me_shard, tokens, gain_two, router_w, routes, places_row, *mixed, w_o, got_grads)
    sent_rows = slots.split(sent_rows)
    got_rows = [slots.exchange(c, blocks) for c, blocks in enumerate(sent_rows)]

    w_in, w_out, _ = lax.optimization_barrier((w_in, w_out, w_cols))
    first_w = lax.all_gather(w_in[0], "shard", axis=0, tiled=True)
    second_w = lax.all_gather(w_out[0], "shard", axis=0, tiled=True)
    out_all = near = None
    sent_dx, kept = [], []
    for c, chunk in enumerate(slots.chunks):
        n = len(chunk)
        out_all, *done = run_expert(
            slots, chunk, me_expert, got_rows[c], got_grads, router_w, first_w, second_w, out_all, near
        )
        sent_dx.append(done[:n])
        near = done[0] if c == 0 else done[n]
        kept.append(done[-4:])
    sent_dx[0] = [near]
    dx = [slots.exchange(c, blocks) for c, blocks in enumerate(sent_dx)]
    grad_first = run_first_grad([k[0] for k in kept], [k[3] for k in kept], width + 128)
    grad_second = run_second_grad([k[2] for k in kept], [k[1] for k in kept])

    dx = [block for blocks in dx for block in blocks]
    out_all, _ = lax.optimization_barrier((out_all, dx))
    returned = over_experts(out_all)
    dx, grad_first, grad_second = lax.optimization_barrier((dx, grad_first, grad_second))

    slot_rows = slots.n_expert * slots.block
    grad_after, branch, gm0, gm1, gm2, gm3, glogits, ggain_two = pl.pallas_call(
        functools.partial(back_kernel, slots),
        in_specs=[SMEM] + [VMEM] * (len(block_shapes) + 8),
        out_specs=[VMEM] * 8,
        out_shape=arrays(
            ((tok, width), F32), ((tok, width), BF16), *[((tok, hw), BF16)] * 4, ((tok, n_experts), BF16), ((8, width), F32)
        ),
        scratch_shapes=[pltpu.VMEM((slot_rows, width), BF16)],
        compiler_params=params(),
        cost_estimate=SHORT,
    )(me_shard, *dx, places, routes, gates, after, gain_two, router_w, cotangent, w_o)
    grad_mixed = swap_all([gm0, gm1, gm2, gm3], "shard")
    grad_first = pl.pallas_call(
        output_grad_kernel,
        in_specs=[SMEM] + [VMEM] * 8 + [ANY],
        out_specs=ANY,
        out_shape=jax.ShapeDtypeStruct(grad_first.shape, BF16),
        scratch_shapes=[pltpu.VMEM((width, width + 128), BF16), pltpu.SemaphoreType.DMA],
        input_output_aliases={9: 0},
        compiler_params=params(),
        cost_estimate=SHORT,
    )(me_shard, branch, normed_two, glogits, ggain_two, *mixed, grad_first)

    grad_w_out = lax.psum_scatter(grad_second, "shard", scatter_dimension=0, tiled=True)
    grad_mixed, grad_w_out = lax.optimization_barrier((grad_mixed, grad_w_out))
    *dqkv, bins = pl.pallas_call(
        functools.partial(attn_backward_kernel, heads),
        in_specs=[SMEM] * 2 + [VMEM] * 11,
        out_specs=[VMEM] * 5,
        out_shape=arrays(*[((tok, wide), BF16)] * 4, ((NB, heads * SEG), F32)),
        scratch_shapes=[
            pltpu.VMEM((tree_len, HW), BF16),
            pltpu.VMEM((tree_len, HW), BF16),
            pltpu.VMEM((tree_len, HW), F32),
            pltpu.VMEM((tree_len, HW), F32),
            pltpu.VMEM((2, SEG, heads * SEG), F32),
        ],
        compiler_params=params(),
        cost_estimate=SHORT,
    )(me_shard, parent_row, queries, keys, values, keys_t, raw, lse, *grad_mixed, bias)
    dqkv_own = swap_all(dqkv, "shard")

    hidden = w_in.shape[2]
    grad_w_out = grad_w_out.astype(F32)[None]
    grad_first = lax.psum_scatter(grad_first, "shard", scatter_dimension=0, tiled=True)
    grad_w_in = grad_first[:, :hidden].astype(F32)[None]
    grad_wo = grad_first[:, hidden:]
    output = pl.pallas_call(
        functools.partial(combine_kernel, slots),
        in_specs=[SMEM] + [VMEM] * 4,
        out_specs=VMEM,
        out_shape=jax.ShapeDtypeStruct((tok, width), BF16),
        scratch_shapes=[pltpu.VMEM((slot_rows, width), BF16)],
        compiler_params=params(),
        cost_estimate=SHORT,
    )(me_expert, returned, places, gates, after)

    w_cols, _ = lax.optimization_barrier((w_cols, after))
    w_all = lax.all_gather(w_cols, "shard", axis=0)
    grad_tokens = pl.pallas_call(
        final_kernel,
        in_specs=[SMEM] + [VMEM] * 8,
        out_specs=VMEM,
        out_shape=jax.ShapeDtypeStruct((tok, width), BF16),
        compiler_params=params(),
        cost_estimate=SHORT,
    )(me_shard, tokens, gain_one, grad_after, *dqkv_own, w_all)

    halving = [bit for bit in (1, 2, 4) if bit < n_expert] if n_expert <= 8 else []
    rels = [0]
    for bit in reversed(halving):
        rels = rels + [rel | bit for rel in rels]
    cols = pl.pallas_call(
        functools.partial(column_grad_kernel, rels, heads),
        in_specs=[SMEM] + [VMEM] * 9,
        out_specs=VMEM,
        out_shape=jax.ShapeDtypeStruct((width, wide), BF16),
        scratch_shapes=[pltpu.VMEM((width, wide), F32)],
        compiler_params=params(),
        cost_estimate=SHORT,
    )(me_expert if halving else jnp.zeros((1,), jnp.int32), bins, *normed_one, *dqkv)
    for bit in halving:
        kept_half, sent_half = jnp.split(cols, 2, axis=0)
        cols = (kept_half.astype(F32) + swap(sent_half, "expert", bit).astype(F32)).astype(BF16)
    if halving:
        grad_wo = grad_wo.reshape(n_expert, rows // n_expert, -1)
        grad_wo = reorder([grad_wo[e] for e in range(n_expert)], me_e)
        grad_wo = jnp.concatenate([grad_wo[rel] for rel in rels], axis=0)
        for bit in halving:
            kept_half, sent_half = jnp.split(grad_wo, 2, axis=0)
            grad_wo = (kept_half.astype(F32) + swap(sent_half, "expert", bit).astype(F32)).astype(BF16)
    else:
        cols, grad_wo = lax.psum((cols.astype(F32), grad_wo.astype(F32)), "expert")
        grad_wo = grad_wo.astype(BF16)
    table = cols[:NB, 3 * hw:3 * hw + heads].astype(F32).T
    share = cols.shape[0] // n_shard
    cols = cols.astype(BF16)[:, :3 * hw].reshape(n_shard, share, 3 * hw)
    cols = reorder([cols[p] for p in range(n_shard)], me_s)
    cols = reorder(swap_all(cols, "shard"), me_s)
    cols = jnp.concatenate([c[:, i * hw:(i + 1) * hw] for i in range(3) for c in cols], axis=1)
    cols = jnp.concatenate([cols, grad_wo], axis=1)
    pieces = swap_all([cols] * n_expert, "expert") if halving else [cols]
    pieces, output, grad_w_in, grad_w_out = lax.optimization_barrier((pieces, output, grad_w_in, grad_w_out))
    grad_q, grad_k, grad_v, grad_wo, grad_gain_one = pl.pallas_call(
        place_kernel,
        in_specs=[SMEM] + [VMEM] * (3 + len(pieces)),
        out_specs=[VMEM] * 5,
        out_shape=arrays(*[((rows, width), F32)] * 3, ((rows, width + 128), F32), ((rows, 1), F32)),
        compiler_params=params(),
        cost_estimate=SHORT,
    )(me_expert if halving else jnp.zeros((1,), jnp.int32), w_query, w_key, w_value, *pieces)
    grad_gain_one = grad_gain_one[:, 0] / gain_attn.astype(F32)

    return (
        output, grad_tokens, grad_gain_one, grad_q, grad_k, grad_v, grad_wo[:, :width],
        table, grad_wo[:, width + n_experts], grad_wo[:, width:width + n_experts], grad_w_in, grad_w_out,
    )


def solution(mesh):
    both, shard = P(("expert", "shard"), None), P("shard", None)
    three = P("expert", "shard", None)
    return jax.shard_map(
        per_device,
        mesh=mesh,
        in_specs=(
            both, P("shard"), shard, shard, shard, shard, shard, P("shard"), shard, three, three, both,
            P("expert", None), both,
        ),
        out_specs=(both, both, P("shard"), shard, shard, shard, shard, shard, P("shard"), shard, three, three),
        check_vma=False,
    )
```

```python
import functools
import math

import jax
import jax.numpy as jnp
from jax import lax
from jax.experimental import pallas as pl
from jax.experimental.pallas import tpu as pltpu
from jax.sharding import PartitionSpec as P

DH = 64
NB = 16
SEG = 128
SEGS = 20
TRUNK = 8
SPARE = 3

THRESHOLDS = (1, 2, 3, 4, 5, 6, 7, 8, 12, 16, 24, 32, 48, 64, 96)
EPS = 1e-06
MASKED = -1e30
HW = 256

F32 = jnp.float32
BF16 = jnp.bfloat16
VMEM = pl.BlockSpec(memory_space=pltpu.VMEM)
SMEM = pl.BlockSpec(memory_space=pltpu.SMEM)
ANY = pl.BlockSpec(memory_space=pl.ANY)

NN = ((1,), (0,))
NT = ((1,), (1,))
TN = ((0,), (0,))


def params(mib=60, **more):
    return pltpu.CompilerParams(vmem_limit_bytes=mib << 20, **more)


SHORT = pl.CostEstimate(flops=0, bytes_accessed=1024, transcendentals=0)
LONG = pl.CostEstimate(flops=1 << 40, bytes_accessed=1 << 32, transcendentals=0)


def dot(left, right, contract):
    return lax.dot_general(left, right, (contract, ((), ())), preferred_element_type=F32)


def arrays(*shapes):
    return [jax.ShapeDtypeStruct(shape, dtype) for shape, dtype in shapes]


def rms_parts(values):
    factor = lax.rsqrt(jnp.mean(values * values, axis=-1, keepdims=True) + EPS)
    return values * factor, factor


def rms_grad(grad_out, gain_row, unit_rows, factor):
    scaled = grad_out * gain_row
    return factor * (scaled - unit_rows * jnp.mean(scaled * unit_rows, axis=-1, keepdims=True))


def columns_kernel(me_ref, q_ref, k_ref, v_ref, more_ref, out_ref):
    groups, depth, width = out_ref.shape
    hw = q_ref.shape[1] // groups
    blank = jnp.zeros((depth, width - 3 * hw - more_ref.shape[1]), BF16)
    for s in range(groups):
        at = slice(s * hw, (s + 1) * hw)
        out_ref[jnp.bitwise_xor(me_ref[0], s)] = jnp.concatenate(
            [q_ref[:, at], k_ref[:, at], v_ref[:, at], more_ref[...], blank], axis=1
        )


def project_kernel(
    heads, me_ref, table_ref, w0, w1, w2, w3, t0, t1, t2, t3, before_ref,
    n0, n1, n2, n3, q_ref, k_ref, v_ref, kt_ref, vt_ref, w_ref, bias_ref, gain_ref, gain_two_ref, router_ref, w_pad,
):
    hw = heads * DH
    blank = jnp.zeros((w0.shape[0], HW - hw), BF16)
    for rel, piece_ref in enumerate((w0, w1, w2, w3)):
        depth = piece_ref.shape[0]
        at = pl.ds(pl.multiple_of(jnp.bitwise_xor(me_ref[0], rel) * depth, 16), depth)
        piece = piece_ref[...]
        blank_end = jnp.zeros((depth, w_ref.shape[1] - 3 * hw), BF16)
        w_ref[at, :] = jnp.concatenate([piece[:, :3 * hw], blank_end], axis=1)
        router_ref[at, :] = piece[:, 3 * hw + 2:3 * hw + 2 + router_ref.shape[1]]
        padded = [part for c in range(3) for part in (piece[:, c * hw:(c + 1) * hw], blank)]
        padded.append(piece[:, 3 * hw:3 * hw + 2])
        padded.append(jnp.zeros((depth, w_pad.shape[1] - 3 * HW - 2), BF16))
        w_pad[at, :] = jnp.concatenate(padded, axis=1)
    gains = jnp.transpose(w_pad[:, 3 * HW:].astype(F32))
    gain_ref[...] = gains[0:1]
    gain_two_ref[...] = gains[1:2]
    for rel, (t_ref, n_ref) in enumerate(zip((t0, t1, t2, t3), (n0, n1, n2, n3))):
        count = t_ref.shape[0]
        unit, _ = rms_parts(t_ref[...].astype(F32))
        n_ref[...] = (unit * gain_ref[...]).astype(BF16)
        at = pl.ds(pl.multiple_of(jnp.bitwise_xor(me_ref[0], rel) * count, SEG), count)
        qkv = dot(n_ref[...], w_pad[:, :3 * HW], NN)
        q_ref[at, :] = qkv[:, :HW].astype(BF16) * jnp.asarray(DH ** -0.5, BF16)
        k_ref[at, :] = qkv[:, HW:2 * HW].astype(BF16)
        v_ref[at, :] = qkv[:, 2 * HW:].astype(BF16)
        kt_ref[:, at] = jnp.transpose(qkv[:, HW:2 * HW]).astype(BF16)
        vt_ref[:, at] = jnp.transpose(qkv[:, 2 * HW:]).astype(BF16)
    key = lax.broadcasted_iota(jnp.int32, (SEG, SEG), 0)
    query = lax.broadcasted_iota(jnp.int32, (SEG, SEG), 1)
    bias_ref[0] = jnp.zeros((SEG, heads * SEG), F32)
    bias_ref[3] = jnp.full((SEG, heads * SEG), MASKED, F32)
    for h in range(heads):
        last = table_ref[h, NB - 1]
        at = slice(h * SEG, (h + 1) * SEG)
        for kind, gap in ((1, query - key + SEG), (2, query - key)):
            tile = jnp.zeros((SEG, SEG), F32) + (table_ref[h, 0] - last)
            for i, threshold in enumerate(THRESHOLDS):
                tile = jnp.where(gap >= threshold, table_ref[h, i + 1] - last, tile)
            bias_ref[kind, :, at] = jnp.where(gap >= 0, tile, MASKED)


def by_head(rows, heads):
    lane = lax.broadcasted_iota(jnp.int32, rows.shape, 1)
    zero = jnp.zeros_like(rows)
    return jnp.concatenate(
        [jnp.where((lane >= h * DH) & (lane < (h + 1) * DH), rows, zero) for h in range(heads)], axis=0
    )


def seg_at(index):
    if isinstance(index, int):
        return slice(index * SEG, (index + 1) * SEG)
    return pl.ds(pl.multiple_of(index * SEG, SEG), SEG)


def head_rows(acc, heads):
    pieces = [acc[h * DH:(h + 1) * DH, h * SEG:(h + 1) * SEG] for h in range(heads)]
    pieces.append(jnp.zeros((HW - heads * DH, SEG), F32))
    return jnp.transpose(jnp.concatenate(pieces, axis=0))


def pair_bias(bias_ref, first, second):
    return jnp.concatenate([bias_ref[first], bias_ref[second]], axis=1)


def attn_forward_kernel(
    heads, me_ref, parent_ref, q_ref, k_ref, v_ref, vt_ref, bias_ref, o0, o1, o2, o3, raw_ref, lse_ref, out_all
):
    cols = heads * SEG
    trunk_len = TRUNK * SEG
    last = trunk_len - SEG

    def queries(b):
        return by_head(q_ref[seg_at(b), :], heads)

    def finish(b, acc, total, top):
        lse_ref[pl.ds(b * 8, 8), :] = jnp.broadcast_to(top + jnp.log(total), (8, cols))
        rows = head_rows(acc / total, heads)
        raw_ref[seg_at(b), :] = rows
        out_all[seg_at(b), :] = rows.astype(BF16)

    for j in range(TRUNK // 2):
        q6 = jnp.concatenate([queries(2 * j), queries(2 * j + 1)], axis=0)
        scores = dot(k_ref[0:(j + 1) * 2 * SEG, :], q6, NT)
        parts = []
        if j > 0:
            far = (2 * j - 1) * SEG
            parts = [scores[:far], scores[far:far + SEG] + pair_bias(bias_ref, 1, 0)]
        parts.append(scores[2 * j * SEG:(2 * j + 1) * SEG] + pair_bias(bias_ref, 2, 1))
        parts.append(scores[(2 * j + 1) * SEG:] + pair_bias(bias_ref, 3, 2))
        top = functools.reduce(jnp.maximum, [jnp.max(part, axis=0, keepdims=True) for part in parts])
        parts = [jnp.exp(part - top) for part in parts]
        total = functools.reduce(jnp.add, [jnp.sum(part, axis=0, keepdims=True) for part in parts])
        acc = dot(vt_ref[:, 0:(j + 1) * 2 * SEG], jnp.concatenate([p.astype(BF16) for p in parts], axis=0), NN)
        for s in range(2):
            at = slice(s * cols, (s + 1) * cols)
            finish(2 * j + s, acc[:, at], total[:, at], top[:, at])

    def other_step(i, carry):
        segs = [TRUNK + 2 * i, TRUNK + 2 * i + 1]
        parents = [parent_ref[b] for b in segs]
        leaf = [(parent >= TRUNK).astype(jnp.int32) for parent in parents]
        q3 = [queries(b) for b in segs]
        q6 = jnp.concatenate(q3, axis=0)
        scores = dot(k_ref[0:trunk_len, :], q6, NT)
        near = scores[last:] + pair_bias(bias_ref, 1 - leaf[0], 1 - leaf[1])
        far = scores[:last]
        extra = []
        for s in range(2):
            keys = jnp.concatenate([k_ref[seg_at(parents[s]), :], k_ref[seg_at(segs[s]), :]], axis=0)
            bias = jnp.concatenate([bias_ref[3 - 2 * leaf[s]], bias_ref[2]], axis=0)
            extra.append(dot(keys, q3[s], NT) + bias)
        top = jnp.maximum(jnp.max(far, axis=0, keepdims=True), jnp.max(near, axis=0, keepdims=True))
        top = jnp.maximum(top, jnp.concatenate([jnp.max(e, axis=0, keepdims=True) for e in extra], axis=1))
        far, near = jnp.exp(far - top), jnp.exp(near - top)
        extra = [jnp.exp(extra[s] - top[:, s * cols:(s + 1) * cols]) for s in range(2)]
        total = jnp.sum(far, axis=0, keepdims=True) + jnp.sum(near, axis=0, keepdims=True)
        total = total + jnp.concatenate([jnp.sum(e, axis=0, keepdims=True) for e in extra], axis=1)
        acc = dot(vt_ref[:, 0:trunk_len], jnp.concatenate([far.astype(BF16), near.astype(BF16)], axis=0), NN)
        for s in range(2):
            at = slice(s * cols, (s + 1) * cols)
            values = jnp.concatenate([vt_ref[:, seg_at(parents[s])], vt_ref[:, seg_at(segs[s])]], axis=1)
            finish(segs[s], acc[:, at] + dot(values, extra[s].astype(BF16), NN), total[:, at], top[:, at])
        return carry

    lax.fori_loop(0, (SEGS - TRUNK) // 2, other_step, 0)
    for rel, o_ref in enumerate((o0, o1, o2, o3)):
        count, width = o_ref.shape
        at = pl.ds(pl.multiple_of(jnp.bitwise_xor(me_ref[0], rel) * count, SEG), count)
        o_ref[...] = out_all[at, :][:, :width]


def attn_backward_kernel(
    heads, me_ref, parent_ref, q_ref, k_ref, v_ref, kt_ref, raw_ref, lse_ref, g0, g1, g2, g3_ref, bias_ref,
    d0, d1, d2, d3, bins_ref, grad_all, dq_all, dk_acc, dv_acc, bins_acc,
):
    cols = heads * SEG
    trunk_len = TRUNK * SEG
    dk_acc[...] = jnp.zeros_like(dk_acc)
    dv_acc[...] = jnp.zeros_like(dv_acc)
    bins_acc[...] = jnp.zeros_like(bins_acc)
    for rel, g_ref in enumerate((g0, g1, g2, g3_ref)):
        count, width = g_ref.shape
        at = pl.ds(pl.multiple_of(jnp.bitwise_xor(me_ref[0], rel) * count, SEG), count)
        grad_all[at, :] = jnp.concatenate([g_ref[...], jnp.zeros((count, HW - width), BF16)], axis=1)

    def common(b):
        q3 = by_head(q_ref[seg_at(b), :], heads)
        grad = grad_all[seg_at(b), :]
        product = by_head(grad.astype(F32) * raw_ref[seg_at(b), :], heads)
        high = product.astype(BF16)
        low = (product - high.astype(F32)).astype(BF16)
        ones = jnp.ones((8, HW), BF16)
        row_dot = (dot(ones, high, NT) + dot(ones, low, NT))[0:1]
        return q3, by_head(grad, heads), row_dot, lse_ref[pl.ds(b * 8, 8), :][0:1]

    def block(keys, values, q, g, row_dot, lse, bias):
        scores = dot(keys, q, NT)
        if bias is not None:
            scores = scores + bias
        prob = jnp.exp(scores - lse)
        grad_score = prob * (dot(values, g, NT) - row_dot)
        return prob.astype(BF16), grad_score

    def write_dq(b, acc):
        dq_all[seg_at(b), :] = (head_rows(acc, heads) * DH ** -0.5).astype(BF16)

    def both(pair):
        return [jnp.concatenate([a, b], axis=0 if a.shape[0] > 1 else 1) for a, b in zip(*pair)]

    zero = 0
    for j in range(TRUNK // 2):
        q6, g6, row_dot, lse = both([common(2 * j), common(2 * j + 1)])
        kept = []
        for i in range(j + 1):
            at = slice(2 * i * SEG, 2 * (i + 1) * SEG)
            bias = None
            if i == j:
                bias = jnp.concatenate([pair_bias(bias_ref, 2, 1), pair_bias(bias_ref, 3, 2)], axis=0)
            if i == j - 1:
                bias = jnp.concatenate([pair_bias(bias_ref, zero, zero), pair_bias(bias_ref, 1, zero)], axis=0)
            prob, score = block(k_ref[at, :], v_ref[at, :], q6, g6, row_dot, lse, bias)
            if i == j:
                bins_acc[0] += score[:SEG, cols:]
                bins_acc[1] += score[:SEG, :cols] + score[SEG:, cols:]
            if i == j - 1:
                bins_acc[0] += score[SEG:, :cols]
            score = score.astype(BF16)
            dv_acc[at, :] += dot(prob, g6, NN)
            dk_acc[at, :] += dot(score, q6, NN)
            kept.append(score)
        acc = dot(kt_ref[:, 0:(j + 1) * 2 * SEG], jnp.concatenate(kept, axis=0), NN)
        for s in range(2):
            write_dq(2 * j + s, acc[:, s * cols:(s + 1) * cols])

    def other_step(step, carry):
        segs = [TRUNK + 2 * step, TRUNK + 2 * step + 1]
        parents = [parent_ref[b] for b in segs]
        leaf = [(parent >= TRUNK).astype(jnp.int32) for parent in parents]
        each = [common(b) for b in segs]
        q6, g6, row_dot, lse = both(each)
        kept = []
        for i in range(TRUNK // 2):
            at = slice(2 * i * SEG, 2 * (i + 1) * SEG)
            bias = None
            if i == TRUNK // 2 - 1:
                near = pair_bias(bias_ref, 1 - leaf[0], 1 - leaf[1])
                bias = jnp.concatenate([jnp.zeros_like(near), near], axis=0)
            prob, score = block(k_ref[at, :], v_ref[at, :], q6, g6, row_dot, lse, bias)
            if i == TRUNK // 2 - 1:
                for s in range(2):
                    bins_acc[0] += jnp.where(leaf[s] == 0, score[SEG:, s * cols:(s + 1) * cols], 0.0)
            score = score.astype(BF16)
            dv_acc[at, :] += dot(prob, g6, NN)
            dk_acc[at, :] += dot(score, q6, NN)
            kept.append(score)
        acc = dot(kt_ref[:, 0:trunk_len], jnp.concatenate(kept, axis=0), NN)
        for s in range(2):
            q3, g3, row, own_lse = each[s]
            first, second = seg_at(parents[s]), seg_at(segs[s])
            keys = jnp.concatenate([k_ref[first, :], k_ref[second, :]], axis=0)
            values = jnp.concatenate([v_ref[first, :], v_ref[second, :]], axis=0)
            keys_t = jnp.concatenate([kt_ref[:, first], kt_ref[:, second]], axis=1)
            bias = jnp.concatenate([bias_ref[3 - 2 * leaf[s]], bias_ref[2]], axis=0)
            prob, score = block(keys, values, q3, g3, row, own_lse, bias)
            bins_acc[0] += score[:SEG]
            bins_acc[1] += score[SEG:]
            score = score.astype(BF16)
            grad_v, grad_k = dot(prob, g3, NN), dot(score, q3, NN)
            dv_acc[first, :] += grad_v[:SEG]
            dv_acc[second, :] += grad_v[SEG:]
            dk_acc[first, :] += grad_k[:SEG]
            dk_acc[second, :] += grad_k[SEG:]
            write_dq(segs[s], acc[:, s * cols:(s + 1) * cols] + dot(keys_t, score, NN))
        return carry

    lax.fori_loop(0, (SEGS - TRUNK) // 2, other_step, 0)
    for rel, d_ref in enumerate((d0, d1, d2, d3)):
        count = d_ref.shape[0]
        width = heads * DH
        at = pl.ds(pl.multiple_of(jnp.bitwise_xor(me_ref[0], rel) * count, SEG), count)
        parts = [dq_all[at, :][:, :width], dk_acc[at, :][:, :width].astype(BF16), dv_acc[at, :][:, :width].astype(BF16)]
        parts.append(jnp.zeros((count, d_ref.shape[1] - 3 * width), BF16))
        d_ref[...] = jnp.concatenate(parts, axis=1)
    key = lax.broadcasted_iota(jnp.int32, (SEG, cols), 0)
    query = lax.broadcasted_iota(jnp.int32, (SEG, cols), 1) % SEG
    gap = query - key
    parent_sum, own_sum = bins_acc[0], bins_acc[1]
    lines = [jnp.sum(parent_sum + own_sum, axis=0, keepdims=True)]
    for threshold in THRESHOLDS:
        hit = jnp.where(gap + SEG >= threshold, parent_sum, 0.0) + jnp.where(gap >= threshold, own_sum, 0.0)
        lines.append(jnp.sum(hit, axis=0, keepdims=True))
    bins_ref[...] = jnp.concatenate(lines, axis=0)


class Slots:
    def __init__(self, n_expert, capacity):
        self.n_expert = n_expert
        self.cut = n_expert == 8
        self.block = -(-(capacity + SPARE) // 16) * 16
        if self.cut:
            self.groups = [[0, 1, 4, 5], [2, 3, 6, 7]]
            self.rels = [2, 3, 6, 7]
            self.chunks = [[[0, 1, 2, 3]], [[4], [5], [6], [7]]]
        else:
            self.groups = None
            self.chunks = [[list(range(n_expert))]]
        self.arrays = [array for chunk in self.chunks for array in chunk]

    def block_of(self, expert, me):
        if not self.cut:
            return expert
        rel = jnp.bitwise_xor(expert, me)
        inside = lambda index: (index & 1) | ((index >> 1) & 2)
        return jnp.where((rel & 2) == 0, inside(expert), 4 + inside(rel))

    def expert_of(self, block, me):
        if not self.cut:
            return block
        if block < 4:
            return (me & 2) | (block & 1) | ((block & 2) << 1)
        return jnp.bitwise_xor(me, self.rels[block - 4])

    def split(self, flat):
        flat = list(flat)
        return [[flat.pop(0) for _ in chunk] for chunk in self.chunks]

    def exchange(self, c, blocks):
        if c == 0:
            return [
                lax.all_to_all(
                    blocks[0], "expert", split_axis=0, concat_axis=0, tiled=True, axis_index_groups=self.groups
                )
            ]
        return [swap(block, "expert", rel) for rel, block in zip(self.rels, blocks)]


def over_experts(block):
    return lax.all_to_all(block, "expert", split_axis=0, concat_axis=0, tiled=True)


def swap(block, axis, rel):
    if rel == 0:
        return block
    return lax.ppermute(block, axis, [(i, i ^ rel) for i in range(lax.axis_size(axis))])


def swap_all(blocks, axis):
    return [swap(block, axis, rel) for rel, block in enumerate(blocks)]


def from_all(block):
    near, far = swap(block, "shard", 1), swap(block, "shard", 2)
    return [block, near, far, swap(far, "shard", 1)]


def reorder(parts, me):
    bit = 1
    while bit < len(parts):
        parts = [jnp.where(me & bit, parts[i ^ bit], parts[i]) for i in range(len(parts))]
        bit *= 2
    return parts


def send_rows(slots, rows, places_ref, out_refs):
    tokens = places_ref.shape[1]
    for array, out_ref in zip(slots.arrays, out_refs):
        for i, block in enumerate(array):
            slot = block * slots.block + lax.broadcasted_iota(jnp.int32, (slots.block, tokens), 0)
            hit = (slot == places_ref[0:1, :]) | (slot == places_ref[1:2, :])
            picked = dot(jnp.where(hit, 1.0, 0.0).astype(BF16), rows, NN).astype(BF16)
            out_ref[i * slots.block:(i + 1) * slots.block, :] = picked


def diagonal(count):
    return lax.broadcasted_iota(jnp.int32, (count, count), 0) == lax.broadcasted_iota(jnp.int32, (count, count), 1)


def padded_row(row, width):
    count = row.shape[1]
    return row if count == width else jnp.concatenate([row, jnp.zeros((1, width - count), row.dtype)], axis=1)


def dispatch_kernel(slots, me_ref, places_ref, others_ref, rows_ref, *refs):
    out_ref = refs[-1]
    tokens = places_ref.shape[1]
    width = rows_ref.shape[1]
    rows = rows_ref[...]
    count = slots.block

    def one(expert, carry):
        slot = slots.block_of(expert, me_ref[0]) * count + lax.broadcasted_iota(jnp.int32, (count, tokens), 0)
        hot = [jnp.where(slot == places_ref[j:j + 1, :], 1.0, 0.0).astype(BF16) for j in range(2)]
        picked = dot(hot[0] + hot[1], rows, NN)
        ids = sum(dot(others_ref[8 * j:8 * j + 8, :], hot[j], NT) for j in range(2))
        line = lax.broadcasted_iota(jnp.int32, picked.shape, 0)
        picked = jnp.where(line == count - 1, padded_row(ids[0:1], width), picked)
        out_ref[pl.ds(pl.multiple_of(expert * count, 16), count), :] = picked.astype(BF16)
        return carry

    lax.fori_loop(0, slots.n_expert, one, 0)


def post_kernel(
    slots, me_ref, x_ref, gain_ref, router_ref, routes_ref, places_ref, m0, m1, m2, m3, w_ref, before_ref,
    after_ref, normed_ref, gates_ref, *out_refs,
):
    after = x_ref[...].astype(F32)
    for rel, m_ref in enumerate((m0, m1, m2, m3)):
        after = after + dot(m_ref[...], w_ref[jnp.bitwise_xor(me_ref[0], rel)], NN)
    after_ref[...] = after
    unit, _ = rms_parts(after)
    normed = (unit * gain_ref[...]).astype(BF16)
    normed_ref[...] = normed
    send_rows(slots, normed_ref[...], places_ref, out_refs)
    logits = dot(normed, router_ref[...], NN)
    expert = lax.broadcasted_iota(jnp.int32, logits.shape, 1)
    first = jnp.sum(jnp.where(expert == routes_ref[:, 0:1], logits, 0.0), axis=-1, keepdims=True)
    second = jnp.sum(jnp.where(expert == routes_ref[:, 1:2], logits, 0.0), axis=-1, keepdims=True)
    top = jnp.maximum(first, second)
    first, second = jnp.exp(first - top), jnp.exp(second - top)
    gates_ref[...] = jnp.concatenate([first / (first + second), second / (first + second)], axis=1)


def expert_kernel(slots, chunk, fresh, me_ref, *refs):
    refs = list(refs)
    take = lambda n: [refs.pop(0) for _ in range(n)]
    x_refs = take(len(chunk))
    g_all, router_ref = take(2)
    first_refs = take(4)
    (second_ref,) = take(1)
    if not fresh:
        take(1)
    (out_all,) = take(1)
    dx_refs = take(len(chunk))
    rows_ref, grad_ref, act_ref, inner_ref, first_buf, second_buf, g_buf, out_buf, out_acc, dx_acc, gate_acc, gates_acc, sem, in_sem = refs
    step = pl.program_id(0)
    slot = lax.rem(step, 2)
    total, width = rows_ref.shape
    depth, units = first_refs[0].shape[0], second_buf.shape[1]

    def fetch(rel, slot):
        column = pl.multiple_of(jnp.bitwise_xor(me_ref[1], rel) * units, 128)
        copies = [pltpu.make_async_copy(second_ref.at[pl.ds(column, units), :], second_buf.at[slot], in_sem.at[slot, 4])]
        for piece, ref in enumerate(first_refs):
            row = pl.multiple_of(jnp.bitwise_xor(me_ref[1], piece) * depth, 16)
            copies.append(
                pltpu.make_async_copy(
                    ref.at[:, pl.ds(column, units)], first_buf.at[slot, pl.ds(row, depth), :], in_sem.at[slot, piece]
                )
            )
        return copies

    @pl.when(step == 0)
    def _():
        for copy in fetch(0, 0):
            copy.start()

    for rel in range(4):
        @pl.when(step == rel)
        def _(rel=rel):
            if rel < 3:
                for copy in fetch(rel + 1, (rel + 1) % 2):
                    copy.start()
    rows = slots.block
    pieces = []
    for x_ref, dx_ref, array in zip(x_refs, dx_refs, chunk):
        for i, block in enumerate(array):
            pieces.append((block, x_ref, dx_ref, i * rows, len(pieces) * rows))

    def home(block):
        return pl.ds(pl.multiple_of(slots.expert_of(block, me_ref[0]) * rows, 16), rows)

    @pl.when(step == 0)
    def _():
        copies = [
            pltpu.make_async_copy(g_all.at[home(block), :], g_buf.at[pl.ds(first, rows), :], sem.at[i])
            for i, (block, _, _, _, first) in enumerate(pieces)
        ]
        for copy in copies:
            copy.start()
        out_acc[...] = jnp.zeros_like(out_acc)
        dx_acc[...] = jnp.zeros_like(dx_acc)
        for _, x_ref, _, inside, first in pieces:
            rows_ref[first:first + rows, :] = x_ref[inside:inside + rows, :]
        for copy in copies:
            copy.wait()
        for *_, first in pieces:
            at = slice(first, first + rows)
            grads = g_buf[at, :].astype(F32)
            other = jnp.sum(jnp.where(diagonal(rows), grads[rows - 1:, :rows], 0.0), axis=1, keepdims=True).astype(jnp.int32)
            logits = dot(rows_ref[at, :], router_ref[...], NN)
            expert = lax.broadcasted_iota(jnp.int32, logits.shape, 1)
            mine = jnp.sum(jnp.where(expert == me_ref[0], logits, 0.0), axis=-1, keepdims=True)
            its = jnp.sum(jnp.where(expert == other, logits, 0.0), axis=-1, keepdims=True)
            top = jnp.maximum(mine, its)
            mine, its = jnp.exp(mine - top), jnp.exp(its - top)
            line = lax.broadcasted_iota(jnp.int32, grads.shape, 0)
            gate = mine / (mine + its)
            gate_acc[at, :] = jnp.broadcast_to(gate, (rows, 128))
            grad_ref[at, :] = jnp.where(line < rows - SPARE, gate * grads, 0.0).astype(BF16)

    for rel in range(4):
        @pl.when(step == rel)
        def _(rel=rel):
            for copy in fetch(rel, rel % 2):
                copy.wait()

    parts = 1
    while total // parts > 512 or total % parts or (total // parts) % 16:
        parts += 1
    part = total // parts
    for i in range(parts):
        at = slice(i * part, (i + 1) * part)
        first_w, second_w = first_buf[slot], second_buf[slot]
        value = dot(rows_ref[at, :], first_w, NN)
        grad_act = dot(grad_ref[at, :], second_w, NT)
        square = value * value
        half = 0.5 * value
        scale = 0.7978845608028654
        th = jnp.tanh(value * (scale + (scale * 0.044715) * square))
        act = (half + half * th).astype(BF16)
        slope = 0.5 + 0.5 * th + (half * (1.0 - th * th)) * (scale + (3 * scale * 0.044715) * square)
        inner = (grad_act * slope).astype(BF16)
        act_ref[at, :] = act
        inner_ref[at, :] = inner
        out_acc[at, :] += dot(act, second_w, NN)
        dx_acc[at, :] += dot(inner, first_w, NT)

    @pl.when(step == pl.num_programs(0) - 1)
    def _():
        for *_, first in pieces:
            at = slice(first, first + rows)
            out = out_acc[at, :].astype(BF16).astype(F32)
            gates = jnp.sum(out * g_buf[at, :].astype(F32), axis=1, keepdims=True)
            gates_acc[at, :] = jnp.broadcast_to(gates, (rows, 128))
            out_buf[at, :] = (gate_acc[at, 0:1] * out).astype(BF16)
        copies = [
            pltpu.make_async_copy(out_buf.at[pl.ds(first, rows), :], out_all.at[home(block), :], sem.at[i])
            for i, (block, _, _, _, first) in enumerate(pieces)
        ]
        for copy in copies:
            copy.start()
        for _, _, dx_ref, inside, first in pieces:
            at = slice(first, first + rows)
            gates = gates_acc[at, 0:1]
            gates = jnp.sum(jnp.where(diagonal(rows), gates, 0.0), axis=0, keepdims=True)
            dx_ref[inside:inside + rows, :] = dx_acc[at, :].astype(BF16)
            tail = dx_acc[first + rows - 16:first + rows, :]
            line = lax.broadcasted_iota(jnp.int32, tail.shape, 0)
            for place in range(SPARE):
                piece = gates.astype(BF16).astype(F32)
                gates = gates - piece
                tail = jnp.where(line == 16 - SPARE + place, padded_row(piece, width), tail)
            dx_ref[inside + rows - 16:inside + rows, :] = tail.astype(BF16)
        for copy in copies:
            copy.wait()


def run_expert(slots, chunk, me, blocks, g_all, router, first_w, second_w, out_all, estimate):
    hidden, width = first_w[0].shape[1], router.shape[0]
    total = sum(block.shape[0] for block in blocks)
    block = hidden // 4
    whole = lambda a: pl.BlockSpec(a.shape, lambda i: (0, 0))
    column = pl.BlockSpec((total, block), lambda i: (0, i))
    rows = pl.BlockSpec((total, width), lambda i: (0, 0))
    fresh = out_all is None
    inputs = [me, *blocks, g_all, router, *first_w, second_w] + ([] if fresh else [out_all])
    return pl.pallas_call(
        functools.partial(expert_kernel, slots, chunk, fresh),
        grid=(4,),
        in_specs=[SMEM] + [whole(b) for b in blocks] + [ANY, whole(router)] + [ANY] * 5 + ([] if fresh else [ANY]),
        out_specs=[ANY] + [whole(b) for b in blocks] + [rows, rows, column, column],
        out_shape=arrays(
            (g_all.shape, BF16), *[(b.shape, BF16) for b in blocks], *[((total, width), BF16)] * 2, *[((total, hidden), BF16)] * 2
        ),
        scratch_shapes=[
            pltpu.VMEM((2, width, block), BF16),
            pltpu.VMEM((2, block, width), BF16),
            pltpu.VMEM((total, width), BF16),
            pltpu.VMEM((total, width), BF16),
            pltpu.VMEM((total, width), F32),
            pltpu.VMEM((total, width), F32),
            pltpu.VMEM((total, 128), F32),
            pltpu.VMEM((total, 128), F32),
            pltpu.SemaphoreType.DMA((sum(len(array) for array in chunk),)),
            pltpu.SemaphoreType.DMA((2, 5)),
        ],
        input_output_aliases={} if fresh else {len(inputs) - 1: 0},
        compiler_params=params(dimension_semantics=("arbitrary",)),
        cost_estimate=estimate,
    )(*inputs)


def first_grad_kernel(parts, me_ref, *refs):
    send_ref, keep_ref, total = refs[-3:]
    total[...] = sum(dot(x[...], inner[...], TN) for x, inner in zip(refs[:parts], refs[parts:2 * parts]))
    depth = send_ref.shape[0] // 2
    for rel in range(4):
        ref = (keep_ref, send_ref)[rel % 2]
        row = pl.multiple_of(jnp.bitwise_xor(me_ref[1], rel) * depth, 16)
        at = rel // 2 * depth
        ref[at:at + depth, :] = total[pl.ds(row, depth), :].astype(BF16)


def run_first_grad(me, rows, inners, depth, *after):
    width, hidden = rows[0].shape[1], inners[0].shape[1]
    block = hidden // 4
    column = pl.BlockSpec((2 * depth, block), lambda i, me_ref: (0, jnp.bitwise_xor(me_ref[1], i)))
    return pl.pallas_call(
        functools.partial(first_grad_kernel, len(rows)),
        grid_spec=pltpu.PrefetchScalarGridSpec(
            num_scalar_prefetch=1,
            grid=(4,),
            in_specs=[pl.BlockSpec(a.shape, lambda i, me_ref: (0, 0)) for a in rows]
            + [pl.BlockSpec((a.shape[0], block), lambda i, me_ref: (0, i)) for a in inners]
            + [ANY] * len(after),
            out_specs=[column, column],
            scratch_shapes=[pltpu.VMEM((width, block), F32)],
        ),
        out_shape=arrays(*[((2 * depth, hidden), BF16)] * 2),
        compiler_params=params(dimension_semantics=("arbitrary",)),
        cost_estimate=SHORT,
    )(me, *rows, *inners, *after)


def second_grad_kernel(parts, *refs):
    send_ref, keep_ref = refs[2 * parts:]
    step = pl.program_id(0)
    block = sum(dot(act[...], g[...], TN) for act, g in zip(refs[:parts], refs[parts:2 * parts])).astype(BF16)

    @pl.when(step < 2)
    def _():
        send_ref[...] = block

    @pl.when(step >= 2)
    def _():
        keep_ref[...] = block


def run_second_grad(acts, grads):
    width, hidden = grads[0].shape[1], acts[0].shape[1]
    block = hidden // 4
    return pl.pallas_call(
        functools.partial(second_grad_kernel, len(acts)),
        grid=(4,),
        in_specs=[pl.BlockSpec((a.shape[0], block), lambda i: (0, 2 * (i % 2) + 1 - i // 2)) for a in acts]
        + [pl.BlockSpec(a.shape, lambda i: (0, 0)) for a in grads],
        out_specs=[
            pl.BlockSpec((block, width), lambda i: (jnp.minimum(i, 1), 0)),
            pl.BlockSpec((block, width), lambda i: (jnp.maximum(i - 2, 0), 0)),
        ],
        out_shape=arrays(*[((2 * block, width), BF16)] * 2),
        compiler_params=params(dimension_semantics=("arbitrary",)),
        cost_estimate=SHORT,
    )(*acts, *grads)


def core_sum(send, keep):
    near = swap(send, "shard", 1)
    half = keep.shape[0] // 2
    other = (keep[half:].astype(F32) + near[half:].astype(F32)).astype(BF16)
    return keep, near, other


def across_sum(parts):
    keep, near, other = parts
    return keep, near, swap(other, "shard", 2)


def total_sum(parts):
    keep, near, far = parts
    half = keep.shape[0] // 2
    return keep[:half].astype(F32) + near[:half].astype(F32) + far.astype(F32)


def gather_blocks(slots, refs, scratch):
    for array, ref in zip(slots.arrays, refs):
        scratch[array[0] * slots.block:(array[-1] + 1) * slots.block, :] = ref[...]


def back_kernel(slots, me_ref, *refs):
    refs_left = list(refs)
    take = lambda n: [refs_left.pop(0) for _ in range(n)]
    ret_refs = take(len(slots.arrays))
    places_ref, routes_ref, gates_ref, after_ref, gain_ref, router_ref, g_ref = take(7)
    w_ref, normed_ref = take(2)
    m_refs = take(4)
    (grad_after_ref,) = take(1)
    mixed_refs = take(4)
    send_ref, keep_ref, branch_ref, glogits_ref, ggain_ref, more, scratch = refs_left
    tokens = after_ref.shape[0]
    part = 128
    gather_blocks(slots, ret_refs, scratch)
    pieces = []
    for end in range(slots.block, scratch.shape[0] + 1, slots.block):
        tail = scratch[end - 16:end, :].astype(F32)[16 - SPARE:, :slots.block]
        pieces.append(jnp.sum(tail, axis=0, keepdims=True))
    gg = jnp.concatenate(pieces, axis=1)
    ggain_ref[...] = jnp.zeros_like(ggain_ref)

    def one(i, carry):
        at = pl.ds(pl.multiple_of(i * part, part), part)
        slot = lax.broadcasted_iota(jnp.int32, (part, gg.shape[1]), 1)
        hit0, hit1 = slot == places_ref[at, 0:1], slot == places_ref[at, 1:2]
        gg0 = jnp.sum(jnp.where(hit0, gg, 0.0), axis=-1, keepdims=True)
        gg1 = jnp.sum(jnp.where(hit1, gg, 0.0), axis=-1, keepdims=True)
        total = dot(jnp.where(hit0 | hit1, 1.0, 0.0).astype(BF16), scratch[...], NN)
        gate0, gate1 = gates_ref[at, 0:1], gates_ref[at, 1:2]
        mean = gate0 * gg0 + gate1 * gg1
        expert = lax.broadcasted_iota(jnp.int32, (part, router_ref.shape[1]), 1)
        glogits = jnp.where(expert == routes_ref[at, 0:1], gate0 * (gg0 - mean), 0.0) + jnp.where(
            expert == routes_ref[at, 1:2], gate1 * (gg1 - mean), 0.0
        )
        glogits = glogits.astype(BF16)
        glogits_ref[at, :] = glogits
        incoming = dot(glogits, router_ref[...], NT) + total
        unit, factor = rms_parts(after_ref[at, :])
        grad_after = g_ref[at, :].astype(F32) + rms_grad(incoming, gain_ref[...], unit, factor)
        ggain_ref[0:1, :] += jnp.sum(incoming * unit, axis=0, keepdims=True)
        grad_after_ref[at, :] = grad_after
        branch = grad_after.astype(BF16)
        branch_ref[at, :] = branch
        for rel, mixed_ref in enumerate(mixed_refs):
            mixed_ref[at, :] = dot(branch, w_ref[jnp.bitwise_xor(me_ref[0], rel)], NT).astype(BF16)
        return carry

    lax.fori_loop(0, tokens // part, one, 0)
    width = branch_ref.shape[1]
    grad_router = dot(normed_ref[...], glogits_ref[...], TN)
    gain = jnp.transpose(jnp.concatenate([ggain_ref[...]] * 16, axis=0))[:, 0:1]
    blank = jnp.zeros((width, more.shape[1] - grad_router.shape[1] - 1), F32)
    more[...] = jnp.concatenate([grad_router, gain, blank], axis=1)
    for rel, m_ref in enumerate(m_refs):
        ref = (keep_ref, send_ref)[rel % 2]
        count = m_ref.shape[1]
        at = slice(rel // 2 * count, (rel // 2 + 1) * count)
        ref[at, 0:width] = dot(m_ref[...], branch_ref[...], TN).astype(BF16)
        row = pl.multiple_of(jnp.bitwise_xor(me_ref[0], rel) * count, 16)
        ref[at, width:] = more[pl.ds(row, count), :].astype(BF16)


def combine_kernel(slots, me_ref, ret_ref, places_ref, after_ref, out_ref, scratch):
    part = 128
    for block in range(slots.n_expert):
        first = pl.multiple_of(slots.expert_of(block, me_ref[0]) * slots.block, 16)
        scratch[block * slots.block:(block + 1) * slots.block, :] = ret_ref[pl.ds(first, slots.block), :]

    def one(i, carry):
        at = pl.ds(pl.multiple_of(i * part, part), part)
        slot = lax.broadcasted_iota(jnp.int32, (part, scratch.shape[0]), 1)
        hit = (slot == places_ref[at, 0:1]) | (slot == places_ref[at, 1:2])
        total = after_ref[at, :] + dot(jnp.where(hit, 1.0, 0.0).astype(BF16), scratch[...], NN)
        out_ref[at, :] = total.astype(BF16)
        return carry

    lax.fori_loop(0, after_ref.shape[0] // part, one, 0)


def final_kernel(me_ref, x_ref, gain_ref, after_ref, d0, d1, d2, d3, w_ref, out_ref):
    grad = sum(
        dot(d_ref[...], w_ref[jnp.bitwise_xor(me_ref[0], rel)], NT) for rel, d_ref in enumerate((d0, d1, d2, d3))
    )
    unit, factor = rms_parts(x_ref[...].astype(F32))
    out_ref[...] = (after_ref[...] + rms_grad(grad, gain_ref[...], unit, factor)).astype(BF16)


def column_grad_kernel(order, heads, me_ref, bins_ref, n0, n1, n2, n3, d0, d1, d2, d3, out_ref, acc):
    acc[...] = sum(dot(n[...], d[...], TN) for n, d in ((n0, d0), (n1, d1), (n2, d2), (n3, d3)))
    cols = 3 * heads * DH
    lane = lax.broadcasted_iota(jnp.int32, (NB, acc.shape[1]), 1)
    table = jnp.zeros((NB, acc.shape[1]), F32)
    for h in range(heads):
        above = jnp.sum(bins_ref[:, h * SEG:(h + 1) * SEG], axis=1, keepdims=True)
        column = above - jnp.concatenate([above[1:], jnp.zeros((1, 1), F32)], axis=0)
        column = jnp.concatenate([column[:-1], -jnp.sum(column[:-1], axis=0, keepdims=True)], axis=0)
        table = jnp.where(lane == cols + h, column, table)
    group = acc.shape[0] // 4
    share = group // len(order)
    for i, rel in enumerate(order):
        first = jnp.bitwise_xor(me_ref[0], rel) * share
        block = [acc[pl.ds(pl.multiple_of(p * group + first, 8), share), :] for p in range(4)]
        block[0] = jnp.concatenate([block[0][:NB] + table, block[0][NB:]], axis=0)
        out_ref[i * 4 * share:(i + 1) * 4 * share, :] = jnp.concatenate(block, axis=0).astype(BF16)


def place_kernel(me_ref, wq_ref, wk_ref, wv_ref, *refs):
    *piece_refs, q_ref, k_ref, v_ref, more_ref, gain_ref = refs
    width = q_ref.shape[1]
    for rel, piece_ref in enumerate(piece_refs):
        count = piece_ref.shape[0]
        at = pl.ds(pl.multiple_of(jnp.bitwise_xor(me_ref[0], rel) * count, 8), count)
        piece = piece_ref[...].astype(F32)
        for c, out_ref in enumerate((q_ref, k_ref, v_ref)):
            out_ref[at, :] = piece[:, c * width:(c + 1) * width]
        more_ref[at, :] = piece[:, 3 * width:]
    total = sum(
        w_ref[...].astype(F32) * out_ref[...] for w_ref, out_ref in ((wq_ref, q_ref), (wk_ref, k_ref), (wv_ref, v_ref))
    )
    gain_ref[...] = jnp.sum(total, axis=1, keepdims=True)


def per_device(
    tokens, gain_attn, w_query, w_key, w_value, w_output, rel_table, gain_moe, router,
    w_in, w_out, routes, parents, cotangent,
):
    n_shard = lax.axis_size("shard")
    n_expert = lax.axis_size("expert")
    tok, width = tokens.shape
    tree_len = tok * n_shard
    n_experts = router.shape[1]
    heads = rel_table.shape[0]
    hw = heads * DH
    wide = -(-3 * hw // 128) * 128
    rows = width // n_shard
    slots = Slots(n_expert, max(2, tok * 20 // (7 * n_experts)))
    me_s, me_e = lax.axis_index("shard").astype(jnp.int32), lax.axis_index("expert").astype(jnp.int32)
    me_shard, me_expert, me = me_s.reshape(1), me_e.reshape(1), jnp.stack([me_e, me_s])

    more = jnp.concatenate([gain_attn[:, None], gain_moe[:, None], router], axis=1)
    w_rel = pl.pallas_call(
        columns_kernel,
        in_specs=[SMEM] + [VMEM] * 4,
        out_specs=VMEM,
        out_shape=jax.ShapeDtypeStruct((n_shard, rows, -(-(3 * hw + 2 + n_experts) // 128) * 128), BF16),
        compiler_params=params(),
        cost_estimate=SHORT,
    )(me_shard, w_query, w_key, w_value, more)
    near_tokens, far_tokens = swap(tokens, "shard", 1), swap(tokens, "shard", 2)
    w_pieces = swap_all([w_rel[rel] for rel in range(n_shard)], "shard")

    expert_range = jnp.arange(n_experts, dtype=jnp.int32)
    flat_routes = routes.reshape(-1)
    expert_hot = (flat_routes[:, None] == expert_range[None, :]).astype(jnp.int32)
    earlier = jnp.cumsum(expert_hot, axis=0) - expert_hot
    rank = jnp.sum(earlier * expert_hot, axis=-1)
    places = (slots.block_of(flat_routes, me_e) * slots.block + rank).reshape(tok, 2)
    places_row = places.T
    others = jnp.repeat(routes.T[::-1], 8, axis=0).astype(BF16)
    block_shapes = [((len(array) * slots.block, width), BF16) for array in slots.arrays]

    sent_grads = pl.pallas_call(
        functools.partial(dispatch_kernel, slots),
        in_specs=[SMEM] + [VMEM] * 3 + [ANY],
        out_specs=VMEM,
        out_shape=jax.ShapeDtypeStruct((n_expert * slots.block, width), BF16),
        compiler_params=params(),
        cost_estimate=SHORT,
    )(me_expert, places_row, others, cotangent, w_rel)
    got_grads = over_experts(sent_grads)
    far_tokens, _ = lax.optimization_barrier((far_tokens, sent_grads))
    tree = [tokens, near_tokens, far_tokens, swap(far_tokens, "shard", 1)]

    *normed_one, queries, keys, values, keys_t, values_t, w_cols, bias, gain_one, gain_two, router_w = pl.pallas_call(
        functools.partial(project_kernel, heads),
        in_specs=[SMEM] * 2 + [VMEM] * 8 + [ANY],
        out_specs=[VMEM] * 14,
        out_shape=arrays(
            *[((tok, width), BF16)] * 4, *[((tree_len, HW), BF16)] * 3, *[((HW, tree_len), BF16)] * 2,
            ((width, wide), BF16), ((4, SEG, heads * SEG), F32), *[((1, width), F32)] * 2, ((width, n_experts), BF16),
        ),
        scratch_shapes=[pltpu.VMEM((width, 3 * HW + 128), BF16)],
        compiler_params=params(),
        cost_estimate=LONG,
    )(me_shard, rel_table.astype(F32), *w_pieces, *tree, sent_grads)
    parent_row = parents[0]
    *mixed, raw, lse = pl.pallas_call(
        functools.partial(attn_forward_kernel, heads),
        in_specs=[SMEM] * 2 + [VMEM] * 5,
        out_specs=[VMEM] * 6,
        out_shape=arrays(*[((tok, hw), BF16)] * 4, ((tree_len, HW), F32), ((SEGS * 8, heads * SEG), F32)),
        scratch_shapes=[pltpu.VMEM((tree_len, HW), BF16)],
        compiler_params=params(),
        cost_estimate=LONG,
    )(me_shard, parent_row, queries, keys, values, values_t, bias)
    first_far = swap(w_in[0], "shard", 2)
    mixed, first_far = lax.optimization_barrier((mixed, first_far))
    mixed = swap_all(mixed, "shard")
    first_w = [w_in[0], swap(w_in[0], "shard", 1), first_far, swap(first_far, "shard", 1)]
    w_out, w_cols, _ = lax.optimization_barrier((w_out, w_cols, mixed))
    second_w = lax.all_gather(w_out[0], "shard", axis=0, tiled=True)
    mixed, first_w = lax.optimization_barrier((mixed, first_w))

    w_o = lax.all_gather(w_output, "shard", axis=0)
    after, normed_two, gates, *sent_rows = pl.pallas_call(
        functools.partial(post_kernel, slots),
        in_specs=[SMEM] + [VMEM] * 10 + [ANY],
        out_specs=[VMEM] * (3 + len(block_shapes)),
        out_shape=arrays(((tok, width), F32), ((tok, width), BF16), ((tok, 2), F32), *block_shapes),
        compiler_params=params(),
        cost_estimate=LONG,
    )(me_shard, tokens, gain_two, router_w, routes, places_row, *mixed, w_o, got_grads)
    sent_rows = slots.split(sent_rows)
    got_rows = [slots.exchange(c, blocks) for c, blocks in enumerate(sent_rows)]

    out_all = None
    dx, kept = [], []
    for c, chunk in enumerate(slots.chunks):
        n = len(chunk)
        out_all, *done = run_expert(
            slots, chunk, me, got_rows[c], got_grads, router_w, first_w, second_w, out_all, LONG if c else SHORT
        )
        dx.append(slots.exchange(c, done[:n]))
        kept.append(done[n:])
    send_second, keep_second = run_second_grad([k[2] for k in kept], [k[1] for k in kept])
    dx = [block for blocks in dx for block in blocks]
    w_cols, _ = lax.optimization_barrier((w_cols, kept[0][0]))
    w_all = lax.all_gather(w_cols, "shard", axis=0)
    send_first, keep_first = run_first_grad(me, [k[0] for k in kept], [k[3] for k in kept], rows, dx[0], w_all)
    out_all, _ = lax.optimization_barrier((out_all, dx))
    returned = over_experts(out_all)
    dx, send_first, send_second = lax.optimization_barrier((dx, send_first, send_second))

    slot_rows = slots.n_expert * slots.block
    grad_after, gm0, gm1, gm2, gm3, send_wo, keep_wo = pl.pallas_call(
        functools.partial(back_kernel, slots),
        in_specs=[SMEM] + [VMEM] * (len(block_shapes) + 13),
        out_specs=[VMEM] * 7,
        out_shape=arrays(((tok, width), F32), *[((tok, hw), BF16)] * 4, *[((2 * rows, width + 128), BF16)] * 2),
        scratch_shapes=[
            pltpu.VMEM((tok, width), BF16),
            pltpu.VMEM((tok, n_experts), BF16),
            pltpu.VMEM((8, width), F32),
            pltpu.VMEM((width, 128), F32),
            pltpu.VMEM((slot_rows, width), BF16),
        ],
        compiler_params=params(),
        cost_estimate=SHORT,
    )(me_shard, *dx, places, routes, gates, after, gain_two, router_w, cotangent, w_o, normed_two, *mixed)
    grad_mixed = swap_all([gm0, gm1, gm2, gm3], "shard")
    sums = [
        core_sum(send, keep)
        for send, keep in ((send_second, keep_second), (send_first, keep_first), (send_wo, keep_wo))
    ]
    grad_mixed, sums = lax.optimization_barrier((grad_mixed, sums))
    second_sum, first_sum, wo_sum = sums
    second_sum, wo_sum = across_sum(second_sum), across_sum(wo_sum)

    *dqkv, bins = pl.pallas_call(
        functools.partial(attn_backward_kernel, heads),
        in_specs=[SMEM] * 2 + [VMEM] * 11,
        out_specs=[VMEM] * 5,
        out_shape=arrays(*[((tok, wide), BF16)] * 4, ((NB, heads * SEG), F32)),
        scratch_shapes=[
            pltpu.VMEM((tree_len, HW), BF16),
            pltpu.VMEM((tree_len, HW), BF16),
            pltpu.VMEM((tree_len, HW), F32),
            pltpu.VMEM((tree_len, HW), F32),
            pltpu.VMEM((2, SEG, heads * SEG), F32),
        ],
        compiler_params=params(),
        cost_estimate=LONG,
    )(me_shard, parent_row, queries, keys, values, keys_t, raw, lse, *grad_mixed, bias)
    dqkv, second_sum, wo_sum = lax.optimization_barrier((dqkv, second_sum, wo_sum))
    dqkv_own = swap_all(dqkv, "shard")

    grad_w_out, grad_wo = total_sum(second_sum)[None], total_sum(wo_sum).astype(BF16)
    halving = [bit for bit in (1, 2, 4) if bit < n_expert] if n_expert <= 8 else []
    rels = [0]
    for bit in reversed(halving):
        rels = rels + [rel | bit for rel in rels]
    cols = pl.pallas_call(
        functools.partial(column_grad_kernel, rels, heads),
        in_specs=[SMEM] + [VMEM] * 9,
        out_specs=VMEM,
        out_shape=jax.ShapeDtypeStruct((width, wide), BF16),
        scratch_shapes=[pltpu.VMEM((width, wide), F32)],
        compiler_params=params(),
        cost_estimate=SHORT,
    )(me_expert if halving else jnp.zeros((1,), jnp.int32), bins, *normed_one, *dqkv)
    for bit in halving:
        kept_half, sent_half = jnp.split(cols, 2, axis=0)
        if bit == halving[-1]:
            sent_half, dqkv_own = lax.optimization_barrier((sent_half, dqkv_own))
        cols = (kept_half.astype(F32) + swap(sent_half, "expert", bit).astype(F32)).astype(BF16)
    if halving:
        grad_wo = grad_wo.reshape(n_expert, rows // n_expert, -1)
        grad_wo = reorder([grad_wo[e] for e in range(n_expert)], me_e)
        grad_wo = jnp.concatenate([grad_wo[rel] for rel in rels], axis=0)
        for bit in halving:
            kept_half, sent_half = jnp.split(grad_wo, 2, axis=0)
            grad_wo = (kept_half.astype(F32) + swap(sent_half, "expert", bit).astype(F32)).astype(BF16)
    else:
        cols, grad_wo = lax.psum((cols.astype(F32), grad_wo.astype(F32)), "expert")
        grad_wo = grad_wo.astype(BF16)
    table = cols[:NB, 3 * hw:3 * hw + heads].astype(F32).T
    share = cols.shape[0] // n_shard
    cols = cols.astype(BF16)[:, :3 * hw].reshape(n_shard, share, 3 * hw)
    cols, dqkv_own = lax.optimization_barrier((cols, dqkv_own))
    grad_tokens = pl.pallas_call(
        final_kernel,
        in_specs=[SMEM] + [VMEM] * 8,
        out_specs=VMEM,
        out_shape=jax.ShapeDtypeStruct((tok, width), BF16),
        compiler_params=params(),
        cost_estimate=SHORT,
    )(me_shard, tokens, gain_one, grad_after, *dqkv_own, w_all)
    cols = reorder([cols[p] for p in range(n_shard)], me_s)
    cols, first_sum = lax.optimization_barrier((swap_all(cols, "shard"), first_sum))
    cols = reorder(cols, me_s)
    grad_w_in = total_sum(across_sum(first_sum))[None]
    cols = jnp.concatenate([c[:, i * hw:(i + 1) * hw] for i in range(3) for c in cols], axis=1)
    cols = jnp.concatenate([cols, grad_wo], axis=1)
    returned, _ = lax.optimization_barrier((returned, cols))
    output = pl.pallas_call(
        functools.partial(combine_kernel, slots),
        in_specs=[SMEM] + [VMEM] * 3,
        out_specs=VMEM,
        out_shape=jax.ShapeDtypeStruct((tok, width), BF16),
        scratch_shapes=[pltpu.VMEM((slot_rows, width), BF16)],
        compiler_params=params(),
        cost_estimate=SHORT,
    )(me_expert, returned, places, after)
    pieces = swap_all([cols] * n_expert, "expert") if halving else [cols]
    pieces, output, grad_w_in, grad_w_out = lax.optimization_barrier((pieces, output, grad_w_in, grad_w_out))
    grad_q, grad_k, grad_v, grad_wo, grad_gain_one = pl.pallas_call(
        place_kernel,
        in_specs=[SMEM] + [VMEM] * (3 + len(pieces)),
        out_specs=[VMEM] * 5,
        out_shape=arrays(*[((rows, width), F32)] * 3, ((rows, width + 128), F32), ((rows, 1), F32)),
        compiler_params=params(),
        cost_estimate=SHORT,
    )(me_expert if halving else jnp.zeros((1,), jnp.int32), w_query, w_key, w_value, *pieces)
    grad_gain_one = grad_gain_one[:, 0] / gain_attn.astype(F32)

    return (
        output, grad_tokens, grad_gain_one, grad_q, grad_k, grad_v, grad_wo[:, :width],
        table, grad_wo[:, width + n_experts], grad_wo[:, width:width + n_experts], grad_w_in, grad_w_out,
    )


def solution(mesh):
    both, shard = P(("expert", "shard"), None), P("shard", None)
    three = P("expert", "shard", None)
    return jax.shard_map(
        per_device,
        mesh=mesh,
        in_specs=(
            both, P("shard"), shard, shard, shard, shard, shard, P("shard"), shard, three, three, both,
            P("expert", None), both,
        ),
        out_specs=(both, both, P("shard"), shard, shard, shard, shard, shard, P("shard"), shard, three, three),
        check_vma=False,
    )
```

```python
import functools
import math

import jax
import jax.numpy as jnp
from jax import lax
from jax.experimental import pallas as pl
from jax.experimental.pallas import tpu as pltpu
from jax.sharding import PartitionSpec as P

DH = 64
NB = 16
SEG = 128
SEGS = 20
TRUNK = 8
SPARE = 3

THRESHOLDS = (1, 2, 3, 4, 5, 6, 7, 8, 12, 16, 24, 32, 48, 64, 96)
EPS = 1e-06
MASKED = -1e30
HW = 256

F32 = jnp.float32
BF16 = jnp.bfloat16
VMEM = pl.BlockSpec(memory_space=pltpu.VMEM)
SMEM = pl.BlockSpec(memory_space=pltpu.SMEM)
ANY = pl.BlockSpec(memory_space=pl.ANY)

NN = ((1,), (0,))
NT = ((1,), (1,))
TN = ((0,), (0,))


def params(mib=60, **more):
    return pltpu.CompilerParams(vmem_limit_bytes=mib << 20, **more)


SHORT = pl.CostEstimate(flops=0, bytes_accessed=1024, transcendentals=0)
LONG = pl.CostEstimate(flops=1 << 40, bytes_accessed=1 << 32, transcendentals=0)


FORWARD = pl.CostEstimate(flops=30_400_000_000, bytes_accessed=1024, transcendentals=0)


def dot(left, right, contract):
    return lax.dot_general(left, right, (contract, ((), ())), preferred_element_type=F32)


def arrays(*shapes):
    return [jax.ShapeDtypeStruct(shape, dtype) for shape, dtype in shapes]


def rms_parts(values):
    factor = lax.rsqrt(jnp.mean(values * values, axis=-1, keepdims=True) + EPS)
    return values * factor, factor


def rms_grad(grad_out, gain_row, unit_rows, factor):
    scaled = grad_out * gain_row
    return factor * (scaled - unit_rows * jnp.mean(scaled * unit_rows, axis=-1, keepdims=True))


def columns_kernel(me_ref, q_ref, k_ref, v_ref, more_ref, out_ref):
    groups, depth, width = out_ref.shape
    hw = q_ref.shape[1] // groups
    blank = jnp.zeros((depth, width - 3 * hw - more_ref.shape[1]), BF16)
    for s in range(groups):
        at = slice(s * hw, (s + 1) * hw)
        out_ref[jnp.bitwise_xor(me_ref[0], s)] = jnp.concatenate(
            [q_ref[:, at], k_ref[:, at], v_ref[:, at], more_ref[...], blank], axis=1
        )


def project_kernel(
    heads, me_ref, table_ref, w0, w1, w2, w3, t0, t1, t2, t3, before_ref,
    n0, n1, n2, n3, q_ref, k_ref, v_ref, kt_ref, vt_ref, w_ref, bias_ref, gain_ref, gain_two_ref, router_ref, w_pad,
):
    hw = heads * DH
    blank = jnp.zeros((w0.shape[0], HW - hw), BF16)
    for rel, piece_ref in enumerate((w0, w1, w2, w3)):
        depth = piece_ref.shape[0]
        at = pl.ds(pl.multiple_of(jnp.bitwise_xor(me_ref[0], rel) * depth, 16), depth)
        piece = piece_ref[...]
        blank_end = jnp.zeros((depth, w_ref.shape[1] - 3 * hw), BF16)
        w_ref[at, :] = jnp.concatenate([piece[:, :3 * hw], blank_end], axis=1)
        router_ref[at, :] = piece[:, 3 * hw + 2:3 * hw + 2 + router_ref.shape[1]]
        padded = [part for c in range(3) for part in (piece[:, c * hw:(c + 1) * hw], blank)]
        padded.append(piece[:, 3 * hw:3 * hw + 2])
        padded.append(jnp.zeros((depth, w_pad.shape[1] - 3 * HW - 2), BF16))
        w_pad[at, :] = jnp.concatenate(padded, axis=1)
    gains = jnp.transpose(w_pad[:, 3 * HW:].astype(F32))
    gain_ref[...] = gains[0:1]
    gain_two_ref[...] = gains[1:2]
    for rel, (t_ref, n_ref) in enumerate(zip((t0, t1, t2, t3), (n0, n1, n2, n3))):
        count = t_ref.shape[0]
        unit, _ = rms_parts(t_ref[...].astype(F32))
        n_ref[...] = (unit * gain_ref[...]).astype(BF16)
        at = pl.ds(pl.multiple_of(jnp.bitwise_xor(me_ref[0], rel) * count, SEG), count)
        qkv = dot(n_ref[...], w_pad[:, :3 * HW], NN)
        q_ref[at, :] = qkv[:, :HW].astype(BF16) * jnp.asarray(DH ** -0.5, BF16)
        k_ref[at, :] = qkv[:, HW:2 * HW].astype(BF16)
        v_ref[at, :] = qkv[:, 2 * HW:].astype(BF16)
        kt_ref[:, at] = jnp.transpose(qkv[:, HW:2 * HW]).astype(BF16)
        vt_ref[:, at] = jnp.transpose(qkv[:, 2 * HW:]).astype(BF16)
    key = lax.broadcasted_iota(jnp.int32, (SEG, SEG), 0)
    query = lax.broadcasted_iota(jnp.int32, (SEG, SEG), 1)
    bias_ref[0] = jnp.zeros((SEG, heads * SEG), F32)
    bias_ref[3] = jnp.full((SEG, heads * SEG), MASKED, F32)
    for h in range(heads):
        last = table_ref[h, NB - 1]
        at = slice(h * SEG, (h + 1) * SEG)
        for kind, gap in ((1, query - key + SEG), (2, query - key)):
            tile = jnp.zeros((SEG, SEG), F32) + (table_ref[h, 0] - last)
            for i, threshold in enumerate(THRESHOLDS):
                tile = jnp.where(gap >= threshold, table_ref[h, i + 1] - last, tile)
            bias_ref[kind, :, at] = jnp.where(gap >= 0, tile, MASKED)


def by_head(rows, heads):
    lane = lax.broadcasted_iota(jnp.int32, rows.shape, 1)
    zero = jnp.zeros_like(rows)
    return jnp.concatenate(
        [jnp.where((lane >= h * DH) & (lane < (h + 1) * DH), rows, zero) for h in range(heads)], axis=0
    )


def seg_at(index):
    if isinstance(index, int):
        return slice(index * SEG, (index + 1) * SEG)
    return pl.ds(pl.multiple_of(index * SEG, SEG), SEG)


def head_columns(acc, heads):
    pieces = [acc[h * DH:(h + 1) * DH, h * SEG:(h + 1) * SEG] for h in range(heads)]
    pieces.append(jnp.zeros((HW - heads * DH, SEG), F32))
    return jnp.concatenate(pieces, axis=0)


def pair_bias(bias_ref, first, second):
    return jnp.concatenate([bias_ref[first], bias_ref[second]], axis=1)


def attn_forward_kernel(
    heads, me_ref, parent_ref, q_ref, k_ref, v_ref, vt_ref, bias_ref, o0, o1, o2, o3, raw_ref, lse_ref, out_all
):
    cols = heads * SEG
    trunk_len = TRUNK * SEG
    last = trunk_len - SEG

    def queries(b):
        return by_head(q_ref[seg_at(b), :], heads)

    def finish(b, acc, total, top):
        lse_ref[pl.ds(b * 8, 8), :] = jnp.broadcast_to(top + jnp.log(total), (8, cols))
        columns = head_columns(acc / total, heads)
        raw_ref[:, seg_at(b)] = columns
        out_all[:, seg_at(b)] = columns.astype(BF16)

    for j in range(TRUNK // 2):
        q6 = jnp.concatenate([queries(2 * j), queries(2 * j + 1)], axis=0)
        scores = dot(k_ref[0:(j + 1) * 2 * SEG, :], q6, NT)
        parts = []
        if j > 0:
            far = (2 * j - 1) * SEG
            parts = [scores[:far], scores[far:far + SEG] + pair_bias(bias_ref, 1, 0)]
        parts.append(scores[2 * j * SEG:(2 * j + 1) * SEG] + pair_bias(bias_ref, 2, 1))
        parts.append(scores[(2 * j + 1) * SEG:] + pair_bias(bias_ref, 3, 2))
        top = functools.reduce(jnp.maximum, [jnp.max(part, axis=0, keepdims=True) for part in parts])
        parts = [jnp.exp(part - top) for part in parts]
        total = functools.reduce(jnp.add, [jnp.sum(part, axis=0, keepdims=True) for part in parts])
        acc = dot(vt_ref[:, 0:(j + 1) * 2 * SEG], jnp.concatenate([p.astype(BF16) for p in parts], axis=0), NN)
        for s in range(2):
            at = slice(s * cols, (s + 1) * cols)
            finish(2 * j + s, acc[:, at], total[:, at], top[:, at])

    def other_step(i, carry):
        segs = [TRUNK + 2 * i, TRUNK + 2 * i + 1]
        parents = [parent_ref[b] for b in segs]
        leaf = [(parent >= TRUNK).astype(jnp.int32) for parent in parents]
        q3 = [queries(b) for b in segs]
        q6 = jnp.concatenate(q3, axis=0)
        scores = dot(k_ref[0:trunk_len, :], q6, NT)
        near = scores[last:] + pair_bias(bias_ref, 1 - leaf[0], 1 - leaf[1])
        far = scores[:last]
        extra = []
        for s in range(2):
            keys = jnp.concatenate([k_ref[seg_at(parents[s]), :], k_ref[seg_at(segs[s]), :]], axis=0)
            bias = jnp.concatenate([bias_ref[3 - 2 * leaf[s]], bias_ref[2]], axis=0)
            extra.append(dot(keys, q3[s], NT) + bias)
        top = jnp.maximum(jnp.max(far, axis=0, keepdims=True), jnp.max(near, axis=0, keepdims=True))
        top = jnp.maximum(top, jnp.concatenate([jnp.max(e, axis=0, keepdims=True) for e in extra], axis=1))
        far, near = jnp.exp(far - top), jnp.exp(near - top)
        extra = [jnp.exp(extra[s] - top[:, s * cols:(s + 1) * cols]) for s in range(2)]
        total = jnp.sum(far, axis=0, keepdims=True) + jnp.sum(near, axis=0, keepdims=True)
        total = total + jnp.concatenate([jnp.sum(e, axis=0, keepdims=True) for e in extra], axis=1)
        acc = dot(vt_ref[:, 0:trunk_len], jnp.concatenate([far.astype(BF16), near.astype(BF16)], axis=0), NN)
        for s in range(2):
            at = slice(s * cols, (s + 1) * cols)
            values = jnp.concatenate([vt_ref[:, seg_at(parents[s])], vt_ref[:, seg_at(segs[s])]], axis=1)
            finish(segs[s], acc[:, at] + dot(values, extra[s].astype(BF16), NN), total[:, at], top[:, at])
        return carry

    lax.fori_loop(0, (SEGS - TRUNK) // 2, other_step, 0)
    for rel, o_ref in enumerate((o0, o1, o2, o3)):
        width, count = o_ref.shape
        at = pl.ds(pl.multiple_of(jnp.bitwise_xor(me_ref[0], rel) * count, SEG), count)
        o_ref[...] = out_all[0:width, at]


TRUNK_FIRST = [SEG * j * (j + 1) for j in range(TRUNK // 2 + 1)]
OTHER_ROWS = (TRUNK + 2) * SEG
PROB_ROWS = TRUNK_FIRST[-1] + (SEGS - TRUNK) // 2 * OTHER_ROWS


def attn_prob_kernel(heads, parent_ref, q_ref, k_ref, lse_ref, bias_ref, before_ref, out_ref):
    cols = heads * SEG

    def common(b):
        return by_head(q_ref[seg_at(b), :], heads), lse_ref[pl.ds(b * 8, 8), :][0:1]

    for j in range(TRUNK // 2):
        (qa, la), (qb, lb) = common(2 * j), common(2 * j + 1)
        q6, lse = jnp.concatenate([qa, qb], axis=0), jnp.concatenate([la, lb], axis=1)
        for i in range(j + 1):
            scores = dot(k_ref[2 * i * SEG:2 * (i + 1) * SEG, :], q6, NT)
            if i == j:
                scores = scores + jnp.concatenate([pair_bias(bias_ref, 2, 1), pair_bias(bias_ref, 3, 2)], axis=0)
            if i == j - 1:
                scores = scores + jnp.concatenate([pair_bias(bias_ref, 0, 0), pair_bias(bias_ref, 1, 0)], axis=0)
            first = TRUNK_FIRST[j] + 2 * i * SEG
            out_ref[first:first + 2 * SEG, :] = jnp.exp(scores - lse).astype(BF16)

    def other_step(step, carry):
        segs = [TRUNK + 2 * step, TRUNK + 2 * step + 1]
        parents = [parent_ref[b] for b in segs]
        leaf = [(parent >= TRUNK).astype(jnp.int32) for parent in parents]
        each = [common(b) for b in segs]
        q6, lse = jnp.concatenate([q for q, _ in each], axis=0), jnp.concatenate([l for _, l in each], axis=1)
        base = TRUNK_FIRST[-1] + step * OTHER_ROWS
        for i in range(TRUNK // 2):
            scores = dot(k_ref[2 * i * SEG:2 * (i + 1) * SEG, :], q6, NT)
            if i == TRUNK // 2 - 1:
                near = pair_bias(bias_ref, 1 - leaf[0], 1 - leaf[1])
                scores = scores + jnp.concatenate([jnp.zeros_like(near), near], axis=0)
            at = pl.ds(pl.multiple_of(base + 2 * i * SEG, SEG), 2 * SEG)
            out_ref[at, :] = jnp.exp(scores - lse).astype(BF16)
        extra = []
        for s in range(2):
            keys = jnp.concatenate([k_ref[seg_at(parents[s]), :], k_ref[seg_at(segs[s]), :]], axis=0)
            bias = jnp.concatenate([bias_ref[3 - 2 * leaf[s]], bias_ref[2]], axis=0)
            extra.append(jnp.exp(dot(keys, each[s][0], NT) + bias - each[s][1]).astype(BF16))
        at = pl.ds(pl.multiple_of(base + TRUNK * SEG, SEG), 2 * SEG)
        out_ref[at, :] = jnp.concatenate(extra, axis=1)
        return carry

    lax.fori_loop(0, (SEGS - TRUNK) // 2, other_step, 0)


def attn_backward_kernel(
    heads, me_ref, parent_ref, q_ref, k_ref, v_ref, kt_ref, raw_ref, prob_ref, g0, g1, g2, g3_ref,
    d0, d1, d2, d3, bins_ref, grad_all, dq_all, dk_acc, dv_acc, bins_acc, probs, sem,
):
    def fetch(step):
        if isinstance(step, int):
            at = pl.ds(TRUNK_FIRST[step], TRUNK_FIRST[step + 1] - TRUNK_FIRST[step])
        else:
            at = pl.ds(pl.multiple_of(TRUNK_FIRST[-1] + (step - TRUNK // 2) * OTHER_ROWS, SEG), OTHER_ROWS)
        return pltpu.make_async_copy(prob_ref.at[at, :], probs.at[at, :], sem.at[step])

    for j in range(TRUNK // 2):
        fetch(j).start()

    def start_other(step, carry):
        fetch(step + TRUNK // 2).start()
        return carry

    lax.fori_loop(0, (SEGS - TRUNK) // 2, start_other, 0)
    cols = heads * SEG
    trunk_len = TRUNK * SEG
    dk_acc[...] = jnp.zeros_like(dk_acc)
    dv_acc[...] = jnp.zeros_like(dv_acc)
    bins_acc[...] = jnp.zeros_like(bins_acc)
    for rel, g_ref in enumerate((g0, g1, g2, g3_ref)):
        width, count = g_ref.shape
        at = pl.ds(pl.multiple_of(jnp.bitwise_xor(me_ref[0], rel) * count, SEG), count)
        grad_all[0:width, at] = g_ref[...]
        grad_all[width:HW, at] = jnp.zeros((HW - width, count), BF16)

    def common(b):
        q3 = by_head(q_ref[seg_at(b), :], heads)
        grad = grad_all[:, seg_at(b)].astype(F32)
        product = grad * raw_ref[:, seg_at(b)]
        row_dot = jnp.concatenate(
            [jnp.sum(product[h * DH:(h + 1) * DH], axis=0, keepdims=True) for h in range(heads)], axis=1
        )
        return q3, by_head(jnp.transpose(grad).astype(BF16), heads), row_dot

    def block(prob, values, g, row_dot):
        return prob.astype(F32) * (dot(values, g, NT) - row_dot)

    def write_dq(b, acc):
        dq_all[seg_at(b), :] = (jnp.transpose(head_columns(acc, heads)) * DH ** -0.5).astype(BF16)

    def both(pair):
        return [jnp.concatenate([a, b], axis=0 if a.shape[0] > 1 else 1) for a, b in zip(*pair)]

    for j in range(TRUNK // 2):
        q6, g6, row_dot = both([common(2 * j), common(2 * j + 1)])
        fetch(j).wait()
        kept = []
        for i in range(j + 1):
            at = slice(2 * i * SEG, 2 * (i + 1) * SEG)
            prob = probs[TRUNK_FIRST[j] + 2 * i * SEG:TRUNK_FIRST[j] + 2 * (i + 1) * SEG, :]
            score = block(prob, v_ref[at, :], g6, row_dot)
            if i == j:
                bins_acc[0] += score[:SEG, cols:]
                bins_acc[1] += score[:SEG, :cols] + score[SEG:, cols:]
            if i == j - 1:
                bins_acc[0] += score[SEG:, :cols]
            score = score.astype(BF16)
            dv_acc[at, :] += dot(prob, g6, NN)
            dk_acc[at, :] += dot(score, q6, NN)
            kept.append(score)
        acc = dot(kt_ref[:, 0:(j + 1) * 2 * SEG], jnp.concatenate(kept, axis=0), NN)
        for s in range(2):
            write_dq(2 * j + s, acc[:, s * cols:(s + 1) * cols])

    def other_step(step, carry):
        segs = [TRUNK + 2 * step, TRUNK + 2 * step + 1]
        parents = [parent_ref[b] for b in segs]
        leaf = [(parent >= TRUNK).astype(jnp.int32) for parent in parents]
        each = [common(b) for b in segs]
        q6, g6, row_dot = both(each)
        base = TRUNK_FIRST[-1] + step * OTHER_ROWS
        fetch(step + TRUNK // 2).wait()
        kept = []
        for i in range(TRUNK // 2):
            at = slice(2 * i * SEG, 2 * (i + 1) * SEG)
            prob = probs[pl.ds(pl.multiple_of(base + 2 * i * SEG, SEG), 2 * SEG), :]
            score = block(prob, v_ref[at, :], g6, row_dot)
            if i == TRUNK // 2 - 1:
                for s in range(2):
                    bins_acc[0] += jnp.where(leaf[s] == 0, score[SEG:, s * cols:(s + 1) * cols], 0.0)
            score = score.astype(BF16)
            dv_acc[at, :] += dot(prob, g6, NN)
            dk_acc[at, :] += dot(score, q6, NN)
            kept.append(score)
        acc = dot(kt_ref[:, 0:trunk_len], jnp.concatenate(kept, axis=0), NN)
        for s in range(2):
            q3, g3, row = each[s]
            first, second = seg_at(parents[s]), seg_at(segs[s])
            values = jnp.concatenate([v_ref[first, :], v_ref[second, :]], axis=0)
            keys_t = jnp.concatenate([kt_ref[:, first], kt_ref[:, second]], axis=1)
            at = pl.ds(pl.multiple_of(base + trunk_len, SEG), 2 * SEG)
            prob = probs[at, s * cols:(s + 1) * cols]
            score = block(prob, values, g3, row)
            bins_acc[0] += score[:SEG]
            bins_acc[1] += score[SEG:]
            score = score.astype(BF16)
            grad_v, grad_k = dot(prob, g3, NN), dot(score, q3, NN)
            dv_acc[first, :] += grad_v[:SEG]
            dv_acc[second, :] += grad_v[SEG:]
            dk_acc[first, :] += grad_k[:SEG]
            dk_acc[second, :] += grad_k[SEG:]
            write_dq(segs[s], acc[:, s * cols:(s + 1) * cols] + dot(keys_t, score, NN))
        return carry

    lax.fori_loop(0, (SEGS - TRUNK) // 2, other_step, 0)
    for rel, d_ref in enumerate((d0, d1, d2, d3)):
        count = d_ref.shape[0]
        width = heads * DH
        at = pl.ds(pl.multiple_of(jnp.bitwise_xor(me_ref[0], rel) * count, SEG), count)
        parts = [dq_all[at, :][:, :width], dk_acc[at, :][:, :width].astype(BF16), dv_acc[at, :][:, :width].astype(BF16)]
        parts.append(jnp.zeros((count, d_ref.shape[1] - 3 * width), BF16))
        d_ref[...] = jnp.concatenate(parts, axis=1)
    key = lax.broadcasted_iota(jnp.int32, (SEG, cols), 0)
    query = lax.broadcasted_iota(jnp.int32, (SEG, cols), 1) % SEG
    gap = query - key
    parent_sum, own_sum = bins_acc[0], bins_acc[1]
    lines = [jnp.sum(parent_sum + own_sum, axis=0, keepdims=True)]
    for threshold in THRESHOLDS:
        hit = jnp.where(gap + SEG >= threshold, parent_sum, 0.0) + jnp.where(gap >= threshold, own_sum, 0.0)
        lines.append(jnp.sum(hit, axis=0, keepdims=True))
    bins_ref[...] = jnp.concatenate(lines, axis=0)


class Slots:
    def __init__(self, n_expert, capacity):
        self.n_expert = n_expert
        self.cut = n_expert == 8
        self.block = -(-(capacity + SPARE) // 16) * 16
        if self.cut:
            self.groups = [[0, 1, 4, 5], [2, 3, 6, 7]]
            self.rels = [2, 3, 6, 7]
            self.chunks = [[[0, 1, 2, 3]], [[4], [5], [6], [7]]]
        else:
            self.groups = None
            self.chunks = [[list(range(n_expert))]]
        self.arrays = [array for chunk in self.chunks for array in chunk]

    def block_of(self, expert, me):
        if not self.cut:
            return expert
        rel = jnp.bitwise_xor(expert, me)
        inside = lambda index: (index & 1) | ((index >> 1) & 2)
        return jnp.where((rel & 2) == 0, inside(expert), 4 + inside(rel))

    def expert_of(self, block, me):
        if not self.cut:
            return block
        if not isinstance(block, int) or block < 4:
            return (me & 2) | (block & 1) | ((block & 2) << 1)
        return jnp.bitwise_xor(me, self.rels[block - 4])

    def near_exchange(self, block):
        return lax.all_to_all(block, "expert", split_axis=0, concat_axis=0, tiled=True, axis_index_groups=self.groups)


def over_experts(block):
    return lax.all_to_all(block, "expert", split_axis=0, concat_axis=0, tiled=True)


def swap(block, axis, rel):
    if rel == 0:
        return block
    return lax.ppermute(block, axis, [(i, i ^ rel) for i in range(lax.axis_size(axis))])


def swap_all(blocks, axis):
    return [swap(block, axis, rel) for rel, block in enumerate(blocks)]


def from_all(block):
    near, far = swap(block, "shard", 1), swap(block, "shard", 2)
    return [block, near, far, swap(far, "shard", 1)]


def reorder(parts, me):
    bit = 1
    while bit < len(parts):
        parts = [jnp.where(me & bit, parts[i ^ bit], parts[i]) for i in range(len(parts))]
        bit *= 2
    return parts


def send_rows(slots, rows, places_ref, out_refs):
    tokens = places_ref.shape[1]
    for array, out_ref in zip(slots.arrays, out_refs):
        for i, block in enumerate(array):
            slot = block * slots.block + lax.broadcasted_iota(jnp.int32, (slots.block, tokens), 0)
            hit = (slot == places_ref[0:1, :]) | (slot == places_ref[1:2, :])
            picked = dot(jnp.where(hit, 1.0, 0.0).astype(BF16), rows, NN).astype(BF16)
            out_ref[i * slots.block:(i + 1) * slots.block, :] = picked


def row_at(first, count):
    return pl.ds(first if isinstance(first, int) else pl.multiple_of(first, 16), count)


def diagonal(count):
    return lax.broadcasted_iota(jnp.int32, (count, count), 0) == lax.broadcasted_iota(jnp.int32, (count, count), 1)


def padded_row(row, width):
    count = row.shape[1]
    return row if count == width else jnp.concatenate([row, jnp.zeros((1, width - count), row.dtype)], axis=1)


def dispatch_kernel(slots, me_ref, places_ref, others_ref, rows_ref, *refs):
    out_ref = refs[-1]
    tokens = places_ref.shape[1]
    width = rows_ref.shape[1]
    rows = rows_ref[...]
    count = slots.block

    def one(expert, carry):
        slot = slots.block_of(expert, me_ref[0]) * count + lax.broadcasted_iota(jnp.int32, (count, tokens), 0)
        hot = [jnp.where(slot == places_ref[j:j + 1, :], 1.0, 0.0).astype(BF16) for j in range(2)]
        picked = dot(hot[0] + hot[1], rows, NN)
        ids = sum(dot(others_ref[8 * j:8 * j + 8, :], hot[j], NT) for j in range(2))
        line = lax.broadcasted_iota(jnp.int32, picked.shape, 0)
        picked = jnp.where(line == count - 1, padded_row(ids[0:1], width), picked)
        out_ref[pl.ds(pl.multiple_of(expert * count, 16), count), :] = picked.astype(BF16)
        return carry

    lax.fori_loop(0, slots.n_expert, one, 0)


def post_kernel(
    slots, me_ref, x_ref, gain_ref, router_ref, routes_ref, places_ref, m0, m1, m2, m3, w_ref,
    after_ref, normed_ref, gates_ref, *out_refs,
):
    after = x_ref[...].astype(F32)
    for rel, m_ref in enumerate((m0, m1, m2, m3)):
        after = after + dot(m_ref[...], w_ref[jnp.bitwise_xor(me_ref[1], rel)], TN)
    after_ref[...] = after
    unit, _ = rms_parts(after)
    normed = (unit * gain_ref[...]).astype(BF16)
    normed_ref[...] = normed
    send_rows(slots, normed_ref[...], places_ref, out_refs)
    logits = dot(normed, router_ref[...], NN)
    expert = lax.broadcasted_iota(jnp.int32, logits.shape, 1)
    first = jnp.sum(jnp.where(expert == routes_ref[:, 0:1], logits, 0.0), axis=-1, keepdims=True)
    second = jnp.sum(jnp.where(expert == routes_ref[:, 1:2], logits, 0.0), axis=-1, keepdims=True)
    top = jnp.maximum(first, second)
    first, second = jnp.exp(first - top), jnp.exp(second - top)
    gates_ref[...] = jnp.concatenate([first / (first + second), second / (first + second)], axis=1)


def expert_kernel(slots, kind, sizes, before, me_ref, *refs):
    refs = list(refs)
    take = lambda n: [refs.pop(0) for _ in range(n)]
    x_refs = take(sizes[0])
    g_all, router_ref = take(2)
    first_refs, second_refs = take(4), take(4)
    extra = take(before)
    own_ref = extra[1] if before == 3 else None
    (out_all,) = take(1)
    dx_refs = take(sizes[1])
    rows_ref, grad_ref, act_ref, inner_ref, first_buf, second_buf, g_buf, out_buf, out_acc, dx_acc, gate_acc, gates_acc, sem, in_sem = refs
    step = pl.program_id(0)
    slot = lax.rem(step, 2)
    total, width = rows_ref.shape
    depth, units = first_refs[0].shape[0], second_buf.shape[1]

    def fetch(rel, slot):
        column = pl.multiple_of(jnp.bitwise_xor(me_ref[1], rel) * units, 128)
        copies = [pltpu.make_async_copy(second_refs[rel], second_buf.at[slot], in_sem.at[slot, 4])]
        for piece, ref in enumerate(first_refs):
            row = pl.multiple_of(jnp.bitwise_xor(me_ref[1], piece) * depth, 16)
            copies.append(
                pltpu.make_async_copy(
                    ref.at[:, pl.ds(column, units)], first_buf.at[slot, pl.ds(row, depth), :], in_sem.at[slot, piece]
                )
            )
        return copies

    @pl.when(step == 0)
    def _():
        for copy in fetch(0, 0):
            copy.start()

    for rel in range(4):
        @pl.when(step == rel)
        def _(rel=rel):
            if rel < 3:
                for copy in fetch(rel + 1, (rel + 1) % 2):
                    copy.start()
    rows = slots.block
    mine = slots.block_of(me_ref[0], me_ref[0])
    if kind == "own":
        pieces = [(mine, x_refs[0], mine * rows, dx_refs[0], 0)]
    elif kind == "near":
        blocks = [jnp.bitwise_xor(mine, i) for i in (1, 2, 3)]
        pieces = [(block, x_refs[0], block * rows, dx_refs[0], block * rows) for block in blocks]
    elif kind == "far":
        pieces = [(4 + i, x_ref, 0, dx_ref, 0) for i, (x_ref, dx_ref) in enumerate(zip(x_refs, dx_refs))]
    else:
        pieces = [(block, x_refs[0], block * rows, dx_refs[0], block * rows) for block in range(slots.n_expert)]
    pieces = [(*piece, i * rows) for i, piece in enumerate(pieces)]

    def home(block):
        return pl.ds(pl.multiple_of(slots.expert_of(block, me_ref[0]) * rows, 16), rows)

    @pl.when(step == 0)
    def _():
        copies = [
            pltpu.make_async_copy(g_all.at[home(block), :], g_buf.at[pl.ds(first, rows), :], sem.at[i])
            for i, (block, *_, first) in enumerate(pieces)
        ]
        for copy in copies:
            copy.start()
        out_acc[...] = jnp.zeros_like(out_acc)
        dx_acc[...] = jnp.zeros_like(dx_acc)
        for _, x_ref, inside, _, _, first in pieces:
            rows_ref[first:first + rows, :] = x_ref[row_at(inside, rows), :]
        for copy in copies:
            copy.wait()
        for *_, first in pieces:
            at = slice(first, first + rows)
            grads = g_buf[at, :].astype(F32)
            other = jnp.sum(jnp.where(diagonal(rows), grads[rows - 1:, :rows], 0.0), axis=1, keepdims=True).astype(jnp.int32)
            logits = dot(rows_ref[at, :], router_ref[...], NN)
            expert = lax.broadcasted_iota(jnp.int32, logits.shape, 1)
            mine = jnp.sum(jnp.where(expert == me_ref[0], logits, 0.0), axis=-1, keepdims=True)
            its = jnp.sum(jnp.where(expert == other, logits, 0.0), axis=-1, keepdims=True)
            top = jnp.maximum(mine, its)
            mine, its = jnp.exp(mine - top), jnp.exp(its - top)
            line = lax.broadcasted_iota(jnp.int32, grads.shape, 0)
            gate = mine / (mine + its)
            gate_acc[at, :] = jnp.broadcast_to(gate, (rows, 128))
            grad_ref[at, :] = jnp.where(line < rows - SPARE, gate * grads, 0.0).astype(BF16)

    for rel in range(4):
        @pl.when(step == rel)
        def _(rel=rel):
            for copy in fetch(rel, rel % 2):
                copy.wait()

    parts = 1
    while total // parts > 512 or total % parts or (total // parts) % 16:
        parts += 1
    part = total // parts
    for i in range(parts):
        at = slice(i * part, (i + 1) * part)
        first_w, second_w = first_buf[slot], second_buf[slot]
        value = dot(rows_ref[at, :], first_w, NN)
        grad_act = dot(grad_ref[at, :], second_w, NT)
        square = value * value
        half = 0.5 * value
        scale = 0.7978845608028654
        th = jnp.tanh(value * (scale + (scale * 0.044715) * square))
        act = (half + half * th).astype(BF16)
        slope = 0.5 + 0.5 * th + (half * (1.0 - th * th)) * (scale + (3 * scale * 0.044715) * square)
        inner = (grad_act * slope).astype(BF16)
        act_ref[at, :] = act
        inner_ref[at, :] = inner
        out_acc[at, :] += dot(act, second_w, NN)
        dx_acc[at, :] += dot(inner, first_w, NT)

    @pl.when(step == pl.num_programs(0) - 1)
    def _():
        for *_, first in pieces:
            at = slice(first, first + rows)
            out = out_acc[at, :].astype(BF16).astype(F32)
            gates = jnp.sum(out * g_buf[at, :].astype(F32), axis=1, keepdims=True)
            gates_acc[at, :] = jnp.broadcast_to(gates, (rows, 128))
            out_buf[at, :] = (gate_acc[at, 0:1] * out).astype(BF16)
        copies = [
            pltpu.make_async_copy(out_buf.at[pl.ds(first, rows), :], out_all.at[home(block), :], sem.at[i])
            for i, (block, *_, first) in enumerate(pieces)
        ]
        for copy in copies:
            copy.start()
        if own_ref is not None:
            dx_refs[0][row_at(mine * rows, rows), :] = own_ref[...]
        for _, _, _, dx_ref, inside, first in pieces:
            at = slice(first, first + rows)
            gates = gates_acc[at, 0:1]
            gates = jnp.sum(jnp.where(diagonal(rows), gates, 0.0), axis=0, keepdims=True)
            dx_ref[row_at(inside, rows), :] = dx_acc[at, :].astype(BF16)
            tail = dx_acc[first + rows - 16:first + rows, :]
            line = lax.broadcasted_iota(jnp.int32, tail.shape, 0)
            for place in range(SPARE):
                piece = gates.astype(BF16).astype(F32)
                gates = gates - piece
                tail = jnp.where(line == 16 - SPARE + place, padded_row(piece, width), tail)
            dx_ref[row_at(inside + rows - 16, 16), :] = tail.astype(BF16)
        for copy in copies:
            copy.wait()


def run_expert(slots, kind, blocks, dx_shape, shared, before, estimate):
    me, g_all, router, first_w, second_w = shared
    hidden, width = first_w[0].shape[1], router.shape[0]
    total = slots.block * {"own": 1, "near": 3, "far": 4, "all": slots.n_expert}[kind]
    block = hidden // 4
    whole = lambda a: pl.BlockSpec(a.shape, lambda i: (0, 0))
    column = pl.BlockSpec((total, block), lambda i: (0, i))
    rows = pl.BlockSpec((total, width), lambda i: (0, 0))
    fresh = len(before) < 2
    dx = [jax.ShapeDtypeStruct(dx_shape, BF16)] * (4 if kind == "far" else 1)
    inputs = [me, *blocks, g_all, router, *first_w, *second_w, *before]
    before_specs = [ANY] * len(before)
    if len(before) == 3:
        before_specs[1] = whole(before[1])
    return pl.pallas_call(
        functools.partial(expert_kernel, slots, kind, (len(blocks), len(dx)), len(before)),
        grid=(4,),
        in_specs=[SMEM] + [whole(b) for b in blocks] + [ANY, whole(router)] + [ANY] * 8 + before_specs,
        out_specs=[ANY] + [whole(b) for b in dx] + [rows, rows, column, column],
        out_shape=arrays(
            (g_all.shape, BF16), *[(b.shape, BF16) for b in dx], *[((total, width), BF16)] * 2, *[((total, hidden), BF16)] * 2
        ),
        scratch_shapes=[
            pltpu.VMEM((2, width, block), BF16),
            pltpu.VMEM((2, block, width), BF16),
            pltpu.VMEM((total, width), BF16),
            pltpu.VMEM((total, width), BF16),
            pltpu.VMEM((total, width), F32),
            pltpu.VMEM((total, width), F32),
            pltpu.VMEM((total, 128), F32),
            pltpu.VMEM((total, 128), F32),
            pltpu.SemaphoreType.DMA((total // slots.block,)),
            pltpu.SemaphoreType.DMA((2, 5)),
        ],
        input_output_aliases={} if fresh else {len(inputs) - 1: 0},
        compiler_params=params(dimension_semantics=("arbitrary",)),
        cost_estimate=estimate,
    )(*inputs)


def first_grad_kernel(parts, me_ref, *refs):
    send_ref, keep_ref, total = refs[-3:]
    total[...] = sum(dot(x[...], inner[...], TN) for x, inner in zip(refs[:parts], refs[parts:2 * parts]))
    depth = send_ref.shape[0] // 2
    for rel in range(4):
        ref = (keep_ref, send_ref)[rel % 2]
        row = pl.multiple_of(jnp.bitwise_xor(me_ref[1], rel) * depth, 16)
        at = rel // 2 * depth
        ref[at:at + depth, :] = total[pl.ds(row, depth), :].astype(BF16)


def run_first_grad(me, rows, inners, depth, *after):
    width, hidden = rows[0].shape[1], inners[0].shape[1]
    block = hidden // 4
    column = pl.BlockSpec((2 * depth, block), lambda i, me_ref: (0, jnp.bitwise_xor(me_ref[1], i)))
    return pl.pallas_call(
        functools.partial(first_grad_kernel, len(rows)),
        grid_spec=pltpu.PrefetchScalarGridSpec(
            num_scalar_prefetch=1,
            grid=(4,),
            in_specs=[pl.BlockSpec(a.shape, lambda i, me_ref: (0, 0)) for a in rows]
            + [pl.BlockSpec((a.shape[0], block), lambda i, me_ref: (0, i)) for a in inners]
            + [ANY] * len(after),
            out_specs=[column, column],
            scratch_shapes=[pltpu.VMEM((width, block), F32)],
        ),
        out_shape=arrays(*[((2 * depth, hidden), BF16)] * 2),
        compiler_params=params(dimension_semantics=("arbitrary",)),
        cost_estimate=SHORT,
    )(me, *rows, *inners, *after)


def second_grad_kernel(parts, *refs):
    send_ref, keep_ref = refs[2 * parts:]
    step = pl.program_id(0)
    block = sum(dot(act[...], g[...], TN) for act, g in zip(refs[:parts], refs[parts:2 * parts])).astype(BF16)

    @pl.when(step < 2)
    def _():
        send_ref[...] = block

    @pl.when(step >= 2)
    def _():
        keep_ref[...] = block


def run_second_grad(acts, grads):
    width, hidden = grads[0].shape[1], acts[0].shape[1]
    block = hidden // 4
    return pl.pallas_call(
        functools.partial(second_grad_kernel, len(acts)),
        grid=(4,),
        in_specs=[pl.BlockSpec((a.shape[0], block), lambda i: (0, 2 * (i % 2) + 1 - i // 2)) for a in acts]
        + [pl.BlockSpec(a.shape, lambda i: (0, 0)) for a in grads],
        out_specs=[
            pl.BlockSpec((block, width), lambda i: (jnp.minimum(i, 1), 0)),
            pl.BlockSpec((block, width), lambda i: (jnp.maximum(i - 2, 0), 0)),
        ],
        out_shape=arrays(*[((2 * block, width), BF16)] * 2),
        compiler_params=params(dimension_semantics=("arbitrary",)),
        cost_estimate=SHORT,
    )(*acts, *grads)


def core_sum(send, keep):
    near = swap(send, "shard", 1)
    half = keep.shape[0] // 2
    other = (keep[half:].astype(F32) + near[half:].astype(F32)).astype(BF16)
    return keep, near, other


def across_sum(parts):
    keep, near, other = parts
    return keep, near, swap(other, "shard", 2)


def total_sum(parts):
    keep, near, far = parts
    half = keep.shape[0] // 2
    return keep[:half].astype(F32) + near[:half].astype(F32) + far.astype(F32)


def gather_blocks(slots, refs, scratch):
    for array, ref in zip(slots.arrays, refs):
        scratch[array[0] * slots.block:(array[-1] + 1) * slots.block, :] = ref[...]


def back_kernel(slots, me_ref, *refs):
    refs_left = list(refs)
    take = lambda n: [refs_left.pop(0) for _ in range(n)]
    ret_refs = take(len(slots.arrays))
    places_ref, routes_ref, gates_ref, after_ref, gain_ref, router_ref, g_ref = take(7)
    w_ref, normed_ref = take(2)
    m_refs = take(4)
    (grad_after_ref,) = take(1)
    mixed_refs = take(4)
    send_ref, keep_ref, branch_ref, glogits_ref, ggain_ref, more, scratch = refs_left
    tokens = after_ref.shape[0]
    part = tokens // 2
    gather_blocks(slots, ret_refs, scratch)
    pieces = []
    for end in range(slots.block, scratch.shape[0] + 1, slots.block):
        tail = scratch[end - 16:end, :].astype(F32)[16 - SPARE:, :slots.block]
        pieces.append(jnp.sum(tail, axis=0, keepdims=True))
    gg = jnp.concatenate(pieces, axis=1)
    ggain_ref[...] = jnp.zeros_like(ggain_ref)

    def one(i, carry):
        at = pl.ds(pl.multiple_of(i * part, part), part)
        slot = lax.broadcasted_iota(jnp.int32, (part, gg.shape[1]), 1)
        hit0, hit1 = slot == places_ref[at, 0:1], slot == places_ref[at, 1:2]
        gg0 = jnp.sum(jnp.where(hit0, gg, 0.0), axis=-1, keepdims=True)
        gg1 = jnp.sum(jnp.where(hit1, gg, 0.0), axis=-1, keepdims=True)
        total = dot(jnp.where(hit0 | hit1, 1.0, 0.0).astype(BF16), scratch[...], NN)
        gate0, gate1 = gates_ref[at, 0:1], gates_ref[at, 1:2]
        mean = gate0 * gg0 + gate1 * gg1
        expert = lax.broadcasted_iota(jnp.int32, (part, router_ref.shape[1]), 1)
        glogits = jnp.where(expert == routes_ref[at, 0:1], gate0 * (gg0 - mean), 0.0) + jnp.where(
            expert == routes_ref[at, 1:2], gate1 * (gg1 - mean), 0.0
        )
        glogits = glogits.astype(BF16)
        glogits_ref[at, :] = glogits
        incoming = dot(glogits, router_ref[...], NT) + total
        unit, factor = rms_parts(after_ref[at, :])
        grad_after = g_ref[at, :].astype(F32) + rms_grad(incoming, gain_ref[...], unit, factor)
        ggain_ref[0:1, :] += jnp.sum(incoming * unit, axis=0, keepdims=True)
        grad_after_ref[at, :] = grad_after
        branch = grad_after.astype(BF16)
        branch_ref[at, :] = branch
        return carry

    lax.fori_loop(0, tokens // part, one, 0)
    for rel, mixed_ref in enumerate(mixed_refs):
        mixed_ref[...] = dot(w_ref[jnp.bitwise_xor(me_ref[0], rel)], branch_ref[...], NT).astype(BF16)
    width = branch_ref.shape[1]
    grad_router = dot(normed_ref[...], glogits_ref[...], TN)
    gain = jnp.transpose(jnp.concatenate([ggain_ref[...]] * 16, axis=0))[:, 0:1]
    blank = jnp.zeros((width, more.shape[1] - grad_router.shape[1] - 1), F32)
    more[...] = jnp.concatenate([grad_router, gain, blank], axis=1)
    for rel, m_ref in enumerate(m_refs):
        ref = (keep_ref, send_ref)[rel % 2]
        count = m_ref.shape[0]
        at = slice(rel // 2 * count, (rel // 2 + 1) * count)
        ref[at, 0:width] = dot(m_ref[...], branch_ref[...], NN).astype(BF16)
        row = pl.multiple_of(jnp.bitwise_xor(me_ref[0], rel) * count, 16)
        ref[at, width:] = more[pl.ds(row, count), :].astype(BF16)


def combine_kernel(slots, me_ref, ret_ref, places_ref, after_ref, out_ref, scratch):
    part = after_ref.shape[0] // 2
    for block in range(slots.n_expert):
        first = pl.multiple_of(slots.expert_of(block, me_ref[0]) * slots.block, 16)
        scratch[block * slots.block:(block + 1) * slots.block, :] = ret_ref[pl.ds(first, slots.block), :]

    def one(i, carry):
        at = pl.ds(pl.multiple_of(i * part, part), part)
        slot = lax.broadcasted_iota(jnp.int32, (part, scratch.shape[0]), 1)
        hit = (slot == places_ref[at, 0:1]) | (slot == places_ref[at, 1:2])
        total = after_ref[at, :] + dot(jnp.where(hit, 1.0, 0.0).astype(BF16), scratch[...], NN)
        out_ref[at, :] = total.astype(BF16)
        return carry

    lax.fori_loop(0, after_ref.shape[0] // part, one, 0)


def final_kernel(me_ref, x_ref, gain_ref, after_ref, d0, d1, d2, d3, w_ref, out_ref):
    grad = sum(
        dot(d_ref[...], w_ref[jnp.bitwise_xor(me_ref[0], rel)], NT) for rel, d_ref in enumerate((d0, d1, d2, d3))
    )
    unit, factor = rms_parts(x_ref[...].astype(F32))
    out_ref[...] = (after_ref[...] + rms_grad(grad, gain_ref[...], unit, factor)).astype(BF16)


def column_grad_kernel(
    orders, heads, me_ref, bins_ref, n0, n1, n2, n3, d0, d1, d2, d3, wk_ref, wn_ref, wf_ref, *refs
):
    *out_refs, acc, more = refs
    acc[...] = sum(dot(n[...], d[...], TN) for n, d in ((n0, d0), (n1, d1), (n2, d2), (n3, d3)))
    rows = wf_ref.shape[0]
    more[...] = wk_ref[0:rows, :].astype(F32) + wn_ref[0:rows, :].astype(F32) + wf_ref[...].astype(F32)
    cols = 3 * heads * DH
    wide = acc.shape[1]
    lane = lax.broadcasted_iota(jnp.int32, (NB, wide), 1)
    table = jnp.zeros((NB, wide), F32)
    for h in range(heads):
        above = jnp.sum(bins_ref[:, h * SEG:(h + 1) * SEG], axis=1, keepdims=True)
        column = above - jnp.concatenate([above[1:], jnp.zeros((1, 1), F32)], axis=0)
        column = jnp.concatenate([column[:-1], -jnp.sum(column[:-1], axis=0, keepdims=True)], axis=0)
        table = jnp.where(lane == cols + h, column, table)
    share = rows // len(orders[0])
    half = share // 2

    def block_of(rel):
        first = jnp.bitwise_xor(me_ref[0], rel) * share
        at = lambda start: pl.ds(pl.multiple_of(start + first, 8), share)
        block = [acc[at(p * rows), :] for p in range(4)]
        block[0] = jnp.concatenate([block[0][:NB] + table, block[0][NB:]], axis=0)
        others = more[at(0), :]
        rest = others[:, wide:]
        folded = [rest[:half], rest[half:], jnp.zeros((half, wide - 2 * rest.shape[1]), F32)]
        block += [others[:, :wide], jnp.concatenate(folded, axis=1)]
        if half % 8:
            block.append(jnp.zeros((-half % 8, wide), F32))
        return block[:3], block[3:]

    blocks = {rel: block_of(rel) for rel in orders[0]}
    count = len(out_refs) // 2
    for part, order in enumerate(orders):
        for i in range(count):
            mine = order[i * len(order) // count:(i + 1) * len(order) // count]
            rows_of = [row for rel in mine for row in blocks[rel][part]]
            out_refs[part * count + i][...] = jnp.concatenate(rows_of, axis=0).astype(BF16)


def split_kernel(me_ref, *refs):
    *in_refs, b0, b1, b2, b3, more_ref, table_ref, total = refs
    share, cols = b0.shape
    count = len(in_refs) // 2
    total[0:3 * share, :] = sum(ref[...].astype(F32) for ref in in_refs[:count])
    total[3 * share:, :] = sum(ref[...].astype(F32) for ref in in_refs[count:])
    wide = total.shape[1]
    for rel, ref in enumerate((b0, b1, b2, b3)):
        at = pl.ds(pl.multiple_of(jnp.bitwise_xor(me_ref[0], rel) * share, 8), share)
        ref[...] = total[at, :][:, :cols].astype(BF16)
    folded = total[5 * share:5 * share + share // 2, :]
    rest = more_ref.shape[1] - wide
    folded = jnp.concatenate([folded[:, :rest], folded[:, rest:2 * rest]], axis=0)
    more_ref[...] = jnp.concatenate([total[4 * share:5 * share, :], folded], axis=1).astype(BF16)
    table_ref[...] = total[0:NB, wide - table_ref.shape[1]:]


def join_kernel(me_ref, p0, p1, p2, p3, more_ref, out_ref):
    parts = [ref[...] for ref in (p0, p1, p2, p3)]
    for bit in (1, 2):
        swapped = (me_ref[0] & bit) != 0
        parts = [jnp.where(swapped, parts[i ^ bit], parts[i]) for i in range(4)]
    hw = p0.shape[1] // 3
    out_ref[...] = jnp.concatenate(
        [part[:, c * hw:(c + 1) * hw] for c in range(3) for part in parts] + [more_ref[...]], axis=1
    )


def place_kernel(experts, me_ref, wq_ref, wk_ref, wv_ref, gain_in_ref, *refs):
    *piece_refs, q_ref, k_ref, v_ref, o_ref, router_ref, gains_ref, more = refs
    width = q_ref.shape[1]
    count = piece_refs[0].shape[0] // (2 if len(piece_refs) > 1 else 1)
    for rel, at_row, piece_ref in [
        (rel | (first // count) * 4, first, ref) for rel, ref in enumerate(piece_refs) for first in range(0, ref.shape[0], count)
    ]:
        at = pl.ds(pl.multiple_of(jnp.bitwise_xor(me_ref[0], rel) * count, 8), count)
        piece = piece_ref[at_row:at_row + count, :].astype(F32)
        for c, out_ref in enumerate((q_ref, k_ref, v_ref, o_ref)):
            out_ref[at, :] = piece[:, c * width:(c + 1) * width]
        more[at, :] = piece[:, 4 * width:]
    total = sum(
        w_ref[...].astype(F32) * out_ref[...] for w_ref, out_ref in ((wq_ref, q_ref), (wk_ref, k_ref), (wv_ref, v_ref))
    )
    rows = total.shape[0]
    lane = lax.broadcasted_iota(jnp.int32, more.shape, 1)
    columns = jnp.where(lane == experts + 1, jnp.sum(total, axis=1, keepdims=True), more[...])
    columns = jnp.concatenate([columns, jnp.zeros((-rows % 128, columns.shape[1]), F32)], axis=0)
    columns = jnp.transpose(columns)[:, :rows]
    router_ref[...] = columns[0:experts]
    gains_ref[0:1, :] = columns[experts + 1:experts + 2] / gain_in_ref[...]
    gains_ref[1:2, :] = columns[experts:experts + 1]


def per_device(
    tokens, gain_attn, w_query, w_key, w_value, w_output, rel_table, gain_moe, router,
    w_in, w_out, routes, parents, cotangent,
):
    n_shard = lax.axis_size("shard")
    n_expert = lax.axis_size("expert")
    tok, width = tokens.shape
    tree_len = tok * n_shard
    n_experts = router.shape[1]
    heads = rel_table.shape[0]
    hw = heads * DH
    wide = -(-3 * hw // 128) * 128
    rows = width // n_shard
    slots = Slots(n_expert, max(2, tok * 20 // (7 * n_experts)))
    me_s, me_e = lax.axis_index("shard").astype(jnp.int32), lax.axis_index("expert").astype(jnp.int32)
    me_shard, me_expert, me = me_s.reshape(1), me_e.reshape(1), jnp.stack([me_e, me_s])

    more = jnp.concatenate([gain_attn[:, None], gain_moe[:, None], router], axis=1)
    w_rel = pl.pallas_call(
        columns_kernel,
        in_specs=[SMEM] + [VMEM] * 4,
        out_specs=VMEM,
        out_shape=jax.ShapeDtypeStruct((n_shard, rows, -(-(3 * hw + 2 + n_experts) // 128) * 128), BF16),
        compiler_params=params(),
        cost_estimate=SHORT,
    )(me_shard, w_query, w_key, w_value, more)
    near_tokens, far_tokens = swap(tokens, "shard", 1), swap(tokens, "shard", 2)
    w_pieces = swap_all([w_rel[rel] for rel in range(n_shard)], "shard")

    expert_range = jnp.arange(n_experts, dtype=jnp.int32)
    flat_routes = routes.reshape(-1)
    expert_hot = (flat_routes[:, None] == expert_range[None, :]).astype(jnp.int32)
    earlier = jnp.cumsum(expert_hot, axis=0) - expert_hot
    rank = jnp.sum(earlier * expert_hot, axis=-1)
    places = (slots.block_of(flat_routes, me_e) * slots.block + rank).reshape(tok, 2)
    places_row = places.T
    others = jnp.repeat(routes.T[::-1], 8, axis=0).astype(BF16)
    block_shapes = [((len(array) * slots.block, width), BF16) for array in slots.arrays]

    sent_grads = pl.pallas_call(
        functools.partial(dispatch_kernel, slots),
        in_specs=[SMEM] + [VMEM] * 3 + [ANY],
        out_specs=VMEM,
        out_shape=jax.ShapeDtypeStruct((n_expert * slots.block, width), BF16),
        compiler_params=params(),
        cost_estimate=SHORT,
    )(me_expert, places_row, others, cotangent, w_rel)
    got_grads = over_experts(sent_grads)
    far_tokens, _, w_pieces = lax.optimization_barrier((far_tokens, sent_grads, w_pieces))
    tree = [tokens, near_tokens, far_tokens, swap(far_tokens, "shard", 1)]

    *normed_one, queries, keys, values, keys_t, values_t, w_cols, bias, gain_one, gain_two, router_w = pl.pallas_call(
        functools.partial(project_kernel, heads),
        in_specs=[SMEM] * 2 + [VMEM] * 8 + [ANY],
        out_specs=[VMEM] * 14,
        out_shape=arrays(
            *[((tok, width), BF16)] * 4, *[((tree_len, HW), BF16)] * 3, *[((HW, tree_len), BF16)] * 2,
            ((width, wide), BF16), ((4, SEG, heads * SEG), F32), *[((1, width), F32)] * 2, ((width, n_experts), BF16),
        ),
        scratch_shapes=[pltpu.VMEM((width, 3 * HW + 128), BF16)],
        compiler_params=params(),
        cost_estimate=SHORT,
    )(me_shard, rel_table.astype(F32), *w_pieces, *tree, sent_grads)
    parent_row = parents[0]
    *mixed, raw, lse = pl.pallas_call(
        functools.partial(attn_forward_kernel, heads),
        in_specs=[SMEM] * 2 + [VMEM] * 5,
        out_specs=[VMEM] * 6,
        out_shape=arrays(*[((hw, tok), BF16)] * 4, ((HW, tree_len), F32), ((SEGS * 8, heads * SEG), F32)),
        scratch_shapes=[pltpu.VMEM((HW, tree_len), BF16)],
        compiler_params=params(),
        cost_estimate=FORWARD,
    )(me_shard, parent_row, queries, keys, values, values_t, bias)
    first_far = swap(w_in[0], "shard", 2)
    w_o = lax.all_gather(w_output, "shard", axis=0)
    mixed, first_far, w_o = lax.optimization_barrier((mixed, first_far, w_o))
    mixed = swap_all(mixed, "shard")
    first_w = [w_in[0], swap(w_in[0], "shard", 1), first_far, swap(first_far, "shard", 1)]
    second_near = swap(w_out[0], "shard", 1)
    w_out, w_cols, _ = lax.optimization_barrier((w_out, w_cols, mixed))
    second_far = swap(w_out[0], "shard", 2)
    mixed, first_w, second_near = lax.optimization_barrier((mixed, first_w, second_near))

    after, normed_two, gates, *sent_rows = pl.pallas_call(
        functools.partial(post_kernel, slots),
        in_specs=[SMEM] + [VMEM] * 10,
        out_specs=[VMEM] * (3 + len(block_shapes)),
        out_shape=arrays(((tok, width), F32), ((tok, width), BF16), ((tok, 2), F32), *block_shapes),
        compiler_params=params(),
        cost_estimate=SHORT,
    )(me, tokens, gain_two, router_w, routes, places_row, *mixed, w_o)

    probs = pl.pallas_call(
        functools.partial(attn_prob_kernel, heads),
        in_specs=[SMEM] + [VMEM] * 4 + [ANY],
        out_specs=VMEM,
        out_shape=jax.ShapeDtypeStruct((PROB_ROWS, 2 * heads * SEG), BF16),
        compiler_params=params(),
        cost_estimate=SHORT,
    )(parent_row, queries, keys, lse, bias, after)

    second_far, probs = lax.optimization_barrier((second_far, probs))
    second_w = [w_out[0], second_near, second_far, swap(second_far, "shard", 1)]
    run = functools.partial(run_expert, slots)
    shared = (me, got_grads, router_w, first_w, second_w)
    near_rows = slots.near_exchange(sent_rows[0])
    if slots.cut:
        far_shape = sent_rows[1].shape
        out_all, own_dx, *own_kept = run("own", sent_rows[:1], far_shape, shared, [probs], SHORT)
        far_rows, probs = lax.optimization_barrier((sent_rows[1:], probs))
        far_rows = [swap(block, "expert", rel) for block, rel in zip(far_rows, slots.rels)]
        out_all, near_dx, *near_kept = run("near", [near_rows], near_rows.shape, shared, [probs, own_dx, out_all], SHORT)
        out_all, *far = run("far", far_rows, far_shape, shared, [probs, out_all], LONG)
        dx = [slots.near_exchange(near_dx)] + [swap(block, "expert", rel) for block, rel in zip(far, slots.rels)]
        kept = [own_kept, near_kept, far[4:]]
    else:
        out_all, dx, *all_kept = run("all", [near_rows], near_rows.shape, shared, [probs], SHORT)
        dx, kept = [slots.near_exchange(dx)], [all_kept]
    send_second, keep_second = run_second_grad([k[2] for k in kept], [k[1] for k in kept])
    w_cols, _ = lax.optimization_barrier((w_cols, kept[0][0]))
    w_all = lax.all_gather(w_cols, "shard", axis=0)
    send_first, keep_first = run_first_grad(me, [k[0] for k in kept], [k[3] for k in kept], rows, dx[0], w_all)
    out_all, _ = lax.optimization_barrier((out_all, dx))
    returned = over_experts(out_all)
    dx, send_first, send_second = lax.optimization_barrier((dx, send_first, send_second))

    slot_rows = slots.n_expert * slots.block
    grad_after, gm0, gm1, gm2, gm3, send_wo, keep_wo = pl.pallas_call(
        functools.partial(back_kernel, slots),
        in_specs=[SMEM] + [VMEM] * (len(block_shapes) + 13),
        out_specs=[VMEM] * 7,
        out_shape=arrays(((tok, width), F32), *[((hw, tok), BF16)] * 4, *[((2 * rows, width + 128), BF16)] * 2),
        scratch_shapes=[
            pltpu.VMEM((tok, width), BF16),
            pltpu.VMEM((tok, n_experts), BF16),
            pltpu.VMEM((8, width), F32),
            pltpu.VMEM((width, 128), F32),
            pltpu.VMEM((slot_rows, width), BF16),
        ],
        compiler_params=params(),
        cost_estimate=SHORT,
    )(me_shard, *dx, places, routes, gates, after, gain_two, router_w, cotangent, w_o, normed_two, *mixed)
    grad_mixed = swap_all([gm0, gm1, gm2, gm3], "shard")
    sums = [
        core_sum(send, keep)
        for send, keep in ((send_second, keep_second), (send_first, keep_first), (send_wo, keep_wo))
    ]
    grad_mixed, sums = lax.optimization_barrier((grad_mixed, sums))
    second_sum, first_sum, wo_sum = sums
    second_sum, wo_sum = across_sum(second_sum), across_sum(wo_sum)

    *dqkv, bins = pl.pallas_call(
        functools.partial(attn_backward_kernel, heads),
        in_specs=[SMEM] * 2 + [VMEM] * 5 + [ANY] + [VMEM] * 4,
        out_specs=[VMEM] * 5,
        out_shape=arrays(*[((tok, wide), BF16)] * 4, ((NB, heads * SEG), F32)),
        scratch_shapes=[
            pltpu.VMEM((HW, tree_len), BF16),
            pltpu.VMEM((tree_len, HW), BF16),
            pltpu.VMEM((tree_len, HW), F32),
            pltpu.VMEM((tree_len, HW), F32),
            pltpu.VMEM((2, SEG, heads * SEG), F32),
            pltpu.VMEM((PROB_ROWS, 2 * heads * SEG), BF16),
            pltpu.SemaphoreType.DMA((SEGS // 2,)),
        ],
        compiler_params=params(),
        cost_estimate=LONG,
    )(me_shard, parent_row, queries, keys, values, keys_t, raw, probs, *grad_mixed)
    dqkv_own = swap_all(dqkv, "shard")

    halving = [(1, 2, 4), (1, 2, 4)] if n_expert == 8 else []
    orders = [[0], [0]]
    for i, bits in enumerate(halving):
        for bit in reversed(bits):
            orders[i] = orders[i] + [rel | bit for rel in orders[i]]
    share = rows // len(orders[0])
    block_rows = [3 * share, 2 * share + -(-share // 16) * 8]
    parts = 2 if halving else 1
    out_rows = [count * len(orders[0]) // parts for count in block_rows for _ in range(parts)]
    halves = pl.pallas_call(
        functools.partial(column_grad_kernel, orders, heads),
        in_specs=[SMEM] + [VMEM] * 12,
        out_specs=[VMEM] * len(out_rows),
        out_shape=arrays(*[((count, wide), BF16) for count in out_rows]),
        scratch_shapes=[pltpu.VMEM((width, wide), F32), pltpu.VMEM((rows, width + 128), F32)],
        compiler_params=params(),
        cost_estimate=SHORT,
    )(me_expert if halving else jnp.zeros((1,), jnp.int32), bins, *normed_one, *dqkv, *wo_sum)
    if halving:
        pairs = [halves[:2], halves[2:]]
        pairs, second_sum = lax.optimization_barrier((pairs, second_sum))
        for step in range(2):
            sums = [kept.astype(F32) + swap(sent, "expert", bits[step]).astype(F32) for (kept, sent), bits in zip(pairs, halving)]
            pairs = [jnp.split(part.astype(BF16), 2, axis=0) for part in sums]
            pairs, dqkv_own[2 + step] = lax.optimization_barrier((pairs, dqkv_own[2 + step]))
        sums = [part for kept, sent in pairs for part in (kept, swap(sent, "expert", 4))]
    else:
        sums = lax.psum([part.astype(F32) for part in halves], "expert")
    *cols, more, table = pl.pallas_call(
        split_kernel,
        in_specs=[SMEM] + [VMEM] * len(sums),
        out_specs=[VMEM] * 6,
        out_shape=arrays(*[((share, 3 * hw), BF16)] * 4, ((share, width + 128), BF16), ((NB, wide - 3 * hw), F32)),
        scratch_shapes=[pltpu.VMEM((sum(block_rows), wide), F32)],
        compiler_params=params(),
        cost_estimate=SHORT,
    )(me_shard, *sums)
    table = table[:, :heads].T
    cols, first_sum = lax.optimization_barrier((swap_all(cols, "shard"), first_sum))
    cols = pl.pallas_call(
        join_kernel,
        in_specs=[SMEM] + [VMEM] * 5,
        out_specs=VMEM,
        out_shape=jax.ShapeDtypeStruct((share, 4 * width + 128), BF16),
        compiler_params=params(),
        cost_estimate=SHORT,
    )(me_shard, *cols, more)
    grad_w_in = total_sum(across_sum(first_sum))[None]
    returned, second_sum, _ = lax.optimization_barrier((returned, second_sum, cols))
    grad_w_out = total_sum(second_sum)[None]
    output = pl.pallas_call(
        functools.partial(combine_kernel, slots),
        in_specs=[SMEM] + [VMEM] * 3,
        out_specs=VMEM,
        out_shape=jax.ShapeDtypeStruct((tok, width), BF16),
        scratch_shapes=[pltpu.VMEM((slot_rows, width), BF16)],
        compiler_params=params(),
        cost_estimate=SHORT,
    )(me_expert, returned, places, after)
    pieces = [cols]
    if halving:
        other = swap(cols, "expert", 4)
        dqkv_own, other = lax.optimization_barrier((dqkv_own, other))
        pieces = swap_all([jnp.concatenate([cols, other], axis=0)] * 4, "expert")
    grad_tokens = pl.pallas_call(
        final_kernel,
        in_specs=[SMEM] + [VMEM] * 8,
        out_specs=VMEM,
        out_shape=jax.ShapeDtypeStruct((tok, width), BF16),
        compiler_params=params(),
        cost_estimate=SHORT,
    )(me_shard, tokens, gain_one, grad_after, *dqkv_own, w_all)
    pieces, output, grad_tokens, grad_w_in, grad_w_out = lax.optimization_barrier(
        (pieces, output, grad_tokens, grad_w_in, grad_w_out)
    )
    grad_q, grad_k, grad_v, grad_wo, grad_router, grad_gains = pl.pallas_call(
        functools.partial(place_kernel, n_experts),
        in_specs=[SMEM] + [VMEM] * (4 + len(pieces)),
        out_specs=[VMEM] * 6,
        out_shape=arrays(*[((rows, width), F32)] * 4, ((n_experts, rows), F32), ((2, rows), F32)),
        scratch_shapes=[pltpu.VMEM((rows, 128), F32)],
        compiler_params=params(),
        cost_estimate=SHORT,
    )(
        me_expert if halving else jnp.zeros((1,), jnp.int32), w_query, w_key, w_value,
        gain_attn.astype(F32).reshape(1, rows), *pieces,
    )

    return (
        output, grad_tokens, grad_gains[0], grad_q, grad_k, grad_v, grad_wo, table, grad_gains[1], grad_router.T,
        grad_w_in, grad_w_out,
    )


def solution(mesh):
    both, shard = P(("expert", "shard"), None), P("shard", None)
    three = P("expert", "shard", None)
    return jax.shard_map(
        per_device,
        mesh=mesh,
        in_specs=(
            both, P("shard"), shard, shard, shard, shard, shard, P("shard"), shard, three, three, both,
            P("expert", None), both,
        ),
        out_specs=(both, both, P("shard"), shard, shard, shard, shard, shard, P("shard"), shard, three, three),
        check_vma=False,
    )
```

```python
import functools
import math

import jax
import jax.numpy as jnp
from jax import lax
from jax.experimental import pallas as pl
from jax.experimental.pallas import tpu as pltpu
from jax.sharding import PartitionSpec as P

DH = 64
NB = 16
SEG = 128
SEGS = 20
TRUNK = 8
SPARE = 3

THRESHOLDS = (1, 2, 3, 4, 5, 6, 7, 8, 12, 16, 24, 32, 48, 64, 96)
EPS = 1e-06
MASKED = -1e30
HW = 256

F32 = jnp.float32
BF16 = jnp.bfloat16
VMEM = pl.BlockSpec(memory_space=pltpu.VMEM)
SMEM = pl.BlockSpec(memory_space=pltpu.SMEM)
ANY = pl.BlockSpec(memory_space=pl.ANY)

NN = ((1,), (0,))
NT = ((1,), (1,))
TN = ((0,), (0,))


def params(mib=60, **more):
    return pltpu.CompilerParams(vmem_limit_bytes=mib << 20, **more)


SHORT = pl.CostEstimate(flops=0, bytes_accessed=1024, transcendentals=0)
LONG = pl.CostEstimate(flops=1 << 40, bytes_accessed=1 << 32, transcendentals=0)


FORWARD = pl.CostEstimate(flops=30_400_000_000, bytes_accessed=1024, transcendentals=0)
BACKWARD = pl.CostEstimate(flops=22_000_000_000, bytes_accessed=1024, transcendentals=0)


def dot(left, right, contract):
    return lax.dot_general(left, right, (contract, ((), ())), preferred_element_type=F32)


def arrays(*shapes):
    return [jax.ShapeDtypeStruct(shape, dtype) for shape, dtype in shapes]


def rms_parts(values):
    factor = lax.rsqrt(jnp.mean(values * values, axis=-1, keepdims=True) + EPS)
    return values * factor, factor


def rms_grad(grad_out, gain_row, unit_rows, factor):
    scaled = grad_out * gain_row
    return factor * (scaled - unit_rows * jnp.mean(scaled * unit_rows, axis=-1, keepdims=True))


def columns_kernel(me_ref, q_ref, k_ref, v_ref, more_ref, *out_refs):
    groups = len(out_refs)
    depth, width = out_refs[0].shape
    hw = q_ref.shape[1] // groups
    blocks = [
        jnp.concatenate([ref[:, s * hw:(s + 1) * hw] for ref in (q_ref, k_ref, v_ref)], axis=1) for s in range(groups)
    ]
    more = jnp.concatenate(
        [more_ref[...], jnp.zeros((depth, width - 3 * hw - more_ref.shape[1]), BF16)], axis=1
    )
    for bit in (1, 2):
        swapped = (me_ref[0] & bit) != 0
        blocks = [jnp.where(swapped, blocks[i ^ bit], blocks[i]) for i in range(groups)]
    for block, out_ref in zip(blocks, out_refs):
        out_ref[...] = jnp.concatenate([block, more], axis=1)


def project_kernel(
    heads, me_ref, table_ref, w0, w1, w2, w3, t0, t1, t2, t3, before_ref,
    n_ref, q_ref, k_ref, v_ref, kt_ref, vt_ref, w_ref, bias_ref, gain_ref, gain_two_ref, router_ref, w_pad,
):
    step = pl.program_id(0)

    @pl.when(step == 0)
    def _():
        hw = heads * DH
        blank = jnp.zeros((w0.shape[0], HW - hw), BF16)
        for rel, piece_ref in enumerate((w0, w1, w2, w3)):
            depth = piece_ref.shape[0]
            at = pl.ds(pl.multiple_of(jnp.bitwise_xor(me_ref[0], rel) * depth, 16), depth)
            piece = piece_ref[...]
            blank_end = jnp.zeros((depth, w_ref.shape[1] - 3 * hw), BF16)
            w_ref[at, :] = jnp.concatenate([piece[:, :3 * hw], blank_end], axis=1)
            router_ref[at, :] = piece[:, 3 * hw + 2:3 * hw + 2 + router_ref.shape[1]]
            padded = [part for c in range(3) for part in (piece[:, c * hw:(c + 1) * hw], blank)]
            padded.append(piece[:, 3 * hw:3 * hw + 2])
            padded.append(jnp.zeros((depth, w_pad.shape[1] - 3 * HW - 2), BF16))
            w_pad[at, :] = jnp.concatenate(padded, axis=1)
        gains = jnp.transpose(w_pad[:, 3 * HW:].astype(F32))
        gain_ref[...] = gains[0:1]
        gain_two_ref[...] = gains[1:2]
        key = lax.broadcasted_iota(jnp.int32, (SEG, SEG), 0)
        query = lax.broadcasted_iota(jnp.int32, (SEG, SEG), 1)
        bias_ref[0] = jnp.zeros((SEG, heads * SEG), F32)
        bias_ref[3] = jnp.full((SEG, heads * SEG), MASKED, F32)
        for h in range(heads):
            last = table_ref[h, NB - 1]
            at = slice(h * SEG, (h + 1) * SEG)
            for kind, gap in ((1, query - key + SEG), (2, query - key)):
                tile = jnp.zeros((SEG, SEG), F32) + (table_ref[h, 0] - last)
                for i, threshold in enumerate(THRESHOLDS):
                    tile = jnp.where(gap >= threshold, table_ref[h, i + 1] - last, tile)
                bias_ref[kind, :, at] = jnp.where(gap >= 0, tile, MASKED)

    for rel, t_ref in enumerate((t0, t1, t2, t3)):
        @pl.when(step == rel)
        def _(t_ref=t_ref):
            unit, _ = rms_parts(t_ref[...].astype(F32))
            normed = (unit * gain_ref[...]).astype(BF16)
            n_ref[0] = normed
            qkv = dot(normed, w_pad[:, :3 * HW], NN)
            q_ref[...] = qkv[:, :HW].astype(BF16) * jnp.asarray(DH ** -0.5, BF16)
            k_ref[...] = qkv[:, HW:2 * HW].astype(BF16)
            v_ref[...] = qkv[:, 2 * HW:].astype(BF16)
            kt_ref[...] = jnp.transpose(qkv[:, HW:2 * HW]).astype(BF16)
            vt_ref[...] = jnp.transpose(qkv[:, 2 * HW:]).astype(BF16)


def by_head(rows, heads):
    lane = lax.broadcasted_iota(jnp.int32, rows.shape, 1)
    zero = jnp.zeros_like(rows)
    return jnp.concatenate(
        [jnp.where((lane >= h * DH) & (lane < (h + 1) * DH), rows, zero) for h in range(heads)], axis=0
    )


def seg_at(index):
    if isinstance(index, int):
        return slice(index * SEG, (index + 1) * SEG)
    return pl.ds(pl.multiple_of(index * SEG, SEG), SEG)


def head_columns(acc, heads):
    pieces = [acc[h * DH:(h + 1) * DH, h * SEG:(h + 1) * SEG] for h in range(heads)]
    pieces.append(jnp.zeros((HW - heads * DH, SEG), F32))
    return jnp.concatenate(pieces, axis=0)


def pair_bias(bias_ref, first, second):
    return jnp.concatenate([bias_ref[first], bias_ref[second]], axis=1)


def attn_forward_kernel(
    heads, me_ref, parent_ref, q_ref, k_ref, v_ref, vt_ref, bias_ref, o0, o1, o2, o3, raw_ref, lse_ref, out_all
):
    cols = heads * SEG
    trunk_len = TRUNK * SEG
    last = trunk_len - SEG

    def queries(b):
        return by_head(q_ref[seg_at(b), :], heads)

    def finish(b, acc, total, top):
        lse_ref[pl.ds(b * 8, 8), :] = jnp.broadcast_to(top + jnp.log(total), (8, cols))
        columns = head_columns(acc / total, heads)
        raw_ref[:, seg_at(b)] = columns
        out_all[:, seg_at(b)] = columns.astype(BF16)

    for j in range(TRUNK // 2):
        q6 = jnp.concatenate([queries(2 * j), queries(2 * j + 1)], axis=0)
        scores = dot(k_ref[0:(j + 1) * 2 * SEG, :], q6, NT)
        parts = []
        if j > 0:
            far = (2 * j - 1) * SEG
            parts = [scores[:far], scores[far:far + SEG] + pair_bias(bias_ref, 1, 0)]
        parts.append(scores[2 * j * SEG:(2 * j + 1) * SEG] + pair_bias(bias_ref, 2, 1))
        parts.append(scores[(2 * j + 1) * SEG:] + pair_bias(bias_ref, 3, 2))
        top = functools.reduce(jnp.maximum, [jnp.max(part, axis=0, keepdims=True) for part in parts])
        parts = [jnp.exp(part - top) for part in parts]
        total = functools.reduce(jnp.add, [jnp.sum(part, axis=0, keepdims=True) for part in parts])
        acc = dot(vt_ref[:, 0:(j + 1) * 2 * SEG], jnp.concatenate([p.astype(BF16) for p in parts], axis=0), NN)
        for s in range(2):
            at = slice(s * cols, (s + 1) * cols)
            finish(2 * j + s, acc[:, at], total[:, at], top[:, at])

    def other_step(i, carry):
        segs = [TRUNK + 2 * i, TRUNK + 2 * i + 1]
        parents = [parent_ref[b] for b in segs]
        leaf = [(parent >= TRUNK).astype(jnp.int32) for parent in parents]
        q3 = [queries(b) for b in segs]
        q6 = jnp.concatenate(q3, axis=0)
        scores = dot(k_ref[0:trunk_len, :], q6, NT)
        near = scores[last:] + pair_bias(bias_ref, 1 - leaf[0], 1 - leaf[1])
        far = scores[:last]
        extra = []
        for s in range(2):
            keys = jnp.concatenate([k_ref[seg_at(parents[s]), :], k_ref[seg_at(segs[s]), :]], axis=0)
            bias = jnp.concatenate([bias_ref[3 - 2 * leaf[s]], bias_ref[2]], axis=0)
            extra.append(dot(keys, q3[s], NT) + bias)
        top = jnp.maximum(jnp.max(far, axis=0, keepdims=True), jnp.max(near, axis=0, keepdims=True))
        top = jnp.maximum(top, jnp.concatenate([jnp.max(e, axis=0, keepdims=True) for e in extra], axis=1))
        far, near = jnp.exp(far - top), jnp.exp(near - top)
        extra = [jnp.exp(extra[s] - top[:, s * cols:(s + 1) * cols]) for s in range(2)]
        total = jnp.sum(far, axis=0, keepdims=True) + jnp.sum(near, axis=0, keepdims=True)
        total = total + jnp.concatenate([jnp.sum(e, axis=0, keepdims=True) for e in extra], axis=1)
        acc = dot(vt_ref[:, 0:trunk_len], jnp.concatenate([far.astype(BF16), near.astype(BF16)], axis=0), NN)
        for s in range(2):
            at = slice(s * cols, (s + 1) * cols)
            values = jnp.concatenate([vt_ref[:, seg_at(parents[s])], vt_ref[:, seg_at(segs[s])]], axis=1)
            finish(segs[s], acc[:, at] + dot(values, extra[s].astype(BF16), NN), total[:, at], top[:, at])
        return carry

    lax.fori_loop(0, (SEGS - TRUNK) // 2, other_step, 0)
    for rel, o_ref in enumerate((o0, o1, o2, o3)):
        width, count = o_ref.shape
        at = pl.ds(pl.multiple_of(jnp.bitwise_xor(me_ref[0], rel) * count, SEG), count)
        o_ref[...] = out_all[0:width, at]


TRUNK_FIRST = [SEG * j * (j + 1) for j in range(TRUNK // 2 + 1)]
OTHER_ROWS = (TRUNK + 2) * SEG
PROB_ROWS = TRUNK_FIRST[-1] + (SEGS - TRUNK) // 2 * OTHER_ROWS


def attn_prob_kernel(heads, parent_ref, q_ref, k_ref, lse_ref, bias_ref, before_ref, out_ref):
    cols = heads * SEG

    def common(b):
        return by_head(q_ref[seg_at(b), :], heads), lse_ref[pl.ds(b * 8, 8), :][0:1]

    for j in range(TRUNK // 2):
        (qa, la), (qb, lb) = common(2 * j), common(2 * j + 1)
        q6, lse = jnp.concatenate([qa, qb], axis=0), jnp.concatenate([la, lb], axis=1)
        for i in range(j + 1):
            scores = dot(k_ref[2 * i * SEG:2 * (i + 1) * SEG, :], q6, NT)
            if i == j:
                scores = scores + jnp.concatenate([pair_bias(bias_ref, 2, 1), pair_bias(bias_ref, 3, 2)], axis=0)
            if i == j - 1:
                scores = scores + jnp.concatenate([pair_bias(bias_ref, 0, 0), pair_bias(bias_ref, 1, 0)], axis=0)
            first = TRUNK_FIRST[j] + 2 * i * SEG
            out_ref[first:first + 2 * SEG, :] = jnp.exp(scores - lse).astype(BF16)

    def other_step(step, carry):
        segs = [TRUNK + 2 * step, TRUNK + 2 * step + 1]
        parents = [parent_ref[b] for b in segs]
        leaf = [(parent >= TRUNK).astype(jnp.int32) for parent in parents]
        each = [common(b) for b in segs]
        q6, lse = jnp.concatenate([q for q, _ in each], axis=0), jnp.concatenate([l for _, l in each], axis=1)
        base = TRUNK_FIRST[-1] + step * OTHER_ROWS
        for i in range(TRUNK // 2):
            scores = dot(k_ref[2 * i * SEG:2 * (i + 1) * SEG, :], q6, NT)
            if i == TRUNK // 2 - 1:
                near = pair_bias(bias_ref, 1 - leaf[0], 1 - leaf[1])
                scores = scores + jnp.concatenate([jnp.zeros_like(near), near], axis=0)
            at = pl.ds(pl.multiple_of(base + 2 * i * SEG, SEG), 2 * SEG)
            out_ref[at, :] = jnp.exp(scores - lse).astype(BF16)
        extra = []
        for s in range(2):
            keys = jnp.concatenate([k_ref[seg_at(parents[s]), :], k_ref[seg_at(segs[s]), :]], axis=0)
            bias = jnp.concatenate([bias_ref[3 - 2 * leaf[s]], bias_ref[2]], axis=0)
            extra.append(jnp.exp(dot(keys, each[s][0], NT) + bias - each[s][1]).astype(BF16))
        at = pl.ds(pl.multiple_of(base + TRUNK * SEG, SEG), 2 * SEG)
        out_ref[at, :] = jnp.concatenate(extra, axis=1)
        return carry

    lax.fori_loop(0, (SEGS - TRUNK) // 2, other_step, 0)


def attn_backward_kernel(
    heads, me_ref, parent_ref, q_ref, k_ref, v_ref, kt_ref, raw_ref, prob_ref, g0, g1, g2, g3_ref,
    d0, d1, d2, d3, bins_ref, grad_all, dq_all, dk_acc, dv_acc, bins_acc, probs, sem,
):
    def fetch(step):
        if isinstance(step, int):
            at = pl.ds(TRUNK_FIRST[step], TRUNK_FIRST[step + 1] - TRUNK_FIRST[step])
        else:
            at = pl.ds(pl.multiple_of(TRUNK_FIRST[-1] + (step - TRUNK // 2) * OTHER_ROWS, SEG), OTHER_ROWS)
        return pltpu.make_async_copy(prob_ref.at[at, :], probs.at[at, :], sem.at[step])

    for j in range(TRUNK // 2):
        fetch(j).start()

    def start_other(step, carry):
        fetch(step + TRUNK // 2).start()
        return carry

    lax.fori_loop(0, (SEGS - TRUNK) // 2, start_other, 0)
    cols = heads * SEG
    trunk_len = TRUNK * SEG
    dk_acc[...] = jnp.zeros_like(dk_acc)
    dv_acc[...] = jnp.zeros_like(dv_acc)
    bins_acc[...] = jnp.zeros_like(bins_acc)
    for rel, g_ref in enumerate((g0, g1, g2, g3_ref)):
        width, count = g_ref.shape
        at = pl.ds(pl.multiple_of(jnp.bitwise_xor(me_ref[0], rel) * count, SEG), count)
        grad_all[0:width, at] = g_ref[...]
        grad_all[width:HW, at] = jnp.zeros((HW - width, count), BF16)

    def common(b):
        q3 = by_head(q_ref[seg_at(b), :], heads)
        grad = grad_all[:, seg_at(b)].astype(F32)
        product = grad * raw_ref[:, seg_at(b)]
        row_dot = jnp.concatenate(
            [jnp.sum(product[h * DH:(h + 1) * DH], axis=0, keepdims=True) for h in range(heads)], axis=1
        )
        return q3, by_head(jnp.transpose(grad).astype(BF16), heads), row_dot

    def block(prob, values, g, row_dot):
        return prob.astype(F32) * (dot(values, g, NT) - row_dot)

    def write_dq(b, acc):
        dq_all[seg_at(b), :] = (jnp.transpose(head_columns(acc, heads)) * DH ** -0.5).astype(BF16)

    def both(pair):
        return [jnp.concatenate([a, b], axis=0 if a.shape[0] > 1 else 1) for a, b in zip(*pair)]

    for j in range(TRUNK // 2):
        q6, g6, row_dot = both([common(2 * j), common(2 * j + 1)])
        fetch(j).wait()
        kept = []
        for i in range(j + 1):
            at = slice(2 * i * SEG, 2 * (i + 1) * SEG)
            prob = probs[TRUNK_FIRST[j] + 2 * i * SEG:TRUNK_FIRST[j] + 2 * (i + 1) * SEG, :]
            score = block(prob, v_ref[at, :], g6, row_dot)
            if i == j:
                bins_acc[0] += score[:SEG, cols:]
                bins_acc[1] += score[:SEG, :cols] + score[SEG:, cols:]
            if i == j - 1:
                bins_acc[0] += score[SEG:, :cols]
            score = score.astype(BF16)
            dv_acc[at, :] += dot(prob, g6, NN)
            dk_acc[at, :] += dot(score, q6, NN)
            kept.append(score)
        acc = dot(kt_ref[:, 0:(j + 1) * 2 * SEG], jnp.concatenate(kept, axis=0), NN)
        for s in range(2):
            write_dq(2 * j + s, acc[:, s * cols:(s + 1) * cols])

    def other_step(step, carry):
        segs = [TRUNK + 2 * step, TRUNK + 2 * step + 1]
        parents = [parent_ref[b] for b in segs]
        leaf = [(parent >= TRUNK).astype(jnp.int32) for parent in parents]
        each = [common(b) for b in segs]
        q6, g6, row_dot = both(each)
        base = TRUNK_FIRST[-1] + step * OTHER_ROWS
        fetch(step + TRUNK // 2).wait()
        kept = []
        for i in range(TRUNK // 2):
            at = slice(2 * i * SEG, 2 * (i + 1) * SEG)
            prob = probs[pl.ds(pl.multiple_of(base + 2 * i * SEG, SEG), 2 * SEG), :]
            score = block(prob, v_ref[at, :], g6, row_dot)
            if i == TRUNK // 2 - 1:
                for s in range(2):
                    bins_acc[0] += jnp.where(leaf[s] == 0, score[SEG:, s * cols:(s + 1) * cols], 0.0)
            score = score.astype(BF16)
            dv_acc[at, :] += dot(prob, g6, NN)
            dk_acc[at, :] += dot(score, q6, NN)
            kept.append(score)
        acc = dot(kt_ref[:, 0:trunk_len], jnp.concatenate(kept, axis=0), NN)
        for s in range(2):
            q3, g3, row = each[s]
            first, second = seg_at(parents[s]), seg_at(segs[s])
            values = jnp.concatenate([v_ref[first, :], v_ref[second, :]], axis=0)
            keys_t = jnp.concatenate([kt_ref[:, first], kt_ref[:, second]], axis=1)
            at = pl.ds(pl.multiple_of(base + trunk_len, SEG), 2 * SEG)
            prob = probs[at, s * cols:(s + 1) * cols]
            score = block(prob, values, g3, row)
            bins_acc[0] += score[:SEG]
            bins_acc[1] += score[SEG:]
            score = score.astype(BF16)
            grad_v, grad_k = dot(prob, g3, NN), dot(score, q3, NN)
            dv_acc[first, :] += grad_v[:SEG]
            dv_acc[second, :] += grad_v[SEG:]
            dk_acc[first, :] += grad_k[:SEG]
            dk_acc[second, :] += grad_k[SEG:]
            write_dq(segs[s], acc[:, s * cols:(s + 1) * cols] + dot(keys_t, score, NN))
        return carry

    lax.fori_loop(0, (SEGS - TRUNK) // 2, other_step, 0)
    for rel, d_ref in enumerate((d0, d1, d2, d3)):
        count = d_ref.shape[0]
        width = heads * DH
        at = pl.ds(pl.multiple_of(jnp.bitwise_xor(me_ref[0], rel) * count, SEG), count)
        parts = [dq_all[at, :][:, :width], dk_acc[at, :][:, :width].astype(BF16), dv_acc[at, :][:, :width].astype(BF16)]
        parts.append(jnp.zeros((count, d_ref.shape[1] - 3 * width), BF16))
        d_ref[...] = jnp.concatenate(parts, axis=1)
    key = lax.broadcasted_iota(jnp.int32, (SEG, cols), 0)
    query = lax.broadcasted_iota(jnp.int32, (SEG, cols), 1) % SEG
    gap = query - key
    parent_sum, own_sum = bins_acc[0], bins_acc[1]
    lines = [jnp.sum(parent_sum + own_sum, axis=0, keepdims=True)]
    for threshold in THRESHOLDS:
        hit = jnp.where(gap + SEG >= threshold, parent_sum, 0.0) + jnp.where(gap >= threshold, own_sum, 0.0)
        lines.append(jnp.sum(hit, axis=0, keepdims=True))
    bins_ref[...] = jnp.concatenate(lines, axis=0)


class Slots:
    def __init__(self, n_expert, capacity):
        self.n_expert = n_expert
        self.cut = n_expert == 8
        self.block = -(-(capacity + SPARE) // 16) * 16
        if self.cut:
            self.groups = [[0, 1, 4, 5], [2, 3, 6, 7]]
            self.rels = [2, 3, 6, 7]
            self.chunks = [[[0, 1, 2, 3]], [[4], [5], [6], [7]]]
        else:
            self.groups = None
            self.chunks = [[list(range(n_expert))]]
        self.arrays = [array for chunk in self.chunks for array in chunk]

    def block_of(self, expert, me):
        if not self.cut:
            return expert
        rel = jnp.bitwise_xor(expert, me)
        inside = lambda index: (index & 1) | ((index >> 1) & 2)
        return jnp.where((rel & 2) == 0, inside(expert), 4 + inside(rel))

    def expert_of(self, block, me):
        if not self.cut:
            return block
        if not isinstance(block, int) or block < 4:
            return (me & 2) | (block & 1) | ((block & 2) << 1)
        return jnp.bitwise_xor(me, self.rels[block - 4])

    def near_exchange(self, block):
        return lax.all_to_all(block, "expert", split_axis=0, concat_axis=0, tiled=True, axis_index_groups=self.groups)


def over_experts(block):
    return lax.all_to_all(block, "expert", split_axis=0, concat_axis=0, tiled=True)


def swap(block, axis, rel):
    if rel == 0:
        return block
    return lax.ppermute(block, axis, [(i, i ^ rel) for i in range(lax.axis_size(axis))])


def swap_all(blocks, axis):
    return [swap(block, axis, rel) for rel, block in enumerate(blocks)]


def from_all(block):
    near, far = swap(block, "shard", 1), swap(block, "shard", 2)
    return [block, near, far, swap(far, "shard", 1)]


def reorder(parts, me):
    bit = 1
    while bit < len(parts):
        parts = [jnp.where(me & bit, parts[i ^ bit], parts[i]) for i in range(len(parts))]
        bit *= 2
    return parts


def send_rows(slots, rows, places_ref, out_refs):
    tokens = places_ref.shape[1]
    for array, out_ref in zip(slots.arrays, out_refs):
        for i, block in enumerate(array):
            slot = block * slots.block + lax.broadcasted_iota(jnp.int32, (slots.block, tokens), 0)
            hit = (slot == places_ref[0:1, :]) | (slot == places_ref[1:2, :])
            picked = dot(jnp.where(hit, 1.0, 0.0).astype(BF16), rows, NN).astype(BF16)
            out_ref[i * slots.block:(i + 1) * slots.block, :] = picked


def row_at(first, count):
    return pl.ds(first if isinstance(first, int) else pl.multiple_of(first, 16), count)


def diagonal(count):
    return lax.broadcasted_iota(jnp.int32, (count, count), 0) == lax.broadcasted_iota(jnp.int32, (count, count), 1)


def padded_row(row, width):
    count = row.shape[1]
    return row if count == width else jnp.concatenate([row, jnp.zeros((1, width - count), row.dtype)], axis=1)


def dispatch_kernel(slots, me_ref, places_ref, others_ref, rows_ref, *refs):
    out_ref = refs[-1]
    tokens = places_ref.shape[1]
    width = rows_ref.shape[1]
    rows = rows_ref[...]
    count = slots.block

    def one(expert, carry):
        slot = slots.block_of(expert, me_ref[0]) * count + lax.broadcasted_iota(jnp.int32, (count, tokens), 0)
        hot = [jnp.where(slot == places_ref[j:j + 1, :], 1.0, 0.0).astype(BF16) for j in range(2)]
        picked = dot(hot[0] + hot[1], rows, NN)
        ids = sum(dot(others_ref[8 * j:8 * j + 8, :], hot[j], NT) for j in range(2))
        line = lax.broadcasted_iota(jnp.int32, picked.shape, 0)
        picked = jnp.where(line == count - 1, padded_row(ids[0:1], width), picked)
        out_ref[pl.ds(pl.multiple_of(expert * count, 16), count), :] = picked.astype(BF16)
        return carry

    lax.fori_loop(0, slots.n_expert, one, 0)


def post_kernel(
    slots, me_ref, x_ref, gain_ref, router_ref, routes_ref, places_ref, m0, m1, m2, m3, w_ref,
    after_ref, normed_ref, gates_ref, *out_refs,
):
    after = x_ref[...].astype(F32)
    for rel, m_ref in enumerate((m0, m1, m2, m3)):
        after = after + dot(m_ref[...], w_ref[jnp.bitwise_xor(me_ref[1], rel)], TN)
    after_ref[...] = after
    unit, _ = rms_parts(after)
    normed = (unit * gain_ref[...]).astype(BF16)
    normed_ref[...] = normed
    send_rows(slots, normed_ref[...], places_ref, out_refs)
    logits = dot(normed, router_ref[...], NN)
    expert = lax.broadcasted_iota(jnp.int32, logits.shape, 1)
    first = jnp.sum(jnp.where(expert == routes_ref[:, 0:1], logits, 0.0), axis=-1, keepdims=True)
    second = jnp.sum(jnp.where(expert == routes_ref[:, 1:2], logits, 0.0), axis=-1, keepdims=True)
    top = jnp.maximum(first, second)
    first, second = jnp.exp(first - top), jnp.exp(second - top)
    gates_ref[...] = jnp.concatenate([first / (first + second), second / (first + second)], axis=1)


def expert_kernel(slots, kind, sizes, before, me_ref, *refs):
    refs = list(refs)
    take = lambda n: [refs.pop(0) for _ in range(n)]
    x_refs = take(sizes[0])
    g_all, router_ref = take(2)
    first_refs, second_refs = take(4), take(4)
    extra = take(before)
    own_ref = extra[1] if before == 3 else None
    (out_all,) = take(1)
    dx_refs = take(sizes[1])
    rows_ref, grad_ref, act_ref, inner_ref, first_buf, second_buf, g_buf, out_buf, out_acc, dx_acc, gate_acc, gates_acc, sem, in_sem = refs
    step = pl.program_id(0)
    slot = lax.rem(step, 2)
    total, width = rows_ref.shape
    depth, units = first_refs[0].shape[0], second_buf.shape[1]

    def fetch(rel, slot):
        column = pl.multiple_of(jnp.bitwise_xor(me_ref[1], rel) * units, 128)
        copies = [pltpu.make_async_copy(second_refs[rel], second_buf.at[slot], in_sem.at[slot, 4])]
        for piece, ref in enumerate(first_refs):
            row = pl.multiple_of(jnp.bitwise_xor(me_ref[1], piece) * depth, 16)
            copies.append(
                pltpu.make_async_copy(
                    ref.at[:, pl.ds(column, units)], first_buf.at[slot, pl.ds(row, depth), :], in_sem.at[slot, piece]
                )
            )
        return copies

    @pl.when(step == 0)
    def _():
        for copy in fetch(0, 0):
            copy.start()

    for rel in range(4):
        @pl.when(step == rel)
        def _(rel=rel):
            if rel < 3:
                for copy in fetch(rel + 1, (rel + 1) % 2):
                    copy.start()
    rows = slots.block
    mine = slots.block_of(me_ref[0], me_ref[0])
    if kind == "own":
        pieces = [(mine, x_refs[0], mine * rows, dx_refs[0], 0)]
    elif kind == "near":
        blocks = [jnp.bitwise_xor(mine, i) for i in (1, 2, 3)]
        pieces = [(block, x_refs[0], block * rows, dx_refs[0], block * rows) for block in blocks]
    elif kind == "far":
        pieces = [(4 + i, x_ref, 0, dx_ref, 0) for i, (x_ref, dx_ref) in enumerate(zip(x_refs, dx_refs))]
    else:
        pieces = [(block, x_refs[0], block * rows, dx_refs[0], block * rows) for block in range(slots.n_expert)]
    pieces = [(*piece, i * rows) for i, piece in enumerate(pieces)]

    def home(block):
        return pl.ds(pl.multiple_of(slots.expert_of(block, me_ref[0]) * rows, 16), rows)

    @pl.when(step == 0)
    def _():
        copies = [
            pltpu.make_async_copy(g_all.at[home(block), :], g_buf.at[pl.ds(first, rows), :], sem.at[i])
            for i, (block, *_, first) in enumerate(pieces)
        ]
        for copy in copies:
            copy.start()
        out_acc[...] = jnp.zeros_like(out_acc)
        dx_acc[...] = jnp.zeros_like(dx_acc)
        for _, x_ref, inside, _, _, first in pieces:
            rows_ref[first:first + rows, :] = x_ref[row_at(inside, rows), :]
        for copy in copies:
            copy.wait()
        for *_, first in pieces:
            at = slice(first, first + rows)
            grads = g_buf[at, :].astype(F32)
            other = jnp.sum(jnp.where(diagonal(rows), grads[rows - 1:, :rows], 0.0), axis=1, keepdims=True).astype(jnp.int32)
            logits = dot(rows_ref[at, :], router_ref[...], NN)
            expert = lax.broadcasted_iota(jnp.int32, logits.shape, 1)
            mine = jnp.sum(jnp.where(expert == me_ref[0], logits, 0.0), axis=-1, keepdims=True)
            its = jnp.sum(jnp.where(expert == other, logits, 0.0), axis=-1, keepdims=True)
            top = jnp.maximum(mine, its)
            mine, its = jnp.exp(mine - top), jnp.exp(its - top)
            line = lax.broadcasted_iota(jnp.int32, grads.shape, 0)
            gate = mine / (mine + its)
            gate_acc[at, :] = jnp.broadcast_to(gate, (rows, 128))
            grad_ref[at, :] = jnp.where(line < rows - SPARE, gate * grads, 0.0).astype(BF16)

    for rel in range(4):
        @pl.when(step == rel)
        def _(rel=rel):
            for copy in fetch(rel, rel % 2):
                copy.wait()

    parts = 1
    while total // parts > 512 or total % parts or (total // parts) % 16:
        parts += 1
    part = total // parts
    for i in range(parts):
        at = slice(i * part, (i + 1) * part)
        first_w, second_w = first_buf[slot], second_buf[slot]
        value = dot(rows_ref[at, :], first_w, NN)
        grad_act = dot(grad_ref[at, :], second_w, NT)
        square = value * value
        half = 0.5 * value
        scale = 0.7978845608028654
        th = jnp.tanh(value * (scale + (scale * 0.044715) * square))
        act = (half + half * th).astype(BF16)
        slope = 0.5 + 0.5 * th + (half * (1.0 - th * th)) * (scale + (3 * scale * 0.044715) * square)
        inner = (grad_act * slope).astype(BF16)
        act_ref[at, :] = act
        inner_ref[at, :] = inner
        out_acc[at, :] += dot(act, second_w, NN)
        dx_acc[at, :] += dot(inner, first_w, NT)

    @pl.when(step == pl.num_programs(0) - 1)
    def _():
        for *_, first in pieces:
            at = slice(first, first + rows)
            out = out_acc[at, :].astype(BF16).astype(F32)
            gates = jnp.sum(out * g_buf[at, :].astype(F32), axis=1, keepdims=True)
            gates_acc[at, :] = jnp.broadcast_to(gates, (rows, 128))
            out_buf[at, :] = (gate_acc[at, 0:1] * out).astype(BF16)
        copies = [
            pltpu.make_async_copy(out_buf.at[pl.ds(first, rows), :], out_all.at[home(block), :], sem.at[i])
            for i, (block, *_, first) in enumerate(pieces)
        ]
        for copy in copies:
            copy.start()
        if own_ref is not None:
            dx_refs[0][row_at(mine * rows, rows), :] = own_ref[...]
        for _, _, _, dx_ref, inside, first in pieces:
            at = slice(first, first + rows)
            gates = gates_acc[at, 0:1]
            gates = jnp.sum(jnp.where(diagonal(rows), gates, 0.0), axis=0, keepdims=True)
            dx_ref[row_at(inside, rows), :] = dx_acc[at, :].astype(BF16)
            tail = dx_acc[first + rows - 16:first + rows, :]
            line = lax.broadcasted_iota(jnp.int32, tail.shape, 0)
            for place in range(SPARE):
                piece = gates.astype(BF16).astype(F32)
                gates = gates - piece
                tail = jnp.where(line == 16 - SPARE + place, padded_row(piece, width), tail)
            dx_ref[row_at(inside + rows - 16, 16), :] = tail.astype(BF16)
        for copy in copies:
            copy.wait()


def run_expert(slots, kind, blocks, dx_shape, shared, before, estimate):
    me, g_all, router, first_w, second_w = shared
    hidden, width = first_w[0].shape[1], router.shape[0]
    total = slots.block * {"own": 1, "near": 3, "far": 4, "all": slots.n_expert}[kind]
    block = hidden // 4
    whole = lambda a: pl.BlockSpec(a.shape, lambda i: (0, 0))
    column = pl.BlockSpec((total, block), lambda i: (0, i))
    rows = pl.BlockSpec((total, width), lambda i: (0, 0))
    fresh = len(before) < 2
    dx = [jax.ShapeDtypeStruct(dx_shape, BF16)] * (4 if kind == "far" else 1)
    inputs = [me, *blocks, g_all, router, *first_w, *second_w, *before]
    before_specs = [ANY] * len(before)
    if len(before) == 3:
        before_specs[1] = whole(before[1])
    return pl.pallas_call(
        functools.partial(expert_kernel, slots, kind, (len(blocks), len(dx)), len(before)),
        grid=(4,),
        in_specs=[SMEM] + [whole(b) for b in blocks] + [ANY, whole(router)] + [ANY] * 8 + before_specs,
        out_specs=[ANY] + [whole(b) for b in dx] + [rows, rows, column, column],
        out_shape=arrays(
            (g_all.shape, BF16), *[(b.shape, BF16) for b in dx], *[((total, width), BF16)] * 2, *[((total, hidden), BF16)] * 2
        ),
        scratch_shapes=[
            pltpu.VMEM((2, width, block), BF16),
            pltpu.VMEM((2, block, width), BF16),
            pltpu.VMEM((total, width), BF16),
            pltpu.VMEM((total, width), BF16),
            pltpu.VMEM((total, width), F32),
            pltpu.VMEM((total, width), F32),
            pltpu.VMEM((total, 128), F32),
            pltpu.VMEM((total, 128), F32),
            pltpu.SemaphoreType.DMA((total // slots.block,)),
            pltpu.SemaphoreType.DMA((2, 5)),
        ],
        input_output_aliases={} if fresh else {len(inputs) - 1: 0},
        compiler_params=params(dimension_semantics=("arbitrary",)),
        cost_estimate=estimate,
    )(*inputs)


def first_grad_kernel(parts, me_ref, *refs):
    send_ref, keep_ref, total = refs[-3:]
    total[...] = sum(dot(x[...], inner[...], TN) for x, inner in zip(refs[:parts], refs[parts:2 * parts]))
    depth = send_ref.shape[0] // 2
    for rel in range(4):
        ref = (keep_ref, send_ref)[rel % 2]
        row = pl.multiple_of(jnp.bitwise_xor(me_ref[1], rel) * depth, 16)
        at = rel // 2 * depth
        ref[at:at + depth, :] = total[pl.ds(row, depth), :].astype(BF16)


def run_first_grad(me, rows, inners, depth, *after):
    width, hidden = rows[0].shape[1], inners[0].shape[1]
    block = hidden // 4
    column = pl.BlockSpec((2 * depth, block), lambda i, me_ref: (0, jnp.bitwise_xor(me_ref[1], i)))
    return pl.pallas_call(
        functools.partial(first_grad_kernel, len(rows)),
        grid_spec=pltpu.PrefetchScalarGridSpec(
            num_scalar_prefetch=1,
            grid=(4,),
            in_specs=[pl.BlockSpec(a.shape, lambda i, me_ref: (0, 0)) for a in rows]
            + [pl.BlockSpec((a.shape[0], block), lambda i, me_ref: (0, i)) for a in inners]
            + [ANY] * len(after),
            out_specs=[column, column],
            scratch_shapes=[pltpu.VMEM((width, block), F32)],
        ),
        out_shape=arrays(*[((2 * depth, hidden), BF16)] * 2),
        compiler_params=params(dimension_semantics=("arbitrary",)),
        cost_estimate=SHORT,
    )(me, *rows, *inners, *after)


def second_grad_kernel(parts, *refs):
    send_ref, keep_ref = refs[2 * parts:]
    step = pl.program_id(0)
    block = sum(dot(act[...], g[...], TN) for act, g in zip(refs[:parts], refs[parts:2 * parts])).astype(BF16)

    @pl.when(step < 2)
    def _():
        send_ref[...] = block

    @pl.when(step >= 2)
    def _():
        keep_ref[...] = block


def run_second_grad(acts, grads):
    width, hidden = grads[0].shape[1], acts[0].shape[1]
    block = hidden // 4
    return pl.pallas_call(
        functools.partial(second_grad_kernel, len(acts)),
        grid=(4,),
        in_specs=[pl.BlockSpec((a.shape[0], block), lambda i: (0, 2 * (i % 2) + 1 - i // 2)) for a in acts]
        + [pl.BlockSpec(a.shape, lambda i: (0, 0)) for a in grads],
        out_specs=[
            pl.BlockSpec((block, width), lambda i: (jnp.minimum(i, 1), 0)),
            pl.BlockSpec((block, width), lambda i: (jnp.maximum(i - 2, 0), 0)),
        ],
        out_shape=arrays(*[((2 * block, width), BF16)] * 2),
        compiler_params=params(dimension_semantics=("arbitrary",)),
        cost_estimate=SHORT,
    )(*acts, *grads)


def core_sum(send, keep):
    near = swap(send, "shard", 1)
    half = keep.shape[0] // 2
    other = (keep[half:].astype(F32) + near[half:].astype(F32)).astype(BF16)
    return keep, near, other


def across_sum(parts):
    keep, near, other = parts
    return keep, near, swap(other, "shard", 2)


def total_sum(parts):
    keep, near, far = parts
    half = keep.shape[0] // 2
    return keep[:half].astype(F32) + near[:half].astype(F32) + far.astype(F32)


def gather_blocks(slots, refs, scratch):
    for array, ref in zip(slots.arrays, refs):
        scratch[array[0] * slots.block:(array[-1] + 1) * slots.block, :] = ref[...]


def back_kernel(slots, me_ref, *refs):
    refs_left = list(refs)
    take = lambda n: [refs_left.pop(0) for _ in range(n)]
    ret_refs = take(len(slots.arrays))
    places_ref, routes_ref, gates_ref, after_ref, gain_ref, router_ref, g_ref = take(7)
    w_ref, normed_ref = take(2)
    m_refs = take(4)
    (grad_after_ref,) = take(1)
    mixed_refs = take(4)
    send_ref, keep_ref, branch_ref, glogits_ref, ggain_ref, more, scratch = refs_left
    tokens = after_ref.shape[0]
    part = tokens // 2
    gather_blocks(slots, ret_refs, scratch)
    pieces = []
    for end in range(slots.block, scratch.shape[0] + 1, slots.block):
        tail = scratch[end - 16:end, :].astype(F32)[16 - SPARE:, :slots.block]
        pieces.append(jnp.sum(tail, axis=0, keepdims=True))
    gg = jnp.concatenate(pieces, axis=1)
    ggain_ref[...] = jnp.zeros_like(ggain_ref)

    def one(i, carry):
        at = pl.ds(pl.multiple_of(i * part, part), part)
        slot = lax.broadcasted_iota(jnp.int32, (part, gg.shape[1]), 1)
        hit0, hit1 = slot == places_ref[at, 0:1], slot == places_ref[at, 1:2]
        gg0 = jnp.sum(jnp.where(hit0, gg, 0.0), axis=-1, keepdims=True)
        gg1 = jnp.sum(jnp.where(hit1, gg, 0.0), axis=-1, keepdims=True)
        total = dot(jnp.where(hit0 | hit1, 1.0, 0.0).astype(BF16), scratch[...], NN)
        gate0, gate1 = gates_ref[at, 0:1], gates_ref[at, 1:2]
        mean = gate0 * gg0 + gate1 * gg1
        expert = lax.broadcasted_iota(jnp.int32, (part, router_ref.shape[1]), 1)
        glogits = jnp.where(expert == routes_ref[at, 0:1], gate0 * (gg0 - mean), 0.0) + jnp.where(
            expert == routes_ref[at, 1:2], gate1 * (gg1 - mean), 0.0
        )
        glogits = glogits.astype(BF16)
        glogits_ref[at, :] = glogits
        incoming = dot(glogits, router_ref[...], NT) + total
        unit, factor = rms_parts(after_ref[at, :])
        grad_after = g_ref[at, :].astype(F32) + rms_grad(incoming, gain_ref[...], unit, factor)
        ggain_ref[0:1, :] += jnp.sum(incoming * unit, axis=0, keepdims=True)
        grad_after_ref[at, :] = grad_after
        branch = grad_after.astype(BF16)
        branch_ref[at, :] = branch
        return carry

    lax.fori_loop(0, tokens // part, one, 0)
    for rel, mixed_ref in enumerate(mixed_refs):
        mixed_ref[...] = dot(w_ref[jnp.bitwise_xor(me_ref[0], rel)], branch_ref[...], NT).astype(BF16)
    width = branch_ref.shape[1]
    grad_router = dot(normed_ref[...], glogits_ref[...], TN)
    gain = jnp.transpose(jnp.concatenate([ggain_ref[...]] * 16, axis=0))[:, 0:1]
    blank = jnp.zeros((width, more.shape[1] - grad_router.shape[1] - 1), F32)
    more[...] = jnp.concatenate([grad_router, gain, blank], axis=1)
    for rel, m_ref in enumerate(m_refs):
        ref = (keep_ref, send_ref)[rel % 2]
        count = m_ref.shape[0]
        at = slice(rel // 2 * count, (rel // 2 + 1) * count)
        ref[at, 0:width] = dot(m_ref[...], branch_ref[...], NN).astype(BF16)
        row = pl.multiple_of(jnp.bitwise_xor(me_ref[0], rel) * count, 16)
        ref[at, width:] = more[pl.ds(row, count), :].astype(BF16)


def combine_kernel(slots, me_ref, ret_ref, places_ref, after_ref, out_ref, scratch):
    part = after_ref.shape[0] // 2
    for block in range(slots.n_expert):
        first = pl.multiple_of(slots.expert_of(block, me_ref[0]) * slots.block, 16)
        scratch[block * slots.block:(block + 1) * slots.block, :] = ret_ref[pl.ds(first, slots.block), :]

    def one(i, carry):
        at = pl.ds(pl.multiple_of(i * part, part), part)
        slot = lax.broadcasted_iota(jnp.int32, (part, scratch.shape[0]), 1)
        hit = (slot == places_ref[at, 0:1]) | (slot == places_ref[at, 1:2])
        total = after_ref[at, :] + dot(jnp.where(hit, 1.0, 0.0).astype(BF16), scratch[...], NN)
        out_ref[at, :] = total.astype(BF16)
        return carry

    lax.fori_loop(0, after_ref.shape[0] // part, one, 0)


def final_kernel(me_ref, x_ref, gain_ref, after_ref, d0, d1, d2, d3, w_ref, out_ref):
    grad = sum(
        dot(d_ref[...], w_ref[jnp.bitwise_xor(me_ref[0], rel)], NT) for rel, d_ref in enumerate((d0, d1, d2, d3))
    )
    unit, factor = rms_parts(x_ref[...].astype(F32))
    out_ref[...] = (after_ref[...] + rms_grad(grad, gain_ref[...], unit, factor)).astype(BF16)


def column_grad_kernel(
    orders, heads, me_ref, bins_ref, n_ref, d0, d1, d2, d3, wk_ref, wn_ref, wf_ref, *refs
):
    *out_refs, acc, more = refs
    acc[...] = sum(dot(n_ref[rel], d_ref[...], TN) for rel, d_ref in enumerate((d0, d1, d2, d3)))
    rows = wf_ref.shape[0]
    more[...] = wk_ref[0:rows, :].astype(F32) + wn_ref[0:rows, :].astype(F32) + wf_ref[...].astype(F32)
    cols = 3 * heads * DH
    wide = acc.shape[1]
    lane = lax.broadcasted_iota(jnp.int32, (NB, wide), 1)
    table = jnp.zeros((NB, wide), F32)
    for h in range(heads):
        above = jnp.sum(bins_ref[:, h * SEG:(h + 1) * SEG], axis=1, keepdims=True)
        column = above - jnp.concatenate([above[1:], jnp.zeros((1, 1), F32)], axis=0)
        column = jnp.concatenate([column[:-1], -jnp.sum(column[:-1], axis=0, keepdims=True)], axis=0)
        table = jnp.where(lane == cols + h, column, table)
    share = rows // len(orders[0])
    half = share // 2

    def block_of(rel):
        first = jnp.bitwise_xor(me_ref[0], rel) * share
        at = lambda start: pl.ds(pl.multiple_of(start + first, 8), share)
        block = [acc[at(p * rows), :] for p in range(4)]
        block[0] = jnp.concatenate([block[0][:NB] + table, block[0][NB:]], axis=0)
        others = more[at(0), :]
        rest = others[:, wide:]
        folded = [rest[:half], rest[half:], jnp.zeros((half, wide - 2 * rest.shape[1]), F32)]
        block += [others[:, :wide], jnp.concatenate(folded, axis=1)]
        if half % 8:
            block.append(jnp.zeros((-half % 8, wide), F32))
        return block[:3], block[3:]

    blocks = {rel: block_of(rel) for rel in orders[0]}
    count = len(out_refs) // 2
    for part, order in enumerate(orders):
        for i in range(count):
            mine = order[i * len(order) // count:(i + 1) * len(order) // count]
            rows_of = [row for rel in mine for row in blocks[rel][part]]
            out_refs[part * count + i][...] = jnp.concatenate(rows_of, axis=0).astype(BF16)


def split_kernel(me_ref, *refs):
    *in_refs, b0, b1, b2, b3, more_ref, table_ref, total = refs
    share, cols = b0.shape
    count = len(in_refs) // 2
    total[0:3 * share, :] = sum(ref[...].astype(F32) for ref in in_refs[:count])
    total[3 * share:, :] = sum(ref[...].astype(F32) for ref in in_refs[count:])
    wide = total.shape[1]
    for rel, ref in enumerate((b0, b1, b2, b3)):
        at = pl.ds(pl.multiple_of(jnp.bitwise_xor(me_ref[0], rel) * share, 8), share)
        ref[...] = total[at, :][:, :cols].astype(BF16)
    folded = total[5 * share:5 * share + share // 2, :]
    rest = more_ref.shape[1] - wide
    folded = jnp.concatenate([folded[:, :rest], folded[:, rest:2 * rest]], axis=0)
    more_ref[...] = jnp.concatenate([total[4 * share:5 * share, :], folded], axis=1).astype(BF16)
    table_ref[...] = total[0:NB, wide - table_ref.shape[1]:]


def join_kernel(me_ref, p0, p1, p2, p3, more_ref, out_ref):
    parts = [ref[...] for ref in (p0, p1, p2, p3)]
    for bit in (1, 2):
        swapped = (me_ref[0] & bit) != 0
        parts = [jnp.where(swapped, parts[i ^ bit], parts[i]) for i in range(4)]
    hw = p0.shape[1] // 3
    out_ref[...] = jnp.concatenate(
        [part[:, c * hw:(c + 1) * hw] for c in range(3) for part in parts] + [more_ref[...]], axis=1
    )


def place_kernel(experts, me_ref, wq_ref, wk_ref, wv_ref, gain_in_ref, *refs):
    *piece_refs, q_ref, k_ref, v_ref, o_ref, router_ref, gains_ref, more = refs
    width = q_ref.shape[1]
    count = piece_refs[0].shape[0] // (2 if len(piece_refs) > 1 else 1)
    for rel, at_row, piece_ref in [
        (rel | (first // count) * 4, first, ref) for rel, ref in enumerate(piece_refs) for first in range(0, ref.shape[0], count)
    ]:
        at = pl.ds(pl.multiple_of(jnp.bitwise_xor(me_ref[0], rel) * count, 8), count)
        piece = piece_ref[at_row:at_row + count, :].astype(F32)
        for c, out_ref in enumerate((q_ref, k_ref, v_ref, o_ref)):
            out_ref[at, :] = piece[:, c * width:(c + 1) * width]
        more[at, :] = piece[:, 4 * width:]
    total = sum(
        w_ref[...].astype(F32) * out_ref[...] for w_ref, out_ref in ((wq_ref, q_ref), (wk_ref, k_ref), (wv_ref, v_ref))
    )
    rows = total.shape[0]
    lane = lax.broadcasted_iota(jnp.int32, more.shape, 1)
    columns = jnp.where(lane == experts + 1, jnp.sum(total, axis=1, keepdims=True), more[...])
    columns = jnp.concatenate([columns, jnp.zeros((-rows % 128, columns.shape[1]), F32)], axis=0)
    columns = jnp.transpose(columns)[:, :rows]
    router_ref[...] = columns[0:experts]
    gains_ref[0:1, :] = columns[experts + 1:experts + 2] / gain_in_ref[...]
    gains_ref[1:2, :] = columns[experts:experts + 1]


def per_device(
    tokens, gain_attn, w_query, w_key, w_value, w_output, rel_table, gain_moe, router,
    w_in, w_out, routes, parents, cotangent,
):
    n_shard = lax.axis_size("shard")
    n_expert = lax.axis_size("expert")
    tok, width = tokens.shape
    tree_len = tok * n_shard
    n_experts = router.shape[1]
    heads = rel_table.shape[0]
    hw = heads * DH
    wide = -(-3 * hw // 128) * 128
    rows = width // n_shard
    slots = Slots(n_expert, max(2, tok * 20 // (7 * n_experts)))
    me_s, me_e = lax.axis_index("shard").astype(jnp.int32), lax.axis_index("expert").astype(jnp.int32)
    me_shard, me_expert, me = me_s.reshape(1), me_e.reshape(1), jnp.stack([me_e, me_s])

    more = jnp.concatenate([gain_attn[:, None], gain_moe[:, None], router], axis=1)
    w_rel = pl.pallas_call(
        columns_kernel,
        in_specs=[SMEM] + [VMEM] * 4,
        out_specs=[VMEM] * n_shard,
        out_shape=arrays(*[((rows, -(-(3 * hw + 2 + n_experts) // 128) * 128), BF16)] * n_shard),
        compiler_params=params(),
        cost_estimate=SHORT,
    )(me_shard, w_query, w_key, w_value, more)
    near_tokens, far_tokens = swap(tokens, "shard", 1), swap(tokens, "shard", 2)
    w_pieces = swap_all(w_rel, "shard")

    expert_range = jnp.arange(n_experts, dtype=jnp.int32)
    flat_routes = routes.reshape(-1)
    expert_hot = (flat_routes[:, None] == expert_range[None, :]).astype(jnp.int32)
    earlier = jnp.cumsum(expert_hot, axis=0) - expert_hot
    rank = jnp.sum(earlier * expert_hot, axis=-1)
    places = (slots.block_of(flat_routes, me_e) * slots.block + rank).reshape(tok, 2)
    places_row = places.T
    others = jnp.repeat(routes.T[::-1], 8, axis=0).astype(BF16)
    block_shapes = [((len(array) * slots.block, width), BF16) for array in slots.arrays]

    sent_grads = pl.pallas_call(
        functools.partial(dispatch_kernel, slots),
        in_specs=[SMEM] + [VMEM] * 3 + [ANY],
        out_specs=VMEM,
        out_shape=jax.ShapeDtypeStruct((n_expert * slots.block, width), BF16),
        compiler_params=params(),
        cost_estimate=SHORT,
    )(me_expert, places_row, others, cotangent, w_rel[0])
    got_grads = over_experts(sent_grads)
    far_tokens, _, w_pieces = lax.optimization_barrier((far_tokens, sent_grads, w_pieces))
    tree = [tokens, near_tokens, far_tokens, swap(far_tokens, "shard", 1)]

    place = lambda i, me_ref: (jnp.bitwise_xor(me_ref[0], i), 0)
    place_t = lambda i, me_ref: (0, jnp.bitwise_xor(me_ref[0], i))
    fixed = [
        ((width, wide), BF16), ((4, SEG, heads * SEG), F32), *[((1, width), F32)] * 2, ((width, n_experts), BF16),
    ]
    normed_one, queries, keys, values, keys_t, values_t, w_cols, bias, gain_one, gain_two, router_w = pl.pallas_call(
        functools.partial(project_kernel, heads),
        grid_spec=pltpu.PrefetchScalarGridSpec(
            num_scalar_prefetch=1,
            grid=(n_shard,),
            in_specs=[SMEM] + [VMEM] * 8 + [ANY],
            out_specs=[pl.BlockSpec((1, tok, width), lambda i, me_ref: (i, 0, 0))]
            + [pl.BlockSpec((tok, HW), place)] * 3
            + [pl.BlockSpec((HW, tok), place_t)] * 2
            + [pl.BlockSpec(shape, lambda i, me_ref, shape=shape: (0,) * len(shape)) for shape, _ in fixed],
            scratch_shapes=[pltpu.VMEM((width, 3 * HW + 128), BF16)],
        ),
        out_shape=arrays(
            ((n_shard, tok, width), BF16), *[((tree_len, HW), BF16)] * 3, *[((HW, tree_len), BF16)] * 2, *fixed
        ),
        compiler_params=params(dimension_semantics=("arbitrary",)),
        cost_estimate=SHORT,
    )(me_shard, rel_table.astype(F32), *w_pieces, *tree, sent_grads)
    parent_row = parents[0]
    *mixed, raw, lse = pl.pallas_call(
        functools.partial(attn_forward_kernel, heads),
        in_specs=[SMEM] * 2 + [VMEM] * 5,
        out_specs=[VMEM] * 6,
        out_shape=arrays(*[((hw, tok), BF16)] * 4, ((HW, tree_len), F32), ((SEGS * 8, heads * SEG), F32)),
        scratch_shapes=[pltpu.VMEM((HW, tree_len), BF16)],
        compiler_params=params(),
        cost_estimate=FORWARD,
    )(me_shard, parent_row, queries, keys, values, values_t, bias)
    first_far = swap(w_in[0], "shard", 2)
    w_o = lax.all_gather(w_output, "shard", axis=0)
    mixed, first_far, w_o = lax.optimization_barrier((mixed, first_far, w_o))
    mixed = swap_all(mixed, "shard")
    first_w = [w_in[0], swap(w_in[0], "shard", 1), first_far, swap(first_far, "shard", 1)]
    second_near = swap(w_out[0], "shard", 1)
    w_out, w_cols, _ = lax.optimization_barrier((w_out, w_cols, mixed))
    second_far = swap(w_out[0], "shard", 2)
    mixed, first_w, second_near = lax.optimization_barrier((mixed, first_w, second_near))

    after, normed_two, gates, *sent_rows = pl.pallas_call(
        functools.partial(post_kernel, slots),
        in_specs=[SMEM] + [VMEM] * 10,
        out_specs=[VMEM] * (3 + len(block_shapes)),
        out_shape=arrays(((tok, width), F32), ((tok, width), BF16), ((tok, 2), F32), *block_shapes),
        compiler_params=params(),
        cost_estimate=SHORT,
    )(me, tokens, gain_two, router_w, routes, places_row, *mixed, w_o)

    probs = pl.pallas_call(
        functools.partial(attn_prob_kernel, heads),
        in_specs=[SMEM] + [VMEM] * 4 + [ANY],
        out_specs=VMEM,
        out_shape=jax.ShapeDtypeStruct((PROB_ROWS, 2 * heads * SEG), BF16),
        compiler_params=params(),
        cost_estimate=SHORT,
    )(parent_row, queries, keys, lse, bias, after)

    second_far, probs = lax.optimization_barrier((second_far, probs))
    second_w = [w_out[0], second_near, second_far, swap(second_far, "shard", 1)]
    run = functools.partial(run_expert, slots)
    shared = (me, got_grads, router_w, first_w, second_w)
    near_rows = slots.near_exchange(sent_rows[0])
    if slots.cut:
        far_shape = sent_rows[1].shape
        out_all, own_dx, *own_kept = run("own", sent_rows[:1], far_shape, shared, [probs], SHORT)
        far_rows, probs = lax.optimization_barrier((sent_rows[1:], probs))
        far_rows = [swap(block, "expert", rel) for block, rel in zip(far_rows, slots.rels)]
        out_all, near_dx, *near_kept = run("near", [near_rows], near_rows.shape, shared, [probs, own_dx, out_all], SHORT)
        out_all, *far = run("far", far_rows, far_shape, shared, [probs, out_all], LONG)
        dx = [slots.near_exchange(near_dx)] + [swap(block, "expert", rel) for block, rel in zip(far, slots.rels)]
        kept = [own_kept, near_kept, far[4:]]
    else:
        out_all, dx, *all_kept = run("all", [near_rows], near_rows.shape, shared, [probs], SHORT)
        dx, kept = [slots.near_exchange(dx)], [all_kept]
    send_second, keep_second = run_second_grad([k[2] for k in kept], [k[1] for k in kept])
    w_cols, _ = lax.optimization_barrier((w_cols, kept[0][0]))
    w_all = lax.all_gather(w_cols, "shard", axis=0)
    send_first, keep_first = run_first_grad(me, [k[0] for k in kept], [k[3] for k in kept], rows, dx[0], w_all)
    out_all, _ = lax.optimization_barrier((out_all, dx[0]))
    returned = over_experts(out_all)
    dx, send_first, send_second = lax.optimization_barrier((dx, send_first, send_second))

    slot_rows = slots.n_expert * slots.block
    grad_after, gm0, gm1, gm2, gm3, send_wo, keep_wo = pl.pallas_call(
        functools.partial(back_kernel, slots),
        in_specs=[SMEM] + [VMEM] * (len(block_shapes) + 13),
        out_specs=[VMEM] * 7,
        out_shape=arrays(((tok, width), F32), *[((hw, tok), BF16)] * 4, *[((2 * rows, width + 128), BF16)] * 2),
        scratch_shapes=[
            pltpu.VMEM((tok, width), BF16),
            pltpu.VMEM((tok, n_experts), BF16),
            pltpu.VMEM((8, width), F32),
            pltpu.VMEM((width, 128), F32),
            pltpu.VMEM((slot_rows, width), BF16),
        ],
        compiler_params=params(),
        cost_estimate=SHORT,
    )(me_shard, *dx, places, routes, gates, after, gain_two, router_w, cotangent, w_o, normed_two, *mixed)
    grad_mixed = swap_all([gm0, gm1, gm2, gm3], "shard")
    sums = [
        core_sum(send, keep)
        for send, keep in ((send_second, keep_second), (send_first, keep_first), (send_wo, keep_wo))
    ]
    grad_mixed, sums = lax.optimization_barrier((grad_mixed, sums))
    second_sum, first_sum, wo_sum = sums
    second_sum, wo_sum = across_sum(second_sum), across_sum(wo_sum)

    *dqkv, bins = pl.pallas_call(
        functools.partial(attn_backward_kernel, heads),
        in_specs=[SMEM] * 2 + [VMEM] * 5 + [ANY] + [VMEM] * 4,
        out_specs=[VMEM] * 5,
        out_shape=arrays(*[((tok, wide), BF16)] * 4, ((NB, heads * SEG), F32)),
        scratch_shapes=[
            pltpu.VMEM((HW, tree_len), BF16),
            pltpu.VMEM((tree_len, HW), BF16),
            pltpu.VMEM((tree_len, HW), F32),
            pltpu.VMEM((tree_len, HW), F32),
            pltpu.VMEM((2, SEG, heads * SEG), F32),
            pltpu.VMEM((PROB_ROWS, 2 * heads * SEG), BF16),
            pltpu.SemaphoreType.DMA((SEGS // 2,)),
        ],
        compiler_params=params(),
        cost_estimate=BACKWARD,
    )(me_shard, parent_row, queries, keys, values, keys_t, raw, probs, *grad_mixed)
    dqkv_own = swap_all(dqkv, "shard")

    halving = [(1, 2, 4), (2, 1, 4)] if n_expert == 8 else []
    orders = [[0], [0]]
    for i, bits in enumerate(halving):
        for bit in reversed(bits):
            orders[i] = orders[i] + [rel | bit for rel in orders[i]]
    share = rows // len(orders[0])
    block_rows = [3 * share, 2 * share + -(-share // 16) * 8]
    parts = 2 if halving else 1
    out_rows = [count * len(orders[0]) // parts for count in block_rows for _ in range(parts)]
    halves = pl.pallas_call(
        functools.partial(column_grad_kernel, orders, heads),
        in_specs=[SMEM] + [VMEM] * 9,
        out_specs=[VMEM] * len(out_rows),
        out_shape=arrays(*[((count, wide), BF16) for count in out_rows]),
        scratch_shapes=[pltpu.VMEM((width, wide), F32), pltpu.VMEM((rows, width + 128), F32)],
        compiler_params=params(),
        cost_estimate=SHORT,
    )(me_expert if halving else jnp.zeros((1,), jnp.int32), bins, normed_one, *dqkv, *wo_sum)
    if halving:
        pairs = [halves[:2], halves[2:]]
        pairs, second_sum, returned = lax.optimization_barrier((pairs, second_sum, returned))
        for step in range(2):
            sums = [kept.astype(F32) + swap(sent, "expert", bits[step]).astype(F32) for (kept, sent), bits in zip(pairs, halving)]
            pairs = [jnp.split(part.astype(BF16), 2, axis=0) for part in sums]
        sums = [part for kept, sent in pairs for part in (kept, swap(sent, "expert", 4))]
    else:
        sums = lax.psum([part.astype(F32) for part in halves], "expert")
    *cols, more, table = pl.pallas_call(
        split_kernel,
        in_specs=[SMEM] + [VMEM] * len(sums),
        out_specs=[VMEM] * 6,
        out_shape=arrays(*[((share, 3 * hw), BF16)] * 4, ((share, width + 128), BF16), ((NB, wide - 3 * hw), F32)),
        scratch_shapes=[pltpu.VMEM((sum(block_rows), wide), F32)],
        compiler_params=params(),
        cost_estimate=SHORT,
    )(me_shard, *sums)
    table = table[:, :heads].T
    cols, dqkv_own = lax.optimization_barrier((cols, dqkv_own))
    cols, first_sum = lax.optimization_barrier((swap_all(cols, "shard"), first_sum))
    cols = pl.pallas_call(
        join_kernel,
        in_specs=[SMEM] + [VMEM] * 5,
        out_specs=VMEM,
        out_shape=jax.ShapeDtypeStruct((share, 4 * width + 128), BF16),
        compiler_params=params(),
        cost_estimate=SHORT,
    )(me_shard, *cols, more)
    grad_w_in = total_sum(across_sum(first_sum))[None]
    returned, second_sum, _ = lax.optimization_barrier((returned, second_sum, cols))
    grad_w_out = total_sum(second_sum)[None]
    output = pl.pallas_call(
        functools.partial(combine_kernel, slots),
        in_specs=[SMEM] + [VMEM] * 3,
        out_specs=VMEM,
        out_shape=jax.ShapeDtypeStruct((tok, width), BF16),
        scratch_shapes=[pltpu.VMEM((slot_rows, width), BF16)],
        compiler_params=params(),
        cost_estimate=SHORT,
    )(me_expert, returned, places, after)
    pieces = [cols]
    if halving:
        other = swap(cols, "expert", 4)
        dqkv_own, other = lax.optimization_barrier((dqkv_own, other))
        pieces = swap_all([jnp.concatenate([cols, other], axis=0)] * 4, "expert")
    grad_tokens = pl.pallas_call(
        final_kernel,
        in_specs=[SMEM] + [VMEM] * 8,
        out_specs=VMEM,
        out_shape=jax.ShapeDtypeStruct((tok, width), BF16),
        compiler_params=params(),
        cost_estimate=SHORT,
    )(me_shard, tokens, gain_one, grad_after, *dqkv_own, w_all)
    pieces, output, grad_tokens, grad_w_in, grad_w_out = lax.optimization_barrier(
        (pieces, output, grad_tokens, grad_w_in, grad_w_out)
    )
    grad_q, grad_k, grad_v, grad_wo, grad_router, grad_gains = pl.pallas_call(
        functools.partial(place_kernel, n_experts),
        in_specs=[SMEM] + [VMEM] * (4 + len(pieces)),
        out_specs=[VMEM] * 6,
        out_shape=arrays(*[((rows, width), F32)] * 4, ((n_experts, rows), F32), ((2, rows), F32)),
        scratch_shapes=[pltpu.VMEM((rows, 128), F32)],
        compiler_params=params(),
        cost_estimate=SHORT,
    )(
        me_expert if halving else jnp.zeros((1,), jnp.int32), w_query, w_key, w_value,
        gain_attn.astype(F32).reshape(1, rows), *pieces,
    )

    return (
        output, grad_tokens, grad_gains[0], grad_q, grad_k, grad_v, grad_wo, table, grad_gains[1], grad_router.T,
        grad_w_in, grad_w_out,
    )


def solution(mesh):
    both, shard = P(("expert", "shard"), None), P("shard", None)
    three = P("expert", "shard", None)
    return jax.shard_map(
        per_device,
        mesh=mesh,
        in_specs=(
            both, P("shard"), shard, shard, shard, shard, shard, P("shard"), shard, three, three, both,
            P("expert", None), both,
        ),
        out_specs=(both, both, P("shard"), shard, shard, shard, shard, shard, P("shard"), shard, three, three),
        check_vma=False,
    )
```

```python
import functools
import math

import jax
import jax.numpy as jnp
from jax import lax
from jax.experimental import pallas as pl
from jax.experimental.pallas import tpu as pltpu
from jax.sharding import PartitionSpec as P

DH = 64
NB = 16
SEG = 128
SEGS = 20
TRUNK = 8
SPARE = 3

THRESHOLDS = (1, 2, 3, 4, 5, 6, 7, 8, 12, 16, 24, 32, 48, 64, 96)
EPS = 1e-06
MASKED = -1e30
HW = 256

F32 = jnp.float32
BF16 = jnp.bfloat16
VMEM = pl.BlockSpec(memory_space=pltpu.VMEM)
SMEM = pl.BlockSpec(memory_space=pltpu.SMEM)
ANY = pl.BlockSpec(memory_space=pl.ANY)

NN = ((1,), (0,))
NT = ((1,), (1,))
TN = ((0,), (0,))


def params(mib=60, **more):
    return pltpu.CompilerParams(vmem_limit_bytes=mib << 20, **more)


SHORT = pl.CostEstimate(flops=0, bytes_accessed=1024, transcendentals=0)
LONG = pl.CostEstimate(flops=1 << 40, bytes_accessed=1 << 32, transcendentals=0)


FORWARD = pl.CostEstimate(flops=30_400_000_000, bytes_accessed=1024, transcendentals=0)
BACKWARD = pl.CostEstimate(flops=22_000_000_000, bytes_accessed=1024, transcendentals=0)


def dot(left, right, contract):
    return lax.dot_general(left, right, (contract, ((), ())), preferred_element_type=F32)


def arrays(*shapes):
    return [jax.ShapeDtypeStruct(shape, dtype) for shape, dtype in shapes]


def rms_parts(values):
    factor = lax.rsqrt(jnp.mean(values * values, axis=-1, keepdims=True) + EPS)
    return values * factor, factor


def rms_grad(grad_out, gain_row, unit_rows, factor):
    scaled = grad_out * gain_row
    return factor * (scaled - unit_rows * jnp.mean(scaled * unit_rows, axis=-1, keepdims=True))


def columns_kernel(me_ref, q_ref, k_ref, v_ref, more_ref, *out_refs):
    groups = len(out_refs)
    depth, width = out_refs[0].shape
    hw = q_ref.shape[1] // groups
    blocks = [
        jnp.concatenate([ref[:, s * hw:(s + 1) * hw] for ref in (q_ref, k_ref, v_ref)], axis=1) for s in range(groups)
    ]
    more = jnp.concatenate(
        [more_ref[...], jnp.zeros((depth, width - 3 * hw - more_ref.shape[1]), BF16)], axis=1
    )
    for bit in (1, 2):
        swapped = (me_ref[0] & bit) != 0
        blocks = [jnp.where(swapped, blocks[i ^ bit], blocks[i]) for i in range(groups)]
    for block, out_ref in zip(blocks, out_refs):
        out_ref[...] = jnp.concatenate([block, more], axis=1)


def project_kernel(
    heads, me_ref, table_ref, w0, w1, w2, w3, t0, t1, t2, t3, before_ref,
    n_ref, q_ref, k_ref, v_ref, kt_ref, vt_ref, w_ref, bias_ref, gain_ref, gain_two_ref, router_ref, w_pad,
):
    step = pl.program_id(0)

    @pl.when(step == 0)
    def _():
        hw = heads * DH
        blank = jnp.zeros((w0.shape[0], HW - hw), BF16)
        for rel, piece_ref in enumerate((w0, w1, w2, w3)):
            depth = piece_ref.shape[0]
            at = pl.ds(pl.multiple_of(jnp.bitwise_xor(me_ref[0], rel) * depth, 16), depth)
            piece = piece_ref[...]
            blank_end = jnp.zeros((depth, w_ref.shape[1] - 3 * hw), BF16)
            w_ref[at, :] = jnp.concatenate([piece[:, :3 * hw], blank_end], axis=1)
            router_ref[at, :] = piece[:, 3 * hw + 2:3 * hw + 2 + router_ref.shape[1]]
            padded = [part for c in range(3) for part in (piece[:, c * hw:(c + 1) * hw], blank)]
            padded.append(piece[:, 3 * hw:3 * hw + 2])
            padded.append(jnp.zeros((depth, w_pad.shape[1] - 3 * HW - 2), BF16))
            w_pad[at, :] = jnp.concatenate(padded, axis=1)
        gains = jnp.transpose(w_pad[:, 3 * HW:].astype(F32))
        gain_ref[...] = gains[0:1]
        gain_two_ref[...] = gains[1:2]
        key = lax.broadcasted_iota(jnp.int32, (SEG, SEG), 0)
        query = lax.broadcasted_iota(jnp.int32, (SEG, SEG), 1)
        bias_ref[0] = jnp.zeros((SEG, heads * SEG), F32)
        bias_ref[3] = jnp.full((SEG, heads * SEG), MASKED, F32)
        for h in range(heads):
            last = table_ref[h, NB - 1]
            at = slice(h * SEG, (h + 1) * SEG)
            for kind, gap in ((1, query - key + SEG), (2, query - key)):
                tile = jnp.zeros((SEG, SEG), F32) + (table_ref[h, 0] - last)
                for i, threshold in enumerate(THRESHOLDS):
                    tile = jnp.where(gap >= threshold, table_ref[h, i + 1] - last, tile)
                bias_ref[kind, :, at] = jnp.where(gap >= 0, tile, MASKED)

    for rel, t_ref in enumerate((t0, t1, t2, t3)):
        @pl.when(step == rel)
        def _(t_ref=t_ref):
            unit, _ = rms_parts(t_ref[...].astype(F32))
            normed = (unit * gain_ref[...]).astype(BF16)
            n_ref[0] = normed
            qkv = dot(normed, w_pad[:, :3 * HW], NN)
            q_ref[...] = qkv[:, :HW].astype(BF16) * jnp.asarray(DH ** -0.5, BF16)
            k_ref[...] = qkv[:, HW:2 * HW].astype(BF16)
            v_ref[...] = qkv[:, 2 * HW:].astype(BF16)
            kt_ref[...] = jnp.transpose(qkv[:, HW:2 * HW]).astype(BF16)
            vt_ref[...] = jnp.transpose(qkv[:, 2 * HW:]).astype(BF16)


def by_head(rows, heads):
    lane = lax.broadcasted_iota(jnp.int32, rows.shape, 1)
    zero = jnp.zeros_like(rows)
    return jnp.concatenate(
        [jnp.where((lane >= h * DH) & (lane < (h + 1) * DH), rows, zero) for h in range(heads)], axis=0
    )


def seg_at(index):
    if isinstance(index, int):
        return slice(index * SEG, (index + 1) * SEG)
    return pl.ds(pl.multiple_of(index * SEG, SEG), SEG)


def head_columns(acc, heads):
    pieces = [acc[h * DH:(h + 1) * DH, h * SEG:(h + 1) * SEG] for h in range(heads)]
    pieces.append(jnp.zeros((HW - heads * DH, SEG), F32))
    return jnp.concatenate(pieces, axis=0)


def pair_bias(bias_ref, first, second):
    return jnp.concatenate([bias_ref[first], bias_ref[second]], axis=1)


def attn_forward_kernel(
    heads, me_ref, parent_ref, q_ref, k_ref, v_ref, vt_ref, bias_ref, o0, o1, o2, o3, raw_ref, lse_ref, out_all
):
    cols = heads * SEG
    trunk_len = TRUNK * SEG
    last = trunk_len - SEG

    def queries(b):
        return by_head(q_ref[seg_at(b), :], heads)

    def finish(b, acc, total, top):
        lse_ref[pl.ds(b * 8, 8), :] = jnp.broadcast_to(top + jnp.log(total), (8, cols))
        columns = head_columns(acc / total, heads)
        raw_ref[:, seg_at(b)] = columns
        out_all[:, seg_at(b)] = columns.astype(BF16)

    for j in range(TRUNK // 2):
        q6 = jnp.concatenate([queries(2 * j), queries(2 * j + 1)], axis=0)
        scores = dot(k_ref[0:(j + 1) * 2 * SEG, :], q6, NT)
        parts = []
        if j > 0:
            far = (2 * j - 1) * SEG
            parts = [scores[:far], scores[far:far + SEG] + pair_bias(bias_ref, 1, 0)]
        parts.append(scores[2 * j * SEG:(2 * j + 1) * SEG] + pair_bias(bias_ref, 2, 1))
        parts.append(scores[(2 * j + 1) * SEG:] + pair_bias(bias_ref, 3, 2))
        top = functools.reduce(jnp.maximum, [jnp.max(part, axis=0, keepdims=True) for part in parts])
        parts = [jnp.exp(part - top) for part in parts]
        total = functools.reduce(jnp.add, [jnp.sum(part, axis=0, keepdims=True) for part in parts])
        acc = dot(vt_ref[:, 0:(j + 1) * 2 * SEG], jnp.concatenate([p.astype(BF16) for p in parts], axis=0), NN)
        for s in range(2):
            at = slice(s * cols, (s + 1) * cols)
            finish(2 * j + s, acc[:, at], total[:, at], top[:, at])

    def other_step(i, carry):
        segs = [TRUNK + 2 * i, TRUNK + 2 * i + 1]
        parents = [parent_ref[b] for b in segs]
        leaf = [(parent >= TRUNK).astype(jnp.int32) for parent in parents]
        q3 = [queries(b) for b in segs]
        q6 = jnp.concatenate(q3, axis=0)
        scores = dot(k_ref[0:trunk_len, :], q6, NT)
        near = scores[last:] + pair_bias(bias_ref, 1 - leaf[0], 1 - leaf[1])
        far = scores[:last]
        extra = []
        for s in range(2):
            keys = jnp.concatenate([k_ref[seg_at(parents[s]), :], k_ref[seg_at(segs[s]), :]], axis=0)
            bias = jnp.concatenate([bias_ref[3 - 2 * leaf[s]], bias_ref[2]], axis=0)
            extra.append(dot(keys, q3[s], NT) + bias)
        top = jnp.maximum(jnp.max(far, axis=0, keepdims=True), jnp.max(near, axis=0, keepdims=True))
        top = jnp.maximum(top, jnp.concatenate([jnp.max(e, axis=0, keepdims=True) for e in extra], axis=1))
        far, near = jnp.exp(far - top), jnp.exp(near - top)
        extra = [jnp.exp(extra[s] - top[:, s * cols:(s + 1) * cols]) for s in range(2)]
        total = jnp.sum(far, axis=0, keepdims=True) + jnp.sum(near, axis=0, keepdims=True)
        total = total + jnp.concatenate([jnp.sum(e, axis=0, keepdims=True) for e in extra], axis=1)
        acc = dot(vt_ref[:, 0:trunk_len], jnp.concatenate([far.astype(BF16), near.astype(BF16)], axis=0), NN)
        for s in range(2):
            at = slice(s * cols, (s + 1) * cols)
            values = jnp.concatenate([vt_ref[:, seg_at(parents[s])], vt_ref[:, seg_at(segs[s])]], axis=1)
            finish(segs[s], acc[:, at] + dot(values, extra[s].astype(BF16), NN), total[:, at], top[:, at])
        return carry

    lax.fori_loop(0, (SEGS - TRUNK) // 2, other_step, 0)
    for rel, o_ref in enumerate((o0, o1, o2, o3)):
        width, count = o_ref.shape
        at = pl.ds(pl.multiple_of(jnp.bitwise_xor(me_ref[0], rel) * count, SEG), count)
        o_ref[...] = out_all[0:width, at]


TRUNK_FIRST = [SEG * j * (j + 1) for j in range(TRUNK // 2 + 1)]
OTHER_ROWS = (TRUNK + 2) * SEG
PROB_ROWS = TRUNK_FIRST[-1] + (SEGS - TRUNK) // 2 * OTHER_ROWS


def attn_prob_kernel(heads, parent_ref, q_ref, k_ref, lse_ref, bias_ref, before_ref, out_ref):
    cols = heads * SEG

    def common(b):
        return by_head(q_ref[seg_at(b), :], heads), lse_ref[pl.ds(b * 8, 8), :][0:1]

    for j in range(TRUNK // 2):
        (qa, la), (qb, lb) = common(2 * j), common(2 * j + 1)
        q6, lse = jnp.concatenate([qa, qb], axis=0), jnp.concatenate([la, lb], axis=1)
        for i in range(j + 1):
            scores = dot(k_ref[2 * i * SEG:2 * (i + 1) * SEG, :], q6, NT)
            if i == j:
                scores = scores + jnp.concatenate([pair_bias(bias_ref, 2, 1), pair_bias(bias_ref, 3, 2)], axis=0)
            if i == j - 1:
                scores = scores + jnp.concatenate([pair_bias(bias_ref, 0, 0), pair_bias(bias_ref, 1, 0)], axis=0)
            first = TRUNK_FIRST[j] + 2 * i * SEG
            out_ref[first:first + 2 * SEG, :] = jnp.exp(scores - lse).astype(BF16)

    def other_step(step, carry):
        segs = [TRUNK + 2 * step, TRUNK + 2 * step + 1]
        parents = [parent_ref[b] for b in segs]
        leaf = [(parent >= TRUNK).astype(jnp.int32) for parent in parents]
        each = [common(b) for b in segs]
        q6, lse = jnp.concatenate([q for q, _ in each], axis=0), jnp.concatenate([l for _, l in each], axis=1)
        base = TRUNK_FIRST[-1] + step * OTHER_ROWS
        for i in range(TRUNK // 2):
            scores = dot(k_ref[2 * i * SEG:2 * (i + 1) * SEG, :], q6, NT)
            if i == TRUNK // 2 - 1:
                near = pair_bias(bias_ref, 1 - leaf[0], 1 - leaf[1])
                scores = scores + jnp.concatenate([jnp.zeros_like(near), near], axis=0)
            at = pl.ds(pl.multiple_of(base + 2 * i * SEG, SEG), 2 * SEG)
            out_ref[at, :] = jnp.exp(scores - lse).astype(BF16)
        extra = []
        for s in range(2):
            keys = jnp.concatenate([k_ref[seg_at(parents[s]), :], k_ref[seg_at(segs[s]), :]], axis=0)
            bias = jnp.concatenate([bias_ref[3 - 2 * leaf[s]], bias_ref[2]], axis=0)
            extra.append(jnp.exp(dot(keys, each[s][0], NT) + bias - each[s][1]).astype(BF16))
        at = pl.ds(pl.multiple_of(base + TRUNK * SEG, SEG), 2 * SEG)
        out_ref[at, :] = jnp.concatenate(extra, axis=1)
        return carry

    lax.fori_loop(0, (SEGS - TRUNK) // 2, other_step, 0)


def attn_backward_kernel(
    heads, me_ref, parent_ref, q_ref, k_ref, v_ref, kt_ref, raw_ref, prob_ref, g0, g1, g2, g3_ref,
    d0, d1, d2, d3, bins_ref, grad_all, dq_all, dk_acc, dv_acc, bins_acc, probs, sem,
):
    def fetch(step):
        if isinstance(step, int):
            at = pl.ds(TRUNK_FIRST[step], TRUNK_FIRST[step + 1] - TRUNK_FIRST[step])
        else:
            at = pl.ds(pl.multiple_of(TRUNK_FIRST[-1] + (step - TRUNK // 2) * OTHER_ROWS, SEG), OTHER_ROWS)
        return pltpu.make_async_copy(prob_ref.at[at, :], probs.at[at, :], sem.at[step])

    for j in range(TRUNK // 2):
        fetch(j).start()

    def start_other(step, carry):
        fetch(step + TRUNK // 2).start()
        return carry

    lax.fori_loop(0, (SEGS - TRUNK) // 2, start_other, 0)
    cols = heads * SEG
    trunk_len = TRUNK * SEG
    dk_acc[...] = jnp.zeros_like(dk_acc)
    dv_acc[...] = jnp.zeros_like(dv_acc)
    bins_acc[...] = jnp.zeros_like(bins_acc)
    for rel, g_ref in enumerate((g0, g1, g2, g3_ref)):
        width, count = g_ref.shape
        at = pl.ds(pl.multiple_of(jnp.bitwise_xor(me_ref[0], rel) * count, SEG), count)
        grad_all[0:width, at] = g_ref[...]
        grad_all[width:HW, at] = jnp.zeros((HW - width, count), BF16)

    def common(b):
        q3 = by_head(q_ref[seg_at(b), :], heads)
        grad = grad_all[:, seg_at(b)].astype(F32)
        product = grad * raw_ref[:, seg_at(b)]
        row_dot = jnp.concatenate(
            [jnp.sum(product[h * DH:(h + 1) * DH], axis=0, keepdims=True) for h in range(heads)], axis=1
        )
        return q3, by_head(jnp.transpose(grad).astype(BF16), heads), row_dot

    def block(prob, values, g, row_dot):
        return prob.astype(F32) * (dot(values, g, NT) - row_dot)

    def write_dq(b, acc):
        dq_all[seg_at(b), :] = (jnp.transpose(head_columns(acc, heads)) * DH ** -0.5).astype(BF16)

    def both(pair):
        return [jnp.concatenate([a, b], axis=0 if a.shape[0] > 1 else 1) for a, b in zip(*pair)]

    for j in range(TRUNK // 2):
        q6, g6, row_dot = both([common(2 * j), common(2 * j + 1)])
        fetch(j).wait()
        kept = []
        for i in range(j + 1):
            at = slice(2 * i * SEG, 2 * (i + 1) * SEG)
            prob = probs[TRUNK_FIRST[j] + 2 * i * SEG:TRUNK_FIRST[j] + 2 * (i + 1) * SEG, :]
            score = block(prob, v_ref[at, :], g6, row_dot)
            if i == j:
                bins_acc[0] += score[:SEG, cols:]
                bins_acc[1] += score[:SEG, :cols] + score[SEG:, cols:]
            if i == j - 1:
                bins_acc[0] += score[SEG:, :cols]
            score = score.astype(BF16)
            dv_acc[at, :] += dot(prob, g6, NN)
            dk_acc[at, :] += dot(score, q6, NN)
            kept.append(score)
        acc = dot(kt_ref[:, 0:(j + 1) * 2 * SEG], jnp.concatenate(kept, axis=0), NN)
        for s in range(2):
            write_dq(2 * j + s, acc[:, s * cols:(s + 1) * cols])

    def other_step(step, carry):
        segs = [TRUNK + 2 * step, TRUNK + 2 * step + 1]
        parents = [parent_ref[b] for b in segs]
        leaf = [(parent >= TRUNK).astype(jnp.int32) for parent in parents]
        each = [common(b) for b in segs]
        q6, g6, row_dot = both(each)
        base = TRUNK_FIRST[-1] + step * OTHER_ROWS
        fetch(step + TRUNK // 2).wait()
        kept = []
        for i in range(TRUNK // 2):
            at = slice(2 * i * SEG, 2 * (i + 1) * SEG)
            prob = probs[pl.ds(pl.multiple_of(base + 2 * i * SEG, SEG), 2 * SEG), :]
            score = block(prob, v_ref[at, :], g6, row_dot)
            if i == TRUNK // 2 - 1:
                for s in range(2):
                    bins_acc[0] += jnp.where(leaf[s] == 0, score[SEG:, s * cols:(s + 1) * cols], 0.0)
            score = score.astype(BF16)
            dv_acc[at, :] += dot(prob, g6, NN)
            dk_acc[at, :] += dot(score, q6, NN)
            kept.append(score)
        acc = dot(kt_ref[:, 0:trunk_len], jnp.concatenate(kept, axis=0), NN)
        for s in range(2):
            q3, g3, row = each[s]
            first, second = seg_at(parents[s]), seg_at(segs[s])
            values = jnp.concatenate([v_ref[first, :], v_ref[second, :]], axis=0)
            keys_t = jnp.concatenate([kt_ref[:, first], kt_ref[:, second]], axis=1)
            at = pl.ds(pl.multiple_of(base + trunk_len, SEG), 2 * SEG)
            prob = probs[at, s * cols:(s + 1) * cols]
            score = block(prob, values, g3, row)
            bins_acc[0] += score[:SEG]
            bins_acc[1] += score[SEG:]
            score = score.astype(BF16)
            grad_v, grad_k = dot(prob, g3, NN), dot(score, q3, NN)
            dv_acc[first, :] += grad_v[:SEG]
            dv_acc[second, :] += grad_v[SEG:]
            dk_acc[first, :] += grad_k[:SEG]
            dk_acc[second, :] += grad_k[SEG:]
            write_dq(segs[s], acc[:, s * cols:(s + 1) * cols] + dot(keys_t, score, NN))
        return carry

    lax.fori_loop(0, (SEGS - TRUNK) // 2, other_step, 0)
    for rel, d_ref in enumerate((d0, d1, d2, d3)):
        count = d_ref.shape[0]
        width = heads * DH
        at = pl.ds(pl.multiple_of(jnp.bitwise_xor(me_ref[0], rel) * count, SEG), count)
        parts = [dq_all[at, :][:, :width], dk_acc[at, :][:, :width].astype(BF16), dv_acc[at, :][:, :width].astype(BF16)]
        parts.append(jnp.zeros((count, d_ref.shape[1] - 3 * width), BF16))
        d_ref[...] = jnp.concatenate(parts, axis=1)
    key = lax.broadcasted_iota(jnp.int32, (SEG, cols), 0)
    query = lax.broadcasted_iota(jnp.int32, (SEG, cols), 1) % SEG
    gap = query - key
    parent_sum, own_sum = bins_acc[0], bins_acc[1]
    lines = [jnp.sum(parent_sum + own_sum, axis=0, keepdims=True)]
    for threshold in THRESHOLDS:
        hit = jnp.where(gap + SEG >= threshold, parent_sum, 0.0) + jnp.where(gap >= threshold, own_sum, 0.0)
        lines.append(jnp.sum(hit, axis=0, keepdims=True))
    bins_ref[...] = jnp.concatenate(lines, axis=0)


class Slots:
    def __init__(self, n_expert, capacity):
        self.n_expert = n_expert
        self.cut = n_expert == 8
        self.block = -(-(capacity + SPARE) // 16) * 16
        if self.cut:
            self.groups = [[0, 1, 4, 5], [2, 3, 6, 7]]
            self.rels = [2, 3, 6, 7]
            self.chunks = [[[0, 1, 2, 3]], [[4], [5], [6], [7]]]
        else:
            self.groups = None
            self.chunks = [[list(range(n_expert))]]
        self.arrays = [array for chunk in self.chunks for array in chunk]

    def block_of(self, expert, me):
        if not self.cut:
            return expert
        rel = jnp.bitwise_xor(expert, me)
        inside = lambda index: (index & 1) | ((index >> 1) & 2)
        return jnp.where((rel & 2) == 0, inside(expert), 4 + inside(rel))

    def expert_of(self, block, me):
        if not self.cut:
            return block
        if not isinstance(block, int) or block < 4:
            return (me & 2) | (block & 1) | ((block & 2) << 1)
        return jnp.bitwise_xor(me, self.rels[block - 4])

    def near_exchange(self, block):
        return lax.all_to_all(block, "expert", split_axis=0, concat_axis=0, tiled=True, axis_index_groups=self.groups)


def over_experts(block):
    return lax.all_to_all(block, "expert", split_axis=0, concat_axis=0, tiled=True)


def swap(block, axis, rel):
    if rel == 0:
        return block
    return lax.ppermute(block, axis, [(i, i ^ rel) for i in range(lax.axis_size(axis))])


def swap_all(blocks, axis):
    return [swap(block, axis, rel) for rel, block in enumerate(blocks)]


def from_all(block):
    near, far = swap(block, "shard", 1), swap(block, "shard", 2)
    return [block, near, far, swap(far, "shard", 1)]


def reorder(parts, me):
    bit = 1
    while bit < len(parts):
        parts = [jnp.where(me & bit, parts[i ^ bit], parts[i]) for i in range(len(parts))]
        bit *= 2
    return parts


def send_rows(slots, rows, places_ref, out_refs):
    tokens = places_ref.shape[1]
    for array, out_ref in zip(slots.arrays, out_refs):
        for i, block in enumerate(array):
            slot = block * slots.block + lax.broadcasted_iota(jnp.int32, (slots.block, tokens), 0)
            hit = (slot == places_ref[0:1, :]) | (slot == places_ref[1:2, :])
            picked = dot(jnp.where(hit, 1.0, 0.0).astype(BF16), rows, NN).astype(BF16)
            out_ref[i * slots.block:(i + 1) * slots.block, :] = picked


def row_at(first, count):
    return pl.ds(first if isinstance(first, int) else pl.multiple_of(first, 16), count)


def diagonal(count):
    return lax.broadcasted_iota(jnp.int32, (count, count), 0) == lax.broadcasted_iota(jnp.int32, (count, count), 1)


def padded_row(row, width):
    count = row.shape[1]
    return row if count == width else jnp.concatenate([row, jnp.zeros((1, width - count), row.dtype)], axis=1)


def dispatch_kernel(slots, me_ref, places_ref, others_ref, rows_ref, *refs):
    out_ref = refs[-1]
    tokens = places_ref.shape[1]
    width = rows_ref.shape[1]
    rows = rows_ref[...]
    count = slots.block

    def one(expert, carry):
        slot = slots.block_of(expert, me_ref[0]) * count + lax.broadcasted_iota(jnp.int32, (count, tokens), 0)
        hot = [jnp.where(slot == places_ref[j:j + 1, :], 1.0, 0.0).astype(BF16) for j in range(2)]
        picked = dot(hot[0] + hot[1], rows, NN)
        ids = sum(dot(others_ref[8 * j:8 * j + 8, :], hot[j], NT) for j in range(2))
        line = lax.broadcasted_iota(jnp.int32, picked.shape, 0)
        picked = jnp.where(line == count - 1, padded_row(ids[0:1], width), picked)
        out_ref[pl.ds(pl.multiple_of(expert * count, 16), count), :] = picked.astype(BF16)
        return carry

    lax.fori_loop(0, slots.n_expert, one, 0)


def post_kernel(
    slots, me_ref, x_ref, gain_ref, router_ref, routes_ref, places_ref, m0, m1, m2, m3, w_ref,
    after_ref, normed_ref, gates_ref, *out_refs,
):
    after = x_ref[...].astype(F32)
    for rel, m_ref in enumerate((m0, m1, m2, m3)):
        after = after + dot(m_ref[...], w_ref[jnp.bitwise_xor(me_ref[1], rel)], TN)
    after_ref[...] = after
    unit, _ = rms_parts(after)
    normed = (unit * gain_ref[...]).astype(BF16)
    normed_ref[...] = normed
    send_rows(slots, normed_ref[...], places_ref, out_refs)
    logits = dot(normed, router_ref[...], NN)
    expert = lax.broadcasted_iota(jnp.int32, logits.shape, 1)
    first = jnp.sum(jnp.where(expert == routes_ref[:, 0:1], logits, 0.0), axis=-1, keepdims=True)
    second = jnp.sum(jnp.where(expert == routes_ref[:, 1:2], logits, 0.0), axis=-1, keepdims=True)
    top = jnp.maximum(first, second)
    first, second = jnp.exp(first - top), jnp.exp(second - top)
    gates_ref[...] = jnp.concatenate([first / (first + second), second / (first + second)], axis=1)


def expert_kernel(slots, kind, sizes, before, me_ref, *refs):
    refs = list(refs)
    take = lambda n: [refs.pop(0) for _ in range(n)]
    x_refs = take(sizes[0])
    g_all, router_ref = take(2)
    first_refs, second_refs = take(4), take(4)
    extra = take(before)
    own_ref = extra[1] if before == 3 else None
    (out_all,) = take(1)
    dx_refs = take(sizes[1])
    rows_out, grad_out, act_ref, inner_ref, rows_ref, grad_ref, first_buf, second_buf, g_buf, out_buf, out_acc, dx_acc, gate_acc, gates_acc, sem, in_sem, keep_sem = refs
    step = pl.program_id(0)
    slot = lax.rem(step, 2)
    total, width = rows_ref.shape
    depth, units = first_refs[0].shape[0], second_buf.shape[1]

    def fetch(rel, slot):
        column = pl.multiple_of(jnp.bitwise_xor(me_ref[1], rel) * units, 128)
        copies = [pltpu.make_async_copy(second_refs[rel], second_buf.at[slot], in_sem.at[slot, 4])]
        for piece, ref in enumerate(first_refs):
            row = pl.multiple_of(jnp.bitwise_xor(me_ref[1], piece) * depth, 16)
            copies.append(
                pltpu.make_async_copy(
                    ref.at[:, pl.ds(column, units)], first_buf.at[slot, pl.ds(row, depth), :], in_sem.at[slot, piece]
                )
            )
        return copies

    @pl.when(step == 0)
    def _():
        for copy in fetch(0, 0):
            copy.start()

    for rel in range(4):
        @pl.when(step == rel)
        def _(rel=rel):
            if rel < 3:
                for copy in fetch(rel + 1, (rel + 1) % 2):
                    copy.start()
    rows = slots.block
    mine = slots.block_of(me_ref[0], me_ref[0])
    if kind == "own":
        pieces = [(mine, x_refs[0], mine * rows, dx_refs[0], 0)]
    elif kind == "near":
        blocks = [jnp.bitwise_xor(mine, i) for i in (1, 2, 3)]
        pieces = [(block, x_refs[0], block * rows, dx_refs[0], block * rows) for block in blocks]
    elif kind == "far":
        pieces = [(4 + i, x_ref, 0, dx_ref, 0) for i, (x_ref, dx_ref) in enumerate(zip(x_refs, dx_refs))]
    else:
        pieces = [(block, x_refs[0], block * rows, dx_refs[0], block * rows) for block in range(slots.n_expert)]
    pieces = [(*piece, i * rows) for i, piece in enumerate(pieces)]

    def home(block):
        return pl.ds(pl.multiple_of(slots.expert_of(block, me_ref[0]) * rows, 16), rows)

    @pl.when(step == 0)
    def _():
        copies = [
            pltpu.make_async_copy(g_all.at[home(block), :], g_buf.at[pl.ds(first, rows), :], sem.at[i])
            for i, (block, *_, first) in enumerate(pieces)
        ]
        for copy in copies:
            copy.start()
        out_acc[...] = jnp.zeros_like(out_acc)
        dx_acc[...] = jnp.zeros_like(dx_acc)
        for _, x_ref, inside, _, _, first in pieces:
            rows_ref[first:first + rows, :] = x_ref[row_at(inside, rows), :]
        for copy in copies:
            copy.wait()
        for *_, first in pieces:
            at = slice(first, first + rows)
            grads = g_buf[at, :].astype(F32)
            other = jnp.sum(jnp.where(diagonal(rows), grads[rows - 1:, :rows], 0.0), axis=1, keepdims=True).astype(jnp.int32)
            logits = dot(rows_ref[at, :], router_ref[...], NN)
            expert = lax.broadcasted_iota(jnp.int32, logits.shape, 1)
            mine = jnp.sum(jnp.where(expert == me_ref[0], logits, 0.0), axis=-1, keepdims=True)
            its = jnp.sum(jnp.where(expert == other, logits, 0.0), axis=-1, keepdims=True)
            top = jnp.maximum(mine, its)
            mine, its = jnp.exp(mine - top), jnp.exp(its - top)
            line = lax.broadcasted_iota(jnp.int32, grads.shape, 0)
            gate = mine / (mine + its)
            gate_acc[at, :] = jnp.broadcast_to(gate, (rows, 128))
            grad_ref[at, :] = jnp.where(line < rows - SPARE, gate * grads, 0.0).astype(BF16)

    keeps = [
        pltpu.make_async_copy(rows_ref, rows_out, keep_sem.at[0]),
        pltpu.make_async_copy(grad_ref, grad_out, keep_sem.at[1]),
    ]

    @pl.when(step == 0)
    def _():
        for copy in keeps:
            copy.start()

    for rel in range(4):
        @pl.when(step == rel)
        def _(rel=rel):
            for copy in fetch(rel, rel % 2):
                copy.wait()

    parts = 1
    while total // parts > 512 or total % parts or (total // parts) % 16:
        parts += 1
    part = total // parts
    for i in range(parts):
        at = slice(i * part, (i + 1) * part)
        first_w, second_w = first_buf[slot], second_buf[slot]
        value = dot(rows_ref[at, :], first_w, NN)
        grad_act = dot(grad_ref[at, :], second_w, NT)
        square = value * value
        half = 0.5 * value
        scale = 0.7978845608028654
        th = jnp.tanh(value * (scale + (scale * 0.044715) * square))
        act = (half + half * th).astype(BF16)
        slope = 0.5 + 0.5 * th + (half * (1.0 - th * th)) * (scale + (3 * scale * 0.044715) * square)
        inner = (grad_act * slope).astype(BF16)
        act_ref[at, :] = act
        inner_ref[at, :] = inner
        out_acc[at, :] += dot(act, second_w, NN)
        dx_acc[at, :] += dot(inner, first_w, NT)

    @pl.when(step == pl.num_programs(0) - 1)
    def _():
        for *_, first in pieces:
            at = slice(first, first + rows)
            out = out_acc[at, :].astype(BF16).astype(F32)
            gates = jnp.sum(out * g_buf[at, :].astype(F32), axis=1, keepdims=True)
            gates_acc[at, :] = jnp.broadcast_to(gates, (rows, 128))
            out_buf[at, :] = (gate_acc[at, 0:1] * out).astype(BF16)
        copies = [
            pltpu.make_async_copy(out_buf.at[pl.ds(first, rows), :], out_all.at[home(block), :], sem.at[i])
            for i, (block, *_, first) in enumerate(pieces)
        ]
        for copy in copies:
            copy.start()
        if own_ref is not None:
            dx_refs[0][row_at(mine * rows, rows), :] = own_ref[...]
        for _, _, _, dx_ref, inside, first in pieces:
            at = slice(first, first + rows)
            gates = gates_acc[at, 0:1]
            gates = jnp.sum(jnp.where(diagonal(rows), gates, 0.0), axis=0, keepdims=True)
            dx_ref[row_at(inside, rows), :] = dx_acc[at, :].astype(BF16)
            tail = dx_acc[first + rows - 16:first + rows, :]
            line = lax.broadcasted_iota(jnp.int32, tail.shape, 0)
            for place in range(SPARE):
                piece = gates.astype(BF16).astype(F32)
                gates = gates - piece
                tail = jnp.where(line == 16 - SPARE + place, padded_row(piece, width), tail)
            dx_ref[row_at(inside + rows - 16, 16), :] = tail.astype(BF16)
        for copy in [*copies, *keeps]:
            copy.wait()


def run_expert(slots, kind, blocks, dx_shape, shared, before, estimate):
    me, g_all, router, first_w, second_w = shared
    hidden, width = first_w[0].shape[1], router.shape[0]
    total = slots.block * {"own": 1, "near": 3, "far": 4, "all": slots.n_expert}[kind]
    block = hidden // 4
    whole = lambda a: pl.BlockSpec(a.shape, lambda i: (0, 0))
    column = pl.BlockSpec((total, block), lambda i: (0, i))
    fresh = len(before) < 2
    dx = [jax.ShapeDtypeStruct(dx_shape, BF16)] * (4 if kind == "far" else 1)
    inputs = [me, *blocks, g_all, router, *first_w, *second_w, *before]
    before_specs = [ANY] * len(before)
    if len(before) == 3:
        before_specs[1] = whole(before[1])
    return pl.pallas_call(
        functools.partial(expert_kernel, slots, kind, (len(blocks), len(dx)), len(before)),
        grid=(4,),
        in_specs=[SMEM] + [whole(b) for b in blocks] + [ANY, whole(router)] + [ANY] * 8 + before_specs,
        out_specs=[ANY] + [whole(b) for b in dx] + [ANY, ANY, column, column],
        out_shape=arrays(
            (g_all.shape, BF16), *[(b.shape, BF16) for b in dx], *[((total, width), BF16)] * 2, *[((total, hidden), BF16)] * 2
        ),
        scratch_shapes=[
            pltpu.VMEM((total, width), BF16),
            pltpu.VMEM((total, width), BF16),
            pltpu.VMEM((2, width, block), BF16),
            pltpu.VMEM((2, block, width), BF16),
            pltpu.VMEM((total, width), BF16),
            pltpu.VMEM((total, width), BF16),
            pltpu.VMEM((total, width), F32),
            pltpu.VMEM((total, width), F32),
            pltpu.VMEM((total, 128), F32),
            pltpu.VMEM((total, 128), F32),
            pltpu.SemaphoreType.DMA((total // slots.block,)),
            pltpu.SemaphoreType.DMA((2, 5)),
            pltpu.SemaphoreType.DMA((2,)),
        ],
        input_output_aliases={} if fresh else {len(inputs) - 1: 0},
        compiler_params=params(dimension_semantics=("arbitrary",)),
        cost_estimate=estimate,
    )(*inputs)


def first_grad_kernel(parts, me_ref, *refs):
    send_ref, keep_ref, total = refs[-3:]
    total[...] = sum(dot(x[...], inner[...], TN) for x, inner in zip(refs[:parts], refs[parts:2 * parts]))
    depth = send_ref.shape[0] // 2
    for rel in range(4):
        ref = (keep_ref, send_ref)[rel % 2]
        row = pl.multiple_of(jnp.bitwise_xor(me_ref[1], rel) * depth, 16)
        at = rel // 2 * depth
        ref[at:at + depth, :] = total[pl.ds(row, depth), :].astype(BF16)


def run_first_grad(me, rows, inners, depth, *after):
    width, hidden = rows[0].shape[1], inners[0].shape[1]
    block = hidden // 4
    column = pl.BlockSpec((2 * depth, block), lambda i, me_ref: (0, jnp.bitwise_xor(me_ref[1], i)))
    return pl.pallas_call(
        functools.partial(first_grad_kernel, len(rows)),
        grid_spec=pltpu.PrefetchScalarGridSpec(
            num_scalar_prefetch=1,
            grid=(4,),
            in_specs=[pl.BlockSpec(a.shape, lambda i, me_ref: (0, 0)) for a in rows]
            + [pl.BlockSpec((a.shape[0], block), lambda i, me_ref: (0, i)) for a in inners]
            + [ANY] * len(after),
            out_specs=[column, column],
            scratch_shapes=[pltpu.VMEM((width, block), F32)],
        ),
        out_shape=arrays(*[((2 * depth, hidden), BF16)] * 2),
        compiler_params=params(dimension_semantics=("arbitrary",)),
        cost_estimate=SHORT,
    )(me, *rows, *inners, *after)


def second_grad_kernel(parts, *refs):
    send_ref, keep_ref = refs[2 * parts:]
    step = pl.program_id(0)
    block = sum(dot(act[...], g[...], TN) for act, g in zip(refs[:parts], refs[parts:2 * parts])).astype(BF16)

    @pl.when(step < 2)
    def _():
        send_ref[...] = block

    @pl.when(step >= 2)
    def _():
        keep_ref[...] = block


def run_second_grad(acts, grads):
    width, hidden = grads[0].shape[1], acts[0].shape[1]
    block = hidden // 4
    return pl.pallas_call(
        functools.partial(second_grad_kernel, len(acts)),
        grid=(4,),
        in_specs=[pl.BlockSpec((a.shape[0], block), lambda i: (0, 2 * (i % 2) + 1 - i // 2)) for a in acts]
        + [pl.BlockSpec(a.shape, lambda i: (0, 0)) for a in grads],
        out_specs=[
            pl.BlockSpec((block, width), lambda i: (jnp.minimum(i, 1), 0)),
            pl.BlockSpec((block, width), lambda i: (jnp.maximum(i - 2, 0), 0)),
        ],
        out_shape=arrays(*[((2 * block, width), BF16)] * 2),
        compiler_params=params(dimension_semantics=("arbitrary",)),
        cost_estimate=SHORT,
    )(*acts, *grads)


def core_sum(send, keep):
    near = swap(send, "shard", 1)
    half = keep.shape[0] // 2
    other = (keep[half:].astype(F32) + near[half:].astype(F32)).astype(BF16)
    return keep, near, other


def across_sum(parts):
    keep, near, other = parts
    return keep, near, swap(other, "shard", 2)


def total_sum(parts):
    keep, near, far = parts
    half = keep.shape[0] // 2
    return keep[:half].astype(F32) + near[:half].astype(F32) + far.astype(F32)


def gather_blocks(slots, refs, scratch):
    for array, ref in zip(slots.arrays, refs):
        scratch[array[0] * slots.block:(array[-1] + 1) * slots.block, :] = ref[...]


def back_kernel(slots, me_ref, *refs):
    refs_left = list(refs)
    take = lambda n: [refs_left.pop(0) for _ in range(n)]
    ret_refs = take(len(slots.arrays))
    places_ref, routes_ref, gates_ref, after_ref, gain_ref, router_ref, g_ref = take(7)
    w_ref, normed_ref = take(2)
    m_refs = take(4)
    (grad_after_ref,) = take(1)
    mixed_refs = take(4)
    send_ref, keep_ref, branch_ref, glogits_ref, ggain_ref, more, scratch = refs_left
    tokens = after_ref.shape[0]
    part = tokens // 2
    gather_blocks(slots, ret_refs, scratch)
    pieces = []
    for end in range(slots.block, scratch.shape[0] + 1, slots.block):
        tail = scratch[end - 16:end, :].astype(F32)[16 - SPARE:, :slots.block]
        pieces.append(jnp.sum(tail, axis=0, keepdims=True))
    gg = jnp.concatenate(pieces, axis=1)
    ggain_ref[...] = jnp.zeros_like(ggain_ref)

    def one(i, carry):
        at = pl.ds(pl.multiple_of(i * part, part), part)
        slot = lax.broadcasted_iota(jnp.int32, (part, gg.shape[1]), 1)
        hit0, hit1 = slot == places_ref[at, 0:1], slot == places_ref[at, 1:2]
        gg0 = jnp.sum(jnp.where(hit0, gg, 0.0), axis=-1, keepdims=True)
        gg1 = jnp.sum(jnp.where(hit1, gg, 0.0), axis=-1, keepdims=True)
        total = dot(jnp.where(hit0 | hit1, 1.0, 0.0).astype(BF16), scratch[...], NN)
        gate0, gate1 = gates_ref[at, 0:1], gates_ref[at, 1:2]
        mean = gate0 * gg0 + gate1 * gg1
        expert = lax.broadcasted_iota(jnp.int32, (part, router_ref.shape[1]), 1)
        glogits = jnp.where(expert == routes_ref[at, 0:1], gate0 * (gg0 - mean), 0.0) + jnp.where(
            expert == routes_ref[at, 1:2], gate1 * (gg1 - mean), 0.0
        )
        glogits = glogits.astype(BF16)
        glogits_ref[at, :] = glogits
        incoming = dot(glogits, router_ref[...], NT) + total
        unit, factor = rms_parts(after_ref[at, :])
        grad_after = g_ref[at, :].astype(F32) + rms_grad(incoming, gain_ref[...], unit, factor)
        ggain_ref[0:1, :] += jnp.sum(incoming * unit, axis=0, keepdims=True)
        grad_after_ref[at, :] = grad_after
        branch = grad_after.astype(BF16)
        branch_ref[at, :] = branch
        return carry

    lax.fori_loop(0, tokens // part, one, 0)
    for rel, mixed_ref in enumerate(mixed_refs):
        mixed_ref[...] = dot(w_ref[jnp.bitwise_xor(me_ref[0], rel)], branch_ref[...], NT).astype(BF16)
    width = branch_ref.shape[1]
    grad_router = dot(normed_ref[...], glogits_ref[...], TN)
    gain = jnp.transpose(jnp.concatenate([ggain_ref[...]] * 16, axis=0))[:, 0:1]
    blank = jnp.zeros((width, more.shape[1] - grad_router.shape[1] - 1), F32)
    more[...] = jnp.concatenate([grad_router, gain, blank], axis=1)
    for rel, m_ref in enumerate(m_refs):
        ref = (keep_ref, send_ref)[rel % 2]
        count = m_ref.shape[0]
        at = slice(rel // 2 * count, (rel // 2 + 1) * count)
        ref[at, 0:width] = dot(m_ref[...], branch_ref[...], NN).astype(BF16)
        row = pl.multiple_of(jnp.bitwise_xor(me_ref[0], rel) * count, 16)
        ref[at, width:] = more[pl.ds(row, count), :].astype(BF16)


def combine_kernel(slots, me_ref, ret_ref, places_ref, after_ref, out_ref, scratch):
    part = after_ref.shape[0] // 2
    for block in range(slots.n_expert):
        first = pl.multiple_of(slots.expert_of(block, me_ref[0]) * slots.block, 16)
        scratch[block * slots.block:(block + 1) * slots.block, :] = ret_ref[pl.ds(first, slots.block), :]

    def one(i, carry):
        at = pl.ds(pl.multiple_of(i * part, part), part)
        slot = lax.broadcasted_iota(jnp.int32, (part, scratch.shape[0]), 1)
        hit = (slot == places_ref[at, 0:1]) | (slot == places_ref[at, 1:2])
        total = after_ref[at, :] + dot(jnp.where(hit, 1.0, 0.0).astype(BF16), scratch[...], NN)
        out_ref[at, :] = total.astype(BF16)
        return carry

    lax.fori_loop(0, after_ref.shape[0] // part, one, 0)


def final_kernel(me_ref, x_ref, gain_ref, after_ref, d0, d1, d2, d3, w_ref, out_ref):
    grad = sum(
        dot(d_ref[...], w_ref[jnp.bitwise_xor(me_ref[0], rel)], NT) for rel, d_ref in enumerate((d0, d1, d2, d3))
    )
    unit, factor = rms_parts(x_ref[...].astype(F32))
    out_ref[...] = (after_ref[...] + rms_grad(grad, gain_ref[...], unit, factor)).astype(BF16)


def column_grad_kernel(
    orders, heads, me_ref, bins_ref, n_ref, d0, d1, d2, d3, wk_ref, wn_ref, wf_ref, *refs
):
    *out_refs, acc, more = refs
    acc[...] = sum(dot(n_ref[rel], d_ref[...], TN) for rel, d_ref in enumerate((d0, d1, d2, d3)))
    rows = wf_ref.shape[0]
    more[...] = wk_ref[0:rows, :].astype(F32) + wn_ref[0:rows, :].astype(F32) + wf_ref[...].astype(F32)
    cols = 3 * heads * DH
    wide = acc.shape[1]
    lane = lax.broadcasted_iota(jnp.int32, (NB, wide), 1)
    table = jnp.zeros((NB, wide), F32)
    for h in range(heads):
        above = jnp.sum(bins_ref[:, h * SEG:(h + 1) * SEG], axis=1, keepdims=True)
        column = above - jnp.concatenate([above[1:], jnp.zeros((1, 1), F32)], axis=0)
        column = jnp.concatenate([column[:-1], -jnp.sum(column[:-1], axis=0, keepdims=True)], axis=0)
        table = jnp.where(lane == cols + h, column, table)
    share = rows // len(orders[0])
    half = share // 2

    def block_of(rel):
        first = jnp.bitwise_xor(me_ref[0], rel) * share
        at = lambda start: pl.ds(pl.multiple_of(start + first, 8), share)
        block = [acc[at(p * rows), :] for p in range(4)]
        block[0] = jnp.concatenate([block[0][:NB] + table, block[0][NB:]], axis=0)
        others = more[at(0), :]
        rest = others[:, wide:]
        folded = [rest[:half], rest[half:], jnp.zeros((half, wide - 2 * rest.shape[1]), F32)]
        block += [others[:, :wide], jnp.concatenate(folded, axis=1)]
        if half % 8:
            block.append(jnp.zeros((-half % 8, wide), F32))
        return block[:3], block[3:]

    blocks = {rel: block_of(rel) for rel in orders[0]}
    count = len(out_refs) // 2
    for part, order in enumerate(orders):
        for i in range(count):
            mine = order[i * len(order) // count:(i + 1) * len(order) // count]
            rows_of = [row for rel in mine for row in blocks[rel][part]]
            out_refs[part * count + i][...] = jnp.concatenate(rows_of, axis=0).astype(BF16)


def split_kernel(me_ref, *refs):
    *in_refs, b0, b1, b2, b3, more_ref, table_ref, total = refs
    share, cols = b0.shape
    count = len(in_refs) // 2
    total[0:3 * share, :] = sum(ref[...].astype(F32) for ref in in_refs[:count])
    total[3 * share:, :] = sum(ref[...].astype(F32) for ref in in_refs[count:])
    wide = total.shape[1]
    for rel, ref in enumerate((b0, b1, b2, b3)):
        at = pl.ds(pl.multiple_of(jnp.bitwise_xor(me_ref[0], rel) * share, 8), share)
        ref[...] = total[at, :][:, :cols].astype(BF16)
    folded = total[5 * share:5 * share + share // 2, :]
    rest = more_ref.shape[1] - wide
    folded = jnp.concatenate([folded[:, :rest], folded[:, rest:2 * rest]], axis=0)
    more_ref[...] = jnp.concatenate([total[4 * share:5 * share, :], folded], axis=1).astype(BF16)
    table_ref[...] = total[0:NB, wide - table_ref.shape[1]:]


def join_kernel(me_ref, p0, p1, p2, p3, more_ref, out_ref):
    parts = [ref[...] for ref in (p0, p1, p2, p3)]
    for bit in (1, 2):
        swapped = (me_ref[0] & bit) != 0
        parts = [jnp.where(swapped, parts[i ^ bit], parts[i]) for i in range(4)]
    hw = p0.shape[1] // 3
    out_ref[...] = jnp.concatenate(
        [part[:, c * hw:(c + 1) * hw] for c in range(3) for part in parts] + [more_ref[...]], axis=1
    )


def place_kernel(experts, me_ref, wq_ref, wk_ref, wv_ref, gain_in_ref, *refs):
    *piece_refs, q_ref, k_ref, v_ref, o_ref, router_ref, gains_ref, more = refs
    width = q_ref.shape[1]
    count = piece_refs[0].shape[0] // (2 if len(piece_refs) > 1 else 1)
    for rel, at_row, piece_ref in [
        (rel | (first // count) * 4, first, ref) for rel, ref in enumerate(piece_refs) for first in range(0, ref.shape[0], count)
    ]:
        at = pl.ds(pl.multiple_of(jnp.bitwise_xor(me_ref[0], rel) * count, 8), count)
        piece = piece_ref[at_row:at_row + count, :].astype(F32)
        for c, out_ref in enumerate((q_ref, k_ref, v_ref, o_ref)):
            out_ref[at, :] = piece[:, c * width:(c + 1) * width]
        more[at, :] = piece[:, 4 * width:]
    total = sum(
        w_ref[...].astype(F32) * out_ref[...] for w_ref, out_ref in ((wq_ref, q_ref), (wk_ref, k_ref), (wv_ref, v_ref))
    )
    rows = total.shape[0]
    lane = lax.broadcasted_iota(jnp.int32, more.shape, 1)
    columns = jnp.where(lane == experts + 1, jnp.sum(total, axis=1, keepdims=True), more[...])
    columns = jnp.concatenate([columns, jnp.zeros((-rows % 128, columns.shape[1]), F32)], axis=0)
    columns = jnp.transpose(columns)[:, :rows]
    router_ref[...] = columns[0:experts]
    gains_ref[0:1, :] = columns[experts + 1:experts + 2] / gain_in_ref[...]
    gains_ref[1:2, :] = columns[experts:experts + 1]


def per_device(
    tokens, gain_attn, w_query, w_key, w_value, w_output, rel_table, gain_moe, router,
    w_in, w_out, routes, parents, cotangent,
):
    n_shard = lax.axis_size("shard")
    n_expert = lax.axis_size("expert")
    tok, width = tokens.shape
    tree_len = tok * n_shard
    n_experts = router.shape[1]
    heads = rel_table.shape[0]
    hw = heads * DH
    wide = -(-3 * hw // 128) * 128
    rows = width // n_shard
    slots = Slots(n_expert, max(2, tok * 20 // (7 * n_experts)))
    me_s, me_e = lax.axis_index("shard").astype(jnp.int32), lax.axis_index("expert").astype(jnp.int32)
    me_shard, me_expert, me = me_s.reshape(1), me_e.reshape(1), jnp.stack([me_e, me_s])

    more = jnp.concatenate([gain_attn[:, None], gain_moe[:, None], router], axis=1)
    w_rel = pl.pallas_call(
        columns_kernel,
        in_specs=[SMEM] + [VMEM] * 4,
        out_specs=[VMEM] * n_shard,
        out_shape=arrays(*[((rows, -(-(3 * hw + 2 + n_experts) // 128) * 128), BF16)] * n_shard),
        compiler_params=params(),
        cost_estimate=SHORT,
    )(me_shard, w_query, w_key, w_value, more)
    near_tokens, far_tokens = swap(tokens, "shard", 1), swap(tokens, "shard", 2)
    w_pieces = swap_all(w_rel, "shard")

    expert_range = jnp.arange(n_experts, dtype=jnp.int32)
    flat_routes = routes.reshape(-1)
    expert_hot = (flat_routes[:, None] == expert_range[None, :]).astype(jnp.int32)
    earlier = jnp.cumsum(expert_hot, axis=0) - expert_hot
    rank = jnp.sum(earlier * expert_hot, axis=-1)
    places = (slots.block_of(flat_routes, me_e) * slots.block + rank).reshape(tok, 2)
    places_row = places.T
    others = jnp.repeat(routes.T[::-1], 8, axis=0).astype(BF16)
    block_shapes = [((len(array) * slots.block, width), BF16) for array in slots.arrays]

    sent_grads = pl.pallas_call(
        functools.partial(dispatch_kernel, slots),
        in_specs=[SMEM] + [VMEM] * 3 + [ANY],
        out_specs=VMEM,
        out_shape=jax.ShapeDtypeStruct((n_expert * slots.block, width), BF16),
        compiler_params=params(),
        cost_estimate=SHORT,
    )(me_expert, places_row, others, cotangent, w_rel[0])
    got_grads = over_experts(sent_grads)
    far_tokens, _, w_pieces = lax.optimization_barrier((far_tokens, sent_grads, w_pieces))
    tree = [tokens, near_tokens, far_tokens, swap(far_tokens, "shard", 1)]

    place = lambda i, me_ref: (jnp.bitwise_xor(me_ref[0], i), 0)
    place_t = lambda i, me_ref: (0, jnp.bitwise_xor(me_ref[0], i))
    fixed = [
        ((width, wide), BF16), ((4, SEG, heads * SEG), F32), *[((1, width), F32)] * 2, ((width, n_experts), BF16),
    ]
    normed_one, queries, keys, values, keys_t, values_t, w_cols, bias, gain_one, gain_two, router_w = pl.pallas_call(
        functools.partial(project_kernel, heads),
        grid_spec=pltpu.PrefetchScalarGridSpec(
            num_scalar_prefetch=1,
            grid=(n_shard,),
            in_specs=[SMEM] + [VMEM] * 8 + [ANY],
            out_specs=[pl.BlockSpec((1, tok, width), lambda i, me_ref: (i, 0, 0))]
            + [pl.BlockSpec((tok, HW), place)] * 3
            + [pl.BlockSpec((HW, tok), place_t)] * 2
            + [pl.BlockSpec(shape, lambda i, me_ref, shape=shape: (0,) * len(shape)) for shape, _ in fixed],
            scratch_shapes=[pltpu.VMEM((width, 3 * HW + 128), BF16)],
        ),
        out_shape=arrays(
            ((n_shard, tok, width), BF16), *[((tree_len, HW), BF16)] * 3, *[((HW, tree_len), BF16)] * 2, *fixed
        ),
        compiler_params=params(dimension_semantics=("arbitrary",)),
        cost_estimate=SHORT,
    )(me_shard, rel_table.astype(F32), *w_pieces, *tree, sent_grads)
    parent_row = parents[0]
    *mixed, raw, lse = pl.pallas_call(
        functools.partial(attn_forward_kernel, heads),
        in_specs=[SMEM] * 2 + [VMEM] * 5,
        out_specs=[VMEM] * 6,
        out_shape=arrays(*[((hw, tok), BF16)] * 4, ((HW, tree_len), F32), ((SEGS * 8, heads * SEG), F32)),
        scratch_shapes=[pltpu.VMEM((HW, tree_len), BF16)],
        compiler_params=params(),
        cost_estimate=FORWARD,
    )(me_shard, parent_row, queries, keys, values, values_t, bias)
    first_far = swap(w_in[0], "shard", 2)
    w_o = lax.all_gather(w_output, "shard", axis=0)
    mixed, first_far, w_o = lax.optimization_barrier((mixed, first_far, w_o))
    mixed = swap_all(mixed, "shard")
    first_w = [w_in[0], swap(w_in[0], "shard", 1), first_far, swap(first_far, "shard", 1)]
    second_near = swap(w_out[0], "shard", 1)
    w_out, w_cols, _ = lax.optimization_barrier((w_out, w_cols, mixed))
    second_far = swap(w_out[0], "shard", 2)
    mixed, first_w, second_near = lax.optimization_barrier((mixed, first_w, second_near))

    after, normed_two, gates, *sent_rows = pl.pallas_call(
        functools.partial(post_kernel, slots),
        in_specs=[SMEM] + [VMEM] * 10,
        out_specs=[VMEM] * (3 + len(block_shapes)),
        out_shape=arrays(((tok, width), F32), ((tok, width), BF16), ((tok, 2), F32), *block_shapes),
        compiler_params=params(),
        cost_estimate=SHORT,
    )(me, tokens, gain_two, router_w, routes, places_row, *mixed, w_o)

    probs = pl.pallas_call(
        functools.partial(attn_prob_kernel, heads),
        in_specs=[SMEM] + [VMEM] * 4 + [ANY],
        out_specs=VMEM,
        out_shape=jax.ShapeDtypeStruct((PROB_ROWS, 2 * heads * SEG), BF16),
        compiler_params=params(),
        cost_estimate=SHORT,
    )(parent_row, queries, keys, lse, bias, after)

    second_far, probs = lax.optimization_barrier((second_far, probs))
    second_w = [w_out[0], second_near, second_far, swap(second_far, "shard", 1)]
    run = functools.partial(run_expert, slots)
    shared = (me, got_grads, router_w, first_w, second_w)
    near_rows = slots.near_exchange(sent_rows[0])
    if slots.cut:
        far_shape = sent_rows[1].shape
        out_all, own_dx, *own_kept = run("own", sent_rows[:1], far_shape, shared, [probs], SHORT)
        far_rows, probs = lax.optimization_barrier((sent_rows[1:], probs))
        far_rows = [swap(block, "expert", rel) for block, rel in zip(far_rows, slots.rels)]
        out_all, near_dx, *near_kept = run("near", [near_rows], near_rows.shape, shared, [probs, own_dx, out_all], SHORT)
        out_all, *far = run("far", far_rows, far_shape, shared, [probs, out_all], LONG)
        dx = [slots.near_exchange(near_dx)] + [swap(block, "expert", rel) for block, rel in zip(far, slots.rels)]
        kept = [own_kept, near_kept, far[4:]]
    else:
        out_all, dx, *all_kept = run("all", [near_rows], near_rows.shape, shared, [probs], SHORT)
        dx, kept = [slots.near_exchange(dx)], [all_kept]
    send_second, keep_second = run_second_grad([k[2] for k in kept], [k[1] for k in kept])
    w_cols, _ = lax.optimization_barrier((w_cols, kept[0][0]))
    w_all = lax.all_gather(w_cols, "shard", axis=0)
    send_first, keep_first = run_first_grad(me, [k[0] for k in kept], [k[3] for k in kept], rows, dx[0], w_all)
    out_all, _ = lax.optimization_barrier((out_all, dx[0]))
    returned = over_experts(out_all)
    dx, send_first, send_second = lax.optimization_barrier((dx, send_first, send_second))

    slot_rows = slots.n_expert * slots.block
    grad_after, gm0, gm1, gm2, gm3, send_wo, keep_wo = pl.pallas_call(
        functools.partial(back_kernel, slots),
        in_specs=[SMEM] + [VMEM] * (len(block_shapes) + 13),
        out_specs=[VMEM] * 7,
        out_shape=arrays(((tok, width), F32), *[((hw, tok), BF16)] * 4, *[((2 * rows, width + 128), BF16)] * 2),
        scratch_shapes=[
            pltpu.VMEM((tok, width), BF16),
            pltpu.VMEM((tok, n_experts), BF16),
            pltpu.VMEM((8, width), F32),
            pltpu.VMEM((width, 128), F32),
            pltpu.VMEM((slot_rows, width), BF16),
        ],
        compiler_params=params(),
        cost_estimate=SHORT,
    )(me_shard, *dx, places, routes, gates, after, gain_two, router_w, cotangent, w_o, normed_two, *mixed)
    grad_mixed = swap_all([gm0, gm1, gm2, gm3], "shard")
    sums = [
        core_sum(send, keep)
        for send, keep in ((send_second, keep_second), (send_first, keep_first), (send_wo, keep_wo))
    ]
    grad_mixed, sums = lax.optimization_barrier((grad_mixed, sums))
    second_sum, first_sum, wo_sum = sums
    second_sum, wo_sum = across_sum(second_sum), across_sum(wo_sum)

    *dqkv, bins = pl.pallas_call(
        functools.partial(attn_backward_kernel, heads),
        in_specs=[SMEM] * 2 + [VMEM] * 5 + [ANY] + [VMEM] * 4,
        out_specs=[VMEM] * 5,
        out_shape=arrays(*[((tok, wide), BF16)] * 4, ((NB, heads * SEG), F32)),
        scratch_shapes=[
            pltpu.VMEM((HW, tree_len), BF16),
            pltpu.VMEM((tree_len, HW), BF16),
            pltpu.VMEM((tree_len, HW), F32),
            pltpu.VMEM((tree_len, HW), F32),
            pltpu.VMEM((2, SEG, heads * SEG), F32),
            pltpu.VMEM((PROB_ROWS, 2 * heads * SEG), BF16),
            pltpu.SemaphoreType.DMA((SEGS // 2,)),
        ],
        compiler_params=params(),
        cost_estimate=BACKWARD,
    )(me_shard, parent_row, queries, keys, values, keys_t, raw, probs, *grad_mixed)
    dqkv_own = swap_all(dqkv, "shard")

    halving = [(1, 2, 4), (2, 1, 4)] if n_expert == 8 else []
    orders = [[0], [0]]
    for i, bits in enumerate(halving):
        for bit in reversed(bits):
            orders[i] = orders[i] + [rel | bit for rel in orders[i]]
    share = rows // len(orders[0])
    block_rows = [3 * share, 2 * share + -(-share // 16) * 8]
    parts = 2 if halving else 1
    out_rows = [count * len(orders[0]) // parts for count in block_rows for _ in range(parts)]
    halves = pl.pallas_call(
        functools.partial(column_grad_kernel, orders, heads),
        in_specs=[SMEM] + [VMEM] * 9,
        out_specs=[VMEM] * len(out_rows),
        out_shape=arrays(*[((count, wide), BF16) for count in out_rows]),
        scratch_shapes=[pltpu.VMEM((width, wide), F32), pltpu.VMEM((rows, width + 128), F32)],
        compiler_params=params(),
        cost_estimate=SHORT,
    )(me_expert if halving else jnp.zeros((1,), jnp.int32), bins, normed_one, *dqkv, *wo_sum)
    if halving:
        pairs = [halves[:2], halves[2:]]
        pairs, second_sum, returned = lax.optimization_barrier((pairs, second_sum, returned))
        for step in range(2):
            sums = [kept.astype(F32) + swap(sent, "expert", bits[step]).astype(F32) for (kept, sent), bits in zip(pairs, halving)]
            pairs = [jnp.split(part.astype(BF16), 2, axis=0) for part in sums]
        sums = [part for kept, sent in pairs for part in (kept, swap(sent, "expert", 4))]
    else:
        sums = lax.psum([part.astype(F32) for part in halves], "expert")
    *cols, more, table = pl.pallas_call(
        split_kernel,
        in_specs=[SMEM] + [VMEM] * len(sums),
        out_specs=[VMEM] * 6,
        out_shape=arrays(*[((share, 3 * hw), BF16)] * 4, ((share, width + 128), BF16), ((NB, wide - 3 * hw), F32)),
        scratch_shapes=[pltpu.VMEM((sum(block_rows), wide), F32)],
        compiler_params=params(),
        cost_estimate=SHORT,
    )(me_shard, *sums)
    table = table[:, :heads].T
    cols, dqkv_own[2] = lax.optimization_barrier((cols, dqkv_own[2]))
    cols, first_sum, dqkv_own = lax.optimization_barrier((swap_all(cols, "shard"), first_sum, dqkv_own))
    cols = pl.pallas_call(
        join_kernel,
        in_specs=[SMEM] + [VMEM] * 5,
        out_specs=VMEM,
        out_shape=jax.ShapeDtypeStruct((share, 4 * width + 128), BF16),
        compiler_params=params(),
        cost_estimate=SHORT,
    )(me_shard, *cols, more)
    grad_w_in = total_sum(across_sum(first_sum))[None]
    returned, second_sum, _ = lax.optimization_barrier((returned, second_sum, cols))
    grad_w_out = total_sum(second_sum)[None]
    output = pl.pallas_call(
        functools.partial(combine_kernel, slots),
        in_specs=[SMEM] + [VMEM] * 3,
        out_specs=VMEM,
        out_shape=jax.ShapeDtypeStruct((tok, width), BF16),
        scratch_shapes=[pltpu.VMEM((slot_rows, width), BF16)],
        compiler_params=params(),
        cost_estimate=SHORT,
    )(me_expert, returned, places, after)
    pieces = [cols]
    if halving:
        other = swap(cols, "expert", 4)
        dqkv_own, other = lax.optimization_barrier((dqkv_own, other))
        pieces = swap_all([jnp.concatenate([cols, other], axis=0)] * 4, "expert")
    grad_tokens = pl.pallas_call(
        final_kernel,
        in_specs=[SMEM] + [VMEM] * 8,
        out_specs=VMEM,
        out_shape=jax.ShapeDtypeStruct((tok, width), BF16),
        compiler_params=params(),
        cost_estimate=SHORT,
    )(me_shard, tokens, gain_one, grad_after, *dqkv_own, w_all)
    pieces, output, grad_tokens, grad_w_in, grad_w_out = lax.optimization_barrier(
        (pieces, output, grad_tokens, grad_w_in, grad_w_out)
    )
    grad_q, grad_k, grad_v, grad_wo, grad_router, grad_gains = pl.pallas_call(
        functools.partial(place_kernel, n_experts),
        in_specs=[SMEM] + [VMEM] * (4 + len(pieces)),
        out_specs=[VMEM] * 6,
        out_shape=arrays(*[((rows, width), F32)] * 4, ((n_experts, rows), F32), ((2, rows), F32)),
        scratch_shapes=[pltpu.VMEM((rows, 128), F32)],
        compiler_params=params(),
        cost_estimate=SHORT,
    )(
        me_expert if halving else jnp.zeros((1,), jnp.int32), w_query, w_key, w_value,
        gain_attn.astype(F32).reshape(1, rows), *pieces,
    )

    return (
        output, grad_tokens, grad_gains[0], grad_q, grad_k, grad_v, grad_wo, table, grad_gains[1], grad_router.T,
        grad_w_in, grad_w_out,
    )


def solution(mesh):
    both, shard = P(("expert", "shard"), None), P("shard", None)
    three = P("expert", "shard", None)
    return jax.shard_map(
        per_device,
        mesh=mesh,
        in_specs=(
            both, P("shard"), shard, shard, shard, shard, shard, P("shard"), shard, three, three, both,
            P("expert", None), both,
        ),
        out_specs=(both, both, P("shard"), shard, shard, shard, shard, shard, P("shard"), shard, three, three),
        check_vma=False,
    )
```

```python
import functools
import math

import jax
import jax.numpy as jnp
from jax import lax
from jax.experimental import pallas as pl
from jax.experimental.pallas import tpu as pltpu
from jax.sharding import PartitionSpec as P

DH = 64
NB = 16
SEG = 128
SEGS = 20
TRUNK = 8
SPARE = 3

THRESHOLDS = (1, 2, 3, 4, 5, 6, 7, 8, 12, 16, 24, 32, 48, 64, 96)
EPS = 1e-06
MASKED = -1e30
HW = 256

F32 = jnp.float32
BF16 = jnp.bfloat16
VMEM = pl.BlockSpec(memory_space=pltpu.VMEM)
SMEM = pl.BlockSpec(memory_space=pltpu.SMEM)
ANY = pl.BlockSpec(memory_space=pl.ANY)

NN = ((1,), (0,))
NT = ((1,), (1,))
TN = ((0,), (0,))


def params(mib=60, **more):
    return pltpu.CompilerParams(vmem_limit_bytes=mib << 20, **more)


SHORT = pl.CostEstimate(flops=0, bytes_accessed=1024, transcendentals=0)
LONG = pl.CostEstimate(flops=1 << 40, bytes_accessed=1 << 32, transcendentals=0)


FORWARD = pl.CostEstimate(flops=30_400_000_000, bytes_accessed=1024, transcendentals=0)
BACKWARD = pl.CostEstimate(flops=22_000_000_000, bytes_accessed=1024, transcendentals=0)


def dot(left, right, contract):
    return lax.dot_general(left, right, (contract, ((), ())), preferred_element_type=F32)


def arrays(*shapes):
    return [jax.ShapeDtypeStruct(shape, dtype) for shape, dtype in shapes]


def rms_parts(values):
    factor = lax.rsqrt(jnp.mean(values * values, axis=-1, keepdims=True) + EPS)
    return values * factor, factor


def rms_grad(grad_out, gain_row, unit_rows, factor):
    scaled = grad_out * gain_row
    return factor * (scaled - unit_rows * jnp.mean(scaled * unit_rows, axis=-1, keepdims=True))


def columns_kernel(me_ref, q_ref, k_ref, v_ref, more_ref, *out_refs):
    groups = len(out_refs)
    depth, width = out_refs[0].shape
    hw = q_ref.shape[1] // groups
    blocks = [
        jnp.concatenate([ref[:, s * hw:(s + 1) * hw] for ref in (q_ref, k_ref, v_ref)], axis=1) for s in range(groups)
    ]
    more = jnp.concatenate(
        [more_ref[...], jnp.zeros((depth, width - 3 * hw - more_ref.shape[1]), BF16)], axis=1
    )
    for bit in (1, 2):
        swapped = (me_ref[0] & bit) != 0
        blocks = [jnp.where(swapped, blocks[i ^ bit], blocks[i]) for i in range(groups)]
    for block, out_ref in zip(blocks, out_refs):
        out_ref[...] = jnp.concatenate([block, more], axis=1)


def project_kernel(
    heads, me_ref, table_ref, w0, w1, w2, w3, t0, t1, t2, t3, before_ref,
    n_ref, q_ref, k_ref, v_ref, kt_ref, vt_ref, w_ref, bias_ref, gain_ref, gain_two_ref, router_ref, w_pad,
):
    step = pl.program_id(0)

    @pl.when(step == 0)
    def _():
        hw = heads * DH
        blank = jnp.zeros((w0.shape[0], HW - hw), BF16)
        for rel, piece_ref in enumerate((w0, w1, w2, w3)):
            depth = piece_ref.shape[0]
            at = pl.ds(pl.multiple_of(jnp.bitwise_xor(me_ref[0], rel) * depth, 16), depth)
            piece = piece_ref[...]
            blank_end = jnp.zeros((depth, w_ref.shape[1] - 3 * hw), BF16)
            w_ref[at, :] = jnp.concatenate([piece[:, :3 * hw], blank_end], axis=1)
            router_ref[at, :] = piece[:, 3 * hw + 2:3 * hw + 2 + router_ref.shape[1]]
            padded = [part for c in range(3) for part in (piece[:, c * hw:(c + 1) * hw], blank)]
            padded.append(piece[:, 3 * hw:3 * hw + 2])
            padded.append(jnp.zeros((depth, w_pad.shape[1] - 3 * HW - 2), BF16))
            w_pad[at, :] = jnp.concatenate(padded, axis=1)
        gains = jnp.transpose(w_pad[:, 3 * HW:].astype(F32))
        gain_ref[...] = gains[0:1]
        gain_two_ref[...] = gains[1:2]
        key = lax.broadcasted_iota(jnp.int32, (SEG, SEG), 0)
        query = lax.broadcasted_iota(jnp.int32, (SEG, SEG), 1)
        bias_ref[0] = jnp.zeros((SEG, heads * SEG), F32)
        bias_ref[3] = jnp.full((SEG, heads * SEG), MASKED, F32)
        for h in range(heads):
            last = table_ref[h, NB - 1]
            at = slice(h * SEG, (h + 1) * SEG)
            for kind, gap in ((1, query - key + SEG), (2, query - key)):
                tile = jnp.zeros((SEG, SEG), F32) + (table_ref[h, 0] - last)
                for i, threshold in enumerate(THRESHOLDS):
                    tile = jnp.where(gap >= threshold, table_ref[h, i + 1] - last, tile)
                bias_ref[kind, :, at] = jnp.where(gap >= 0, tile, MASKED)

    for rel, t_ref in enumerate((t0, t1, t2, t3)):
        @pl.when(step == rel)
        def _(t_ref=t_ref):
            unit, _ = rms_parts(t_ref[...].astype(F32))
            normed = (unit * gain_ref[...]).astype(BF16)
            n_ref[0] = normed
            qkv = dot(normed, w_pad[:, :3 * HW], NN)
            q_ref[...] = qkv[:, :HW].astype(BF16) * jnp.asarray(DH ** -0.5, BF16)
            k_ref[...] = qkv[:, HW:2 * HW].astype(BF16)
            v_ref[...] = qkv[:, 2 * HW:].astype(BF16)
            kt_ref[...] = jnp.transpose(qkv[:, HW:2 * HW]).astype(BF16)
            vt_ref[...] = jnp.transpose(qkv[:, 2 * HW:]).astype(BF16)


def by_head(rows, heads):
    lane = lax.broadcasted_iota(jnp.int32, rows.shape, 1)
    zero = jnp.zeros_like(rows)
    return jnp.concatenate(
        [jnp.where((lane >= h * DH) & (lane < (h + 1) * DH), rows, zero) for h in range(heads)], axis=0
    )


def seg_at(index):
    if isinstance(index, int):
        return slice(index * SEG, (index + 1) * SEG)
    return pl.ds(pl.multiple_of(index * SEG, SEG), SEG)


def head_columns(acc, heads):
    pieces = [acc[h * DH:(h + 1) * DH, h * SEG:(h + 1) * SEG] for h in range(heads)]
    pieces.append(jnp.zeros((HW - heads * DH, SEG), F32))
    return jnp.concatenate(pieces, axis=0)


def pair_bias(bias_ref, first, second):
    return jnp.concatenate([bias_ref[first], bias_ref[second]], axis=1)


def attn_forward_kernel(
    heads, me_ref, parent_ref, q_ref, k_ref, v_ref, vt_ref, bias_ref, o0, o1, o2, o3, raw_ref, lse_ref, out_all
):
    cols = heads * SEG
    trunk_len = TRUNK * SEG
    last = trunk_len - SEG

    def queries(b):
        return by_head(q_ref[seg_at(b), :], heads)

    def finish(b, acc, total, top):
        lse_ref[pl.ds(b * 8, 8), :] = jnp.broadcast_to(top + jnp.log(total), (8, cols))
        columns = head_columns(acc / total, heads)
        raw_ref[:, seg_at(b)] = columns
        out_all[:, seg_at(b)] = columns.astype(BF16)

    for j in range(TRUNK // 2):
        q6 = jnp.concatenate([queries(2 * j), queries(2 * j + 1)], axis=0)
        scores = dot(k_ref[0:(j + 1) * 2 * SEG, :], q6, NT)
        parts = []
        if j > 0:
            far = (2 * j - 1) * SEG
            parts = [scores[:far], scores[far:far + SEG] + pair_bias(bias_ref, 1, 0)]
        parts.append(scores[2 * j * SEG:(2 * j + 1) * SEG] + pair_bias(bias_ref, 2, 1))
        parts.append(scores[(2 * j + 1) * SEG:] + pair_bias(bias_ref, 3, 2))
        top = functools.reduce(jnp.maximum, [jnp.max(part, axis=0, keepdims=True) for part in parts])
        parts = [jnp.exp(part - top) for part in parts]
        total = functools.reduce(jnp.add, [jnp.sum(part, axis=0, keepdims=True) for part in parts])
        acc = dot(vt_ref[:, 0:(j + 1) * 2 * SEG], jnp.concatenate([p.astype(BF16) for p in parts], axis=0), NN)
        for s in range(2):
            at = slice(s * cols, (s + 1) * cols)
            finish(2 * j + s, acc[:, at], total[:, at], top[:, at])

    def other_step(i, carry):
        segs = [TRUNK + 2 * i, TRUNK + 2 * i + 1]
        parents = [parent_ref[b] for b in segs]
        leaf = [(parent >= TRUNK).astype(jnp.int32) for parent in parents]
        q3 = [queries(b) for b in segs]
        q6 = jnp.concatenate(q3, axis=0)
        scores = dot(k_ref[0:trunk_len, :], q6, NT)
        near = scores[last:] + pair_bias(bias_ref, 1 - leaf[0], 1 - leaf[1])
        far = scores[:last]
        extra = []
        for s in range(2):
            keys = jnp.concatenate([k_ref[seg_at(parents[s]), :], k_ref[seg_at(segs[s]), :]], axis=0)
            bias = jnp.concatenate([bias_ref[3 - 2 * leaf[s]], bias_ref[2]], axis=0)
            extra.append(dot(keys, q3[s], NT) + bias)
        top = jnp.maximum(jnp.max(far, axis=0, keepdims=True), jnp.max(near, axis=0, keepdims=True))
        top = jnp.maximum(top, jnp.concatenate([jnp.max(e, axis=0, keepdims=True) for e in extra], axis=1))
        far, near = jnp.exp(far - top), jnp.exp(near - top)
        extra = [jnp.exp(extra[s] - top[:, s * cols:(s + 1) * cols]) for s in range(2)]
        total = jnp.sum(far, axis=0, keepdims=True) + jnp.sum(near, axis=0, keepdims=True)
        total = total + jnp.concatenate([jnp.sum(e, axis=0, keepdims=True) for e in extra], axis=1)
        acc = dot(vt_ref[:, 0:trunk_len], jnp.concatenate([far.astype(BF16), near.astype(BF16)], axis=0), NN)
        for s in range(2):
            at = slice(s * cols, (s + 1) * cols)
            values = jnp.concatenate([vt_ref[:, seg_at(parents[s])], vt_ref[:, seg_at(segs[s])]], axis=1)
            finish(segs[s], acc[:, at] + dot(values, extra[s].astype(BF16), NN), total[:, at], top[:, at])
        return carry

    lax.fori_loop(0, (SEGS - TRUNK) // 2, other_step, 0)
    for rel, o_ref in enumerate((o0, o1, o2, o3)):
        width, count = o_ref.shape
        at = pl.ds(pl.multiple_of(jnp.bitwise_xor(me_ref[0], rel) * count, SEG), count)
        o_ref[...] = out_all[0:width, at]


TRUNK_FIRST = [SEG * j * (j + 1) for j in range(TRUNK // 2 + 1)]
OTHER_ROWS = (TRUNK + 2) * SEG
PROB_ROWS = TRUNK_FIRST[-1] + (SEGS - TRUNK) // 2 * OTHER_ROWS


def attn_prob_kernel(heads, parent_ref, q_ref, k_ref, lse_ref, bias_ref, before_ref, out_ref):
    cols = heads * SEG

    def common(b):
        return by_head(q_ref[seg_at(b), :], heads), lse_ref[pl.ds(b * 8, 8), :][0:1]

    for j in range(TRUNK // 2):
        (qa, la), (qb, lb) = common(2 * j), common(2 * j + 1)
        q6, lse = jnp.concatenate([qa, qb], axis=0), jnp.concatenate([la, lb], axis=1)
        for i in range(j + 1):
            scores = dot(k_ref[2 * i * SEG:2 * (i + 1) * SEG, :], q6, NT)
            if i == j:
                scores = scores + jnp.concatenate([pair_bias(bias_ref, 2, 1), pair_bias(bias_ref, 3, 2)], axis=0)
            if i == j - 1:
                scores = scores + jnp.concatenate([pair_bias(bias_ref, 0, 0), pair_bias(bias_ref, 1, 0)], axis=0)
            first = TRUNK_FIRST[j] + 2 * i * SEG
            out_ref[first:first + 2 * SEG, :] = jnp.exp(scores - lse).astype(BF16)

    def other_step(step, carry):
        segs = [TRUNK + 2 * step, TRUNK + 2 * step + 1]
        parents = [parent_ref[b] for b in segs]
        leaf = [(parent >= TRUNK).astype(jnp.int32) for parent in parents]
        each = [common(b) for b in segs]
        q6, lse = jnp.concatenate([q for q, _ in each], axis=0), jnp.concatenate([l for _, l in each], axis=1)
        base = TRUNK_FIRST[-1] + step * OTHER_ROWS
        for i in range(TRUNK // 2):
            scores = dot(k_ref[2 * i * SEG:2 * (i + 1) * SEG, :], q6, NT)
            if i == TRUNK // 2 - 1:
                near = pair_bias(bias_ref, 1 - leaf[0], 1 - leaf[1])
                scores = scores + jnp.concatenate([jnp.zeros_like(near), near], axis=0)
            at = pl.ds(pl.multiple_of(base + 2 * i * SEG, SEG), 2 * SEG)
            out_ref[at, :] = jnp.exp(scores - lse).astype(BF16)
        extra = []
        for s in range(2):
            keys = jnp.concatenate([k_ref[seg_at(parents[s]), :], k_ref[seg_at(segs[s]), :]], axis=0)
            bias = jnp.concatenate([bias_ref[3 - 2 * leaf[s]], bias_ref[2]], axis=0)
            extra.append(jnp.exp(dot(keys, each[s][0], NT) + bias - each[s][1]).astype(BF16))
        at = pl.ds(pl.multiple_of(base + TRUNK * SEG, SEG), 2 * SEG)
        out_ref[at, :] = jnp.concatenate(extra, axis=1)
        return carry

    lax.fori_loop(0, (SEGS - TRUNK) // 2, other_step, 0)


def attn_backward_kernel(
    heads, me_ref, parent_ref, q_ref, k_ref, v_ref, kt_ref, raw_ref, prob_ref, g0, g1, g2, g3_ref,
    d0, d1, d2, d3, bins_ref, grad_all, dq_all, dk_acc, dv_acc, bins_acc, probs, sem,
):
    def fetch(step):
        if isinstance(step, int):
            at = pl.ds(TRUNK_FIRST[step], TRUNK_FIRST[step + 1] - TRUNK_FIRST[step])
        else:
            at = pl.ds(pl.multiple_of(TRUNK_FIRST[-1] + (step - TRUNK // 2) * OTHER_ROWS, SEG), OTHER_ROWS)
        return pltpu.make_async_copy(prob_ref.at[at, :], probs.at[at, :], sem.at[step])

    for j in range(TRUNK // 2):
        fetch(j).start()

    def start_other(step, carry):
        fetch(step + TRUNK // 2).start()
        return carry

    lax.fori_loop(0, (SEGS - TRUNK) // 2, start_other, 0)
    cols = heads * SEG
    trunk_len = TRUNK * SEG
    dk_acc[...] = jnp.zeros_like(dk_acc)
    dv_acc[...] = jnp.zeros_like(dv_acc)
    bins_acc[...] = jnp.zeros_like(bins_acc)
    for rel, g_ref in enumerate((g0, g1, g2, g3_ref)):
        width, count = g_ref.shape
        at = pl.ds(pl.multiple_of(jnp.bitwise_xor(me_ref[0], rel) * count, SEG), count)
        grad_all[0:width, at] = g_ref[...]
        grad_all[width:HW, at] = jnp.zeros((HW - width, count), BF16)

    def common(b):
        q3 = by_head(q_ref[seg_at(b), :], heads)
        grad = grad_all[:, seg_at(b)].astype(F32)
        product = grad * raw_ref[:, seg_at(b)]
        row_dot = jnp.concatenate(
            [jnp.sum(product[h * DH:(h + 1) * DH], axis=0, keepdims=True) for h in range(heads)], axis=1
        )
        return q3, by_head(jnp.transpose(grad).astype(BF16), heads), row_dot

    def block(prob, values, g, row_dot):
        return prob.astype(F32) * (dot(values, g, NT) - row_dot)

    def write_dq(b, acc):
        dq_all[seg_at(b), :] = (jnp.transpose(head_columns(acc, heads)) * DH ** -0.5).astype(BF16)

    def both(pair):
        return [jnp.concatenate([a, b], axis=0 if a.shape[0] > 1 else 1) for a, b in zip(*pair)]

    for j in range(TRUNK // 2):
        q6, g6, row_dot = both([common(2 * j), common(2 * j + 1)])
        fetch(j).wait()
        kept = []
        for i in range(j + 1):
            at = slice(2 * i * SEG, 2 * (i + 1) * SEG)
            prob = probs[TRUNK_FIRST[j] + 2 * i * SEG:TRUNK_FIRST[j] + 2 * (i + 1) * SEG, :]
            score = block(prob, v_ref[at, :], g6, row_dot)
            if i == j:
                bins_acc[0] += score[:SEG, cols:]
                bins_acc[1] += score[:SEG, :cols] + score[SEG:, cols:]
            if i == j - 1:
                bins_acc[0] += score[SEG:, :cols]
            score = score.astype(BF16)
            dv_acc[at, :] += dot(prob, g6, NN)
            dk_acc[at, :] += dot(score, q6, NN)
            kept.append(score)
        acc = dot(kt_ref[:, 0:(j + 1) * 2 * SEG], jnp.concatenate(kept, axis=0), NN)
        for s in range(2):
            write_dq(2 * j + s, acc[:, s * cols:(s + 1) * cols])

    def other_step(step, carry):
        segs = [TRUNK + 2 * step, TRUNK + 2 * step + 1]
        parents = [parent_ref[b] for b in segs]
        leaf = [(parent >= TRUNK).astype(jnp.int32) for parent in parents]
        each = [common(b) for b in segs]
        q6, g6, row_dot = both(each)
        base = TRUNK_FIRST[-1] + step * OTHER_ROWS
        fetch(step + TRUNK // 2).wait()
        kept = []
        for i in range(TRUNK // 2):
            at = slice(2 * i * SEG, 2 * (i + 1) * SEG)
            prob = probs[pl.ds(pl.multiple_of(base + 2 * i * SEG, SEG), 2 * SEG), :]
            score = block(prob, v_ref[at, :], g6, row_dot)
            if i == TRUNK // 2 - 1:
                for s in range(2):
                    bins_acc[0] += jnp.where(leaf[s] == 0, score[SEG:, s * cols:(s + 1) * cols], 0.0)
            score = score.astype(BF16)
            dv_acc[at, :] += dot(prob, g6, NN)
            dk_acc[at, :] += dot(score, q6, NN)
            kept.append(score)
        acc = dot(kt_ref[:, 0:trunk_len], jnp.concatenate(kept, axis=0), NN)
        for s in range(2):
            q3, g3, row = each[s]
            first, second = seg_at(parents[s]), seg_at(segs[s])
            values = jnp.concatenate([v_ref[first, :], v_ref[second, :]], axis=0)
            keys_t = jnp.concatenate([kt_ref[:, first], kt_ref[:, second]], axis=1)
            at = pl.ds(pl.multiple_of(base + trunk_len, SEG), 2 * SEG)
            prob = probs[at, s * cols:(s + 1) * cols]
            score = block(prob, values, g3, row)
            bins_acc[0] += score[:SEG]
            bins_acc[1] += score[SEG:]
            score = score.astype(BF16)
            grad_v, grad_k = dot(prob, g3, NN), dot(score, q3, NN)
            dv_acc[first, :] += grad_v[:SEG]
            dv_acc[second, :] += grad_v[SEG:]
            dk_acc[first, :] += grad_k[:SEG]
            dk_acc[second, :] += grad_k[SEG:]
            write_dq(segs[s], acc[:, s * cols:(s + 1) * cols] + dot(keys_t, score, NN))
        return carry

    lax.fori_loop(0, (SEGS - TRUNK) // 2, other_step, 0)
    for rel, d_ref in enumerate((d0, d1, d2, d3)):
        count = d_ref.shape[0]
        width = heads * DH
        at = pl.ds(pl.multiple_of(jnp.bitwise_xor(me_ref[0], rel) * count, SEG), count)
        parts = [dq_all[at, :][:, :width], dk_acc[at, :][:, :width].astype(BF16), dv_acc[at, :][:, :width].astype(BF16)]
        parts.append(jnp.zeros((count, d_ref.shape[1] - 3 * width), BF16))
        d_ref[...] = jnp.concatenate(parts, axis=1)
    key = lax.broadcasted_iota(jnp.int32, (SEG, cols), 0)
    query = lax.broadcasted_iota(jnp.int32, (SEG, cols), 1) % SEG
    gap = query - key
    parent_sum, own_sum = bins_acc[0], bins_acc[1]
    lines = [jnp.sum(parent_sum + own_sum, axis=0, keepdims=True)]
    for threshold in THRESHOLDS:
        hit = jnp.where(gap + SEG >= threshold, parent_sum, 0.0) + jnp.where(gap >= threshold, own_sum, 0.0)
        lines.append(jnp.sum(hit, axis=0, keepdims=True))
    bins_ref[...] = jnp.concatenate(lines, axis=0)


class Slots:
    def __init__(self, n_expert, capacity):
        self.n_expert = n_expert
        self.cut = n_expert == 8
        self.block = -(-(capacity + SPARE) // 16) * 16
        if self.cut:
            self.groups = [[0, 1, 4, 5], [2, 3, 6, 7]]
            self.rels = [2, 3, 6, 7]
            self.chunks = [[[0, 1, 2, 3]], [[4], [5], [6], [7]]]
        else:
            self.groups = None
            self.chunks = [[list(range(n_expert))]]
        self.arrays = [array for chunk in self.chunks for array in chunk]

    def block_of(self, expert, me):
        if not self.cut:
            return expert
        rel = jnp.bitwise_xor(expert, me)
        inside = lambda index: (index & 1) | ((index >> 1) & 2)
        return jnp.where((rel & 2) == 0, inside(expert), 4 + inside(rel))

    def expert_of(self, block, me):
        if not self.cut:
            return block
        if not isinstance(block, int) or block < 4:
            return (me & 2) | (block & 1) | ((block & 2) << 1)
        return jnp.bitwise_xor(me, self.rels[block - 4])

    def near_exchange(self, block):
        return lax.all_to_all(block, "expert", split_axis=0, concat_axis=0, tiled=True, axis_index_groups=self.groups)


def over_experts(block):
    return lax.all_to_all(block, "expert", split_axis=0, concat_axis=0, tiled=True)


def swap(block, axis, rel):
    if rel == 0:
        return block
    return lax.ppermute(block, axis, [(i, i ^ rel) for i in range(lax.axis_size(axis))])


def swap_all(blocks, axis):
    return [swap(block, axis, rel) for rel, block in enumerate(blocks)]


def from_all(block):
    near, far = swap(block, "shard", 1), swap(block, "shard", 2)
    return [block, near, far, swap(far, "shard", 1)]


def reorder(parts, me):
    bit = 1
    while bit < len(parts):
        parts = [jnp.where(me & bit, parts[i ^ bit], parts[i]) for i in range(len(parts))]
        bit *= 2
    return parts


def send_rows(slots, rows, places_ref, out_refs):
    tokens = places_ref.shape[1]
    for array, out_ref in zip(slots.arrays, out_refs):
        for i, block in enumerate(array):
            slot = block * slots.block + lax.broadcasted_iota(jnp.int32, (slots.block, tokens), 0)
            hit = (slot == places_ref[0:1, :]) | (slot == places_ref[1:2, :])
            picked = dot(jnp.where(hit, 1.0, 0.0).astype(BF16), rows, NN).astype(BF16)
            out_ref[i * slots.block:(i + 1) * slots.block, :] = picked


def row_at(first, count):
    return pl.ds(first if isinstance(first, int) else pl.multiple_of(first, 16), count)


def diagonal(count):
    return lax.broadcasted_iota(jnp.int32, (count, count), 0) == lax.broadcasted_iota(jnp.int32, (count, count), 1)


def padded_row(row, width):
    count = row.shape[1]
    return row if count == width else jnp.concatenate([row, jnp.zeros((1, width - count), row.dtype)], axis=1)


def dispatch_kernel(slots, me_ref, places_ref, others_ref, rows_ref, *refs):
    out_ref = refs[-1]
    tokens = places_ref.shape[1]
    width = rows_ref.shape[1]
    rows = rows_ref[...]
    count = slots.block

    def one(expert, carry):
        slot = slots.block_of(expert, me_ref[0]) * count + lax.broadcasted_iota(jnp.int32, (count, tokens), 0)
        hot = [jnp.where(slot == places_ref[j:j + 1, :], 1.0, 0.0).astype(BF16) for j in range(2)]
        picked = dot(hot[0] + hot[1], rows, NN)
        ids = sum(dot(others_ref[8 * j:8 * j + 8, :], hot[j], NT) for j in range(2))
        line = lax.broadcasted_iota(jnp.int32, picked.shape, 0)
        picked = jnp.where(line == count - 1, padded_row(ids[0:1], width), picked)
        out_ref[pl.ds(pl.multiple_of(expert * count, 16), count), :] = picked.astype(BF16)
        return carry

    lax.fori_loop(0, slots.n_expert, one, 0, unroll=2)


def post_kernel(
    slots, me_ref, x_ref, gain_ref, router_ref, routes_ref, places_ref, m0, m1, m2, m3, w_ref,
    after_ref, normed_ref, gates_ref, *out_refs,
):
    after = x_ref[...].astype(F32)
    for rel, m_ref in enumerate((m0, m1, m2, m3)):
        after = after + dot(m_ref[...], w_ref[jnp.bitwise_xor(me_ref[1], rel)], TN)
    after_ref[...] = after
    unit, _ = rms_parts(after)
    normed = (unit * gain_ref[...]).astype(BF16)
    normed_ref[...] = normed
    send_rows(slots, normed_ref[...], places_ref, out_refs)
    logits = dot(normed, router_ref[...], NN)
    expert = lax.broadcasted_iota(jnp.int32, logits.shape, 1)
    first = jnp.sum(jnp.where(expert == routes_ref[:, 0:1], logits, 0.0), axis=-1, keepdims=True)
    second = jnp.sum(jnp.where(expert == routes_ref[:, 1:2], logits, 0.0), axis=-1, keepdims=True)
    top = jnp.maximum(first, second)
    first, second = jnp.exp(first - top), jnp.exp(second - top)
    gates_ref[...] = jnp.concatenate([first / (first + second), second / (first + second)], axis=1)


def expert_kernel(slots, kind, sizes, before, me_ref, *refs):
    refs = list(refs)
    take = lambda n: [refs.pop(0) for _ in range(n)]
    x_refs = take(sizes[0])
    g_all, router_ref = take(2)
    first_refs, second_refs = take(4), take(4)
    extra = take(before)
    own_ref = extra[1] if before == 3 else None
    (out_all,) = take(1)
    dx_refs = take(sizes[1])
    rows_out, grad_out, act_ref, inner_ref, rows_ref, grad_ref, first_buf, second_buf, g_buf, out_buf, out_acc, dx_acc, gate_acc, gates_acc, sem, in_sem, keep_sem = refs
    step = pl.program_id(0)
    slot = lax.rem(step, 2)
    total, width = rows_ref.shape
    depth, units = first_refs[0].shape[0], second_buf.shape[1]

    def fetch(rel, slot):
        column = pl.multiple_of(jnp.bitwise_xor(me_ref[1], rel) * units, 128)
        copies = [pltpu.make_async_copy(second_refs[rel], second_buf.at[slot], in_sem.at[slot, 4])]
        for piece, ref in enumerate(first_refs):
            row = pl.multiple_of(jnp.bitwise_xor(me_ref[1], piece) * depth, 16)
            copies.append(
                pltpu.make_async_copy(
                    ref.at[:, pl.ds(column, units)], first_buf.at[slot, pl.ds(row, depth), :], in_sem.at[slot, piece]
                )
            )
        return copies

    @pl.when(step == 0)
    def _():
        for copy in fetch(0, 0):
            copy.start()

    for rel in range(4):
        @pl.when(step == rel)
        def _(rel=rel):
            if rel < 3:
                for copy in fetch(rel + 1, (rel + 1) % 2):
                    copy.start()
    rows = slots.block
    mine = slots.block_of(me_ref[0], me_ref[0])
    if kind == "own":
        pieces = [(mine, x_refs[0], mine * rows, dx_refs[0], 0)]
    elif kind == "near":
        blocks = [jnp.bitwise_xor(mine, i) for i in (1, 2, 3)]
        pieces = [(block, x_refs[0], block * rows, dx_refs[0], block * rows) for block in blocks]
    elif kind == "far":
        pieces = [(4 + i, x_ref, 0, dx_ref, 0) for i, (x_ref, dx_ref) in enumerate(zip(x_refs, dx_refs))]
    else:
        pieces = [(block, x_refs[0], block * rows, dx_refs[0], block * rows) for block in range(slots.n_expert)]
    pieces = [(*piece, i * rows) for i, piece in enumerate(pieces)]

    def home(block):
        return pl.ds(pl.multiple_of(slots.expert_of(block, me_ref[0]) * rows, 16), rows)

    @pl.when(step == 0)
    def _():
        copies = [
            pltpu.make_async_copy(g_all.at[home(block), :], g_buf.at[pl.ds(first, rows), :], sem.at[i])
            for i, (block, *_, first) in enumerate(pieces)
        ]
        for copy in copies:
            copy.start()
        out_acc[...] = jnp.zeros_like(out_acc)
        dx_acc[...] = jnp.zeros_like(dx_acc)
        for _, x_ref, inside, _, _, first in pieces:
            rows_ref[first:first + rows, :] = x_ref[row_at(inside, rows), :]
        for copy in copies:
            copy.wait()
        for *_, first in pieces:
            at = slice(first, first + rows)
            grads = g_buf[at, :].astype(F32)
            other = jnp.sum(jnp.where(diagonal(rows), grads[rows - 1:, :rows], 0.0), axis=1, keepdims=True).astype(jnp.int32)
            logits = dot(rows_ref[at, :], router_ref[...], NN)
            expert = lax.broadcasted_iota(jnp.int32, logits.shape, 1)
            mine = jnp.sum(jnp.where(expert == me_ref[0], logits, 0.0), axis=-1, keepdims=True)
            its = jnp.sum(jnp.where(expert == other, logits, 0.0), axis=-1, keepdims=True)
            top = jnp.maximum(mine, its)
            mine, its = jnp.exp(mine - top), jnp.exp(its - top)
            line = lax.broadcasted_iota(jnp.int32, grads.shape, 0)
            gate = mine / (mine + its)
            gate_acc[at, :] = jnp.broadcast_to(gate, (rows, 128))
            grad_ref[at, :] = jnp.where(line < rows - SPARE, gate * grads, 0.0).astype(BF16)

    keeps = [
        pltpu.make_async_copy(rows_ref, rows_out, keep_sem.at[0]),
        pltpu.make_async_copy(grad_ref, grad_out, keep_sem.at[1]),
    ]

    @pl.when(step == 0)
    def _():
        for copy in keeps:
            copy.start()

    for rel in range(4):
        @pl.when(step == rel)
        def _(rel=rel):
            for copy in fetch(rel, rel % 2):
                copy.wait()

    parts = 1
    while total // parts > 512 or total % parts or (total // parts) % 16:
        parts += 1
    part = total // parts
    for i in range(parts):
        at = slice(i * part, (i + 1) * part)
        first_w, second_w = first_buf[slot], second_buf[slot]
        value = dot(rows_ref[at, :], first_w, NN)
        grad_act = dot(grad_ref[at, :], second_w, NT)
        square = value * value
        half = 0.5 * value
        scale = 0.7978845608028654
        th = jnp.tanh(value * (scale + (scale * 0.044715) * square))
        act = (half + half * th).astype(BF16)
        slope = 0.5 + 0.5 * th + (half * (1.0 - th * th)) * (scale + (3 * scale * 0.044715) * square)
        inner = (grad_act * slope).astype(BF16)
        act_ref[at, :] = act
        inner_ref[at, :] = inner
        out_acc[at, :] += dot(act, second_w, NN)
        dx_acc[at, :] += dot(inner, first_w, NT)

    @pl.when(step == pl.num_programs(0) - 1)
    def _():
        for *_, first in pieces:
            at = slice(first, first + rows)
            out = out_acc[at, :].astype(BF16).astype(F32)
            gates = jnp.sum(out * g_buf[at, :].astype(F32), axis=1, keepdims=True)
            gates_acc[at, :] = jnp.broadcast_to(gates, (rows, 128))
            out_buf[at, :] = (gate_acc[at, 0:1] * out).astype(BF16)
        copies = [
            pltpu.make_async_copy(out_buf.at[pl.ds(first, rows), :], out_all.at[home(block), :], sem.at[i])
            for i, (block, *_, first) in enumerate(pieces)
        ]
        for copy in copies:
            copy.start()
        if own_ref is not None:
            dx_refs[0][row_at(mine * rows, rows), :] = own_ref[...]
        for _, _, _, dx_ref, inside, first in pieces:
            at = slice(first, first + rows)
            gates = gates_acc[at, 0:1]
            gates = jnp.sum(jnp.where(diagonal(rows), gates, 0.0), axis=0, keepdims=True)
            dx_ref[row_at(inside, rows), :] = dx_acc[at, :].astype(BF16)
            tail = dx_acc[first + rows - 16:first + rows, :]
            line = lax.broadcasted_iota(jnp.int32, tail.shape, 0)
            for place in range(SPARE):
                piece = gates.astype(BF16).astype(F32)
                gates = gates - piece
                tail = jnp.where(line == 16 - SPARE + place, padded_row(piece, width), tail)
            dx_ref[row_at(inside + rows - 16, 16), :] = tail.astype(BF16)
        for copy in [*copies, *keeps]:
            copy.wait()


def run_expert(slots, kind, blocks, dx_shape, shared, before, estimate):
    me, g_all, router, first_w, second_w = shared
    hidden, width = first_w[0].shape[1], router.shape[0]
    total = slots.block * {"own": 1, "near": 3, "far": 4, "all": slots.n_expert}[kind]
    block = hidden // 4
    whole = lambda a: pl.BlockSpec(a.shape, lambda i: (0, 0))
    column = pl.BlockSpec((total, block), lambda i: (0, i))
    fresh = len(before) < 2
    dx = [jax.ShapeDtypeStruct(dx_shape, BF16)] * (4 if kind == "far" else 1)
    inputs = [me, *blocks, g_all, router, *first_w, *second_w, *before]
    before_specs = [ANY] * len(before)
    if len(before) == 3:
        before_specs[1] = whole(before[1])
    return pl.pallas_call(
        functools.partial(expert_kernel, slots, kind, (len(blocks), len(dx)), len(before)),
        grid=(4,),
        in_specs=[SMEM] + [whole(b) for b in blocks] + [ANY, whole(router)] + [ANY] * 8 + before_specs,
        out_specs=[ANY] + [whole(b) for b in dx] + [ANY, ANY, column, column],
        out_shape=arrays(
            (g_all.shape, BF16), *[(b.shape, BF16) for b in dx], *[((total, width), BF16)] * 2, *[((total, hidden), BF16)] * 2
        ),
        scratch_shapes=[
            pltpu.VMEM((total, width), BF16),
            pltpu.VMEM((total, width), BF16),
            pltpu.VMEM((2, width, block), BF16),
            pltpu.VMEM((2, block, width), BF16),
            pltpu.VMEM((total, width), BF16),
            pltpu.VMEM((total, width), BF16),
            pltpu.VMEM((total, width), F32),
            pltpu.VMEM((total, width), F32),
            pltpu.VMEM((total, 128), F32),
            pltpu.VMEM((total, 128), F32),
            pltpu.SemaphoreType.DMA((total // slots.block,)),
            pltpu.SemaphoreType.DMA((2, 5)),
            pltpu.SemaphoreType.DMA((2,)),
        ],
        input_output_aliases={} if fresh else {len(inputs) - 1: 0},
        compiler_params=params(dimension_semantics=("arbitrary",)),
        cost_estimate=estimate,
    )(*inputs)


def first_grad_kernel(parts, me_ref, *refs):
    send_ref, keep_ref, total = refs[-3:]
    total[...] = sum(dot(x[...], inner[...], TN) for x, inner in zip(refs[:parts], refs[parts:2 * parts]))
    depth = send_ref.shape[0] // 2
    for rel in range(4):
        ref = (keep_ref, send_ref)[rel % 2]
        row = pl.multiple_of(jnp.bitwise_xor(me_ref[1], rel) * depth, 16)
        at = rel // 2 * depth
        ref[at:at + depth, :] = total[pl.ds(row, depth), :].astype(BF16)


def run_first_grad(me, rows, inners, depth, *after):
    width, hidden = rows[0].shape[1], inners[0].shape[1]
    block = hidden // 4
    column = pl.BlockSpec((2 * depth, block), lambda i, me_ref: (0, jnp.bitwise_xor(me_ref[1], i)))
    return pl.pallas_call(
        functools.partial(first_grad_kernel, len(rows)),
        grid_spec=pltpu.PrefetchScalarGridSpec(
            num_scalar_prefetch=1,
            grid=(4,),
            in_specs=[pl.BlockSpec(a.shape, lambda i, me_ref: (0, 0)) for a in rows]
            + [pl.BlockSpec((a.shape[0], block), lambda i, me_ref: (0, i)) for a in inners]
            + [ANY] * len(after),
            out_specs=[column, column],
            scratch_shapes=[pltpu.VMEM((width, block), F32)],
        ),
        out_shape=arrays(*[((2 * depth, hidden), BF16)] * 2),
        compiler_params=params(dimension_semantics=("arbitrary",)),
        cost_estimate=SHORT,
    )(me, *rows, *inners, *after)


def second_grad_kernel(parts, *refs):
    send_ref, keep_ref = refs[2 * parts:]
    step = pl.program_id(0)
    block = sum(dot(act[...], g[...], TN) for act, g in zip(refs[:parts], refs[parts:2 * parts])).astype(BF16)

    @pl.when(step < 2)
    def _():
        send_ref[...] = block

    @pl.when(step >= 2)
    def _():
        keep_ref[...] = block


def run_second_grad(acts, grads):
    width, hidden = grads[0].shape[1], acts[0].shape[1]
    block = hidden // 4
    return pl.pallas_call(
        functools.partial(second_grad_kernel, len(acts)),
        grid=(4,),
        in_specs=[pl.BlockSpec((a.shape[0], block), lambda i: (0, 2 * (i % 2) + 1 - i // 2)) for a in acts]
        + [pl.BlockSpec(a.shape, lambda i: (0, 0)) for a in grads],
        out_specs=[
            pl.BlockSpec((block, width), lambda i: (jnp.minimum(i, 1), 0)),
            pl.BlockSpec((block, width), lambda i: (jnp.maximum(i - 2, 0), 0)),
        ],
        out_shape=arrays(*[((2 * block, width), BF16)] * 2),
        compiler_params=params(dimension_semantics=("arbitrary",)),
        cost_estimate=SHORT,
    )(*acts, *grads)


def core_sum(send, keep):
    near = swap(send, "shard", 1)
    half = keep.shape[0] // 2
    other = (keep[half:].astype(F32) + near[half:].astype(F32)).astype(BF16)
    return keep, near, other


def across_sum(parts):
    keep, near, other = parts
    return keep, near, swap(other, "shard", 2)


def total_sum(parts):
    keep, near, far = parts
    half = keep.shape[0] // 2
    return keep[:half].astype(F32) + near[:half].astype(F32) + far.astype(F32)


def gather_blocks(slots, refs, scratch):
    for array, ref in zip(slots.arrays, refs):
        scratch[array[0] * slots.block:(array[-1] + 1) * slots.block, :] = ref[...]


def back_kernel(slots, me_ref, *refs):
    refs_left = list(refs)
    take = lambda n: [refs_left.pop(0) for _ in range(n)]
    ret_refs = take(len(slots.arrays))
    places_ref, routes_ref, gates_ref, after_ref, gain_ref, router_ref, g_ref = take(7)
    w_ref, normed_ref = take(2)
    m_refs = take(4)
    (grad_after_ref,) = take(1)
    mixed_refs = take(4)
    send_ref, keep_ref, branch_ref, glogits_ref, ggain_ref, more, scratch = refs_left
    tokens = after_ref.shape[0]
    part = tokens // 2
    gather_blocks(slots, ret_refs, scratch)
    pieces = []
    for end in range(slots.block, scratch.shape[0] + 1, slots.block):
        tail = scratch[end - 16:end, :].astype(F32)[16 - SPARE:, :slots.block]
        pieces.append(jnp.sum(tail, axis=0, keepdims=True))
    gg = jnp.concatenate(pieces, axis=1)
    ggain_ref[...] = jnp.zeros_like(ggain_ref)

    def one(i, carry):
        at = pl.ds(pl.multiple_of(i * part, part), part)
        slot = lax.broadcasted_iota(jnp.int32, (part, gg.shape[1]), 1)
        hit0, hit1 = slot == places_ref[at, 0:1], slot == places_ref[at, 1:2]
        gg0 = jnp.sum(jnp.where(hit0, gg, 0.0), axis=-1, keepdims=True)
        gg1 = jnp.sum(jnp.where(hit1, gg, 0.0), axis=-1, keepdims=True)
        total = dot(jnp.where(hit0 | hit1, 1.0, 0.0).astype(BF16), scratch[...], NN)
        gate0, gate1 = gates_ref[at, 0:1], gates_ref[at, 1:2]
        mean = gate0 * gg0 + gate1 * gg1
        expert = lax.broadcasted_iota(jnp.int32, (part, router_ref.shape[1]), 1)
        glogits = jnp.where(expert == routes_ref[at, 0:1], gate0 * (gg0 - mean), 0.0) + jnp.where(
            expert == routes_ref[at, 1:2], gate1 * (gg1 - mean), 0.0
        )
        glogits = glogits.astype(BF16)
        glogits_ref[at, :] = glogits
        incoming = dot(glogits, router_ref[...], NT) + total
        unit, factor = rms_parts(after_ref[at, :])
        grad_after = g_ref[at, :].astype(F32) + rms_grad(incoming, gain_ref[...], unit, factor)
        ggain_ref[0:1, :] += jnp.sum(incoming * unit, axis=0, keepdims=True)
        grad_after_ref[at, :] = grad_after
        branch = grad_after.astype(BF16)
        branch_ref[at, :] = branch
        return carry

    lax.fori_loop(0, tokens // part, one, 0, unroll=2)
    for rel, mixed_ref in enumerate(mixed_refs):
        mixed_ref[...] = dot(w_ref[jnp.bitwise_xor(me_ref[0], rel)], branch_ref[...], NT).astype(BF16)
    width = branch_ref.shape[1]
    grad_router = dot(normed_ref[...], glogits_ref[...], TN)
    gain = jnp.transpose(jnp.concatenate([ggain_ref[...]] * 16, axis=0))[:, 0:1]
    blank = jnp.zeros((width, more.shape[1] - grad_router.shape[1] - 1), F32)
    more[...] = jnp.concatenate([grad_router, gain, blank], axis=1)
    for rel, m_ref in enumerate(m_refs):
        ref = (keep_ref, send_ref)[rel % 2]
        count = m_ref.shape[0]
        at = slice(rel // 2 * count, (rel // 2 + 1) * count)
        ref[at, 0:width] = dot(m_ref[...], branch_ref[...], NN).astype(BF16)
        row = pl.multiple_of(jnp.bitwise_xor(me_ref[0], rel) * count, 16)
        ref[at, width:] = more[pl.ds(row, count), :].astype(BF16)


def combine_kernel(slots, me_ref, ret_ref, places_ref, after_ref, out_ref, scratch):
    part = after_ref.shape[0] // 2
    for block in range(slots.n_expert):
        first = pl.multiple_of(slots.expert_of(block, me_ref[0]) * slots.block, 16)
        scratch[block * slots.block:(block + 1) * slots.block, :] = ret_ref[pl.ds(first, slots.block), :]

    def one(i, carry):
        at = pl.ds(pl.multiple_of(i * part, part), part)
        slot = lax.broadcasted_iota(jnp.int32, (part, scratch.shape[0]), 1)
        hit = (slot == places_ref[at, 0:1]) | (slot == places_ref[at, 1:2])
        total = after_ref[at, :] + dot(jnp.where(hit, 1.0, 0.0).astype(BF16), scratch[...], NN)
        out_ref[at, :] = total.astype(BF16)
        return carry

    lax.fori_loop(0, after_ref.shape[0] // part, one, 0, unroll=2)


def final_kernel(me_ref, x_ref, gain_ref, after_ref, d0, d1, d2, d3, w_ref, out_ref):
    grad = sum(
        dot(d_ref[...], w_ref[jnp.bitwise_xor(me_ref[0], rel)], NT) for rel, d_ref in enumerate((d0, d1, d2, d3))
    )
    unit, factor = rms_parts(x_ref[...].astype(F32))
    out_ref[...] = (after_ref[...] + rms_grad(grad, gain_ref[...], unit, factor)).astype(BF16)


def column_grad_kernel(
    orders, heads, me_ref, bins_ref, n_ref, d0, d1, d2, d3, wk_ref, wn_ref, wf_ref, *refs
):
    *out_refs, acc, more = refs
    acc[...] = sum(dot(n_ref[rel], d_ref[...], TN) for rel, d_ref in enumerate((d0, d1, d2, d3)))
    rows = wf_ref.shape[0]
    more[...] = wk_ref[0:rows, :].astype(F32) + wn_ref[0:rows, :].astype(F32) + wf_ref[...].astype(F32)
    cols = 3 * heads * DH
    wide = acc.shape[1]
    lane = lax.broadcasted_iota(jnp.int32, (NB, wide), 1)
    table = jnp.zeros((NB, wide), F32)
    for h in range(heads):
        above = jnp.sum(bins_ref[:, h * SEG:(h + 1) * SEG], axis=1, keepdims=True)
        column = above - jnp.concatenate([above[1:], jnp.zeros((1, 1), F32)], axis=0)
        column = jnp.concatenate([column[:-1], -jnp.sum(column[:-1], axis=0, keepdims=True)], axis=0)
        table = jnp.where(lane == cols + h, column, table)
    share = rows // len(orders[0])
    half = share // 2

    def block_of(rel):
        first = jnp.bitwise_xor(me_ref[0], rel) * share
        at = lambda start: pl.ds(pl.multiple_of(start + first, 8), share)
        block = [acc[at(p * rows), :] for p in range(4)]
        block[0] = jnp.concatenate([block[0][:NB] + table, block[0][NB:]], axis=0)
        others = more[at(0), :]
        rest = others[:, wide:]
        folded = [rest[:half], rest[half:], jnp.zeros((half, wide - 2 * rest.shape[1]), F32)]
        block += [others[:, :wide], jnp.concatenate(folded, axis=1)]
        if half % 8:
            block.append(jnp.zeros((-half % 8, wide), F32))
        return block[:3], block[3:]

    blocks = {rel: block_of(rel) for rel in orders[0]}
    count = len(out_refs) // 2
    for part, order in enumerate(orders):
        for i in range(count):
            mine = order[i * len(order) // count:(i + 1) * len(order) // count]
            rows_of = [row for rel in mine for row in blocks[rel][part]]
            out_refs[part * count + i][...] = jnp.concatenate(rows_of, axis=0).astype(BF16)


def split_kernel(me_ref, *refs):
    *in_refs, b0, b1, b2, b3, more_ref, table_ref, total = refs
    share, cols = b0.shape
    count = len(in_refs) // 2
    total[0:3 * share, :] = sum(ref[...].astype(F32) for ref in in_refs[:count])
    total[3 * share:, :] = sum(ref[...].astype(F32) for ref in in_refs[count:])
    wide = total.shape[1]
    for rel, ref in enumerate((b0, b1, b2, b3)):
        at = pl.ds(pl.multiple_of(jnp.bitwise_xor(me_ref[0], rel) * share, 8), share)
        ref[...] = total[at, :][:, :cols].astype(BF16)
    folded = total[5 * share:5 * share + share // 2, :]
    rest = more_ref.shape[1] - wide
    folded = jnp.concatenate([folded[:, :rest], folded[:, rest:2 * rest]], axis=0)
    more_ref[...] = jnp.concatenate([total[4 * share:5 * share, :], folded], axis=1).astype(BF16)
    table_ref[...] = total[0:NB, wide - table_ref.shape[1]:]


def join_kernel(me_ref, p0, p1, p2, p3, more_ref, out_ref):
    parts = [ref[...] for ref in (p0, p1, p2, p3)]
    for bit in (1, 2):
        swapped = (me_ref[0] & bit) != 0
        parts = [jnp.where(swapped, parts[i ^ bit], parts[i]) for i in range(4)]
    hw = p0.shape[1] // 3
    out_ref[...] = jnp.concatenate(
        [part[:, c * hw:(c + 1) * hw] for c in range(3) for part in parts] + [more_ref[...]], axis=1
    )


def place_kernel(experts, me_ref, wq_ref, wk_ref, wv_ref, gain_in_ref, *refs):
    *piece_refs, q_ref, k_ref, v_ref, o_ref, router_ref, gains_ref, more = refs
    width = q_ref.shape[1]
    count = piece_refs[0].shape[0] // (2 if len(piece_refs) > 1 else 1)
    for rel, at_row, piece_ref in [
        (rel | (first // count) * 4, first, ref) for rel, ref in enumerate(piece_refs) for first in range(0, ref.shape[0], count)
    ]:
        at = pl.ds(pl.multiple_of(jnp.bitwise_xor(me_ref[0], rel) * count, 8), count)
        piece = piece_ref[at_row:at_row + count, :].astype(F32)
        for c, out_ref in enumerate((q_ref, k_ref, v_ref, o_ref)):
            out_ref[at, :] = piece[:, c * width:(c + 1) * width]
        more[at, :] = piece[:, 4 * width:]
    total = sum(
        w_ref[...].astype(F32) * out_ref[...] for w_ref, out_ref in ((wq_ref, q_ref), (wk_ref, k_ref), (wv_ref, v_ref))
    )
    rows = total.shape[0]
    lane = lax.broadcasted_iota(jnp.int32, more.shape, 1)
    columns = jnp.where(lane == experts + 1, jnp.sum(total, axis=1, keepdims=True), more[...])
    columns = jnp.concatenate([columns, jnp.zeros((-rows % 128, columns.shape[1]), F32)], axis=0)
    columns = jnp.transpose(columns)[:, :rows]
    router_ref[...] = columns[0:experts]
    gains_ref[0:1, :] = columns[experts + 1:experts + 2] / gain_in_ref[...]
    gains_ref[1:2, :] = columns[experts:experts + 1]


def per_device(
    tokens, gain_attn, w_query, w_key, w_value, w_output, rel_table, gain_moe, router,
    w_in, w_out, routes, parents, cotangent,
):
    n_shard = lax.axis_size("shard")
    n_expert = lax.axis_size("expert")
    tok, width = tokens.shape
    tree_len = tok * n_shard
    n_experts = router.shape[1]
    heads = rel_table.shape[0]
    hw = heads * DH
    wide = -(-3 * hw // 128) * 128
    rows = width // n_shard
    slots = Slots(n_expert, max(2, tok * 20 // (7 * n_experts)))
    me_s, me_e = lax.axis_index("shard").astype(jnp.int32), lax.axis_index("expert").astype(jnp.int32)
    me_shard, me_expert, me = me_s.reshape(1), me_e.reshape(1), jnp.stack([me_e, me_s])

    more = jnp.concatenate([gain_attn[:, None], gain_moe[:, None], router], axis=1)
    w_rel = pl.pallas_call(
        columns_kernel,
        in_specs=[SMEM] + [VMEM] * 4,
        out_specs=[VMEM] * n_shard,
        out_shape=arrays(*[((rows, -(-(3 * hw + 2 + n_experts) // 128) * 128), BF16)] * n_shard),
        compiler_params=params(),
        cost_estimate=SHORT,
    )(me_shard, w_query, w_key, w_value, more)
    near_tokens, far_tokens = swap(tokens, "shard", 1), swap(tokens, "shard", 2)
    w_pieces = swap_all(w_rel, "shard")

    expert_range = jnp.arange(n_experts, dtype=jnp.int32)
    flat_routes = routes.reshape(-1)
    expert_hot = (flat_routes[:, None] == expert_range[None, :]).astype(jnp.int32)
    earlier = jnp.cumsum(expert_hot, axis=0) - expert_hot
    rank = jnp.sum(earlier * expert_hot, axis=-1)
    places = (slots.block_of(flat_routes, me_e) * slots.block + rank).reshape(tok, 2)
    places_row = places.T
    others = jnp.repeat(routes.T[::-1], 8, axis=0).astype(BF16)
    block_shapes = [((len(array) * slots.block, width), BF16) for array in slots.arrays]

    sent_grads = pl.pallas_call(
        functools.partial(dispatch_kernel, slots),
        in_specs=[SMEM] + [VMEM] * 3 + [ANY],
        out_specs=VMEM,
        out_shape=jax.ShapeDtypeStruct((n_expert * slots.block, width), BF16),
        compiler_params=params(),
        cost_estimate=SHORT,
    )(me_expert, places_row, others, cotangent, w_rel[0])
    got_grads = over_experts(sent_grads)
    far_tokens, _, w_pieces = lax.optimization_barrier((far_tokens, sent_grads, w_pieces))
    tree = [tokens, near_tokens, far_tokens, swap(far_tokens, "shard", 1)]

    place = lambda i, me_ref: (jnp.bitwise_xor(me_ref[0], i), 0)
    place_t = lambda i, me_ref: (0, jnp.bitwise_xor(me_ref[0], i))
    fixed = [
        ((width, wide), BF16), ((4, SEG, heads * SEG), F32), *[((1, width), F32)] * 2, ((width, n_experts), BF16),
    ]
    normed_one, queries, keys, values, keys_t, values_t, w_cols, bias, gain_one, gain_two, router_w = pl.pallas_call(
        functools.partial(project_kernel, heads),
        grid_spec=pltpu.PrefetchScalarGridSpec(
            num_scalar_prefetch=1,
            grid=(n_shard,),
            in_specs=[SMEM] + [VMEM] * 8 + [ANY],
            out_specs=[pl.BlockSpec((1, tok, width), lambda i, me_ref: (i, 0, 0))]
            + [pl.BlockSpec((tok, HW), place)] * 3
            + [pl.BlockSpec((HW, tok), place_t)] * 2
            + [pl.BlockSpec(shape, lambda i, me_ref, shape=shape: (0,) * len(shape)) for shape, _ in fixed],
            scratch_shapes=[pltpu.VMEM((width, 3 * HW + 128), BF16)],
        ),
        out_shape=arrays(
            ((n_shard, tok, width), BF16), *[((tree_len, HW), BF16)] * 3, *[((HW, tree_len), BF16)] * 2, *fixed
        ),
        compiler_params=params(dimension_semantics=("arbitrary",)),
        cost_estimate=SHORT,
    )(me_shard, rel_table.astype(F32), *w_pieces, *tree, sent_grads)
    parent_row = parents[0]
    *mixed, raw, lse = pl.pallas_call(
        functools.partial(attn_forward_kernel, heads),
        in_specs=[SMEM] * 2 + [VMEM] * 5,
        out_specs=[VMEM] * 6,
        out_shape=arrays(*[((hw, tok), BF16)] * 4, ((HW, tree_len), F32), ((SEGS * 8, heads * SEG), F32)),
        scratch_shapes=[pltpu.VMEM((HW, tree_len), BF16)],
        compiler_params=params(),
        cost_estimate=FORWARD,
    )(me_shard, parent_row, queries, keys, values, values_t, bias)
    first_far = swap(w_in[0], "shard", 2)
    w_o = lax.all_gather(w_output, "shard", axis=0)
    mixed, first_far, w_o = lax.optimization_barrier((mixed, first_far, w_o))
    mixed = swap_all(mixed, "shard")
    first_w = [w_in[0], swap(w_in[0], "shard", 1), first_far, swap(first_far, "shard", 1)]
    second_near = swap(w_out[0], "shard", 1)
    w_out, w_cols, _ = lax.optimization_barrier((w_out, w_cols, mixed))
    second_far = swap(w_out[0], "shard", 2)
    mixed, first_w, second_near = lax.optimization_barrier((mixed, first_w, second_near))

    after, normed_two, gates, *sent_rows = pl.pallas_call(
        functools.partial(post_kernel, slots),
        in_specs=[SMEM] + [VMEM] * 10,
        out_specs=[VMEM] * (3 + len(block_shapes)),
        out_shape=arrays(((tok, width), F32), ((tok, width), BF16), ((tok, 2), F32), *block_shapes),
        compiler_params=params(),
        cost_estimate=SHORT,
    )(me, tokens, gain_two, router_w, routes, places_row, *mixed, w_o)

    probs = pl.pallas_call(
        functools.partial(attn_prob_kernel, heads),
        in_specs=[SMEM] + [VMEM] * 4 + [ANY],
        out_specs=VMEM,
        out_shape=jax.ShapeDtypeStruct((PROB_ROWS, 2 * heads * SEG), BF16),
        compiler_params=params(),
        cost_estimate=SHORT,
    )(parent_row, queries, keys, lse, bias, after)

    second_far, probs = lax.optimization_barrier((second_far, probs))
    second_w = [w_out[0], second_near, second_far, swap(second_far, "shard", 1)]
    run = functools.partial(run_expert, slots)
    shared = (me, got_grads, router_w, first_w, second_w)
    near_rows = slots.near_exchange(sent_rows[0])
    if slots.cut:
        far_shape = sent_rows[1].shape
        out_all, own_dx, *own_kept = run("own", sent_rows[:1], far_shape, shared, [probs], SHORT)
        far_rows, probs = lax.optimization_barrier((sent_rows[1:], probs))
        far_rows = [swap(block, "expert", rel) for block, rel in zip(far_rows, slots.rels)]
        out_all, near_dx, *near_kept = run("near", [near_rows], near_rows.shape, shared, [probs, own_dx, out_all], SHORT)
        out_all, *far = run("far", far_rows, far_shape, shared, [probs, out_all], LONG)
        dx = [slots.near_exchange(near_dx)] + [swap(block, "expert", rel) for block, rel in zip(far, slots.rels)]
        kept = [own_kept, near_kept, far[4:]]
    else:
        out_all, dx, *all_kept = run("all", [near_rows], near_rows.shape, shared, [probs], SHORT)
        dx, kept = [slots.near_exchange(dx)], [all_kept]
    send_second, keep_second = run_second_grad([k[2] for k in kept], [k[1] for k in kept])
    w_cols, _ = lax.optimization_barrier((w_cols, kept[0][0]))
    w_all = lax.all_gather(w_cols, "shard", axis=0)
    send_first, keep_first = run_first_grad(me, [k[0] for k in kept], [k[3] for k in kept], rows, dx[0], w_all)
    out_all, _ = lax.optimization_barrier((out_all, dx[0]))
    returned = over_experts(out_all)
    dx, send_first, send_second = lax.optimization_barrier((dx, send_first, send_second))

    slot_rows = slots.n_expert * slots.block
    grad_after, gm0, gm1, gm2, gm3, send_wo, keep_wo = pl.pallas_call(
        functools.partial(back_kernel, slots),
        in_specs=[SMEM] + [VMEM] * (len(block_shapes) + 13),
        out_specs=[VMEM] * 7,
        out_shape=arrays(((tok, width), F32), *[((hw, tok), BF16)] * 4, *[((2 * rows, width + 128), BF16)] * 2),
        scratch_shapes=[
            pltpu.VMEM((tok, width), BF16),
            pltpu.VMEM((tok, n_experts), BF16),
            pltpu.VMEM((8, width), F32),
            pltpu.VMEM((width, 128), F32),
            pltpu.VMEM((slot_rows, width), BF16),
        ],
        compiler_params=params(),
        cost_estimate=SHORT,
    )(me_shard, *dx, places, routes, gates, after, gain_two, router_w, cotangent, w_o, normed_two, *mixed)
    grad_mixed = swap_all([gm0, gm1, gm2, gm3], "shard")
    sums = [
        core_sum(send, keep)
        for send, keep in ((send_second, keep_second), (send_first, keep_first), (send_wo, keep_wo))
    ]
    grad_mixed, sums = lax.optimization_barrier((grad_mixed, sums))
    second_sum, first_sum, wo_sum = sums
    second_sum, wo_sum = across_sum(second_sum), across_sum(wo_sum)

    *dqkv, bins = pl.pallas_call(
        functools.partial(attn_backward_kernel, heads),
        in_specs=[SMEM] * 2 + [VMEM] * 5 + [ANY] + [VMEM] * 4,
        out_specs=[VMEM] * 5,
        out_shape=arrays(*[((tok, wide), BF16)] * 4, ((NB, heads * SEG), F32)),
        scratch_shapes=[
            pltpu.VMEM((HW, tree_len), BF16),
            pltpu.VMEM((tree_len, HW), BF16),
            pltpu.VMEM((tree_len, HW), F32),
            pltpu.VMEM((tree_len, HW), F32),
            pltpu.VMEM((2, SEG, heads * SEG), F32),
            pltpu.VMEM((PROB_ROWS, 2 * heads * SEG), BF16),
            pltpu.SemaphoreType.DMA((SEGS // 2,)),
        ],
        compiler_params=params(),
        cost_estimate=BACKWARD,
    )(me_shard, parent_row, queries, keys, values, keys_t, raw, probs, *grad_mixed)
    dqkv_own = swap_all(dqkv, "shard")

    halving = [(1, 2, 4), (2, 1, 4)] if n_expert == 8 else []
    orders = [[0], [0]]
    for i, bits in enumerate(halving):
        for bit in reversed(bits):
            orders[i] = orders[i] + [rel | bit for rel in orders[i]]
    share = rows // len(orders[0])
    block_rows = [3 * share, 2 * share + -(-share // 16) * 8]
    parts = 2 if halving else 1
    out_rows = [count * len(orders[0]) // parts for count in block_rows for _ in range(parts)]
    halves = pl.pallas_call(
        functools.partial(column_grad_kernel, orders, heads),
        in_specs=[SMEM] + [VMEM] * 9,
        out_specs=[VMEM] * len(out_rows),
        out_shape=arrays(*[((count, wide), BF16) for count in out_rows]),
        scratch_shapes=[pltpu.VMEM((width, wide), F32), pltpu.VMEM((rows, width + 128), F32)],
        compiler_params=params(),
        cost_estimate=SHORT,
    )(me_expert if halving else jnp.zeros((1,), jnp.int32), bins, normed_one, *dqkv, *wo_sum)
    if halving:
        pairs = [halves[:2], halves[2:]]
        pairs, second_sum, returned = lax.optimization_barrier((pairs, second_sum, returned))
        for step in range(2):
            sums = [kept.astype(F32) + swap(sent, "expert", bits[step]).astype(F32) for (kept, sent), bits in zip(pairs, halving)]
            pairs = [jnp.split(part.astype(BF16), 2, axis=0) for part in sums]
        sums = [part for kept, sent in pairs for part in (kept, swap(sent, "expert", 4))]
    else:
        sums = lax.psum([part.astype(F32) for part in halves], "expert")
    *cols, more, table = pl.pallas_call(
        split_kernel,
        in_specs=[SMEM] + [VMEM] * len(sums),
        out_specs=[VMEM] * 6,
        out_shape=arrays(*[((share, 3 * hw), BF16)] * 4, ((share, width + 128), BF16), ((NB, wide - 3 * hw), F32)),
        scratch_shapes=[pltpu.VMEM((sum(block_rows), wide), F32)],
        compiler_params=params(),
        cost_estimate=SHORT,
    )(me_shard, *sums)
    table = table[:, :heads].T
    cols, dqkv_own[2] = lax.optimization_barrier((cols, dqkv_own[2]))
    cols, first_sum, dqkv_own = lax.optimization_barrier((swap_all(cols, "shard"), first_sum, dqkv_own))
    cols = pl.pallas_call(
        join_kernel,
        in_specs=[SMEM] + [VMEM] * 5,
        out_specs=VMEM,
        out_shape=jax.ShapeDtypeStruct((share, 4 * width + 128), BF16),
        compiler_params=params(),
        cost_estimate=SHORT,
    )(me_shard, *cols, more)
    grad_w_in = total_sum(across_sum(first_sum))[None]
    returned, second_sum, _ = lax.optimization_barrier((returned, second_sum, cols))
    grad_w_out = total_sum(second_sum)[None]
    output = pl.pallas_call(
        functools.partial(combine_kernel, slots),
        in_specs=[SMEM] + [VMEM] * 3,
        out_specs=VMEM,
        out_shape=jax.ShapeDtypeStruct((tok, width), BF16),
        scratch_shapes=[pltpu.VMEM((slot_rows, width), BF16)],
        compiler_params=params(),
        cost_estimate=SHORT,
    )(me_expert, returned, places, after)
    pieces = [cols]
    if halving:
        other = swap(cols, "expert", 4)
        dqkv_own, other = lax.optimization_barrier((dqkv_own, other))
        pieces = swap_all([jnp.concatenate([cols, other], axis=0)] * 4, "expert")
    grad_tokens = pl.pallas_call(
        final_kernel,
        in_specs=[SMEM] + [VMEM] * 8,
        out_specs=VMEM,
        out_shape=jax.ShapeDtypeStruct((tok, width), BF16),
        compiler_params=params(),
        cost_estimate=SHORT,
    )(me_shard, tokens, gain_one, grad_after, *dqkv_own, w_all)
    pieces, output, grad_tokens, grad_w_in, grad_w_out = lax.optimization_barrier(
        (pieces, output, grad_tokens, grad_w_in, grad_w_out)
    )
    grad_q, grad_k, grad_v, grad_wo, grad_router, grad_gains = pl.pallas_call(
        functools.partial(place_kernel, n_experts),
        in_specs=[SMEM] + [VMEM] * (4 + len(pieces)),
        out_specs=[VMEM] * 6,
        out_shape=arrays(*[((rows, width), F32)] * 4, ((n_experts, rows), F32), ((2, rows), F32)),
        scratch_shapes=[pltpu.VMEM((rows, 128), F32)],
        compiler_params=params(),
        cost_estimate=SHORT,
    )(
        me_expert if halving else jnp.zeros((1,), jnp.int32), w_query, w_key, w_value,
        gain_attn.astype(F32).reshape(1, rows), *pieces,
    )

    return (
        output, grad_tokens, grad_gains[0], grad_q, grad_k, grad_v, grad_wo, table, grad_gains[1], grad_router.T,
        grad_w_in, grad_w_out,
    )


def solution(mesh):
    both, shard = P(("expert", "shard"), None), P("shard", None)
    three = P("expert", "shard", None)
    return jax.shard_map(
        per_device,
        mesh=mesh,
        in_specs=(
            both, P("shard"), shard, shard, shard, shard, shard, P("shard"), shard, three, three, both,
            P("expert", None), both,
        ),
        out_specs=(both, both, P("shard"), shard, shard, shard, shard, shard, P("shard"), shard, three, three),
        check_vma=False,
    )
```
